32 devices in a mesh: dp: 8 (over z, y), ctx: 4 (over x, core).
Axes of the slice: x: 2, y: 2, z: 4, core: 2. Of those that a mesh axis runs over, the one named last changes fastest.
Arguments:
- tokens: bfloat16 [8, 1024, 2048], P('dp', 'ctx'), may hold values from -6 to 6
- lengths: int32 [8], P('dp'), may hold values from 256 to 1024, as said below
- ln_gain: bfloat16 [2048], P(('dp', 'ctx')), may hold values from 0.25 to 1.75
- ln_bias: bfloat16 [2048], P(('dp', 'ctx')), may hold values from -4 to 4
- w_qkv: bfloat16 [2048, 6144], P(('dp', 'ctx')), may hold values from -0.125 to 0.125
- b_qkv: bfloat16 [6144], P(('dp', 'ctx')), may hold values from -4 to 4
- w_out: bfloat16 [2048, 2048], P(('dp', 'ctx')), may hold values from -2 to 2
- b_out: bfloat16 [2048], P(('dp', 'ctx')), may hold values from -4 to 4
- w_fc1: bfloat16 [2048, 8192], P(('dp', 'ctx')), may hold values from -0.125 to 0.125
- b_fc1: bfloat16 [8192], P(('dp', 'ctx')), may hold values from -6 to 6
- w_fc2: bfloat16 [8192, 2048], P(('dp', 'ctx')), may hold values from -0.0625 to 0.0625
- b_fc2: bfloat16 [2048], P(('dp', 'ctx')), may hold values from -4 to 4
- cotangent: bfloat16 [8, 1024, 2048], P('dp', 'ctx'), may hold values from -6 to 6
Outputs:
- output: bfloat16 [8, 1024, 2048], P('dp', 'ctx')
- grad_input: bfloat16 [8, 1024, 2048], P('dp', 'ctx')
- grad_ln_gain: float32 [2048], P(('dp', 'ctx'))
- grad_ln_bias: float32 [2048], P(('dp', 'ctx'))
- grad_w_qkv: float32 [2048, 6144], P(('dp', 'ctx'))
- grad_b_qkv: float32 [6144], P(('dp', 'ctx'))
- grad_w_out: float32 [2048, 2048], P(('dp', 'ctx'))
- grad_b_out: float32 [2048], P(('dp', 'ctx'))
- grad_w_fc1: float32 [2048, 8192], P(('dp', 'ctx'))
- grad_b_fc1: float32 [8192], P(('dp', 'ctx'))
- grad_w_fc2: float32 [8192, 2048], P(('dp', 'ctx'))
- grad_b_fc2: float32 [2048], P(('dp', 'ctx'))
The draws below stay inside these ranges and needn't reach their ends.
Inputs may be any that keep to these rules, and one draw needn't show every extreme that they name: Each sequence's valid tokens are its first lengths; some sequence is 1024 long in every draw.
All inputs are finite; a program needn't handle non-finite values.
Results may differ from the reference program's by a relative error of at most 0.011.
Values may be sent and summed in bfloat16 or wider, within the bound.
A program may use at most 768 MiB of HBM per device.

```python
import math
import jax
import jax.numpy as jnp
from jax import lax

D = 2048
HEADS = 32
HEAD_DIM = 64
ROT = 32
FF = 8192
LEN = 1024
SEQS = 8


def draw_lengths(key, part):
    key = jax.random.fold_in(key, 11)
    pick_key, full_key, span_key = jax.random.split(key, 3)
    drawn = jax.random.randint(span_key, (SEQS,), LEN // 4, LEN + 1)
    long_mask = jax.random.randint(full_key, (SEQS,), 0, 2) == 1
    chosen = jax.random.randint(pick_key, (), 0, SEQS)
    long_mask = long_mask | (jnp.arange(SEQS) == chosen)
    return jnp.where(long_mask, LEN, drawn).astype(jnp.int32)


def with_spikes(values, own_key, source, target, blocks, factor):
    def block_of(position):
        return (jnp.arange(values.shape[position]) // (values.shape[position] // blocks)).reshape((-1,) + (1,) * (values.ndim - 1 - position))

    one_side = jax.random.permutation(own_key, blocks)[block_of(target)]
    other_side = (block_of(target) + blocks // 2) % blocks
    return jnp.where((block_of(source) == one_side) | (block_of(source) == other_side), factor * values, values)


def block_levels(rng, dims, cuts, least, top_value):
    loudness = 1.0
    for position, blocks in cuts:
        draws = jax.random.uniform(jax.random.fold_in(jax.random.fold_in(rng, 6), position), (blocks,), jnp.float32, least / len(cuts), top_value / len(cuts))
        loudness = loudness * jnp.repeat(jnp.exp(draws), dims[position] // blocks).reshape((-1,) + (1,) * (len(dims) - 1 - position))
    return loudness


def scatter_about(key, dims, deviation, reach, cuts=(), held_as=jnp.bfloat16):
    loudness = block_levels(key, dims, cuts, -0.22, 0.18) if cuts else 1.0
    values = jax.random.normal(key, dims, jnp.float32) * deviation * loudness
    return jnp.minimum(jnp.maximum(values, -reach), reach).astype(held_as)


def bell_draw_with(key, dims, spread, limit, pieces, heavy, kind=jnp.bfloat16):
    values = spread * jax.random.normal(key, dims, jnp.float32)
    if pieces:
        values = values * block_levels(key, dims, pieces, -0.22, 0.18)
    return jnp.clip(with_spikes(values, jax.random.fold_in(key, 3), *heavy), -limit, limit).astype(kind)


def setup_inputs(seed: int = 0) -> dict:
    key_of = jax.random.split(jax.random.key(seed), 14)
    tokens = scatter_about(key_of[0], (SEQS, LEN, D), 1.0, 6.0, ((0, 8), (1, 4)))
    lengths = draw_lengths(jax.random.fold_in(key_of[13], 71), 0)
    ln_gain = jnp.clip(1.0 + 0.15 * jax.random.normal(key_of[2], (D,), jnp.float32), 0.25, 1.75).astype(jnp.bfloat16)
    ln_bias = scatter_about(key_of[3], (D,), 0.3, 4.0, ((0, 32),))
    w_qkv = scatter_about(key_of[4], (D, 3 * D), D ** -0.5, 0.125, ((0, 32),))
    b_qkv = scatter_about(key_of[5], (3 * D,), 0.3, 4.0, ((0, 32),))
    w_out = scatter_about(key_of[6], (D, D), (4 * D // LEN) ** -0.5, 2.0, ((0, 32),))
    b_out = scatter_about(key_of[7], (D,), 0.3, 4.0, ((0, 32),))
    w_fc1 = scatter_about(key_of[8], (D, FF), D ** -0.5, 0.125, ((0, 32),))
    b_fc1 = scatter_about(key_of[9], (FF,), 0.5, 6.0, ((0, 32),))
    w_fc2 = scatter_about(key_of[10], (FF, D), FF ** -0.5, 0.0625, ((0, 32),))
    b_fc2 = scatter_about(key_of[11], (D,), 0.3, 4.0, ((0, 32),))
    cotangent = bell_draw_with(key_of[12], (SEQS, LEN, D), 1.0, 6.0, ((0, 8), (1, 4)), (0, 2, 8, 2.0))
    return dict(tokens=tokens, lengths=lengths, ln_gain=ln_gain, ln_bias=ln_bias, w_qkv=w_qkv, b_qkv=b_qkv, w_out=w_out, b_out=b_out, w_fc1=w_fc1, b_fc1=b_fc1, w_fc2=w_fc2, b_fc2=b_fc2, cotangent=cotangent)


@jax.custom_vjp
def low(v):
    return lax.optimization_barrier(v.astype(jnp.bfloat16)).astype(jnp.float32)

@jax.custom_vjp
def low_back(v):
    return v

def low_keep(v):
    return (low(v), None)

def low_pass(kept, grad):
    return (grad,)

def back_keep(v):
    return (v, None)

def back_low(kept, grad):
    return (low(grad),)
low.defvjp(low_keep, low_pass)
low_back.defvjp(back_keep, back_low)
eps_norm = 1e-05
gelu_coef = 0.7978845608028654

def gelu_tanh(values):
    return 0.5 * values * (1.0 + jnp.tanh(gelu_coef * (values + 0.044715 * values * values * values)))

def matmul_high(left_side, right_side):
    return jnp.dot(left_side, right_side, precision=lax.Precision.HIGHEST, preferred_element_type=jnp.float32)

def rotary_angles(positions, rot_dims):
    half_dims = rot_dims // 2
    freq_index = jnp.arange(half_dims, dtype=jnp.float32)
    inv_freq = jnp.exp(-math.log(10000.0) * 2.0 * freq_index / rot_dims)
    return positions.astype(jnp.float32)[:, None] * inv_freq[None, :]

def rotary(vectors, angles):
    half_dims = angles.shape[-1]
    cosines = jnp.cos(angles)[:, None, :]
    sine_vals = jnp.sin(angles)[:, None, :]
    leading = vectors[..., :half_dims]
    trailing = vectors[..., half_dims:2 * half_dims]
    return jnp.concatenate([leading * cosines - trailing * sine_vals, trailing * cosines + leading * sine_vals, vectors[..., 2 * half_dims:]], axis=-1)

def attend_one(packed):
    queries, key_rows, values, length = packed
    scores = low_back(jnp.einsum('qhd,khd->hqk', queries, key_rows, precision=lax.Precision.HIGHEST))
    places = jnp.arange(LEN, dtype=jnp.int32)
    allowed = (places[None, :] <= places[:, None]) & (places[None, :] < length)
    scores = jnp.where(allowed[None], scores, -1e+30)
    row_max = lax.optimization_barrier(jnp.max(scores, axis=-1, keepdims=True))
    exponent = jnp.exp(scores - row_max)
    probability = low(exponent / lax.optimization_barrier(jnp.sum(exponent, axis=-1, keepdims=True)))
    return jnp.einsum('hqk,khd->qhd', probability, values, precision=lax.Precision.HIGHEST)

def block_forward(inputs, weights, lengths_now):
    ln_gain, ln_bias, w_qkv, b_qkv, w_out, b_out, w_fc1, b_fc1, w_fc2, b_fc2 = weights
    group_size = inputs.shape[0]
    average = lax.optimization_barrier(jnp.mean(inputs, axis=-1, keepdims=True))
    centered = inputs - average
    variance = lax.optimization_barrier(jnp.mean(centered * centered, axis=-1, keepdims=True))
    normed = centered * lax.rsqrt(variance + eps_norm)
    hidden = low(normed * ln_gain + ln_bias).reshape(-1, D)
    qkv_proj = low_back(matmul_high(hidden, w_qkv) + b_qkv).reshape(group_size, LEN, 3, HEADS, HEAD_DIM)
    angles = rotary_angles(jnp.arange(LEN, dtype=jnp.int32), ROT)
    queries = low(rotary(qkv_proj[:, :, 0], angles) * 0.125)
    key_rows = low(rotary(qkv_proj[:, :, 1], angles))
    values = low(qkv_proj[:, :, 2])
    attention = lax.map(jax.checkpoint(attend_one), (queries, key_rows, values, lengths_now))
    attn_mixed = low(low_back(attention.reshape(-1, D)))
    up_proj = low_back(matmul_high(hidden, w_fc1) + b_fc1)
    activated = low(gelu_tanh(up_proj))
    branch = matmul_high(attn_mixed, w_out) + b_out + matmul_high(activated, w_fc2) + b_fc2
    return inputs + branch.reshape(group_size, LEN, D)

def reference(tokens, lengths, ln_gain, ln_bias, w_qkv, b_qkv, w_out, b_out, w_fc1, b_fc1, w_fc2, b_fc2, cotangent):
    parameters = tuple((weight.astype(jnp.float32) for weight in (ln_gain, ln_bias, w_qkv, b_qkv, w_out, b_out, w_fc1, b_fc1, w_fc2, b_fc2)))
    group_size = math.gcd(SEQS, 4)
    batches = SEQS // group_size
    places = jnp.arange(LEN, dtype=jnp.int32)
    live_mask = (places[None, :] < lengths[:, None]).astype(jnp.float32)
    masked_cot = cotangent.astype(jnp.float32) * live_mask[:, :, None]
    grouped = (tokens.astype(jnp.float32).reshape(batches, group_size, LEN, D), lengths.reshape(batches, group_size), masked_cot.reshape(batches, group_size, LEN, D))

    def step(summed, scan_item):
        inputs, lengths_now, cot_now = scan_item

        def forward(inputs_now, *weights):
            return block_forward(inputs_now, weights, lengths_now)
        result, pullback = jax.vjp(forward, inputs, *parameters)
        gradients = pullback(cot_now)
        summed = tuple((running + addend for running, addend in zip(summed, gradients[1:])))
        return (summed, (result.astype(jnp.bfloat16), gradients[0].astype(jnp.bfloat16)))
    initial = tuple((jnp.zeros_like(weight) for weight in parameters))
    summed, (results, input_grads) = lax.scan(step, initial, grouped)
    return (results.reshape(SEQS, LEN, D), input_grads.reshape(SEQS, LEN, D), summed[0], summed[1], summed[2], summed[3], summed[4], summed[5], summed[6], summed[7], summed[8], summed[9])
```

```python
import math

import jax
import jax.numpy as jnp
import numpy as np
from jax import lax
from jax.sharding import PartitionSpec as P

HEAD_DIM = 64
ROT = 32


eps_norm = 1e-05
gelu_coef = 0.7978845608028654


def gelu_tanh(values):
    return (
        0.5 * values * (1.0 + jnp.tanh(gelu_coef * (values + 0.044715 * values * values * values)))
    )


def rotary_angles(positions, rot_dims):
    half_dims = rot_dims // 2
    freq_index = jnp.arange(half_dims, dtype=jnp.float32)
    inv_freq = jnp.exp(-math.log(10000.0) * 2.0 * freq_index / rot_dims)
    return positions.astype(jnp.float32)[:, None] * inv_freq[None, :]


def rotary(vectors, angles):
    half_dims = angles.shape[-1]
    cosines = jnp.cos(angles)[:, None, :]
    sine_vals = jnp.sin(angles)[:, None, :]
    leading = vectors[..., :half_dims]
    trailing = vectors[..., half_dims : 2 * half_dims]
    return jnp.concatenate(
        [
            leading * cosines - trailing * sine_vals,
            trailing * cosines + leading * sine_vals,
            vectors[..., 2 * half_dims :],
        ],
        axis=-1,
    )


def rotary_back(gradients, angles):
    half_dims = angles.shape[-1]
    cosines = jnp.cos(angles)[:, None, :]
    sine_vals = jnp.sin(angles)[:, None, :]
    leading = gradients[..., :half_dims]
    trailing = gradients[..., half_dims : 2 * half_dims]
    return jnp.concatenate(
        [
            leading * cosines + trailing * sine_vals,
            trailing * cosines - leading * sine_vals,
            gradients[..., 2 * half_dims :],
        ],
        axis=-1,
    )


def masked_scores(queries, key_rows, places, length):
    scores = jnp.einsum("qhd,khd->hqk", queries, key_rows, preferred_element_type=jnp.float32)
    key_places = jnp.arange(key_rows.shape[0], dtype=jnp.int32)
    allowed = (key_places[None, :] <= places[:, None]) & (key_places[None, :] < length)
    return jnp.where(allowed[None], scores, -1e30)


def on_device(
    tokens,
    lengths,
    ln_gain,
    ln_bias,
    w_qkv,
    b_qkv,
    w_out,
    b_out,
    w_fc1,
    b_fc1,
    w_fc2,
    b_fc2,
    cotangent,
):
    seq_count, local_len, model_width = tokens.shape
    shard_rows = w_qkv.shape[0]
    hidden_ratio = w_fc1.shape[1] // model_width
    head_count = model_width // HEAD_DIM
    token_count = seq_count * local_len
    places = lax.axis_index("ctx") * local_len + jnp.arange(local_len, dtype=jnp.int32)
    angles = rotary_angles(places, ROT)
    live_mask = places[None, :] < lengths[:, None]
    inputs = tokens.astype(jnp.float32).reshape(token_count, model_width)
    average = jnp.mean(inputs, axis=-1, keepdims=True)
    centered = inputs - average
    variance = jnp.mean(centered * centered, axis=-1, keepdims=True)
    inv_std = lax.rsqrt(variance + eps_norm)
    normed = centered * inv_std
    qkv_bias_rows = b_qkv.reshape(shard_rows, 3)
    fc1_bias_rows = b_fc1.reshape(shard_rows, hidden_ratio)
    fc2_rows = w_fc2.reshape(shard_rows, hidden_ratio * model_width)
    inner_full = (
        lax.all_gather(w_qkv, ("dp", "ctx"), axis=0, tiled=True),
        lax.all_gather(w_fc1, ("dp", "ctx"), axis=0, tiled=True),
        lax.all_gather(ln_gain, ("dp", "ctx"), axis=0, tiled=True),
        lax.all_gather(ln_bias, ("dp", "ctx"), axis=0, tiled=True),
        lax.all_gather(qkv_bias_rows, ("dp", "ctx"), axis=0, tiled=True),
        lax.all_gather(fc1_bias_rows, ("dp", "ctx"), axis=0, tiled=True),
    )
    gain_full = inner_full[2].astype(jnp.float32)
    shift_full = inner_full[3].astype(jnp.float32)
    hidden = (normed * gain_full + shift_full).astype(jnp.bfloat16)
    qkv_acc = jnp.dot(hidden, inner_full[0], preferred_element_type=jnp.float32)
    up_acc = jnp.dot(hidden, inner_full[1], preferred_element_type=jnp.float32)
    qkv_bias = inner_full[4].reshape(-1).astype(jnp.float32)
    fc1_bias = inner_full[5].reshape(-1).astype(jnp.float32)
    qkv_proj = (qkv_acc + qkv_bias).reshape(seq_count, local_len, 3, head_count, HEAD_DIM)
    queries = (rotary(qkv_proj[:, :, 0], angles) * 0.125).astype(jnp.bfloat16)
    key_local = (
        rotary(qkv_proj[:, :, 1], angles)
        .astype(jnp.bfloat16)
        .reshape(seq_count, local_len, model_width)
    )
    value_local = qkv_proj[:, :, 2].astype(jnp.bfloat16).reshape(seq_count, local_len, model_width)
    key_full, value_full = (
        lax.all_gather(key_local, "ctx", axis=1, tiled=True),
        lax.all_gather(value_local, "ctx", axis=1, tiled=True),
    )
    total_len = key_full.shape[1]

    def attend_forward(packed):
        query_seq, key_seq, value_seq, length = packed
        key_heads = key_seq.reshape(total_len, head_count, HEAD_DIM)
        value_heads = value_seq.reshape(total_len, head_count, HEAD_DIM)
        scores = masked_scores(query_seq, key_heads, places, length)
        row_max = jnp.max(scores, axis=-1, keepdims=True)
        exponent = jnp.exp(scores - row_max)
        row_sum = jnp.sum(exponent, axis=-1, keepdims=True)
        probability = (exponent / row_sum).astype(jnp.bfloat16)
        attended = jnp.einsum(
            "hqk,khd->qhd", probability, value_heads, preferred_element_type=jnp.float32
        )
        log_total = (row_max + jnp.log(row_sum))[..., 0]
        return (attended.reshape(local_len, model_width).astype(jnp.bfloat16), log_total)

    attn_seq, log_totals = lax.map(attend_forward, (queries, key_full, value_full, lengths))
    attn_mixed = attn_seq.reshape(token_count, model_width)
    up_proj = up_acc + fc1_bias
    activated = gelu_tanh(up_proj).astype(jnp.bfloat16)
    outer_full = (
        lax.all_gather(w_out, ("dp", "ctx"), axis=0, tiled=True),
        lax.all_gather(fc2_rows, ("dp", "ctx"), axis=0, tiled=True),
        lax.all_gather(b_out, ("dp", "ctx"), axis=0, tiled=True),
        lax.all_gather(b_fc2, ("dp", "ctx"), axis=0, tiled=True),
    )
    branch = jnp.dot(attn_mixed, outer_full[0], preferred_element_type=jnp.float32) + jnp.dot(
        activated,
        outer_full[1].reshape(hidden_ratio * model_width, model_width),
        preferred_element_type=jnp.float32,
    )
    out_bias = outer_full[2].astype(jnp.float32)
    fc2_bias = outer_full[3].astype(jnp.float32)
    output = (
        (inputs + branch + out_bias + fc2_bias)
        .astype(jnp.bfloat16)
        .reshape(seq_count, local_len, model_width)
    )
    grad_out = jnp.where(live_mask[:, :, None], cotangent, jnp.zeros((), jnp.bfloat16)).reshape(
        token_count, model_width
    )
    out_back, fc2_back = (
        lax.all_gather(w_out, ("dp", "ctx"), axis=0, tiled=True),
        lax.all_gather(fc2_rows, ("dp", "ctx"), axis=0, tiled=True),
    )
    fc2_matrix = fc2_back.reshape(hidden_ratio * model_width, model_width)
    grad_mixed = jnp.einsum(
        "td,kd->tk", grad_out, out_back, preferred_element_type=jnp.float32
    ).astype(jnp.bfloat16)
    grad_act = jnp.einsum("td,kd->tk", grad_out, fc2_matrix, preferred_element_type=jnp.float32)
    gelu_value, gelu_pull = jax.vjp(gelu_tanh, up_proj)
    grad_up = gelu_pull(grad_act)[0].astype(jnp.bfloat16)
    key_back, value_back = (
        lax.all_gather(key_local, "ctx", axis=1, tiled=True),
        lax.all_gather(value_local, "ctx", axis=1, tiled=True),
    )

    def attend_backward(packed):
        query_seq, key_seq, value_seq, grad_seq, log_total, length = packed
        key_heads = key_seq.reshape(total_len, head_count, HEAD_DIM)
        value_heads = value_seq.reshape(total_len, head_count, HEAD_DIM)
        grad_heads = grad_seq.reshape(local_len, head_count, HEAD_DIM)
        scores = masked_scores(query_seq, key_heads, places, length)
        probability = jnp.exp(scores - log_total[:, :, None])
        grad_probs = jnp.einsum(
            "qhd,khd->hqk", grad_heads, value_heads, preferred_element_type=jnp.float32
        )
        inner = jnp.sum(probability * grad_probs, axis=-1, keepdims=True)
        grad_scores = (probability * (grad_probs - inner)).astype(jnp.bfloat16)
        grad_query = jnp.einsum(
            "hqk,khd->qhd", grad_scores, key_heads, preferred_element_type=jnp.float32
        )
        grad_keys = jnp.einsum(
            "hqk,qhd->khd", grad_scores, query_seq, preferred_element_type=jnp.float32
        )
        grad_values = jnp.einsum(
            "hqk,qhd->khd",
            probability.astype(jnp.bfloat16),
            grad_heads,
            preferred_element_type=jnp.float32,
        )
        return (
            grad_query,
            grad_keys.reshape(total_len, model_width),
            grad_values.reshape(total_len, model_width),
        )

    grad_query, grad_keys_all, grad_values_all = lax.map(
        attend_backward,
        (
            queries,
            key_back,
            value_back,
            grad_mixed.reshape(seq_count, local_len, model_width),
            log_totals,
            lengths,
        ),
    )
    grad_keys_own, grad_values_own = (
        lax.psum_scatter(grad_keys_all, "ctx", scatter_dimension=1, tiled=True),
        lax.psum_scatter(grad_values_all, "ctx", scatter_dimension=1, tiled=True),
    )
    grad_query_pre = rotary_back(grad_query * 0.125, angles).reshape(token_count, model_width)
    grad_keys_pre = rotary_back(
        grad_keys_own.reshape(seq_count, local_len, head_count, HEAD_DIM), angles
    ).reshape(token_count, model_width)
    grad_qkv = jnp.concatenate(
        [grad_query_pre, grad_keys_pre, grad_values_own.reshape(token_count, model_width)], axis=-1
    ).astype(jnp.bfloat16)
    qkv_matrix, fc1_matrix = (
        lax.all_gather(w_qkv, ("dp", "ctx"), axis=0, tiled=True),
        lax.all_gather(w_fc1, ("dp", "ctx"), axis=0, tiled=True),
    )
    grad_hidden = jnp.einsum(
        "tj,dj->td", grad_qkv, qkv_matrix, preferred_element_type=jnp.float32
    ) + jnp.einsum("tj,dj->td", grad_up, fc1_matrix, preferred_element_type=jnp.float32)
    gain_term = jnp.sum(grad_hidden * normed, axis=0)
    shift_term = jnp.sum(grad_hidden, axis=0)
    grad_norm = grad_hidden * gain_full
    grad_input = grad_out.astype(jnp.float32) + inv_std * (
        grad_norm
        - jnp.mean(grad_norm, axis=-1, keepdims=True)
        - normed * jnp.mean(grad_norm * normed, axis=-1, keepdims=True)
    )
    grad_input = grad_input.astype(jnp.bfloat16).reshape(seq_count, local_len, model_width)
    wout_term = jnp.einsum("tk,td->kd", attn_mixed, grad_out, preferred_element_type=jnp.float32)
    wfc2_term = jnp.einsum(
        "tk,td->kd", activated, grad_out, preferred_element_type=jnp.float32
    ).reshape(model_width, hidden_ratio * model_width)
    bias_term = jnp.sum(grad_out, axis=0, dtype=jnp.float32)
    bqkv_term = jnp.sum(grad_qkv, axis=0, dtype=jnp.float32).reshape(model_width, 3)
    bfc1_term = jnp.sum(grad_up, axis=0, dtype=jnp.float32).reshape(model_width, hidden_ratio)
    grad_wout, grad_wfc2, grad_bias, grad_gain, grad_shift, grad_bqkv, grad_bfc1 = (
        lax.psum_scatter(wout_term, ("dp", "ctx"), scatter_dimension=0, tiled=True),
        lax.psum_scatter(wfc2_term, ("dp", "ctx"), scatter_dimension=0, tiled=True),
        lax.psum_scatter(bias_term, ("dp", "ctx"), scatter_dimension=0, tiled=True),
        lax.psum_scatter(gain_term, ("dp", "ctx"), scatter_dimension=0, tiled=True),
        lax.psum_scatter(shift_term, ("dp", "ctx"), scatter_dimension=0, tiled=True),
        lax.psum_scatter(bqkv_term, ("dp", "ctx"), scatter_dimension=0, tiled=True),
        lax.psum_scatter(bfc1_term, ("dp", "ctx"), scatter_dimension=0, tiled=True),
    )
    qkv_part = jnp.einsum("tk,tj->kj", hidden, grad_qkv, preferred_element_type=jnp.float32)
    fc1_part = jnp.einsum("tk,tj->kj", hidden, grad_up, preferred_element_type=jnp.float32)
    inner_sum = lax.psum_scatter(
        jnp.concatenate([qkv_part, fc1_part], axis=1),
        ("dp", "ctx"),
        scatter_dimension=0,
        tiled=True,
    )
    grad_wqkv = inner_sum[:, : 3 * model_width]
    grad_wfc1 = inner_sum[:, 3 * model_width :]
    return (
        output,
        grad_input,
        grad_gain,
        grad_shift,
        grad_wqkv,
        grad_bqkv.reshape(-1),
        grad_wout,
        grad_bias,
        grad_wfc1,
        grad_bfc1.reshape(-1),
        grad_wfc2.reshape(shard_rows * hidden_ratio, model_width),
        grad_bias,
    )


def general_solution(mesh):
    placed = (
        P("dp", "ctx", None),
        P("dp"),
        P(("dp", "ctx")),
        P(("dp", "ctx")),
        P(("dp", "ctx"), None),
        P(("dp", "ctx")),
        P(("dp", "ctx"), None),
        P(("dp", "ctx")),
        P(("dp", "ctx"), None),
        P(("dp", "ctx")),
        P(("dp", "ctx"), None),
        P(("dp", "ctx")),
        P("dp", "ctx", None),
    )
    return jax.shard_map(
        on_device,
        mesh=mesh,
        in_specs=placed,
        out_specs=(
            P("dp", "ctx", None),
            P("dp", "ctx", None),
            P(("dp", "ctx")),
            P(("dp", "ctx")),
            P(("dp", "ctx"), None),
            P(("dp", "ctx")),
            P(("dp", "ctx"), None),
            P(("dp", "ctx")),
            P(("dp", "ctx"), None),
            P(("dp", "ctx")),
            P(("dp", "ctx"), None),
            P(("dp", "ctx")),
        ),
        check_vma=False,
    )


FINE = ("zh", "zl", "y", "x", "c")
ROWS_AXES = ("zl", "x", "c")


def swap(values, axis):
    return lax.ppermute(values, axis, [(0, 1), (1, 0)])


def flip_if(values, dim, flag):
    return jnp.where(flag, jnp.flip(values, dim), values)


def gather_blocks(own):
    across = swap(own, "zh")
    beside = swap(own, "y")
    both = swap(across, "y")
    return own, beside, across, both


def reduce_blocks(blocks):
    own, beside, across, both = blocks
    got_beside = swap(beside, "y")
    got_both = swap(both, "y")
    passed = (across.astype(jnp.float32) + got_both.astype(jnp.float32)).astype(jnp.bfloat16)
    got = swap(passed, "zh")
    return own.astype(jnp.float32) + got_beside.astype(jnp.float32) + got.astype(jnp.float32)


def by_place(blocks, zh, y):
    first, second, third, fourth = blocks
    a, b = jnp.where(y == 1, second, first), jnp.where(y == 1, first, second)
    c, d = jnp.where(y == 1, fourth, third), jnp.where(y == 1, third, fourth)
    return (
        jnp.where(zh == 1, c, a),
        jnp.where(zh == 1, d, b),
        jnp.where(zh == 1, a, c),
        jnp.where(zh == 1, b, d),
    )


def dot(left, right, dims):
    return lax.dot_general(left, right, (dims, ((), ())), preferred_element_type=jnp.float32)


def split_device(
    tokens,
    lengths,
    ln_gain,
    ln_bias,
    w_qkv,
    b_qkv,
    w_out,
    b_out,
    w_fc1,
    b_fc1,
    w_fc2,
    b_fc2,
    cotangent,
):
    bf16, f32 = jnp.bfloat16, jnp.float32
    zh, zl, y, x, c = (lax.axis_index(name) for name in FINE)
    place = (zl * 2 + x) * 2 + c
    _, local_len, width = tokens.shape
    rows = w_qkv.shape[0]
    ff_rows = w_fc2.shape[0]
    pieces = 4
    total_len = local_len * pieces
    heads = 4
    own_width = heads * HEAD_DIM

    small = jnp.concatenate([ln_gain, ln_bias, b_qkv, b_out, b_fc1, b_fc2])
    small_all = lax.all_gather(small[None], FINE, axis=0, tiled=True).astype(f32)
    ends = np.cumsum([rows, rows, 3 * rows, rows, ff_rows, rows])
    gain_all, shift_all, bqkv_all, bout_all, bfc1_all, bfc2_all = (
        part.reshape(-1) for part in jnp.split(small_all, ends[:-1], axis=1)
    )
    length_pair = lax.all_gather(lengths, "zl", axis=0, tiled=True)

    def own_columns(weight, shape, order):
        spread = weight.reshape((rows,) + shape).transpose(order)
        spread = spread.reshape(8, rows, -1)
        return lax.all_to_all(spread, ROWS_AXES, 0, 0, tiled=True).reshape(8 * rows, -1)

    qkv_own = own_columns(w_qkv, (3, 2, 2, 2, 2, 2, HEAD_DIM), (3, 5, 6, 0, 1, 2, 4, 7))
    fc1_own = own_columns(w_fc1, (2, 2, 2, 2, 2, ff_rows), (2, 4, 5, 0, 1, 3, 6))
    out_blocks = by_place(gather_blocks(w_out), zh, y)
    qkv_blocks = gather_blocks(qkv_own)
    fc2_blocks = by_place(gather_blocks(w_fc2), zh, y)
    fc1_blocks = gather_blocks(fc1_own)
    out_mat = jnp.concatenate(out_blocks, axis=0)
    fc2_mat = jnp.concatenate(fc2_blocks, axis=0)
    qkv_mat = jnp.concatenate(qkv_blocks, axis=0)
    fc1_mat = jnp.concatenate(fc1_blocks, axis=0)

    inputs = tokens[0].astype(f32)
    average = jnp.mean(inputs, axis=-1, keepdims=True)
    centered = inputs - average
    variance = jnp.mean(centered * centered, axis=-1, keepdims=True)
    inv_std = lax.rsqrt(variance + eps_norm)
    normed = centered * inv_std
    hidden_own = (normed * gain_all + shift_all).astype(bf16)

    def mixed_order(values):
        v = values.reshape(-1, 2, 2, 2, 4, rows).transpose(0, 1, 3, 2, 4, 5)
        v = flip_if(flip_if(v, 1, zh == 1), 2, y == 1)
        return v.reshape(values.shape)

    def plain_order(values):
        v = values.reshape(-1, 2, 2, 2, 4, rows)
        v = flip_if(flip_if(v, 1, zh == 1), 2, y == 1)
        return v.transpose(0, 1, 3, 2, 4, 5).reshape(values.shape)

    hidden = lax.all_gather(mixed_order(hidden_own), ROWS_AXES, axis=0, tiled=True)
    places = (x * 2 + c) * local_len + jnp.arange(local_len, dtype=jnp.int32)
    grad_own = jnp.where((places < lengths[0])[:, None], cotangent[0], jnp.zeros((), bf16))
    grad_out = lax.all_gather(grad_own, ROWS_AXES, axis=0, tiled=True)

    bqkv = lax.dynamic_index_in_dim(
        bqkv_all.reshape(3, 2, 2, 2, 4, HEAD_DIM).transpose(2, 4, 0, 1, 3, 5).reshape(8, -1),
        place,
        keepdims=False,
    )
    bfc1 = lax.dynamic_index_in_dim(
        bfc1_all.reshape(2, 2, 2, 4, ff_rows).transpose(1, 3, 0, 2, 4).reshape(8, -1),
        place,
        keepdims=False,
    )

    angles = rotary_angles(jnp.arange(total_len, dtype=jnp.int32), ROT)
    qkv = dot(hidden, qkv_mat, ((1,), (0,))) + bqkv
    qkv = qkv.reshape(2, total_len, 3, heads, HEAD_DIM)
    turn = jax.vmap(lambda v: rotary(v, angles))
    queries = (turn(qkv[:, :, 0]) * 0.125).astype(bf16)
    key_rows = turn(qkv[:, :, 1]).astype(bf16)
    values = qkv[:, :, 2].astype(bf16)
    all_places = jnp.arange(total_len, dtype=jnp.int32)

    def attend_forward(packed):
        query_seq, key_seq, value_seq, length = packed
        scores = masked_scores(query_seq, key_seq, all_places, length)
        row_max = jnp.max(scores, axis=-1, keepdims=True)
        exponent = jnp.exp(scores - row_max)
        row_sum = jnp.sum(exponent, axis=-1, keepdims=True)
        probability = (exponent / row_sum).astype(bf16)
        attended = jnp.einsum("hqk,khd->qhd", probability, value_seq, preferred_element_type=f32)
        return attended.astype(bf16), (row_max + jnp.log(row_sum))[..., 0]

    attended, log_totals = lax.map(attend_forward, (queries, key_rows, values, length_pair))
    attn_mixed = attended.reshape(2 * total_len, own_width)

    up_proj = dot(hidden, fc1_mat, ((1,), (0,))) + bfc1
    activated = gelu_tanh(up_proj).astype(bf16)
    branch = dot(attn_mixed, out_mat, ((1,), (0,))) + dot(activated, fc2_mat, ((1,), (0,)))
    branch_own = lax.psum_scatter(
        branch.astype(bf16), ROWS_AXES, scatter_dimension=0, tiled=True
    ).astype(f32)
    output = (inputs + branch_own + bout_all + bfc2_all).astype(bf16)[None]

    grad_mixed = dot(grad_out, out_mat, ((1,), (1,))).astype(bf16)
    grad_act = dot(grad_out, fc2_mat, ((1,), (1,)))
    _, gelu_pull = jax.vjp(gelu_tanh, up_proj)
    grad_up = gelu_pull(grad_act)[0].astype(bf16)

    def attend_backward(packed):
        query_seq, key_seq, value_seq, grad_heads, log_total, length = packed
        scores = masked_scores(query_seq, key_seq, all_places, length)
        probability = jnp.exp(scores - log_total[:, :, None])
        grad_probs = jnp.einsum("qhd,khd->hqk", grad_heads, value_seq, preferred_element_type=f32)
        inner = jnp.sum(probability * grad_probs, axis=-1, keepdims=True)
        grad_scores = (probability * (grad_probs - inner)).astype(bf16)
        grad_query = jnp.einsum("hqk,khd->qhd", grad_scores, key_seq, preferred_element_type=f32)
        grad_keys = jnp.einsum("hqk,qhd->khd", grad_scores, query_seq, preferred_element_type=f32)
        grad_values = jnp.einsum(
            "hqk,qhd->khd", probability.astype(bf16), grad_heads, preferred_element_type=f32
        )
        return grad_query, grad_keys, grad_values

    grad_query, grad_keys, grad_values = lax.map(
        attend_backward,
        (
            queries,
            key_rows,
            values,
            grad_mixed.reshape(2, total_len, heads, HEAD_DIM),
            log_totals,
            length_pair,
        ),
    )
    turn_back = jax.vmap(lambda v: rotary_back(v, angles))
    grad_qkv = (
        jnp.stack([turn_back(grad_query * 0.125), turn_back(grad_keys), grad_values], axis=2)
        .reshape(2 * total_len, 3 * own_width)
        .astype(bf16)
    )

    grad_hidden = dot(grad_qkv, qkv_mat, ((1,), (1,))) + dot(grad_up, fc1_mat, ((1,), (1,)))
    grad_hidden_own = plain_order(
        lax.psum_scatter(grad_hidden.astype(bf16), ROWS_AXES, scatter_dimension=0, tiled=True)
    ).astype(f32)
    grad_norm = grad_hidden_own * gain_all
    grad_input = grad_own.astype(f32) + inv_std * (
        grad_norm
        - jnp.mean(grad_norm, axis=-1, keepdims=True)
        - normed * jnp.mean(grad_norm * normed, axis=-1, keepdims=True)
    )
    grad_input = grad_input.astype(bf16)[None]

    def place_blocks(values):
        return by_place(jnp.split(values, 4, axis=0), zh, y)

    fc2_part = dot(activated, grad_out, ((0,), (0,))).astype(bf16)
    grad_fc2 = reduce_blocks(place_blocks(fc2_part))
    fc1_part = dot(hidden, grad_up, ((0,), (0,))).astype(bf16)
    fc1_total = reduce_blocks(jnp.split(fc1_part, 4, axis=0)).astype(bf16)
    out_part = dot(attn_mixed, grad_out, ((0,), (0,))).astype(bf16)
    grad_wout = reduce_blocks(place_blocks(out_part))
    qkv_part = dot(hidden, grad_qkv, ((0,), (0,))).astype(bf16)
    qkv_total = reduce_blocks(jnp.split(qkv_part, 4, axis=0)).astype(bf16)

    def all_columns(total, shape, order, out_width):
        spread = lax.all_to_all(total.reshape(8, rows, -1), ROWS_AXES, 0, 0, tiled=True)
        spread = spread.reshape((2, 2, 2, rows) + shape).transpose(order)
        return spread.reshape(rows, out_width).astype(f32)

    grad_wfc1 = all_columns(fc1_total, (2, 2, ff_rows), (3, 4, 0, 5, 1, 2, 6), w_fc1.shape[1])
    grad_wqkv = all_columns(
        qkv_total, (3, 2, 2, HEAD_DIM), (3, 4, 5, 0, 6, 1, 2, 7), w_qkv.shape[1]
    )

    mine = (jnp.arange(8) == place).astype(f32)
    bqkv_term = (
        (jnp.sum(grad_qkv, axis=0, dtype=f32).reshape(1, 3, 2, 2, HEAD_DIM) * mine[:, None, None, None, None])
        .reshape(2, 4, 3, 2, 2, HEAD_DIM)
        .transpose(2, 3, 0, 4, 1, 5)
        .reshape(-1)
    )
    bfc1_term = (
        (jnp.sum(grad_up, axis=0, dtype=f32).reshape(1, 2, 2, ff_rows) * mine[:, None, None, None])
        .reshape(2, 4, 2, 2, ff_rows)
        .transpose(2, 0, 3, 1, 4)
        .reshape(-1)
    )
    bias_term = jnp.sum(grad_own, axis=0, dtype=f32)
    gain_term = jnp.sum(grad_hidden_own * normed, axis=0)
    shift_term = jnp.sum(grad_hidden_own, axis=0)
    terms = jnp.concatenate(
        [v.reshape(32, -1) for v in (bqkv_term, bfc1_term, bias_term, gain_term, shift_term)], axis=1
    )
    sums = lax.psum_scatter(terms, FINE, scatter_dimension=0, tiled=True)[0]
    grad_bqkv, grad_bfc1, grad_bias, grad_gain, grad_shift = jnp.split(
        sums, np.cumsum([3 * rows, ff_rows, rows, rows])
    )
    return (
        output,
        grad_input,
        grad_gain,
        grad_shift,
        grad_wqkv,
        grad_bqkv,
        grad_wout,
        grad_bias,
        grad_wfc1,
        grad_bfc1,
        grad_fc2,
        grad_bias,
    )


def fine_mesh(mesh):
    return jax.sharding.Mesh(mesh.devices.reshape(2, 2, 2, 2, 2), FINE)


def fine_solution(mesh):
    everyone, seqs, parts = FINE, ("zh", "zl", "y"), ("x", "c")
    placed = (
        P(seqs, parts, None),
        P(seqs),
        P(everyone),
        P(everyone),
        P(everyone, None),
        P(everyone),
        P(everyone, None),
        P(everyone),
        P(everyone, None),
        P(everyone),
        P(everyone, None),
        P(everyone),
        P(seqs, parts, None),
    )
    given = (
        P(seqs, parts, None),
        P(seqs, parts, None),
        P(everyone),
        P(everyone),
        P(everyone, None),
        P(everyone),
        P(everyone, None),
        P(everyone),
        P(everyone, None),
        P(everyone),
        P(everyone, None),
        P(everyone),
    )
    return jax.shard_map(
        split_device, mesh=fine_mesh(mesh), in_specs=placed, out_specs=given, check_vma=False
    )


def solution(mesh):
    if mesh.shape["dp"] == 8 and mesh.shape["ctx"] == 4:
        return fine_solution(mesh)
    return general_solution(mesh)
```

```python
import functools
import math

import jax
import jax.numpy as jnp
import numpy as np
from jax import lax
from jax.experimental import pallas as pl
from jax.experimental.pallas import tpu as pltpu
from jax.sharding import PartitionSpec as P

HEAD_DIM = 64
ROT = 32


eps_norm = 1e-05
gelu_coef = 0.7978845608028654


def gelu_tanh(values):
    return (
        0.5 * values * (1.0 + jnp.tanh(gelu_coef * (values + 0.044715 * values * values * values)))
    )


def rotary_angles(positions, rot_dims):
    half_dims = rot_dims // 2
    freq_index = jnp.arange(half_dims, dtype=jnp.float32)
    inv_freq = jnp.exp(-math.log(10000.0) * 2.0 * freq_index / rot_dims)
    return positions.astype(jnp.float32)[:, None] * inv_freq[None, :]


def rotary(vectors, angles):
    half_dims = angles.shape[-1]
    cosines = jnp.cos(angles)[:, None, :]
    sine_vals = jnp.sin(angles)[:, None, :]
    leading = vectors[..., :half_dims]
    trailing = vectors[..., half_dims : 2 * half_dims]
    return jnp.concatenate(
        [
            leading * cosines - trailing * sine_vals,
            trailing * cosines + leading * sine_vals,
            vectors[..., 2 * half_dims :],
        ],
        axis=-1,
    )


def rotary_back(gradients, angles):
    half_dims = angles.shape[-1]
    cosines = jnp.cos(angles)[:, None, :]
    sine_vals = jnp.sin(angles)[:, None, :]
    leading = gradients[..., :half_dims]
    trailing = gradients[..., half_dims : 2 * half_dims]
    return jnp.concatenate(
        [
            leading * cosines + trailing * sine_vals,
            trailing * cosines - leading * sine_vals,
            gradients[..., 2 * half_dims :],
        ],
        axis=-1,
    )


def masked_scores(queries, key_rows, places, length):
    scores = jnp.einsum("qhd,khd->hqk", queries, key_rows, preferred_element_type=jnp.float32)
    key_places = jnp.arange(key_rows.shape[0], dtype=jnp.int32)
    allowed = (key_places[None, :] <= places[:, None]) & (key_places[None, :] < length)
    return jnp.where(allowed[None], scores, -1e30)


def on_device(
    tokens,
    lengths,
    ln_gain,
    ln_bias,
    w_qkv,
    b_qkv,
    w_out,
    b_out,
    w_fc1,
    b_fc1,
    w_fc2,
    b_fc2,
    cotangent,
):
    seq_count, local_len, model_width = tokens.shape
    shard_rows = w_qkv.shape[0]
    hidden_ratio = w_fc1.shape[1] // model_width
    head_count = model_width // HEAD_DIM
    token_count = seq_count * local_len
    places = lax.axis_index("ctx") * local_len + jnp.arange(local_len, dtype=jnp.int32)
    angles = rotary_angles(places, ROT)
    live_mask = places[None, :] < lengths[:, None]
    inputs = tokens.astype(jnp.float32).reshape(token_count, model_width)
    average = jnp.mean(inputs, axis=-1, keepdims=True)
    centered = inputs - average
    variance = jnp.mean(centered * centered, axis=-1, keepdims=True)
    inv_std = lax.rsqrt(variance + eps_norm)
    normed = centered * inv_std
    qkv_bias_rows = b_qkv.reshape(shard_rows, 3)
    fc1_bias_rows = b_fc1.reshape(shard_rows, hidden_ratio)
    fc2_rows = w_fc2.reshape(shard_rows, hidden_ratio * model_width)
    inner_full = (
        lax.all_gather(w_qkv, ("dp", "ctx"), axis=0, tiled=True),
        lax.all_gather(w_fc1, ("dp", "ctx"), axis=0, tiled=True),
        lax.all_gather(ln_gain, ("dp", "ctx"), axis=0, tiled=True),
        lax.all_gather(ln_bias, ("dp", "ctx"), axis=0, tiled=True),
        lax.all_gather(qkv_bias_rows, ("dp", "ctx"), axis=0, tiled=True),
        lax.all_gather(fc1_bias_rows, ("dp", "ctx"), axis=0, tiled=True),
    )
    gain_full = inner_full[2].astype(jnp.float32)
    shift_full = inner_full[3].astype(jnp.float32)
    hidden = (normed * gain_full + shift_full).astype(jnp.bfloat16)
    qkv_acc = jnp.dot(hidden, inner_full[0], preferred_element_type=jnp.float32)
    up_acc = jnp.dot(hidden, inner_full[1], preferred_element_type=jnp.float32)
    qkv_bias = inner_full[4].reshape(-1).astype(jnp.float32)
    fc1_bias = inner_full[5].reshape(-1).astype(jnp.float32)
    qkv_proj = (qkv_acc + qkv_bias).reshape(seq_count, local_len, 3, head_count, HEAD_DIM)
    queries = (rotary(qkv_proj[:, :, 0], angles) * 0.125).astype(jnp.bfloat16)
    key_local = (
        rotary(qkv_proj[:, :, 1], angles)
        .astype(jnp.bfloat16)
        .reshape(seq_count, local_len, model_width)
    )
    value_local = qkv_proj[:, :, 2].astype(jnp.bfloat16).reshape(seq_count, local_len, model_width)
    key_full, value_full = (
        lax.all_gather(key_local, "ctx", axis=1, tiled=True),
        lax.all_gather(value_local, "ctx", axis=1, tiled=True),
    )
    total_len = key_full.shape[1]

    def attend_forward(packed):
        query_seq, key_seq, value_seq, length = packed
        key_heads = key_seq.reshape(total_len, head_count, HEAD_DIM)
        value_heads = value_seq.reshape(total_len, head_count, HEAD_DIM)
        scores = masked_scores(query_seq, key_heads, places, length)
        row_max = jnp.max(scores, axis=-1, keepdims=True)
        exponent = jnp.exp(scores - row_max)
        row_sum = jnp.sum(exponent, axis=-1, keepdims=True)
        probability = (exponent / row_sum).astype(jnp.bfloat16)
        attended = jnp.einsum(
            "hqk,khd->qhd", probability, value_heads, preferred_element_type=jnp.float32
        )
        log_total = (row_max + jnp.log(row_sum))[..., 0]
        return (attended.reshape(local_len, model_width).astype(jnp.bfloat16), log_total)

    attn_seq, log_totals = lax.map(attend_forward, (queries, key_full, value_full, lengths))
    attn_mixed = attn_seq.reshape(token_count, model_width)
    up_proj = up_acc + fc1_bias
    activated = gelu_tanh(up_proj).astype(jnp.bfloat16)
    outer_full = (
        lax.all_gather(w_out, ("dp", "ctx"), axis=0, tiled=True),
        lax.all_gather(fc2_rows, ("dp", "ctx"), axis=0, tiled=True),
        lax.all_gather(b_out, ("dp", "ctx"), axis=0, tiled=True),
        lax.all_gather(b_fc2, ("dp", "ctx"), axis=0, tiled=True),
    )
    branch = jnp.dot(attn_mixed, outer_full[0], preferred_element_type=jnp.float32) + jnp.dot(
        activated,
        outer_full[1].reshape(hidden_ratio * model_width, model_width),
        preferred_element_type=jnp.float32,
    )
    out_bias = outer_full[2].astype(jnp.float32)
    fc2_bias = outer_full[3].astype(jnp.float32)
    output = (
        (inputs + branch + out_bias + fc2_bias)
        .astype(jnp.bfloat16)
        .reshape(seq_count, local_len, model_width)
    )
    grad_out = jnp.where(live_mask[:, :, None], cotangent, jnp.zeros((), jnp.bfloat16)).reshape(
        token_count, model_width
    )
    out_back, fc2_back = (
        lax.all_gather(w_out, ("dp", "ctx"), axis=0, tiled=True),
        lax.all_gather(fc2_rows, ("dp", "ctx"), axis=0, tiled=True),
    )
    fc2_matrix = fc2_back.reshape(hidden_ratio * model_width, model_width)
    grad_mixed = jnp.einsum(
        "td,kd->tk", grad_out, out_back, preferred_element_type=jnp.float32
    ).astype(jnp.bfloat16)
    grad_act = jnp.einsum("td,kd->tk", grad_out, fc2_matrix, preferred_element_type=jnp.float32)
    gelu_value, gelu_pull = jax.vjp(gelu_tanh, up_proj)
    grad_up = gelu_pull(grad_act)[0].astype(jnp.bfloat16)
    key_back, value_back = (
        lax.all_gather(key_local, "ctx", axis=1, tiled=True),
        lax.all_gather(value_local, "ctx", axis=1, tiled=True),
    )

    def attend_backward(packed):
        query_seq, key_seq, value_seq, grad_seq, log_total, length = packed
        key_heads = key_seq.reshape(total_len, head_count, HEAD_DIM)
        value_heads = value_seq.reshape(total_len, head_count, HEAD_DIM)
        grad_heads = grad_seq.reshape(local_len, head_count, HEAD_DIM)
        scores = masked_scores(query_seq, key_heads, places, length)
        probability = jnp.exp(scores - log_total[:, :, None])
        grad_probs = jnp.einsum(
            "qhd,khd->hqk", grad_heads, value_heads, preferred_element_type=jnp.float32
        )
        inner = jnp.sum(probability * grad_probs, axis=-1, keepdims=True)
        grad_scores = (probability * (grad_probs - inner)).astype(jnp.bfloat16)
        grad_query = jnp.einsum(
            "hqk,khd->qhd", grad_scores, key_heads, preferred_element_type=jnp.float32
        )
        grad_keys = jnp.einsum(
            "hqk,qhd->khd", grad_scores, query_seq, preferred_element_type=jnp.float32
        )
        grad_values = jnp.einsum(
            "hqk,qhd->khd",
            probability.astype(jnp.bfloat16),
            grad_heads,
            preferred_element_type=jnp.float32,
        )
        return (
            grad_query,
            grad_keys.reshape(total_len, model_width),
            grad_values.reshape(total_len, model_width),
        )

    grad_query, grad_keys_all, grad_values_all = lax.map(
        attend_backward,
        (
            queries,
            key_back,
            value_back,
            grad_mixed.reshape(seq_count, local_len, model_width),
            log_totals,
            lengths,
        ),
    )
    grad_keys_own, grad_values_own = (
        lax.psum_scatter(grad_keys_all, "ctx", scatter_dimension=1, tiled=True),
        lax.psum_scatter(grad_values_all, "ctx", scatter_dimension=1, tiled=True),
    )
    grad_query_pre = rotary_back(grad_query * 0.125, angles).reshape(token_count, model_width)
    grad_keys_pre = rotary_back(
        grad_keys_own.reshape(seq_count, local_len, head_count, HEAD_DIM), angles
    ).reshape(token_count, model_width)
    grad_qkv = jnp.concatenate(
        [grad_query_pre, grad_keys_pre, grad_values_own.reshape(token_count, model_width)], axis=-1
    ).astype(jnp.bfloat16)
    qkv_matrix, fc1_matrix = (
        lax.all_gather(w_qkv, ("dp", "ctx"), axis=0, tiled=True),
        lax.all_gather(w_fc1, ("dp", "ctx"), axis=0, tiled=True),
    )
    grad_hidden = jnp.einsum(
        "tj,dj->td", grad_qkv, qkv_matrix, preferred_element_type=jnp.float32
    ) + jnp.einsum("tj,dj->td", grad_up, fc1_matrix, preferred_element_type=jnp.float32)
    gain_term = jnp.sum(grad_hidden * normed, axis=0)
    shift_term = jnp.sum(grad_hidden, axis=0)
    grad_norm = grad_hidden * gain_full
    grad_input = grad_out.astype(jnp.float32) + inv_std * (
        grad_norm
        - jnp.mean(grad_norm, axis=-1, keepdims=True)
        - normed * jnp.mean(grad_norm * normed, axis=-1, keepdims=True)
    )
    grad_input = grad_input.astype(jnp.bfloat16).reshape(seq_count, local_len, model_width)
    wout_term = jnp.einsum("tk,td->kd", attn_mixed, grad_out, preferred_element_type=jnp.float32)
    wfc2_term = jnp.einsum(
        "tk,td->kd", activated, grad_out, preferred_element_type=jnp.float32
    ).reshape(model_width, hidden_ratio * model_width)
    bias_term = jnp.sum(grad_out, axis=0, dtype=jnp.float32)
    bqkv_term = jnp.sum(grad_qkv, axis=0, dtype=jnp.float32).reshape(model_width, 3)
    bfc1_term = jnp.sum(grad_up, axis=0, dtype=jnp.float32).reshape(model_width, hidden_ratio)
    grad_wout, grad_wfc2, grad_bias, grad_gain, grad_shift, grad_bqkv, grad_bfc1 = (
        lax.psum_scatter(wout_term, ("dp", "ctx"), scatter_dimension=0, tiled=True),
        lax.psum_scatter(wfc2_term, ("dp", "ctx"), scatter_dimension=0, tiled=True),
        lax.psum_scatter(bias_term, ("dp", "ctx"), scatter_dimension=0, tiled=True),
        lax.psum_scatter(gain_term, ("dp", "ctx"), scatter_dimension=0, tiled=True),
        lax.psum_scatter(shift_term, ("dp", "ctx"), scatter_dimension=0, tiled=True),
        lax.psum_scatter(bqkv_term, ("dp", "ctx"), scatter_dimension=0, tiled=True),
        lax.psum_scatter(bfc1_term, ("dp", "ctx"), scatter_dimension=0, tiled=True),
    )
    qkv_part = jnp.einsum("tk,tj->kj", hidden, grad_qkv, preferred_element_type=jnp.float32)
    fc1_part = jnp.einsum("tk,tj->kj", hidden, grad_up, preferred_element_type=jnp.float32)
    inner_sum = lax.psum_scatter(
        jnp.concatenate([qkv_part, fc1_part], axis=1),
        ("dp", "ctx"),
        scatter_dimension=0,
        tiled=True,
    )
    grad_wqkv = inner_sum[:, : 3 * model_width]
    grad_wfc1 = inner_sum[:, 3 * model_width :]
    return (
        output,
        grad_input,
        grad_gain,
        grad_shift,
        grad_wqkv,
        grad_bqkv.reshape(-1),
        grad_wout,
        grad_bias,
        grad_wfc1,
        grad_bfc1.reshape(-1),
        grad_wfc2.reshape(shard_rows * hidden_ratio, model_width),
        grad_bias,
    )


def general_solution(mesh):
    placed = (
        P("dp", "ctx", None),
        P("dp"),
        P(("dp", "ctx")),
        P(("dp", "ctx")),
        P(("dp", "ctx"), None),
        P(("dp", "ctx")),
        P(("dp", "ctx"), None),
        P(("dp", "ctx")),
        P(("dp", "ctx"), None),
        P(("dp", "ctx")),
        P(("dp", "ctx"), None),
        P(("dp", "ctx")),
        P("dp", "ctx", None),
    )
    return jax.shard_map(
        on_device,
        mesh=mesh,
        in_specs=placed,
        out_specs=(
            P("dp", "ctx", None),
            P("dp", "ctx", None),
            P(("dp", "ctx")),
            P(("dp", "ctx")),
            P(("dp", "ctx"), None),
            P(("dp", "ctx")),
            P(("dp", "ctx"), None),
            P(("dp", "ctx")),
            P(("dp", "ctx"), None),
            P(("dp", "ctx")),
            P(("dp", "ctx"), None),
            P(("dp", "ctx")),
        ),
        check_vma=False,
    )


FINE = ("zh", "zl", "y", "x", "c")
ROWS_AXES = ("zl", "x", "c")


def swap(values, axis):
    return lax.ppermute(values, axis, [(0, 1), (1, 0)])


def gather_blocks(own):
    across = swap(own, "zh")
    beside = swap(own, "y")
    both = swap(across, "y")
    return own, beside, across, both


def reduce_blocks(blocks):
    own, beside, across, both = blocks
    got_beside = swap(beside, "y")
    got_both = swap(both, "y")
    passed = (across.astype(jnp.float32) + got_both.astype(jnp.float32)).astype(jnp.bfloat16)
    got = swap(passed, "zh")
    return own.astype(jnp.float32) + got_beside.astype(jnp.float32) + got.astype(jnp.float32)


def by_place(blocks, zh, y):
    first, second, third, fourth = blocks
    a, b = jnp.where(y == 1, second, first), jnp.where(y == 1, first, second)
    c, d = jnp.where(y == 1, fourth, third), jnp.where(y == 1, third, fourth)
    return (
        jnp.where(zh == 1, c, a),
        jnp.where(zh == 1, d, b),
        jnp.where(zh == 1, a, c),
        jnp.where(zh == 1, b, d),
    )


def natural_rows(blocks):
    halves = [jnp.split(block, 2, axis=0) for block in blocks]
    return jnp.concatenate(
        [halves[2 * zh + y][zl] for zh in range(2) for zl in range(2) for y in range(2)], axis=0
    )


def blocks_of_rows(values):
    parts = jnp.split(values, 8, axis=0)
    return [
        jnp.concatenate([parts[4 * zh + 2 * zl + y] for zl in range(2)], axis=0)
        for zh in range(2)
        for y in range(2)
    ]


def dot(left, right, dims):
    return lax.dot_general(left, right, (dims, ((), ())), preferred_element_type=jnp.float32)


QB = 256


def nt(a, b):
    return dot(a, b, ((1,), (1,)))


def nn(a, b):
    return dot(a, b, ((1,), (0,)))


def tn(a, b):
    return dot(a, b, ((0,), (0,)))


def attention_kernel(len_ref, bias_ref, cos_ref, sin_ref, q_in, k_in, v_in, go_in, mixed_ref, grad_ref, sum_ref,
                     q_s, k_s, v_s, g_s, gk_s, gv_s, *, total, pairs):
    f32, bf16 = jnp.float32, jnp.bfloat16
    pair = pl.program_id(1)
    lane = lax.broadcasted_iota(jnp.int32, (1, 128), 1)
    in_head = lane % 64
    first = in_head < 16
    heads = [(lane < 64), (lane >= 64)]
    length = len_ref[pl.program_id(0)]

    def other(v):
        return jnp.where(first, pltpu.roll(v, 112, 1), pltpu.roll(v, 16, 1))
    def col(part):
        return pl.multiple_of(part * (pairs * 128) + pair * 128, 128)
    cosines, sines = cos_ref[...], sin_ref[...]
    def turn(v): return v * cosines + other(v) * sines
    def turn_back(v): return v * cosines - other(v) * sines
    q = turn(q_in[...] + bias_ref[:, pl.ds(col(0), 128)]) * 0.125
    k = turn(k_in[...] + bias_ref[:, pl.ds(col(1), 128)])
    v = v_in[...] + bias_ref[:, pl.ds(col(2), 128)]
    g = go_in[...]
    for h in range(2):
        q_s[h] = jnp.where(heads[h], q, 0.0).astype(bf16)
        k_s[h] = jnp.where(heads[h], k, 0.0).astype(bf16)
        v_s[h] = jnp.where(heads[h], v, 0.0).astype(bf16)
        g_s[h] = jnp.where(heads[h], g, 0.0).astype(bf16)
    gk_s[...] = jnp.zeros_like(gk_s)
    gv_s[...] = jnp.zeros_like(gv_s)
    gq_sum = jnp.zeros((1, 128), f32)
    for b in range(total // QB):
        rows = pl.ds(b * QB, QB)
        upto = (b + 1) * QB
        keys = pl.ds(0, upto)
        limit = jnp.minimum(lax.broadcasted_iota(jnp.int32, (1, QB), 1) + (b * QB + 1), length)
        allowed = lax.broadcasted_iota(jnp.int32, (upto, QB), 0) < limit
        mixed = None
        for h in range(2):
            qh, gh = q_s[h, rows], g_s[h, rows]
            s = nt(k_s[h, keys], qh)
            s = jnp.where(allowed, s, -1e30)
            m = jnp.max(s, axis=0, keepdims=True)
            e = jnp.exp(s - m)
            p = e * (1.0 / jnp.sum(e, axis=0, keepdims=True))
            pr = p.astype(bf16)
            gp = nt(v_s[h, keys], gh)
            inner = jnp.sum(p * gp, axis=0, keepdims=True)
            gs = (p * (gp - inner)).astype(bf16)
            gv_s[keys] += nn(pr, gh)
            gk_s[keys] += nn(gs, qh)
            o = tn(pr, v_s[h, keys])
            gq = tn(gs, k_s[h, keys])
            mixed = o if mixed is None else mixed + o
            gq_all = gq if h == 0 else gq_all + gq
        mixed_ref[rows, :] = mixed
        cs, sn = cos_ref[rows], sin_ref[rows]
        gq_all = gq_all * 0.125
        back = (gq_all * cs - other(gq_all) * sn).astype(bf16)
        grad_ref[rows, pl.ds(col(0), 128)] = back.astype(f32)
        gq_sum += jnp.sum(back.astype(f32), axis=0, keepdims=True)
    gk = turn_back(gk_s[...]).astype(bf16)
    gv = gv_s[...].astype(bf16)
    grad_ref[:, pl.ds(col(1), 128)] = gk.astype(f32)
    grad_ref[:, pl.ds(col(2), 128)] = gv.astype(f32)
    sum_ref[0, :, pl.ds(col(0), 128)] = gq_sum
    sum_ref[0, :, pl.ds(col(1), 128)] = jnp.sum(gk.astype(f32), axis=0, keepdims=True)
    sum_ref[0, :, pl.ds(col(2), 128)] = jnp.sum(gv.astype(f32), axis=0, keepdims=True)

def attention(lengths, qkv, bias, grad_mixed, cosines, sines):
    seqs = lengths.shape[0]
    total = qkv.shape[0] // seqs
    width = qkv.shape[1] // 3
    pairs = width // 128
    blk = lambda part: pl.BlockSpec((total, 128), lambda s, p: (s, part * pairs + p))
    whole = lambda shape: pl.BlockSpec(shape, lambda s, p: (0,) * len(shape))
    f32, bf16 = jnp.float32, jnp.bfloat16
    return pl.pallas_call(
        functools.partial(attention_kernel, total=total, pairs=pairs),
        grid=(seqs, pairs),
        in_specs=[
            pl.BlockSpec(memory_space=pltpu.SMEM),
            whole((1, 3 * width)), whole((total, 128)), whole((total, 128)),
            blk(0), blk(1), blk(2),
            pl.BlockSpec((total, 128), lambda s, p: (s, p)),
        ],
        out_specs=[
            pl.BlockSpec((total, 128), lambda s, p: (s, p)),
            pl.BlockSpec((total, 3 * width), lambda s, p: (s, 0)),
            pl.BlockSpec((1, 1, 3 * width), lambda s, p: (s, 0, 0)),
        ],
        out_shape=[
            jax.ShapeDtypeStruct((seqs * total, width), f32),
            jax.ShapeDtypeStruct((seqs * total, 3 * width), f32),
            jax.ShapeDtypeStruct((seqs, 1, 3 * width), f32),
        ],
        scratch_shapes=[pltpu.VMEM((2, total, 128), bf16)] * 4 + [pltpu.VMEM((total, 128), f32)] * 2,
        compiler_params=pltpu.CompilerParams(vmem_limit_bytes=48 * 2**20),
        cost_estimate=pl.CostEstimate(flops=seqs*pairs*2*6*total*total*64*2, bytes_accessed=20*2**20, transcendentals=seqs*pairs*2*total*total),
    )(lengths, bias, cosines, sines, qkv, qkv, qkv, grad_mixed)

def tables(total, rot):
    half = rot // 2
    inv = jnp.exp(-math.log(10000.0) * 2.0 * jnp.arange(half, dtype=jnp.float32) / rot)
    ang = jnp.arange(total, dtype=jnp.int32).astype(jnp.float32)[:, None] * inv[None, :]
    c, s = jnp.cos(ang), jnp.sin(ang)
    one, nil = jnp.ones((total, 64 - rot), jnp.float32), jnp.zeros((total, 64 - rot), jnp.float32)
    cosines = jnp.concatenate([c, c, one] * 2, axis=1)
    sines = jnp.concatenate([-s, s, nil] * 2, axis=1)
    return cosines, sines


MESH_ID = pl.DeviceIdType.MESH


def exchange_kernel(src, dst, send_sem, recv_sem, *, spread):
    place = [lax.axis_index(name) for name in FINE]
    me = 0
    for p in place:
        me = me * 2 + p

    def away(k):
        return tuple((p + k // 2 ** (4 - i)) % 2 for i, p in enumerate(place))

    def index_of(where):
        number = 0
        for p in where:
            number = number * 2 + p
        return number

    barrier = pltpu.get_barrier_semaphore()

    def greet(k, carry):
        pl.semaphore_signal(barrier, inc=1, device_id=away(k), device_id_type=MESH_ID)
        return carry

    lax.fori_loop(1, 32, greet, 0)
    pl.semaphore_wait(barrier, 31)

    def copy(k):
        where = away(k)
        return pltpu.make_async_remote_copy(
            src_ref=src.at[index_of(where) if spread else 0],
            dst_ref=dst.at[me],
            send_sem=send_sem.at[k],
            recv_sem=recv_sem.at[k],
            device_id=where,
            device_id_type=MESH_ID,
        )

    def send(k, carry):
        copy(k).start()
        return carry

    lax.fori_loop(1, 32, send, 0)
    dst[me] = src[me if spread else 0]

    def finish(k, carry):
        copy(k).wait()
        return carry

    lax.fori_loop(1, 32, finish, 0)


def sum_kernel(src, out, dst, send_sem, recv_sem):
    exchange_kernel(src, dst, send_sem, recv_sem, spread=True)
    out[...] = jnp.sum(dst[...], axis=0)


def gather_small(values):
    n = values.shape[0]
    return pl.pallas_call(
        functools.partial(exchange_kernel, spread=False),
        out_shape=jax.ShapeDtypeStruct((32, n, 128), jnp.float32),
        in_specs=[pl.BlockSpec(memory_space=pltpu.VMEM)],
        out_specs=pl.BlockSpec(memory_space=pltpu.VMEM),
        scratch_shapes=[pltpu.SemaphoreType.DMA((32,)), pltpu.SemaphoreType.DMA((32,))],
        compiler_params=pltpu.CompilerParams(collective_id=0, has_side_effects=True),
    )(values[None])


def sum_small(values, collective_id):
    n = values.shape[1]
    return pl.pallas_call(
        sum_kernel,
        out_shape=jax.ShapeDtypeStruct((n, 128), jnp.float32),
        in_specs=[pl.BlockSpec(memory_space=pltpu.VMEM)],
        out_specs=pl.BlockSpec(memory_space=pltpu.VMEM),
        scratch_shapes=[
            pltpu.VMEM((32, n, 128), jnp.float32),
            pltpu.SemaphoreType.DMA((32,)),
            pltpu.SemaphoreType.DMA((32,)),
        ],
        compiler_params=pltpu.CompilerParams(collective_id=collective_id, has_side_effects=True),
    )(values)


def split_device(
    tokens,
    lengths,
    ln_gain,
    ln_bias,
    w_qkv,
    b_qkv,
    w_out,
    b_out,
    w_fc1,
    b_fc1,
    w_fc2,
    b_fc2,
    cotangent,
):
    bf16, f32 = jnp.bfloat16, jnp.float32
    zh, zl, y, x, c = (lax.axis_index(name) for name in FINE)
    place = (zl * 2 + x) * 2 + c
    _, local_len, width = tokens.shape
    rows = w_qkv.shape[0]
    ff_rows = w_fc2.shape[0]
    pieces = 4
    total_len = local_len * pieces
    heads = 4
    own_width = heads * HEAD_DIM

    small = jnp.concatenate(
        [v.astype(f32) for v in (ln_gain, ln_bias, b_qkv, b_out, b_fc1, b_fc2, lengths)]
    )
    filled = -(-small.shape[0] // 128) * 128
    small = jnp.pad(small, (0, filled - small.shape[0])).reshape(-1, 128)
    small_all = gather_small(small).reshape(32, filled)
    ends = np.cumsum([rows, rows, 3 * rows, rows, ff_rows, rows, 1])
    gain_all, shift_all, bqkv_all, bout_all, bfc1_all, bfc2_all, lengths_all = (
        part.reshape(-1) for part in jnp.split(small_all, ends, axis=1)[:-1]
    )
    pair_lengths = lax.dynamic_index_in_dim(
        lengths_all.reshape(2, 2, 2, 4)[:, :, :, 0].transpose(0, 2, 1).reshape(4, 2),
        zh * 2 + y,
        keepdims=False,
    ).astype(jnp.int32)

    def own_columns(weight, shape, order):
        spread = weight.reshape((rows,) + shape).transpose(order)
        spread = spread.reshape(8, rows, -1)
        return lax.all_to_all(spread, ROWS_AXES, 0, 0, tiled=True).reshape(8 * rows, -1)

    qkv_own = own_columns(w_qkv, (3, 2, 2, 2, 2, 2, HEAD_DIM), (3, 5, 6, 0, 1, 2, 4, 7))
    fc1_own = own_columns(w_fc1, (2, 2, 2, 2, 2, ff_rows), (2, 4, 5, 0, 1, 3, 6))
    out_blocks = by_place(gather_blocks(w_out), zh, y)
    qkv_blocks = gather_blocks(qkv_own)
    fc2_blocks = by_place(gather_blocks(w_fc2), zh, y)
    fc1_blocks = gather_blocks(fc1_own)
    out_mat = jnp.concatenate(out_blocks, axis=0)
    fc2_mat = jnp.concatenate(fc2_blocks, axis=0)
    qkv_mat = natural_rows(by_place(qkv_blocks, zh, y))
    fc1_mat = natural_rows(by_place(fc1_blocks, zh, y))

    inputs = tokens[0].astype(f32)
    average = jnp.mean(inputs, axis=-1, keepdims=True)
    centered = inputs - average
    variance = jnp.mean(centered * centered, axis=-1, keepdims=True)
    inv_std = lax.rsqrt(variance + eps_norm)
    normed = centered * inv_std
    hidden_own = (normed * gain_all + shift_all).astype(bf16)

    hidden = lax.all_gather(hidden_own, ROWS_AXES, axis=0, tiled=True)
    places = (x * 2 + c) * local_len + jnp.arange(local_len, dtype=jnp.int32)
    grad_own = jnp.where((places < lengths[0])[:, None], cotangent[0], jnp.zeros((), bf16))
    grad_out = lax.all_gather(grad_own, ROWS_AXES, axis=0, tiled=True)

    bqkv = lax.dynamic_index_in_dim(
        bqkv_all.reshape(3, 2, 2, 2, 4, HEAD_DIM).transpose(2, 4, 0, 1, 3, 5).reshape(8, -1),
        place,
        keepdims=False,
    )
    bfc1 = lax.dynamic_index_in_dim(
        bfc1_all.reshape(2, 2, 2, 4, ff_rows).transpose(1, 3, 0, 2, 4).reshape(8, -1),
        place,
        keepdims=False,
    )

    grad_mixed = dot(grad_out, out_mat, ((1,), (1,)))
    qkv = dot(hidden, qkv_mat, ((1,), (0,)))
    cosines, sines = tables(total_len, ROT)
    attn_mixed, grad_qkv, grad_qkv_sum = attention(
        pair_lengths, qkv, bqkv[None], grad_mixed, cosines, sines
    )
    attn_mixed, grad_qkv = attn_mixed.astype(bf16), grad_qkv.astype(bf16)

    up_proj = dot(hidden, fc1_mat, ((1,), (0,))) + bfc1
    activated = gelu_tanh(up_proj).astype(bf16)
    branch = dot(attn_mixed, out_mat, ((1,), (0,))) + dot(activated, fc2_mat, ((1,), (0,)))
    branch_own = lax.psum_scatter(
        branch.astype(bf16), ROWS_AXES, scatter_dimension=0, tiled=True
    ).astype(f32)
    output = (inputs + branch_own + bout_all + bfc2_all).astype(bf16)[None]

    grad_act = dot(grad_out, fc2_mat, ((1,), (1,)))
    _, gelu_pull = jax.vjp(gelu_tanh, up_proj)
    grad_up = gelu_pull(grad_act)[0].astype(bf16)

    grad_hidden = dot(grad_qkv, qkv_mat, ((1,), (1,))) + dot(grad_up, fc1_mat, ((1,), (1,)))
    grad_hidden_own = lax.psum_scatter(
        grad_hidden.astype(bf16), ROWS_AXES, scatter_dimension=0, tiled=True
    ).astype(f32)
    grad_norm = grad_hidden_own * gain_all
    grad_input = grad_own.astype(f32) + inv_std * (
        grad_norm
        - jnp.mean(grad_norm, axis=-1, keepdims=True)
        - normed * jnp.mean(grad_norm * normed, axis=-1, keepdims=True)
    )
    grad_input = grad_input.astype(bf16)[None]

    def place_blocks(values):
        return by_place(jnp.split(values, 4, axis=0), zh, y)

    fc2_part = dot(activated, grad_out, ((0,), (0,))).astype(bf16)
    grad_fc2 = reduce_blocks(place_blocks(fc2_part))
    fc1_part = dot(hidden, grad_up, ((0,), (0,))).astype(bf16)
    fc1_total = reduce_blocks(by_place(blocks_of_rows(fc1_part), zh, y)).astype(bf16)
    out_part = dot(attn_mixed, grad_out, ((0,), (0,))).astype(bf16)
    grad_wout = reduce_blocks(place_blocks(out_part))
    qkv_part = dot(hidden, grad_qkv, ((0,), (0,))).astype(bf16)
    qkv_total = reduce_blocks(by_place(blocks_of_rows(qkv_part), zh, y)).astype(bf16)

    def all_columns(total, shape, order, out_width):
        spread = lax.all_to_all(total.reshape(8, rows, -1), ROWS_AXES, 0, 0, tiled=True)
        spread = spread.reshape((2, 2, 2, rows) + shape).transpose(order)
        return spread.reshape(rows, out_width).astype(f32)

    grad_wfc1 = all_columns(fc1_total, (2, 2, ff_rows), (3, 4, 0, 5, 1, 2, 6), w_fc1.shape[1])
    grad_wqkv = all_columns(
        qkv_total, (3, 2, 2, HEAD_DIM), (3, 4, 5, 0, 6, 1, 2, 7), w_qkv.shape[1]
    )

    mine = (jnp.arange(8) == place).astype(f32)
    bqkv_term = (
        (jnp.sum(grad_qkv_sum, axis=0).reshape(1, 3, 2, 2, HEAD_DIM) * mine[:, None, None, None, None])
        .reshape(2, 4, 3, 2, 2, HEAD_DIM)
        .transpose(2, 3, 0, 4, 1, 5)
        .reshape(-1)
    )
    bfc1_term = (
        (jnp.sum(grad_up, axis=0, dtype=f32).reshape(1, 2, 2, ff_rows) * mine[:, None, None, None])
        .reshape(2, 4, 2, 2, ff_rows)
        .transpose(2, 0, 3, 1, 4)
        .reshape(-1)
    )
    bias_term = jnp.sum(grad_own, axis=0, dtype=f32)
    terms = jnp.concatenate([v.reshape(32, -1) for v in (bqkv_term, bfc1_term, bias_term)], axis=1)
    sums = sum_small(terms.reshape(32, -1, 128), 1).reshape(-1)
    grad_bqkv, grad_bfc1, grad_bias = jnp.split(sums, np.cumsum([3 * rows, ff_rows]))
    gain_term = jnp.sum(grad_hidden_own * normed, axis=0)
    shift_term = jnp.sum(grad_hidden_own, axis=0)
    terms = jnp.concatenate([gain_term.reshape(32, -1), shift_term.reshape(32, -1)], axis=1)
    sums = sum_small(terms.reshape(32, -1, 128), 2).reshape(-1)
    grad_gain, grad_shift = jnp.split(sums, [rows])
    return (
        output,
        grad_input,
        grad_gain,
        grad_shift,
        grad_wqkv,
        grad_bqkv,
        grad_wout,
        grad_bias,
        grad_wfc1,
        grad_bfc1,
        grad_fc2,
        grad_bias,
    )


def fine_mesh(mesh):
    return jax.sharding.Mesh(mesh.devices.reshape(2, 2, 2, 2, 2), FINE)


def fine_solution(mesh):
    everyone, seqs, parts = FINE, ("zh", "zl", "y"), ("x", "c")
    placed = (
        P(seqs, parts, None),
        P(seqs),
        P(everyone),
        P(everyone),
        P(everyone, None),
        P(everyone),
        P(everyone, None),
        P(everyone),
        P(everyone, None),
        P(everyone),
        P(everyone, None),
        P(everyone),
        P(seqs, parts, None),
    )
    given = (
        P(seqs, parts, None),
        P(seqs, parts, None),
        P(everyone),
        P(everyone),
        P(everyone, None),
        P(everyone),
        P(everyone, None),
        P(everyone),
        P(everyone, None),
        P(everyone),
        P(everyone, None),
        P(everyone),
    )
    return jax.shard_map(
        split_device, mesh=fine_mesh(mesh), in_specs=placed, out_specs=given, check_vma=False
    )


def solution(mesh):
    if mesh.shape["dp"] == 8 and mesh.shape["ctx"] == 4:
        return fine_solution(mesh)
    return general_solution(mesh)
```

```python
import functools
import math

import jax
import jax.numpy as jnp
import numpy as np
from jax import lax
from jax.experimental import pallas as pl
from jax.experimental.pallas import tpu as pltpu
from jax.sharding import PartitionSpec as P

HEAD_DIM = 64
ROT = 32


eps_norm = 1e-05
gelu_coef = 0.7978845608028654


def gelu_tanh(values):
    return (
        0.5 * values * (1.0 + jnp.tanh(gelu_coef * (values + 0.044715 * values * values * values)))
    )


def rotary_angles(positions, rot_dims):
    half_dims = rot_dims // 2
    freq_index = jnp.arange(half_dims, dtype=jnp.float32)
    inv_freq = jnp.exp(-math.log(10000.0) * 2.0 * freq_index / rot_dims)
    return positions.astype(jnp.float32)[:, None] * inv_freq[None, :]


def rotary(vectors, angles):
    half_dims = angles.shape[-1]
    cosines = jnp.cos(angles)[:, None, :]
    sine_vals = jnp.sin(angles)[:, None, :]
    leading = vectors[..., :half_dims]
    trailing = vectors[..., half_dims : 2 * half_dims]
    return jnp.concatenate(
        [
            leading * cosines - trailing * sine_vals,
            trailing * cosines + leading * sine_vals,
            vectors[..., 2 * half_dims :],
        ],
        axis=-1,
    )


def rotary_back(gradients, angles):
    half_dims = angles.shape[-1]
    cosines = jnp.cos(angles)[:, None, :]
    sine_vals = jnp.sin(angles)[:, None, :]
    leading = gradients[..., :half_dims]
    trailing = gradients[..., half_dims : 2 * half_dims]
    return jnp.concatenate(
        [
            leading * cosines + trailing * sine_vals,
            trailing * cosines - leading * sine_vals,
            gradients[..., 2 * half_dims :],
        ],
        axis=-1,
    )


def masked_scores(queries, key_rows, places, length):
    scores = jnp.einsum("qhd,khd->hqk", queries, key_rows, preferred_element_type=jnp.float32)
    key_places = jnp.arange(key_rows.shape[0], dtype=jnp.int32)
    allowed = (key_places[None, :] <= places[:, None]) & (key_places[None, :] < length)
    return jnp.where(allowed[None], scores, -1e30)


def on_device(
    tokens,
    lengths,
    ln_gain,
    ln_bias,
    w_qkv,
    b_qkv,
    w_out,
    b_out,
    w_fc1,
    b_fc1,
    w_fc2,
    b_fc2,
    cotangent,
):
    seq_count, local_len, model_width = tokens.shape
    shard_rows = w_qkv.shape[0]
    hidden_ratio = w_fc1.shape[1] // model_width
    head_count = model_width // HEAD_DIM
    token_count = seq_count * local_len
    places = lax.axis_index("ctx") * local_len + jnp.arange(local_len, dtype=jnp.int32)
    angles = rotary_angles(places, ROT)
    live_mask = places[None, :] < lengths[:, None]
    inputs = tokens.astype(jnp.float32).reshape(token_count, model_width)
    average = jnp.mean(inputs, axis=-1, keepdims=True)
    centered = inputs - average
    variance = jnp.mean(centered * centered, axis=-1, keepdims=True)
    inv_std = lax.rsqrt(variance + eps_norm)
    normed = centered * inv_std
    qkv_bias_rows = b_qkv.reshape(shard_rows, 3)
    fc1_bias_rows = b_fc1.reshape(shard_rows, hidden_ratio)
    fc2_rows = w_fc2.reshape(shard_rows, hidden_ratio * model_width)
    inner_full = (
        lax.all_gather(w_qkv, ("dp", "ctx"), axis=0, tiled=True),
        lax.all_gather(w_fc1, ("dp", "ctx"), axis=0, tiled=True),
        lax.all_gather(ln_gain, ("dp", "ctx"), axis=0, tiled=True),
        lax.all_gather(ln_bias, ("dp", "ctx"), axis=0, tiled=True),
        lax.all_gather(qkv_bias_rows, ("dp", "ctx"), axis=0, tiled=True),
        lax.all_gather(fc1_bias_rows, ("dp", "ctx"), axis=0, tiled=True),
    )
    gain_full = inner_full[2].astype(jnp.float32)
    shift_full = inner_full[3].astype(jnp.float32)
    hidden = (normed * gain_full + shift_full).astype(jnp.bfloat16)
    qkv_acc = jnp.dot(hidden, inner_full[0], preferred_element_type=jnp.float32)
    up_acc = jnp.dot(hidden, inner_full[1], preferred_element_type=jnp.float32)
    qkv_bias = inner_full[4].reshape(-1).astype(jnp.float32)
    fc1_bias = inner_full[5].reshape(-1).astype(jnp.float32)
    qkv_proj = (qkv_acc + qkv_bias).reshape(seq_count, local_len, 3, head_count, HEAD_DIM)
    queries = (rotary(qkv_proj[:, :, 0], angles) * 0.125).astype(jnp.bfloat16)
    key_local = (
        rotary(qkv_proj[:, :, 1], angles)
        .astype(jnp.bfloat16)
        .reshape(seq_count, local_len, model_width)
    )
    value_local = qkv_proj[:, :, 2].astype(jnp.bfloat16).reshape(seq_count, local_len, model_width)
    key_full, value_full = (
        lax.all_gather(key_local, "ctx", axis=1, tiled=True),
        lax.all_gather(value_local, "ctx", axis=1, tiled=True),
    )
    total_len = key_full.shape[1]

    def attend_forward(packed):
        query_seq, key_seq, value_seq, length = packed
        key_heads = key_seq.reshape(total_len, head_count, HEAD_DIM)
        value_heads = value_seq.reshape(total_len, head_count, HEAD_DIM)
        scores = masked_scores(query_seq, key_heads, places, length)
        row_max = jnp.max(scores, axis=-1, keepdims=True)
        exponent = jnp.exp(scores - row_max)
        row_sum = jnp.sum(exponent, axis=-1, keepdims=True)
        probability = (exponent / row_sum).astype(jnp.bfloat16)
        attended = jnp.einsum(
            "hqk,khd->qhd", probability, value_heads, preferred_element_type=jnp.float32
        )
        log_total = (row_max + jnp.log(row_sum))[..., 0]
        return (attended.reshape(local_len, model_width).astype(jnp.bfloat16), log_total)

    attn_seq, log_totals = lax.map(attend_forward, (queries, key_full, value_full, lengths))
    attn_mixed = attn_seq.reshape(token_count, model_width)
    up_proj = up_acc + fc1_bias
    activated = gelu_tanh(up_proj).astype(jnp.bfloat16)
    outer_full = (
        lax.all_gather(w_out, ("dp", "ctx"), axis=0, tiled=True),
        lax.all_gather(fc2_rows, ("dp", "ctx"), axis=0, tiled=True),
        lax.all_gather(b_out, ("dp", "ctx"), axis=0, tiled=True),
        lax.all_gather(b_fc2, ("dp", "ctx"), axis=0, tiled=True),
    )
    branch = jnp.dot(attn_mixed, outer_full[0], preferred_element_type=jnp.float32) + jnp.dot(
        activated,
        outer_full[1].reshape(hidden_ratio * model_width, model_width),
        preferred_element_type=jnp.float32,
    )
    out_bias = outer_full[2].astype(jnp.float32)
    fc2_bias = outer_full[3].astype(jnp.float32)
    output = (
        (inputs + branch + out_bias + fc2_bias)
        .astype(jnp.bfloat16)
        .reshape(seq_count, local_len, model_width)
    )
    grad_out = jnp.where(live_mask[:, :, None], cotangent, jnp.zeros((), jnp.bfloat16)).reshape(
        token_count, model_width
    )
    out_back, fc2_back = (
        lax.all_gather(w_out, ("dp", "ctx"), axis=0, tiled=True),
        lax.all_gather(fc2_rows, ("dp", "ctx"), axis=0, tiled=True),
    )
    fc2_matrix = fc2_back.reshape(hidden_ratio * model_width, model_width)
    grad_mixed = jnp.einsum(
        "td,kd->tk", grad_out, out_back, preferred_element_type=jnp.float32
    ).astype(jnp.bfloat16)
    grad_act = jnp.einsum("td,kd->tk", grad_out, fc2_matrix, preferred_element_type=jnp.float32)
    gelu_value, gelu_pull = jax.vjp(gelu_tanh, up_proj)
    grad_up = gelu_pull(grad_act)[0].astype(jnp.bfloat16)
    key_back, value_back = (
        lax.all_gather(key_local, "ctx", axis=1, tiled=True),
        lax.all_gather(value_local, "ctx", axis=1, tiled=True),
    )

    def attend_backward(packed):
        query_seq, key_seq, value_seq, grad_seq, log_total, length = packed
        key_heads = key_seq.reshape(total_len, head_count, HEAD_DIM)
        value_heads = value_seq.reshape(total_len, head_count, HEAD_DIM)
        grad_heads = grad_seq.reshape(local_len, head_count, HEAD_DIM)
        scores = masked_scores(query_seq, key_heads, places, length)
        probability = jnp.exp(scores - log_total[:, :, None])
        grad_probs = jnp.einsum(
            "qhd,khd->hqk", grad_heads, value_heads, preferred_element_type=jnp.float32
        )
        inner = jnp.sum(probability * grad_probs, axis=-1, keepdims=True)
        grad_scores = (probability * (grad_probs - inner)).astype(jnp.bfloat16)
        grad_query = jnp.einsum(
            "hqk,khd->qhd", grad_scores, key_heads, preferred_element_type=jnp.float32
        )
        grad_keys = jnp.einsum(
            "hqk,qhd->khd", grad_scores, query_seq, preferred_element_type=jnp.float32
        )
        grad_values = jnp.einsum(
            "hqk,qhd->khd",
            probability.astype(jnp.bfloat16),
            grad_heads,
            preferred_element_type=jnp.float32,
        )
        return (
            grad_query,
            grad_keys.reshape(total_len, model_width),
            grad_values.reshape(total_len, model_width),
        )

    grad_query, grad_keys_all, grad_values_all = lax.map(
        attend_backward,
        (
            queries,
            key_back,
            value_back,
            grad_mixed.reshape(seq_count, local_len, model_width),
            log_totals,
            lengths,
        ),
    )
    grad_keys_own, grad_values_own = (
        lax.psum_scatter(grad_keys_all, "ctx", scatter_dimension=1, tiled=True),
        lax.psum_scatter(grad_values_all, "ctx", scatter_dimension=1, tiled=True),
    )
    grad_query_pre = rotary_back(grad_query * 0.125, angles).reshape(token_count, model_width)
    grad_keys_pre = rotary_back(
        grad_keys_own.reshape(seq_count, local_len, head_count, HEAD_DIM), angles
    ).reshape(token_count, model_width)
    grad_qkv = jnp.concatenate(
        [grad_query_pre, grad_keys_pre, grad_values_own.reshape(token_count, model_width)], axis=-1
    ).astype(jnp.bfloat16)
    qkv_matrix, fc1_matrix = (
        lax.all_gather(w_qkv, ("dp", "ctx"), axis=0, tiled=True),
        lax.all_gather(w_fc1, ("dp", "ctx"), axis=0, tiled=True),
    )
    grad_hidden = jnp.einsum(
        "tj,dj->td", grad_qkv, qkv_matrix, preferred_element_type=jnp.float32
    ) + jnp.einsum("tj,dj->td", grad_up, fc1_matrix, preferred_element_type=jnp.float32)
    gain_term = jnp.sum(grad_hidden * normed, axis=0)
    shift_term = jnp.sum(grad_hidden, axis=0)
    grad_norm = grad_hidden * gain_full
    grad_input = grad_out.astype(jnp.float32) + inv_std * (
        grad_norm
        - jnp.mean(grad_norm, axis=-1, keepdims=True)
        - normed * jnp.mean(grad_norm * normed, axis=-1, keepdims=True)
    )
    grad_input = grad_input.astype(jnp.bfloat16).reshape(seq_count, local_len, model_width)
    wout_term = jnp.einsum("tk,td->kd", attn_mixed, grad_out, preferred_element_type=jnp.float32)
    wfc2_term = jnp.einsum(
        "tk,td->kd", activated, grad_out, preferred_element_type=jnp.float32
    ).reshape(model_width, hidden_ratio * model_width)
    bias_term = jnp.sum(grad_out, axis=0, dtype=jnp.float32)
    bqkv_term = jnp.sum(grad_qkv, axis=0, dtype=jnp.float32).reshape(model_width, 3)
    bfc1_term = jnp.sum(grad_up, axis=0, dtype=jnp.float32).reshape(model_width, hidden_ratio)
    grad_wout, grad_wfc2, grad_bias, grad_gain, grad_shift, grad_bqkv, grad_bfc1 = (
        lax.psum_scatter(wout_term, ("dp", "ctx"), scatter_dimension=0, tiled=True),
        lax.psum_scatter(wfc2_term, ("dp", "ctx"), scatter_dimension=0, tiled=True),
        lax.psum_scatter(bias_term, ("dp", "ctx"), scatter_dimension=0, tiled=True),
        lax.psum_scatter(gain_term, ("dp", "ctx"), scatter_dimension=0, tiled=True),
        lax.psum_scatter(shift_term, ("dp", "ctx"), scatter_dimension=0, tiled=True),
        lax.psum_scatter(bqkv_term, ("dp", "ctx"), scatter_dimension=0, tiled=True),
        lax.psum_scatter(bfc1_term, ("dp", "ctx"), scatter_dimension=0, tiled=True),
    )
    qkv_part = jnp.einsum("tk,tj->kj", hidden, grad_qkv, preferred_element_type=jnp.float32)
    fc1_part = jnp.einsum("tk,tj->kj", hidden, grad_up, preferred_element_type=jnp.float32)
    inner_sum = lax.psum_scatter(
        jnp.concatenate([qkv_part, fc1_part], axis=1),
        ("dp", "ctx"),
        scatter_dimension=0,
        tiled=True,
    )
    grad_wqkv = inner_sum[:, : 3 * model_width]
    grad_wfc1 = inner_sum[:, 3 * model_width :]
    return (
        output,
        grad_input,
        grad_gain,
        grad_shift,
        grad_wqkv,
        grad_bqkv.reshape(-1),
        grad_wout,
        grad_bias,
        grad_wfc1,
        grad_bfc1.reshape(-1),
        grad_wfc2.reshape(shard_rows * hidden_ratio, model_width),
        grad_bias,
    )


def general_solution(mesh):
    placed = (
        P("dp", "ctx", None),
        P("dp"),
        P(("dp", "ctx")),
        P(("dp", "ctx")),
        P(("dp", "ctx"), None),
        P(("dp", "ctx")),
        P(("dp", "ctx"), None),
        P(("dp", "ctx")),
        P(("dp", "ctx"), None),
        P(("dp", "ctx")),
        P(("dp", "ctx"), None),
        P(("dp", "ctx")),
        P("dp", "ctx", None),
    )
    return jax.shard_map(
        on_device,
        mesh=mesh,
        in_specs=placed,
        out_specs=(
            P("dp", "ctx", None),
            P("dp", "ctx", None),
            P(("dp", "ctx")),
            P(("dp", "ctx")),
            P(("dp", "ctx"), None),
            P(("dp", "ctx")),
            P(("dp", "ctx"), None),
            P(("dp", "ctx")),
            P(("dp", "ctx"), None),
            P(("dp", "ctx")),
            P(("dp", "ctx"), None),
            P(("dp", "ctx")),
        ),
        check_vma=False,
    )


FINE = ("zh", "zl", "y", "x", "c")
ROWS_AXES = ("zl", "x", "c")


def swap(values, axis):
    return lax.ppermute(values, axis, [(0, 1), (1, 0)])


def after(values, earlier):
    return lax.optimization_barrier((values, earlier))[0]


def gather_blocks(own):
    across = swap(own, "zh")
    beside = swap(own, "y")
    both = swap(across, "y")
    return own, beside, across, both


def by_place(blocks, zh, y):
    first, second, third, fourth = blocks
    a, b = jnp.where(y == 1, second, first), jnp.where(y == 1, first, second)
    c, d = jnp.where(y == 1, fourth, third), jnp.where(y == 1, third, fourth)
    return (
        jnp.where(zh == 1, c, a),
        jnp.where(zh == 1, d, b),
        jnp.where(zh == 1, a, c),
        jnp.where(zh == 1, b, d),
    )


def natural_rows(blocks):
    halves = [jnp.split(block, 2, axis=0) for block in blocks]
    return jnp.concatenate(
        [halves[2 * zh + y][zl] for zh in range(2) for zl in range(2) for y in range(2)], axis=0
    )


def dot(left, right, dims):
    return lax.dot_general(left, right, (dims, ((), ())), preferred_element_type=jnp.float32)


QB = 256


def nt(a, b):
    return dot(a, b, ((1,), (1,)))


def nn(a, b):
    return dot(a, b, ((1,), (0,)))


def tn(a, b):
    return dot(a, b, ((0,), (0,)))


def attention_kernel(len_ref, bias_ref, cos_ref, sin_ref, q_in, k_in, v_in, go_in, mixed_ref, grad_ref, sum_ref,
                     q_s, k_s, v_s, g_s, gk_s, gv_s, *, total, pairs):
    f32, bf16 = jnp.float32, jnp.bfloat16
    pair = pl.program_id(1)
    lane = lax.broadcasted_iota(jnp.int32, (1, 128), 1)
    in_head = lane % 64
    first = in_head < 16
    heads = [(lane < 64), (lane >= 64)]
    length = len_ref[pl.program_id(0)]

    def other(v):
        return jnp.where(first, pltpu.roll(v, 112, 1), pltpu.roll(v, 16, 1))
    def col(part):
        return pl.multiple_of(part * (pairs * 128) + pair * 128, 128)
    cosines, sines = cos_ref[...], sin_ref[...]
    def turn(v): return v * cosines + other(v) * sines
    def turn_back(v): return v * cosines - other(v) * sines
    q = turn(q_in[...] + bias_ref[:, pl.ds(col(0), 128)]) * 0.125
    k = turn(k_in[...] + bias_ref[:, pl.ds(col(1), 128)])
    v = v_in[...] + bias_ref[:, pl.ds(col(2), 128)]
    g = go_in[...]
    for h in range(2):
        q_s[h] = jnp.where(heads[h], q, 0.0).astype(bf16)
        k_s[h] = jnp.where(heads[h], k, 0.0).astype(bf16)
        v_s[h] = jnp.where(heads[h], v, 0.0).astype(bf16)
        g_s[h] = jnp.where(heads[h], g, 0.0).astype(bf16)
    gk_s[...] = jnp.zeros_like(gk_s)
    gv_s[...] = jnp.zeros_like(gv_s)
    gq_sum = jnp.zeros((1, 128), f32)
    for b in range(total // QB):
        rows = pl.ds(b * QB, QB)
        upto = (b + 1) * QB
        keys = pl.ds(0, upto)
        limit = jnp.minimum(lax.broadcasted_iota(jnp.int32, (1, QB), 1) + (b * QB + 1), length)
        allowed = lax.broadcasted_iota(jnp.int32, (upto, QB), 0) < limit
        mixed = None
        for h in range(2):
            qh, gh = q_s[h, rows], g_s[h, rows]
            s = nt(k_s[h, keys], qh)
            s = jnp.where(allowed, s, -1e30)
            m = jnp.max(s, axis=0, keepdims=True)
            e = jnp.exp(s - m)
            p = e * (1.0 / jnp.sum(e, axis=0, keepdims=True))
            pr = p.astype(bf16)
            gp = nt(v_s[h, keys], gh)
            inner = jnp.sum(p * gp, axis=0, keepdims=True)
            gs = (p * (gp - inner)).astype(bf16)
            gv_s[keys] += nn(pr, gh)
            gk_s[keys] += nn(gs, qh)
            o = tn(pr, v_s[h, keys])
            gq = tn(gs, k_s[h, keys])
            mixed = o if mixed is None else mixed + o
            gq_all = gq if h == 0 else gq_all + gq
        mixed_ref[rows, :] = mixed
        cs, sn = cos_ref[rows], sin_ref[rows]
        gq_all = gq_all * 0.125
        back = (gq_all * cs - other(gq_all) * sn).astype(bf16)
        grad_ref[rows, pl.ds(col(0), 128)] = back.astype(f32)
        gq_sum += jnp.sum(back.astype(f32), axis=0, keepdims=True)
    gk = turn_back(gk_s[...]).astype(bf16)
    gv = gv_s[...].astype(bf16)
    grad_ref[:, pl.ds(col(1), 128)] = gk.astype(f32)
    grad_ref[:, pl.ds(col(2), 128)] = gv.astype(f32)
    sum_ref[0, :, pl.ds(col(0), 128)] = gq_sum
    sum_ref[0, :, pl.ds(col(1), 128)] = jnp.sum(gk.astype(f32), axis=0, keepdims=True)
    sum_ref[0, :, pl.ds(col(2), 128)] = jnp.sum(gv.astype(f32), axis=0, keepdims=True)

def attention(lengths, qkv, bias, grad_mixed, cosines, sines):
    seqs = lengths.shape[0]
    total = qkv.shape[0] // seqs
    width = qkv.shape[1] // 3
    pairs = width // 128
    blk = lambda part: pl.BlockSpec((total, 128), lambda s, p: (s, part * pairs + p))
    whole = lambda shape: pl.BlockSpec(shape, lambda s, p: (0,) * len(shape))
    f32, bf16 = jnp.float32, jnp.bfloat16
    return pl.pallas_call(
        functools.partial(attention_kernel, total=total, pairs=pairs),
        grid=(seqs, pairs),
        in_specs=[
            pl.BlockSpec(memory_space=pltpu.SMEM),
            whole((1, 3 * width)), whole((total, 128)), whole((total, 128)),
            blk(0), blk(1), blk(2),
            pl.BlockSpec((total, 128), lambda s, p: (s, p)),
        ],
        out_specs=[
            pl.BlockSpec((total, 128), lambda s, p: (s, p)),
            pl.BlockSpec((total, 3 * width), lambda s, p: (s, 0)),
            pl.BlockSpec((1, 1, 3 * width), lambda s, p: (s, 0, 0)),
        ],
        out_shape=[
            jax.ShapeDtypeStruct((seqs * total, width), f32),
            jax.ShapeDtypeStruct((seqs * total, 3 * width), f32),
            jax.ShapeDtypeStruct((seqs, 1, 3 * width), f32),
        ],
        scratch_shapes=[pltpu.VMEM((2, total, 128), bf16)] * 4 + [pltpu.VMEM((total, 128), f32)] * 2,
        compiler_params=pltpu.CompilerParams(vmem_limit_bytes=48 * 2**20),
        cost_estimate=pl.CostEstimate(flops=seqs*pairs*2*6*total*total*64*2, bytes_accessed=20*2**20, transcendentals=seqs*pairs*2*total*total),
    )(lengths, bias, cosines, sines, qkv, qkv, qkv, grad_mixed)

def tables(total, rot):
    half = rot // 2
    inv = jnp.exp(-math.log(10000.0) * 2.0 * jnp.arange(half, dtype=jnp.float32) / rot)
    ang = jnp.arange(total, dtype=jnp.int32).astype(jnp.float32)[:, None] * inv[None, :]
    c, s = jnp.cos(ang), jnp.sin(ang)
    one, nil = jnp.ones((total, 64 - rot), jnp.float32), jnp.zeros((total, 64 - rot), jnp.float32)
    cosines = jnp.concatenate([c, c, one] * 2, axis=1)
    sines = jnp.concatenate([-s, s, nil] * 2, axis=1)
    return cosines, sines


MESH_ID = pl.DeviceIdType.MESH


def exchange_kernel(src, dst, send_sem, recv_sem):
    place = [lax.axis_index(name) for name in FINE]
    me = 0
    for p in place:
        me = me * 2 + p

    def away(k):
        return tuple((p + k // 2 ** (4 - i)) % 2 for i, p in enumerate(place))

    def index_of(where):
        number = 0
        for p in where:
            number = number * 2 + p
        return number

    barrier = pltpu.get_barrier_semaphore()

    def greet(k, carry):
        pl.semaphore_signal(barrier, inc=1, device_id=away(k), device_id_type=MESH_ID)
        return carry

    lax.fori_loop(1, 32, greet, 0)
    pl.semaphore_wait(barrier, 31)

    def copy(k):
        where = away(k)
        return pltpu.make_async_remote_copy(
            src_ref=src.at[index_of(where)],
            dst_ref=dst.at[me],
            send_sem=send_sem.at[k],
            recv_sem=recv_sem.at[k],
            device_id=where,
            device_id_type=MESH_ID,
        )

    def send(k, carry):
        copy(k).start()
        return carry

    lax.fori_loop(1, 32, send, 0)
    dst[me] = src[me]

    def finish(k, carry):
        copy(k).wait()
        return carry

    lax.fori_loop(1, 32, finish, 0)


def sum_kernel(src, out, dst, send_sem, recv_sem):
    exchange_kernel(src, dst, send_sem, recv_sem)
    out[...] = jnp.sum(dst[...], axis=0)


def feed_kernel(hidden, fc1, bias, cot, fc2, act, grad, sums):
    up = nn(hidden[...], fc1[...]) + bias[...]
    inner = gelu_coef * (up + 0.044715 * up * up * up)
    bent = jnp.tanh(inner)
    act[...] = (0.5 * up * (1.0 + bent)).astype(jnp.bfloat16)
    slope = 0.5 * (1.0 + bent) + 0.5 * up * (1.0 - bent * bent) * gelu_coef * (
        1.0 + 3.0 * 0.044715 * up * up
    )
    back = (nt(cot[...], fc2[...]) * slope).astype(jnp.bfloat16)
    grad[...] = back

    @pl.when(pl.program_id(0) == 0)
    def _():
        sums[...] = jnp.zeros_like(sums)

    sums[...] += jnp.sum(back.astype(jnp.float32), axis=0, keepdims=True)


def feed(hidden, fc1, bias, cot, fc2):
    tokens, width = hidden.shape
    units = fc1.shape[1]
    block = 256
    some = lambda n: pl.BlockSpec((block, n), lambda i: (i, 0))
    whole = lambda *shape: pl.BlockSpec(shape, lambda i: (0, 0))
    return pl.pallas_call(
        feed_kernel,
        grid=(tokens // block,),
        in_specs=[some(width), whole(width, units), whole(1, units), some(width), whole(units, width)],
        out_specs=[some(units), some(units), whole(1, units)],
        out_shape=[
            jax.ShapeDtypeStruct((tokens, units), jnp.bfloat16),
            jax.ShapeDtypeStruct((tokens, units), jnp.bfloat16),
            jax.ShapeDtypeStruct((1, units), jnp.float32),
        ],
        compiler_params=pltpu.CompilerParams(vmem_limit_bytes=48 * 2**20),
        cost_estimate=pl.CostEstimate(
            flops=4 * tokens * width * units, bytes_accessed=32 * 2**20, transcendentals=tokens * units
        ),
    )(hidden, fc1, bias, cot, fc2)


W_PEERS = [(k // 4, k // 2 % 2, k % 2) for k in range(1, 8)]


def front_kernel(*refs, direct, spread, onward, width):
    f32, bf16 = jnp.float32, jnp.bfloat16
    n_in = 3 + direct + spread
    small, tokens, cot = refs[:3]
    whole_w, spread_w = refs[3 : 3 + direct], refs[3 + direct : n_in]
    small_all, hidden_all, cot_all = refs[n_in : n_in + 3]
    whole_m = refs[n_in + 3 : n_in + 3 + direct]
    spread_m = refs[n_in + 3 + direct : 2 * n_in]
    hidden, send_sem, recv_sem, local_sem, small_send, small_recv = refs[2 * n_in :]
    zh, zl, y, x, c = place = [lax.axis_index(name) for name in FINE]
    me = (((zh * 2 + zl) * 2 + y) * 2 + x) * 2 + c
    names = dict(zip(FINE, place))
    started, used, used_local = [], [0], [0]

    def away(k):
        return tuple((p + k // 2 ** (4 - i)) % 2 for i, p in enumerate(place))

    def send(src, dst, target):
        copy = pltpu.make_async_remote_copy(
            src_ref=src,
            dst_ref=dst,
            send_sem=send_sem.at[used[0]],
            recv_sem=recv_sem.at[used[0]],
            device_id=target,
            device_id_type=MESH_ID,
        )
        used[0] += 1
        copy.start()
        started.append(copy)
        return copy

    def swap_with(src, dst, axis):
        return send(src, dst, tuple(1 - p if name == axis else p for name, p in zip(FINE, place)))

    def keep(src, dst):
        copy = pltpu.make_async_copy(src, dst, local_sem.at[used_local[0]])
        used_local[0] += 1
        copy.start()
        return copy

    barrier = pltpu.get_barrier_semaphore()

    def greet(k, carry):
        pl.semaphore_signal(barrier, inc=1, device_id=away(k), device_id_type=MESH_ID)
        return carry

    lax.fori_loop(1, 32, greet, 0)
    pl.semaphore_wait(barrier, 31)

    def small_copy(k):
        return pltpu.make_async_remote_copy(
            src_ref=small,
            dst_ref=small_all.at[me],
            send_sem=small_send.at[k],
            recv_sem=small_recv.at[k],
            device_id=away(k),
            device_id_type=MESH_ID,
        )

    def small_start(k, carry):
        small_copy(k).start()
        return carry

    def small_wait(k, carry):
        small_copy(k).wait()
        return carry

    lax.fori_loop(1, 32, small_start, 0)
    small_all[me] = small[...]

    columns, kept = [], []
    for weight, matrix, goes in zip(spread_w, spread_m, onward):
        pieces = []
        for dl, dx, dc in W_PEERS:
            where = (zh, (zl + dl) % 2, y, (x + dx) % 2, (c + dc) % 2)
            pieces.append(
                send(
                    weight.at[(where[1] * 2 + where[3]) * 2 + where[4]],
                    matrix.at[zh, zl, y, x * 2 + c] if goes else matrix.at[zl, x * 2 + c],
                    where,
                )
            )
        own = keep(
            weight.at[(zl * 2 + x) * 2 + c],
            matrix.at[zh, zl, y, x * 2 + c] if goes else matrix.at[zl, x * 2 + c],
        )
        columns.append((pieces, own))
    direct_zh = []
    for weight, matrix in zip(whole_w, whole_m):
        direct_zh.append(swap_with(weight, matrix.at[zh, y], "zh"))
        swap_with(weight, matrix.at[zh, y], "y")
        kept.append(keep(weight, matrix.at[zh, y]))
    cot_zl = swap_with(cot, cot_all.at[zl, x, c], "zl")
    cot_x = swap_with(cot, cot_all.at[zl, x, c], "x")
    cot_c = swap_with(cot, cot_all.at[zl, x, c], "c")
    kept.append(keep(cot, cot_all.at[zl, x, c]))

    lax.fori_loop(1, 32, small_wait, 0)
    rows_of = lax.broadcasted_iota(jnp.int32, (32, width), 0)
    lanes_of = lax.broadcasted_iota(jnp.int32, (32, width), 1)
    in_place = lanes_of // (width // 32) == rows_of

    def vector(row):
        part = small_all[:, row, :]
        spread_out = jnp.concatenate([part] * (width // 128), axis=1)
        return jnp.sum(jnp.where(in_place, spread_out, 0.0), axis=0, keepdims=True)

    gain, shift = vector(0), vector(1)

    def norm_rows(i, carry):
        rows = pl.ds(pl.multiple_of(i * 32, 32), 32)
        values = tokens[rows].astype(f32)
        centered = values - jnp.mean(values, axis=-1, keepdims=True)
        variance = jnp.mean(centered * centered, axis=-1, keepdims=True)
        hidden[rows] = (centered * lax.rsqrt(variance + eps_norm) * gain + shift).astype(bf16)
        return carry

    lax.fori_loop(0, tokens.shape[0] // 32, norm_rows, 0)
    hid_zl = swap_with(hidden, hidden_all.at[zl, x, c], "zl")
    hid_x = swap_with(hidden, hidden_all.at[zl, x, c], "x")
    hid_c = swap_with(hidden, hidden_all.at[zl, x, c], "c")
    kept.append(keep(hidden, hidden_all.at[zl, x, c]))

    def forward_columns(i):
        pieces, own = columns[i]
        for piece in pieces:
            piece.wait_recv()
        own.wait()
        waits = []
        if not onward[i]:
            return waits
        for half in range(2):
            block = spread_m[i].at[zh, half, y]
            waits.append(swap_with(block, block, "zh"))
            swap_with(block, block, "y")
        return waits

    def forward_zh(copies, blocks):
        for copy, block in zip(copies, blocks):
            copy.wait_recv()
            swap_with(block, block, "y")
        return copies

    def halves(i):
        return [spread_m[i].at[1 - zh, half, y] for half in range(2)]

    received = []
    columns_zh = [forward_columns(0)]
    cot_zl.wait_recv()
    block = cot_all.at[1 - zl, x, c]
    cot_zx = swap_with(block, block, "x")
    cot_zc = swap_with(block, block, "c")
    columns_zh += [forward_columns(i) if onward[i] else [] for i in range(1, spread)]
    hid_zl.wait_recv()
    block = hidden_all.at[1 - zl, x, c]
    hid_zx = swap_with(block, block, "x")
    hid_zc = swap_with(block, block, "c")
    forward_zh(direct_zh[:1], [whole_m[0].at[1 - zh, y]])
    received += direct_zh[:1]
    for copy, where in ((cot_x, cot_all.at[zl, 1 - x, c]), (cot_zx, cot_all.at[1 - zl, 1 - x, c])):
        copy.wait_recv()
        swap_with(where, where, "c")
        received.append(copy)
    for copy, where in ((hid_x, hidden_all.at[zl, 1 - x, c]), (hid_zx, hidden_all.at[1 - zl, 1 - x, c])):
        copy.wait_recv()
        swap_with(where, where, "c")
        received.append(copy)
    received += forward_zh(direct_zh[1:], [m.at[1 - zh, y] for m in whole_m[1:]])
    for i in range(spread):
        if onward[i]:
            received += forward_zh(columns_zh[i], halves(i))
        else:
            for piece in columns[i][0]:
                piece.wait_recv()
            kept.append(columns[i][1])
        received += columns[i][0]
    received += [cot_zl, hid_zl]
    seen = {id(copy) for copy in received}
    for copy in started:
        if id(copy) not in seen:
            copy.wait_recv()
    for copy in started:
        copy.wait_send()
    for copy in kept:
        copy.wait()


def front(small, tokens, cot, whole_w, spread_w, onward):
    direct, spread = len(whole_w), len(spread_w)
    n, width, rows = small.shape[0], tokens.shape[1], tokens.shape[0]
    bf16 = jnp.bfloat16
    n_copies = spread * 7 + sum(onward) * 6 + direct * 3 + 14
    n_local = spread + direct + 2
    hbm, vmem = pl.BlockSpec(memory_space=pl.ANY), pl.BlockSpec(memory_space=pltpu.VMEM)
    shapes = [
        jax.ShapeDtypeStruct((32, n, 128), jnp.float32),
        jax.ShapeDtypeStruct((2, 2, 2, rows, width), bf16),
        jax.ShapeDtypeStruct((2, 2, 2, rows, width), bf16),
    ]
    shapes += [jax.ShapeDtypeStruct((2, 2) + w.shape, bf16) for w in whole_w]
    shapes += [
        jax.ShapeDtypeStruct(((2, 2, 2, 4) if goes else (2, 4)) + w.shape[1:], bf16)
        for w, goes in zip(spread_w, onward)
    ]
    return pl.pallas_call(
        functools.partial(
            front_kernel, direct=direct, spread=spread, onward=onward, width=width
        ),
        out_shape=shapes,
        in_specs=[vmem, vmem, hbm] + [hbm] * (direct + spread),
        out_specs=[vmem] + [hbm] * (2 + direct + spread),
        scratch_shapes=[
            pltpu.VMEM((rows, width), bf16),
            pltpu.SemaphoreType.DMA((n_copies,)),
            pltpu.SemaphoreType.DMA((n_copies,)),
            pltpu.SemaphoreType.DMA((n_local,)),
            pltpu.SemaphoreType.DMA((32,)),
            pltpu.SemaphoreType.DMA((32,)),
        ],
        compiler_params=pltpu.CompilerParams(
            collective_id=0, has_side_effects=True, vmem_limit_bytes=24 * 2**20
        ),
    )(small, tokens, cot, *whole_w, *spread_w)


def sum_small(values, collective_id):
    n = values.shape[1]
    return pl.pallas_call(
        sum_kernel,
        out_shape=jax.ShapeDtypeStruct((n, 128), jnp.float32),
        in_specs=[pl.BlockSpec(memory_space=pltpu.VMEM)],
        out_specs=pl.BlockSpec(memory_space=pltpu.VMEM),
        scratch_shapes=[
            pltpu.VMEM((32, n, 128), jnp.float32),
            pltpu.SemaphoreType.DMA((32,)),
            pltpu.SemaphoreType.DMA((32,)),
        ],
        compiler_params=pltpu.CompilerParams(collective_id=collective_id, has_side_effects=True),
    )(values)


def back_kernel(
    gqkv, gup, attn, act, qkv_hbm, fc1_hbm, out_hbm, fc2_hbm, fc2_part, fc1_part, out_part, qkv_part,
    gh_own, br_own, fc2_out, out_out, fc1_out, qkv_out, c_got, w_got, wide_y, wide_z, cols_y, cols_z,
    qkv_w, fc1_w, out_w, fc2_w, mine, sent, stage, full, wide, cols, wide_s, cols_s, fc1_a, qkv_a,
    send_sem, recv_sem, local_sem, c_send, c_recv,
):
    f32, bf16 = jnp.float32, jnp.bfloat16
    zh, zl, y, x, c = place = [lax.axis_index(name) for name in FINE]
    used, used_local = [0], [0]
    sends = []

    def remote(src, dst, target):
        copy = pltpu.make_async_remote_copy(
            src_ref=src,
            dst_ref=dst,
            send_sem=send_sem.at[used[0]],
            recv_sem=recv_sem.at[used[0]],
            device_id=target,
            device_id_type=MESH_ID,
        )
        used[0] += 1
        copy.start()
        sends.append(copy)
        return copy

    def partner(axis):
        return tuple(1 - p if name == axis else p for name, p in zip(FINE, place))

    def local(src, dst):
        copy = pltpu.make_async_copy(src, dst, local_sem.at[used_local[0]])
        used_local[0] += 1
        copy.start()
        return copy

    def load(*pairs):
        copies = [local(src, dst) for src, dst in pairs]
        for copy in copies:
            copy.wait()

    barrier = pltpu.get_barrier_semaphore()
    peers = [(zh, (zl + dl) % 2, y, (x + dx) % 2, (c + dc) % 2) for dl, dx, dc in W_PEERS]
    for where in peers + [partner("zh"), partner("y")]:
        pl.semaphore_signal(barrier, inc=1, device_id=where, device_id_type=MESH_ID)
    pl.semaphore_wait(barrier, 9)

    gh_weights = [local(qkv_hbm, qkv_w), local(fc1_hbm, fc1_w)]
    br_weights = [local(out_hbm, out_w), local(fc2_hbm, fc2_w)]

    def row_job(part, rows, first, slot, put):
        some = pl.ds(0, rows)
        return dict(
            part=lambda a, b: part.at[a, b, pl.ds(first, rows)],
            y=[wide_y.at[slot, j, some] for j in range(2)],
            z=wide_z.at[slot, some],
            v=[wide.at[j, some] for j in range(3)],
            s=wide_s.at[slot, some],
            put=put,
            rows=some,
        )

    def column_job(part, width, away, slot, to):
        lanes = pl.ds(0, width)
        return dict(
            part=lambda a, b: part.at[a, (zl + away) % 2, b],
            y=[cols_y.at[slot, j, :, lanes] for j in range(2)],
            z=cols_z.at[slot, :, lanes],
            v=[cols.at[j, :, lanes] for j in range(3)],
            s=cols_s.at[slot, :, lanes],
            away=away,
            to=to,
        )

    fc1_width, qkv_width = fc1_w.shape[1], qkv_w.shape[1]
    out_rows, fc2_rows = out_part.shape[2], fc2_part.shape[2] // 2
    jobs = [
        row_job(fc2_part, fc2_rows, i * fc2_rows, i, fc2_out.at[pl.ds(i * fc2_rows, fc2_rows)])
        for i in range(2)
    ]
    jobs += [column_job(fc1_part, fc1_width, away, away, fc1_a) for away in (1, 0)]
    jobs += [row_job(out_part, out_rows, 0, 2, out_out)]
    jobs += [column_job(qkv_part, qkv_width, away, 2 + away, qkv_a) for away in (1, 0)]
    for job in jobs:
        job["y_far"] = remote(job["part"](1 - zh, 1 - y), job["y"][1], partner("y"))
        job["y_own"] = remote(job["part"](zh, 1 - y), job["y"][0], partner("y"))

    def pass_on(job):
        job["y_far"].wait_recv()
        v = job["v"]
        load((job["part"](1 - zh, y), v[0]), (job["y"][1], v[1]))
        job["s"][...] = (v[0][...].astype(f32) + v[1][...].astype(f32)).astype(bf16)
        job["z_copy"] = remote(job["s"], job["z"], partner("zh"))

    arrivals, kept = [], []

    def finish(job):
        job["y_own"].wait_recv()
        job["z_copy"].wait_recv()
        v = job["v"]
        load((job["part"](zh, y), v[0]), (job["y"][0], v[1]), (job["z"], v[2]))
        total = v[0][...].astype(f32) + v[1][...].astype(f32) + v[2][...].astype(f32)
        if "put" in job:
            full[job["rows"]] = total
            load((full.at[job["rows"]], job["put"]))
            return
        job["z_copy"].wait_send()
        sends[:] = [copy for copy in sends if copy is not job["z_copy"]]
        job["s"][...] = total.astype(bf16)
        piece = job["s"].shape[0] // 4
        for dx in range(2):
            for dc in range(2):
                where = (zh, (zl + job["away"]) % 2, y, (x + dx) % 2, (c + dc) % 2)
                row = pl.multiple_of((where[3] * 2 + where[4]) * piece, piece)
                src = job["s"].at[pl.ds(row, piece)]
                dst = job["to"].at[(zl * 2 + x) * 2 + c]
                if job["away"] or dx or dc:
                    arrivals.append(remote(src, dst, where))
                else:
                    kept.append(local(src, dst))

    def core_copy(n, g):
        return pltpu.make_async_remote_copy(
            src_ref=sent.at[n, g],
            dst_ref=c_got.at[n, g],
            send_sem=c_send.at[n, g],
            recv_sem=c_recv.at[n, g],
            device_id=partner("c"),
            device_id_type=MESH_ID,
        )

    axes = (("x", "zl"), ("zl", "x"))

    def multiply_groups(n, first, a, v, b, w, multiply):
        def step(g, carry):
            one, two = 1 - g // 2, 1 - g % 2
            dl, dx = (two, one) if n == 0 else (one, two)
            rest = ((zl + dl) % 2 * 2 + (x + dx) % 2) * 2

            def block(where):
                rows = pl.ds(pl.multiple_of((rest + where) * 256, 256), 256)
                return (multiply(a[rows], v[...]) + multiply(b[rows], w[...])).astype(bf16)

            sent[n, g] = block(1 - c)
            core_copy(n, g).start()
            mine[n, g] = block(c)
            return carry

        lax.fori_loop(first, first + 2, step, 0)

    def add(n, g, got):
        load((got, stage))
        mine[n, g] = (mine[n, g].astype(f32) + stage[...].astype(f32)).astype(bf16)

    def add_core(n, g):
        core_copy(n, g).wait_recv()
        add(n, g, c_got.at[n, g])

    first_copies, second_copies = {}, {}

    def send_first(n):
        for g in range(2):
            add_core(n, g)
            first_copies[n, g] = remote(mine.at[n, g], w_got.at[n, g], partner(axes[n][0]))

    def send_second(n):
        first_copies[n, 0].wait_recv()
        add(n, 2, w_got.at[n, 0])
        second_copies[n] = remote(mine.at[n, 2], w_got.at[n, 2], partner(axes[n][1]))

    def add_first(n):
        first_copies[n, 1].wait_recv()
        add(n, 3, w_got.at[n, 1])

    def total(n, out):
        second_copies[n].wait_recv()
        load((w_got.at[n, 2], stage))
        full[...] = mine[n, 3].astype(f32) + stage[...].astype(f32)
        load((full, out))

    for copy in gh_weights:
        copy.wait()
    multiply_groups(0, 0, gqkv, qkv_w, gup, fc1_w, nt)
    send_first(0)
    for copy in br_weights:
        copy.wait()
    multiply_groups(1, 0, attn, out_w, act, fc2_w, nn)
    send_first(1)
    pass_on(jobs[0])
    multiply_groups(0, 2, gqkv, qkv_w, gup, fc1_w, nt)
    multiply_groups(1, 2, attn, out_w, act, fc2_w, nn)
    for n in range(2):
        add_core(n, 2)
        add_core(n, 3)
    send_second(0)
    pass_on(jobs[1])
    send_second(1)
    finish(jobs[0])
    add_first(0)
    add_first(1)
    pass_on(jobs[2])
    finish(jobs[1])
    total(0, gh_own)
    total(1, br_own)
    pass_on(jobs[3])
    finish(jobs[2])
    pass_on(jobs[4])
    pass_on(jobs[5])
    finish(jobs[3])
    pass_on(jobs[6])
    for job in jobs[4:]:
        finish(job)

    for copy in arrivals:
        copy.wait_recv()
    for copy in kept:
        copy.wait()
    unit = fc1_width // 4
    for w in range(8):
        for t in range(4):
            at = ((t // 2 * 2 + w // 4) * 2 + t % 2) * 4 * unit + w % 4 * unit
            fc1_out[:, at : at + unit] = fc1_a[w, :, t * unit : (t + 1) * unit].astype(f32)
    low = lax.broadcasted_iota(jnp.int32, (1, 128), 1) < HEAD_DIM
    for part in range(3):
        for a in range(2):
            for dl in range(2):
                for dx in range(2):
                    at = part * (qkv_width // 3) + a * 128
                    even, odd = (
                        qkv_a[dl * 4 + dx * 2 + k, :, at : at + 128].astype(f32) for k in range(2)
                    )
                    to = part * (8 * qkv_width // 3) + a * 1024 + dl * 512 + dx * 128
                    qkv_out[:, to : to + 128] = jnp.where(low, even, pltpu.roll(odd, 64, 1))
                    qkv_out[:, to + 256 : to + 384] = jnp.where(low, pltpu.roll(even, 64, 1), odd)

    for copy in sends:
        copy.wait_send()
    for n in range(2):
        for g in range(4):
            core_copy(n, g).wait_send()


def back(gqkv, gup, attn, act, qkv_w, fc1_w, out_w, fc2_w, fc2_part, fc1_part, out_part, qkv_part):
    bf16, f32 = jnp.bfloat16, jnp.float32
    width = qkv_w.shape[0]
    block = gqkv.shape[0] // 8
    rows, ff_rows = out_w.shape[0] // 4, fc2_w.shape[0] // 4
    fc1_width, qkv_width = fc1_w.shape[1], qkv_w.shape[1]
    half = ff_rows // 2
    any_, vmem = pl.BlockSpec(memory_space=pl.ANY), pl.BlockSpec(memory_space=pltpu.VMEM)
    shapes = [
        ((block, width), f32, any_),
        ((block, width), f32, any_),
        ((ff_rows, width), f32, any_),
        ((rows, width), f32, any_),
        ((rows, 8 * fc1_width), f32, vmem),
        ((rows, 8 * qkv_width), f32, vmem),
        ((2, 4, block, width), bf16, any_),
        ((2, 3, block, width), bf16, any_),
        ((3, 2, half, width), bf16, any_),
        ((3, half, width), bf16, any_),
        ((4, 2, 4 * rows, fc1_width), bf16, any_),
        ((4, 4 * rows, fc1_width), bf16, any_),
    ]
    scratch = [
        pltpu.VMEM(qkv_w.shape, bf16),
        pltpu.VMEM(fc1_w.shape, bf16),
        pltpu.VMEM(out_w.shape, bf16),
        pltpu.VMEM(fc2_w.shape, bf16),
        pltpu.VMEM((2, 4, block, width), bf16),
        pltpu.VMEM((2, 4, block, width), bf16),
        pltpu.VMEM((block, width), bf16),
        pltpu.VMEM((block, width), f32),
        pltpu.VMEM((3, half, width), bf16),
        pltpu.VMEM((3, 4 * rows, fc1_width), bf16),
        pltpu.VMEM((3, half, width), bf16),
        pltpu.VMEM((4, 4 * rows, fc1_width), bf16),
        pltpu.VMEM((8, rows, fc1_width), bf16),
        pltpu.VMEM((8, rows, qkv_width), bf16),
        pltpu.SemaphoreType.DMA((48,)),
        pltpu.SemaphoreType.DMA((48,)),
        pltpu.SemaphoreType.DMA((96,)),
        pltpu.SemaphoreType.DMA((2, 4)),
        pltpu.SemaphoreType.DMA((2, 4)),
    ]
    parts = [
        fc2_part.reshape(2, 2, ff_rows, width),
        fc1_part.reshape(2, 2, 2, 4 * rows, fc1_width),
        out_part.reshape(2, 2, rows, width),
        qkv_part.reshape(2, 2, 2, 4 * rows, qkv_width),
    ]
    return pl.pallas_call(
        back_kernel,
        out_shape=[jax.ShapeDtypeStruct(shape, kind) for shape, kind, _ in shapes],
        in_specs=[vmem] * 4 + [any_] * 8,
        out_specs=[spec for _, _, spec in shapes],
        scratch_shapes=scratch,
        compiler_params=pltpu.CompilerParams(
            collective_id=2, has_side_effects=True, vmem_limit_bytes=62 * 2**20
        ),
    )(gqkv, gup, attn, act, qkv_w, fc1_w, out_w, fc2_w, *parts)[:6]


def split_device(
    tokens,
    lengths,
    ln_gain,
    ln_bias,
    w_qkv,
    b_qkv,
    w_out,
    b_out,
    w_fc1,
    b_fc1,
    w_fc2,
    b_fc2,
    cotangent,
):
    bf16, f32 = jnp.bfloat16, jnp.float32
    zh, zl, y, x, c = (lax.axis_index(name) for name in FINE)
    place = (zl * 2 + x) * 2 + c
    _, local_len, width = tokens.shape
    rows = w_qkv.shape[0]
    ff_rows = w_fc2.shape[0]
    pieces = 4
    total_len = local_len * pieces
    heads = 4
    own_width = heads * HEAD_DIM

    twice = [jnp.concatenate([v, v]).astype(f32) for v in (ln_gain, ln_bias)]
    small = jnp.concatenate(
        twice + [v.astype(f32) for v in (b_qkv, b_out, b_fc1, b_fc2, lengths)]
    )
    filled = -(-small.shape[0] // 128) * 128
    small = jnp.pad(small, (0, filled - small.shape[0])).reshape(-1, 128)
    places = (x * 2 + c) * local_len + jnp.arange(local_len, dtype=jnp.int32)
    grad_own = jnp.where((places < lengths[0])[:, None], cotangent[0], jnp.zeros((), bf16))
    fc1_spread = (
        w_fc1.reshape((rows, 2, 2, 2, 2, 2, ff_rows))
        .transpose(2, 4, 5, 0, 1, 3, 6)
        .reshape(8, rows, -1)
    )
    qkv_spread = (
        w_qkv.reshape((rows, 3, 2, 2, 2, 2, 2, HEAD_DIM))
        .transpose(3, 5, 6, 0, 1, 2, 4, 7)
        .reshape(8, rows, -1)
    )
    small_all, hidden, grad_out, fc2_mat, fc1_mat, qkv_own = front(
        small, tokens[0], grad_own, [w_fc2], [fc1_spread, qkv_spread], (True, False)
    )
    hidden, grad_out = hidden.reshape(-1, width), grad_out.reshape(-1, width)
    fc2_mat, fc1_mat = fc2_mat.reshape(-1, width), fc1_mat.reshape(width, -1)
    qkv_got = gather_blocks(after(qkv_own.reshape(8 * rows, -1), fc2_mat))
    out_got = gather_blocks(after(w_out, fc2_mat))
    small_all = small_all.reshape(32, filled)
    ends = np.cumsum([2 * rows, 2 * rows, 3 * rows, rows, ff_rows, rows, 1])
    gain_all, shift_all, bqkv_all, bout_all, bfc1_all, bfc2_all, lengths_all = jnp.split(
        small_all, ends, axis=1
    )[:-1]
    gain_all = gain_all[:, :rows].reshape(-1)
    bqkv_all, bout_all, bfc1_all, bfc2_all = (
        part.reshape(-1) for part in (bqkv_all, bout_all, bfc1_all, bfc2_all)
    )
    pair_lengths = lax.dynamic_index_in_dim(
        lengths_all.reshape(2, 2, 2, 4)[:, :, :, 0].transpose(0, 2, 1).reshape(4, 2),
        zh * 2 + y,
        keepdims=False,
    ).astype(jnp.int32)

    inputs = tokens[0].astype(f32)
    average = jnp.mean(inputs, axis=-1, keepdims=True)
    centered = inputs - average
    variance = jnp.mean(centered * centered, axis=-1, keepdims=True)
    inv_std = lax.rsqrt(variance + eps_norm)
    normed = centered * inv_std

    bqkv = lax.dynamic_index_in_dim(
        bqkv_all.reshape(3, 2, 2, 2, 4, HEAD_DIM).transpose(2, 4, 0, 1, 3, 5).reshape(8, -1),
        place,
        keepdims=False,
    )
    bfc1 = lax.dynamic_index_in_dim(
        bfc1_all.reshape(2, 2, 2, 4, ff_rows).transpose(1, 3, 0, 2, 4).reshape(8, -1),
        place,
        keepdims=False,
    )

    activated, grad_up, grad_up_sum = feed(hidden, fc1_mat, bfc1[None], grad_out, fc2_mat)

    fc2_part = dot(activated, grad_out, ((0,), (0,))).astype(bf16)
    fc1_part = dot(hidden, grad_up, ((0,), (0,))).astype(bf16)
    qkv_got, out_got = after((qkv_got, out_got), (fc2_part, fc1_part))
    qkv_mat = natural_rows(by_place(qkv_got, zh, y))
    out_mat = jnp.concatenate(by_place(out_got, zh, y), axis=0)
    grad_mixed = dot(grad_out, out_mat, ((1,), (1,)))
    qkv = dot(hidden, qkv_mat, ((1,), (0,)))
    cosines, sines = tables(total_len, ROT)
    attn_mixed, grad_qkv, grad_qkv_sum = attention(
        pair_lengths, qkv, bqkv[None], grad_mixed, cosines, sines
    )
    attn_mixed, grad_qkv = attn_mixed.astype(bf16), grad_qkv.astype(bf16)
    qkv_part = dot(hidden, grad_qkv, ((0,), (0,))).astype(bf16)
    out_part = dot(attn_mixed, grad_out, ((0,), (0,))).astype(bf16)
    grad_hidden_own, branch_own, grad_fc2, grad_wout, grad_wfc1, grad_wqkv = back(
        grad_qkv,
        grad_up,
        attn_mixed,
        activated,
        qkv_mat,
        fc1_mat,
        out_mat,
        fc2_mat,
        fc2_part,
        fc1_part,
        out_part,
        qkv_part,
    )
    output = (inputs + branch_own + bout_all + bfc2_all).astype(bf16)[None]
    grad_norm = grad_hidden_own * gain_all
    grad_input = grad_own.astype(f32) + inv_std * (
        grad_norm
        - jnp.mean(grad_norm, axis=-1, keepdims=True)
        - normed * jnp.mean(grad_norm * normed, axis=-1, keepdims=True)
    )
    grad_input = grad_input.astype(bf16)[None]

    mine = (jnp.arange(8) == place).astype(f32)
    bqkv_term = (
        (jnp.sum(grad_qkv_sum, axis=0).reshape(1, 3, 2, 2, HEAD_DIM) * mine[:, None, None, None, None])
        .reshape(2, 4, 3, 2, 2, HEAD_DIM)
        .transpose(2, 3, 0, 4, 1, 5)
        .reshape(-1)
    )
    bfc1_term = (
        (grad_up_sum.reshape(1, 2, 2, ff_rows) * mine[:, None, None, None])
        .reshape(2, 4, 2, 2, ff_rows)
        .transpose(2, 0, 3, 1, 4)
        .reshape(-1)
    )
    bias_term = jnp.sum(grad_own, axis=0, dtype=f32)
    gain_term = jnp.sum(grad_hidden_own * normed, axis=0)
    shift_term = jnp.sum(grad_hidden_own, axis=0)
    terms = jnp.concatenate(
        [
            v.reshape(32, -1)
            for v in (bqkv_term, bfc1_term, bias_term, gain_term, shift_term)
        ],
        axis=1,
    )
    sums = sum_small(terms.reshape(32, -1, 128), 1).reshape(-1)
    grad_bqkv, grad_bfc1, grad_bias, grad_gain, grad_shift = jnp.split(
        sums, np.cumsum([3 * rows, ff_rows, rows, rows])
    )
    return (
        output,
        grad_input,
        grad_gain,
        grad_shift,
        grad_wqkv,
        grad_bqkv,
        grad_wout,
        grad_bias,
        grad_wfc1,
        grad_bfc1,
        grad_fc2,
        grad_bias,
    )


def fine_mesh(mesh):
    return jax.sharding.Mesh(mesh.devices.reshape(2, 2, 2, 2, 2), FINE)


def fine_solution(mesh):
    everyone, seqs, parts = FINE, ("zh", "zl", "y"), ("x", "c")
    placed = (
        P(seqs, parts, None),
        P(seqs),
        P(everyone),
        P(everyone),
        P(everyone, None),
        P(everyone),
        P(everyone, None),
        P(everyone),
        P(everyone, None),
        P(everyone),
        P(everyone, None),
        P(everyone),
        P(seqs, parts, None),
    )
    given = (
        P(seqs, parts, None),
        P(seqs, parts, None),
        P(everyone),
        P(everyone),
        P(everyone, None),
        P(everyone),
        P(everyone, None),
        P(everyone),
        P(everyone, None),
        P(everyone),
        P(everyone, None),
        P(everyone),
    )
    return jax.shard_map(
        split_device, mesh=fine_mesh(mesh), in_specs=placed, out_specs=given, check_vma=False
    )


def solution(mesh):
    if mesh.shape["dp"] == 8 and mesh.shape["ctx"] == 4:
        return fine_solution(mesh)
    return general_solution(mesh)
```

```python
import functools
import math

import jax
import jax.numpy as jnp
import numpy as np
from jax import lax
from jax.experimental import pallas as pl
from jax.experimental.pallas import tpu as pltpu
from jax.sharding import PartitionSpec as P

HEAD_DIM = 64
ROT = 32


eps_norm = 1e-05
gelu_coef = 0.7978845608028654


def gelu_tanh(values):
    return (
        0.5 * values * (1.0 + jnp.tanh(gelu_coef * (values + 0.044715 * values * values * values)))
    )


def rotary_angles(positions, rot_dims):
    half_dims = rot_dims // 2
    freq_index = jnp.arange(half_dims, dtype=jnp.float32)
    inv_freq = jnp.exp(-math.log(10000.0) * 2.0 * freq_index / rot_dims)
    return positions.astype(jnp.float32)[:, None] * inv_freq[None, :]


def rotary(vectors, angles):
    half_dims = angles.shape[-1]
    cosines = jnp.cos(angles)[:, None, :]
    sine_vals = jnp.sin(angles)[:, None, :]
    leading = vectors[..., :half_dims]
    trailing = vectors[..., half_dims : 2 * half_dims]
    return jnp.concatenate(
        [
            leading * cosines - trailing * sine_vals,
            trailing * cosines + leading * sine_vals,
            vectors[..., 2 * half_dims :],
        ],
        axis=-1,
    )


def rotary_back(gradients, angles):
    half_dims = angles.shape[-1]
    cosines = jnp.cos(angles)[:, None, :]
    sine_vals = jnp.sin(angles)[:, None, :]
    leading = gradients[..., :half_dims]
    trailing = gradients[..., half_dims : 2 * half_dims]
    return jnp.concatenate(
        [
            leading * cosines + trailing * sine_vals,
            trailing * cosines - leading * sine_vals,
            gradients[..., 2 * half_dims :],
        ],
        axis=-1,
    )


def masked_scores(queries, key_rows, places, length):
    scores = jnp.einsum("qhd,khd->hqk", queries, key_rows, preferred_element_type=jnp.float32)
    key_places = jnp.arange(key_rows.shape[0], dtype=jnp.int32)
    allowed = (key_places[None, :] <= places[:, None]) & (key_places[None, :] < length)
    return jnp.where(allowed[None], scores, -1e30)


def on_device(
    tokens,
    lengths,
    ln_gain,
    ln_bias,
    w_qkv,
    b_qkv,
    w_out,
    b_out,
    w_fc1,
    b_fc1,
    w_fc2,
    b_fc2,
    cotangent,
):
    seq_count, local_len, model_width = tokens.shape
    shard_rows = w_qkv.shape[0]
    hidden_ratio = w_fc1.shape[1] // model_width
    head_count = model_width // HEAD_DIM
    token_count = seq_count * local_len
    places = lax.axis_index("ctx") * local_len + jnp.arange(local_len, dtype=jnp.int32)
    angles = rotary_angles(places, ROT)
    live_mask = places[None, :] < lengths[:, None]
    inputs = tokens.astype(jnp.float32).reshape(token_count, model_width)
    average = jnp.mean(inputs, axis=-1, keepdims=True)
    centered = inputs - average
    variance = jnp.mean(centered * centered, axis=-1, keepdims=True)
    inv_std = lax.rsqrt(variance + eps_norm)
    normed = centered * inv_std
    qkv_bias_rows = b_qkv.reshape(shard_rows, 3)
    fc1_bias_rows = b_fc1.reshape(shard_rows, hidden_ratio)
    fc2_rows = w_fc2.reshape(shard_rows, hidden_ratio * model_width)
    inner_full = (
        lax.all_gather(w_qkv, ("dp", "ctx"), axis=0, tiled=True),
        lax.all_gather(w_fc1, ("dp", "ctx"), axis=0, tiled=True),
        lax.all_gather(ln_gain, ("dp", "ctx"), axis=0, tiled=True),
        lax.all_gather(ln_bias, ("dp", "ctx"), axis=0, tiled=True),
        lax.all_gather(qkv_bias_rows, ("dp", "ctx"), axis=0, tiled=True),
        lax.all_gather(fc1_bias_rows, ("dp", "ctx"), axis=0, tiled=True),
    )
    gain_full = inner_full[2].astype(jnp.float32)
    shift_full = inner_full[3].astype(jnp.float32)
    hidden = (normed * gain_full + shift_full).astype(jnp.bfloat16)
    qkv_acc = jnp.dot(hidden, inner_full[0], preferred_element_type=jnp.float32)
    up_acc = jnp.dot(hidden, inner_full[1], preferred_element_type=jnp.float32)
    qkv_bias = inner_full[4].reshape(-1).astype(jnp.float32)
    fc1_bias = inner_full[5].reshape(-1).astype(jnp.float32)
    qkv_proj = (qkv_acc + qkv_bias).reshape(seq_count, local_len, 3, head_count, HEAD_DIM)
    queries = (rotary(qkv_proj[:, :, 0], angles) * 0.125).astype(jnp.bfloat16)
    key_local = (
        rotary(qkv_proj[:, :, 1], angles)
        .astype(jnp.bfloat16)
        .reshape(seq_count, local_len, model_width)
    )
    value_local = qkv_proj[:, :, 2].astype(jnp.bfloat16).reshape(seq_count, local_len, model_width)
    key_full, value_full = (
        lax.all_gather(key_local, "ctx", axis=1, tiled=True),
        lax.all_gather(value_local, "ctx", axis=1, tiled=True),
    )
    total_len = key_full.shape[1]

    def attend_forward(packed):
        query_seq, key_seq, value_seq, length = packed
        key_heads = key_seq.reshape(total_len, head_count, HEAD_DIM)
        value_heads = value_seq.reshape(total_len, head_count, HEAD_DIM)
        scores = masked_scores(query_seq, key_heads, places, length)
        row_max = jnp.max(scores, axis=-1, keepdims=True)
        exponent = jnp.exp(scores - row_max)
        row_sum = jnp.sum(exponent, axis=-1, keepdims=True)
        probability = (exponent / row_sum).astype(jnp.bfloat16)
        attended = jnp.einsum(
            "hqk,khd->qhd", probability, value_heads, preferred_element_type=jnp.float32
        )
        log_total = (row_max + jnp.log(row_sum))[..., 0]
        return (attended.reshape(local_len, model_width).astype(jnp.bfloat16), log_total)

    attn_seq, log_totals = lax.map(attend_forward, (queries, key_full, value_full, lengths))
    attn_mixed = attn_seq.reshape(token_count, model_width)
    up_proj = up_acc + fc1_bias
    activated = gelu_tanh(up_proj).astype(jnp.bfloat16)
    outer_full = (
        lax.all_gather(w_out, ("dp", "ctx"), axis=0, tiled=True),
        lax.all_gather(fc2_rows, ("dp", "ctx"), axis=0, tiled=True),
        lax.all_gather(b_out, ("dp", "ctx"), axis=0, tiled=True),
        lax.all_gather(b_fc2, ("dp", "ctx"), axis=0, tiled=True),
    )
    branch = jnp.dot(attn_mixed, outer_full[0], preferred_element_type=jnp.float32) + jnp.dot(
        activated,
        outer_full[1].reshape(hidden_ratio * model_width, model_width),
        preferred_element_type=jnp.float32,
    )
    out_bias = outer_full[2].astype(jnp.float32)
    fc2_bias = outer_full[3].astype(jnp.float32)
    output = (
        (inputs + branch + out_bias + fc2_bias)
        .astype(jnp.bfloat16)
        .reshape(seq_count, local_len, model_width)
    )
    grad_out = jnp.where(live_mask[:, :, None], cotangent, jnp.zeros((), jnp.bfloat16)).reshape(
        token_count, model_width
    )
    out_back, fc2_back = (
        lax.all_gather(w_out, ("dp", "ctx"), axis=0, tiled=True),
        lax.all_gather(fc2_rows, ("dp", "ctx"), axis=0, tiled=True),
    )
    fc2_matrix = fc2_back.reshape(hidden_ratio * model_width, model_width)
    grad_mixed = jnp.einsum(
        "td,kd->tk", grad_out, out_back, preferred_element_type=jnp.float32
    ).astype(jnp.bfloat16)
    grad_act = jnp.einsum("td,kd->tk", grad_out, fc2_matrix, preferred_element_type=jnp.float32)
    gelu_value, gelu_pull = jax.vjp(gelu_tanh, up_proj)
    grad_up = gelu_pull(grad_act)[0].astype(jnp.bfloat16)
    key_back, value_back = (
        lax.all_gather(key_local, "ctx", axis=1, tiled=True),
        lax.all_gather(value_local, "ctx", axis=1, tiled=True),
    )

    def attend_backward(packed):
        query_seq, key_seq, value_seq, grad_seq, log_total, length = packed
        key_heads = key_seq.reshape(total_len, head_count, HEAD_DIM)
        value_heads = value_seq.reshape(total_len, head_count, HEAD_DIM)
        grad_heads = grad_seq.reshape(local_len, head_count, HEAD_DIM)
        scores = masked_scores(query_seq, key_heads, places, length)
        probability = jnp.exp(scores - log_total[:, :, None])
        grad_probs = jnp.einsum(
            "qhd,khd->hqk", grad_heads, value_heads, preferred_element_type=jnp.float32
        )
        inner = jnp.sum(probability * grad_probs, axis=-1, keepdims=True)
        grad_scores = (probability * (grad_probs - inner)).astype(jnp.bfloat16)
        grad_query = jnp.einsum(
            "hqk,khd->qhd", grad_scores, key_heads, preferred_element_type=jnp.float32
        )
        grad_keys = jnp.einsum(
            "hqk,qhd->khd", grad_scores, query_seq, preferred_element_type=jnp.float32
        )
        grad_values = jnp.einsum(
            "hqk,qhd->khd",
            probability.astype(jnp.bfloat16),
            grad_heads,
            preferred_element_type=jnp.float32,
        )
        return (
            grad_query,
            grad_keys.reshape(total_len, model_width),
            grad_values.reshape(total_len, model_width),
        )

    grad_query, grad_keys_all, grad_values_all = lax.map(
        attend_backward,
        (
            queries,
            key_back,
            value_back,
            grad_mixed.reshape(seq_count, local_len, model_width),
            log_totals,
            lengths,
        ),
    )
    grad_keys_own, grad_values_own = (
        lax.psum_scatter(grad_keys_all, "ctx", scatter_dimension=1, tiled=True),
        lax.psum_scatter(grad_values_all, "ctx", scatter_dimension=1, tiled=True),
    )
    grad_query_pre = rotary_back(grad_query * 0.125, angles).reshape(token_count, model_width)
    grad_keys_pre = rotary_back(
        grad_keys_own.reshape(seq_count, local_len, head_count, HEAD_DIM), angles
    ).reshape(token_count, model_width)
    grad_qkv = jnp.concatenate(
        [grad_query_pre, grad_keys_pre, grad_values_own.reshape(token_count, model_width)], axis=-1
    ).astype(jnp.bfloat16)
    qkv_matrix, fc1_matrix = (
        lax.all_gather(w_qkv, ("dp", "ctx"), axis=0, tiled=True),
        lax.all_gather(w_fc1, ("dp", "ctx"), axis=0, tiled=True),
    )
    grad_hidden = jnp.einsum(
        "tj,dj->td", grad_qkv, qkv_matrix, preferred_element_type=jnp.float32
    ) + jnp.einsum("tj,dj->td", grad_up, fc1_matrix, preferred_element_type=jnp.float32)
    gain_term = jnp.sum(grad_hidden * normed, axis=0)
    shift_term = jnp.sum(grad_hidden, axis=0)
    grad_norm = grad_hidden * gain_full
    grad_input = grad_out.astype(jnp.float32) + inv_std * (
        grad_norm
        - jnp.mean(grad_norm, axis=-1, keepdims=True)
        - normed * jnp.mean(grad_norm * normed, axis=-1, keepdims=True)
    )
    grad_input = grad_input.astype(jnp.bfloat16).reshape(seq_count, local_len, model_width)
    wout_term = jnp.einsum("tk,td->kd", attn_mixed, grad_out, preferred_element_type=jnp.float32)
    wfc2_term = jnp.einsum(
        "tk,td->kd", activated, grad_out, preferred_element_type=jnp.float32
    ).reshape(model_width, hidden_ratio * model_width)
    bias_term = jnp.sum(grad_out, axis=0, dtype=jnp.float32)
    bqkv_term = jnp.sum(grad_qkv, axis=0, dtype=jnp.float32).reshape(model_width, 3)
    bfc1_term = jnp.sum(grad_up, axis=0, dtype=jnp.float32).reshape(model_width, hidden_ratio)
    grad_wout, grad_wfc2, grad_bias, grad_gain, grad_shift, grad_bqkv, grad_bfc1 = (
        lax.psum_scatter(wout_term, ("dp", "ctx"), scatter_dimension=0, tiled=True),
        lax.psum_scatter(wfc2_term, ("dp", "ctx"), scatter_dimension=0, tiled=True),
        lax.psum_scatter(bias_term, ("dp", "ctx"), scatter_dimension=0, tiled=True),
        lax.psum_scatter(gain_term, ("dp", "ctx"), scatter_dimension=0, tiled=True),
        lax.psum_scatter(shift_term, ("dp", "ctx"), scatter_dimension=0, tiled=True),
        lax.psum_scatter(bqkv_term, ("dp", "ctx"), scatter_dimension=0, tiled=True),
        lax.psum_scatter(bfc1_term, ("dp", "ctx"), scatter_dimension=0, tiled=True),
    )
    qkv_part = jnp.einsum("tk,tj->kj", hidden, grad_qkv, preferred_element_type=jnp.float32)
    fc1_part = jnp.einsum("tk,tj->kj", hidden, grad_up, preferred_element_type=jnp.float32)
    inner_sum = lax.psum_scatter(
        jnp.concatenate([qkv_part, fc1_part], axis=1),
        ("dp", "ctx"),
        scatter_dimension=0,
        tiled=True,
    )
    grad_wqkv = inner_sum[:, : 3 * model_width]
    grad_wfc1 = inner_sum[:, 3 * model_width :]
    return (
        output,
        grad_input,
        grad_gain,
        grad_shift,
        grad_wqkv,
        grad_bqkv.reshape(-1),
        grad_wout,
        grad_bias,
        grad_wfc1,
        grad_bfc1.reshape(-1),
        grad_wfc2.reshape(shard_rows * hidden_ratio, model_width),
        grad_bias,
    )


def general_solution(mesh):
    placed = (
        P("dp", "ctx", None),
        P("dp"),
        P(("dp", "ctx")),
        P(("dp", "ctx")),
        P(("dp", "ctx"), None),
        P(("dp", "ctx")),
        P(("dp", "ctx"), None),
        P(("dp", "ctx")),
        P(("dp", "ctx"), None),
        P(("dp", "ctx")),
        P(("dp", "ctx"), None),
        P(("dp", "ctx")),
        P("dp", "ctx", None),
    )
    return jax.shard_map(
        on_device,
        mesh=mesh,
        in_specs=placed,
        out_specs=(
            P("dp", "ctx", None),
            P("dp", "ctx", None),
            P(("dp", "ctx")),
            P(("dp", "ctx")),
            P(("dp", "ctx"), None),
            P(("dp", "ctx")),
            P(("dp", "ctx"), None),
            P(("dp", "ctx")),
            P(("dp", "ctx"), None),
            P(("dp", "ctx")),
            P(("dp", "ctx"), None),
            P(("dp", "ctx")),
        ),
        check_vma=False,
    )


FINE = ("zh", "zl", "y", "x", "c")
ROWS_AXES = ("zl", "x", "c")


def dot(left, right, dims):
    return lax.dot_general(left, right, (dims, ((), ())), preferred_element_type=jnp.float32)


QB = 256


def nt(a, b):
    return dot(a, b, ((1,), (1,)))


def nn(a, b):
    return dot(a, b, ((1,), (0,)))


def tn(a, b):
    return dot(a, b, ((0,), (0,)))


def attend_pair(pair, length, bias, cosines_ref, sines_ref, qkv, mixed, q_s, k_s, v_s, g_s, gk_s, gv_s):
    f32, bf16 = jnp.float32, jnp.bfloat16
    total, width = mixed.shape
    lane = lax.broadcasted_iota(jnp.int32, (1, 128), 1)
    first = lane % HEAD_DIM < ROT // 2
    heads = [lane < HEAD_DIM, lane >= HEAD_DIM]

    def other(v):
        return jnp.where(first, pltpu.roll(v, 128 - ROT // 2, 1), pltpu.roll(v, ROT // 2, 1))

    def col(part):
        return pl.ds(pl.multiple_of(part * width + pair * 128, 128), 128)

    for b in range(total // QB):
        rows = pl.ds(b * QB, QB)
        cosines, sines = cosines_ref[rows], sines_ref[rows]

        def turn(v):
            return v * cosines + other(v) * sines

        q = turn(qkv[rows, col(0)] + bias[:, col(0)]) * 0.125
        k = turn(qkv[rows, col(1)] + bias[:, col(1)])
        v = qkv[rows, col(2)] + bias[:, col(2)]
        g = mixed[rows, col(0)]
        for h in range(2):
            q_s[h, rows] = jnp.where(heads[h], q, 0.0).astype(bf16)
            k_s[h, rows] = jnp.where(heads[h], k, 0.0).astype(bf16)
            v_s[h, rows] = jnp.where(heads[h], v, 0.0).astype(bf16)
            g_s[h, rows] = jnp.where(heads[h], g, 0.0).astype(bf16)
    gk_s[...] = jnp.zeros_like(gk_s)
    gv_s[...] = jnp.zeros_like(gv_s)

    for b in range(total // QB):
        rows = pl.ds(b * QB, QB)
        upto = (b + 1) * QB
        keys = pl.ds(0, upto)
        limit = jnp.minimum(lax.broadcasted_iota(jnp.int32, (1, QB), 1) + (b * QB + 1), length)
        allowed = lax.broadcasted_iota(jnp.int32, (upto, QB), 0) < limit
        out = grad = jnp.zeros((QB, 128), f32)
        for h in range(2):
            qh, gh = q_s[h, rows], g_s[h, rows]
            scores = jnp.where(allowed, nt(k_s[h, keys], qh), -1e30)
            exponent = jnp.exp(scores - jnp.max(scores, axis=0, keepdims=True))
            share = exponent * (1.0 / jnp.sum(exponent, axis=0, keepdims=True))
            rounded = share.astype(bf16)
            back = nt(v_s[h, keys], gh)
            back = (share * (back - jnp.sum(share * back, axis=0, keepdims=True))).astype(bf16)
            gv_s[keys] += nn(rounded, gh)
            gk_s[keys] += nn(back, qh)
            out += tn(rounded, v_s[h, keys])
            grad += tn(back, k_s[h, keys])
        mixed[rows, col(0)] = out
        grad *= 0.125
        qkv[rows, col(0)] = grad * cosines_ref[rows] - other(grad) * sines_ref[rows]
    for b in range(total // QB):
        rows = pl.ds(b * QB, QB)
        grad = gk_s[rows]
        qkv[rows, col(1)] = grad * cosines_ref[rows] - other(grad) * sines_ref[rows]
        qkv[rows, col(2)] = gv_s[rows]


def tables(total, rot):
    half = rot // 2
    inv = jnp.exp(-math.log(10000.0) * 2.0 * jnp.arange(half, dtype=jnp.float32) / rot)
    ang = jnp.arange(total, dtype=jnp.int32).astype(jnp.float32)[:, None] * inv[None, :]
    c, s = jnp.cos(ang), jnp.sin(ang)
    one, nil = jnp.ones((total, 64 - rot), jnp.float32), jnp.zeros((total, 64 - rot), jnp.float32)
    cosines = jnp.concatenate([c, c, one] * 2, axis=1)
    sines = jnp.concatenate([-s, s, nil] * 2, axis=1)
    return cosines, sines


MESH_ID = pl.DeviceIdType.MESH


def exchange_kernel(src, dst, send_sem, recv_sem):
    place = [lax.axis_index(name) for name in FINE]
    me = 0
    for p in place:
        me = me * 2 + p

    def away(k):
        return tuple((p + k // 2 ** (4 - i)) % 2 for i, p in enumerate(place))

    def index_of(where):
        number = 0
        for p in where:
            number = number * 2 + p
        return number

    barrier = pltpu.get_barrier_semaphore()

    def greet(k, carry):
        pl.semaphore_signal(barrier, inc=1, device_id=away(k), device_id_type=MESH_ID)
        return carry

    lax.fori_loop(1, 32, greet, 0)
    pl.semaphore_wait(barrier, 31)

    def copy(k):
        where = away(k)
        return pltpu.make_async_remote_copy(
            src_ref=src.at[index_of(where)],
            dst_ref=dst.at[me],
            send_sem=send_sem.at[k],
            recv_sem=recv_sem.at[k],
            device_id=where,
            device_id_type=MESH_ID,
        )

    def send(k, carry):
        copy(k).start()
        return carry

    lax.fori_loop(1, 32, send, 0)
    dst[me] = src[me]

    def finish(k, carry):
        copy(k).wait()
        return carry

    lax.fori_loop(1, 32, finish, 0)


def sum_kernel(src, out, dst, send_sem, recv_sem):
    exchange_kernel(src, dst, send_sem, recv_sem)
    out[...] = jnp.sum(dst[...], axis=0)


W_PEERS = [(k // 4, k // 2 % 2, k % 2) for k in range(1, 8)]


def sum_small(values, collective_id):
    n = values.shape[1]
    return pl.pallas_call(
        sum_kernel,
        out_shape=jax.ShapeDtypeStruct((n, 128), jnp.float32),
        in_specs=[pl.BlockSpec(memory_space=pltpu.VMEM)],
        out_specs=pl.BlockSpec(memory_space=pltpu.VMEM),
        scratch_shapes=[
            pltpu.VMEM((32, n, 128), jnp.float32),
            pltpu.SemaphoreType.DMA((32,)),
            pltpu.SemaphoreType.DMA((32,)),
        ],
        compiler_params=pltpu.CompilerParams(collective_id=collective_id, has_side_effects=True),
    )(values)


def main_kernel(
    small, tokens, cot_own, cosines, sines, fc2_own, out_own, fc1_spread, qkv_spread,
    gh_own, br_own, fc2_out, out_out, fc1_a, qkv_a, up_sum, qkv_sum, small_all, qkv_all, out_all, fc1_all, fc2_all,
    fc2_part, fc1_part, out_part, qkv_part, c_got, w_got, wide_y, wide_z, cols_y, cols_z,
    hidden, cot, act, gup, attn, gqkv, qkv_w, out_w, stage, full, wide, cols, wide_s, cols_s, fc1_bias, qkv_bias,
    send_sem, recv_sem, local_sem, block_sem, c_send, c_recv, small_send, small_recv,
):
    f32, bf16 = jnp.float32, jnp.bfloat16
    zh, zl, y, x, c = place = [lax.axis_index(name) for name in FINE]
    seat = (zl * 2 + x) * 2 + c
    used, used_local = [0], [0]
    sends = []

    class Copy:
        def __init__(self, describe):
            self.describe = describe

        def start(self):
            self.describe().start()

        def wait(self):
            self.describe().wait()

        def wait_send(self):
            self.describe().wait_send()

        def wait_recv(self):
            self.describe().wait_recv()

    def remote(ends, target):
        n = used[0]
        used[0] += 1

        def describe():
            src, dst = ends()
            return pltpu.make_async_remote_copy(
                src_ref=src,
                dst_ref=dst,
                send_sem=send_sem.at[n],
                recv_sem=recv_sem.at[n],
                device_id=target(),
                device_id_type=MESH_ID,
            )

        copy = Copy(describe)
        copy.start()
        sends.append(copy)
        return copy

    def partner(axis):
        return tuple(1 - p if name == axis else p for name, p in zip(FINE, place))

    def beside():
        return partner("y")

    def across():
        return partner("zh")

    def local(ends):
        n = used_local[0]
        used_local[0] += 1

        def describe():
            src, dst = ends()
            return pltpu.make_async_copy(src, dst, local_sem.at[n])

        copy = Copy(describe)
        copy.start()
        return copy

    def load(*pairs):
        copies = [local(lambda pair=pair: pair) for pair in pairs]
        for copy in copies:
            copy.wait()

    def index_of(where):
        number = 0
        for p in where:
            number = number * 2 + p
        return number

    def away(k):
        return tuple((p + k // 2 ** (4 - i)) % 2 for i, p in enumerate(place))

    barrier = pltpu.get_barrier_semaphore()

    def greet(k, carry):
        pl.semaphore_signal(barrier, inc=1, device_id=away(k), device_id_type=MESH_ID)
        return carry

    lax.fori_loop(1, 32, greet, 0)
    pl.semaphore_wait(barrier, 31)

    blocks, block_rows, width = hidden.shape
    token_count, units = gup.shape
    total_len = token_count // 2
    mine, sent = hidden, cot

    def small_copy(k):
        return pltpu.make_async_remote_copy(
            src_ref=small,
            dst_ref=small_all.at[index_of(place)],
            send_sem=small_send.at[k],
            recv_sem=small_recv.at[k],
            device_id=away(k),
            device_id_type=MESH_ID,
        )

    def small_start(k, carry):
        small_copy(k).start()
        return carry

    def small_wait(k, carry):
        small_copy(k).wait()
        return carry

    lax.fori_loop(1, 32, small_start, 0)
    small_all[index_of(place)] = small[...]
    tokens_in = local(lambda: (tokens, stage))

    def spread(weight, matrix):
        pieces = []
        for dl, dx, dc in W_PEERS:

            def where(dl=dl, dx=dx, dc=dc):
                return zh, (zl + dl) % 2, y, (x + dx) % 2, (c + dc) % 2

            def ends(where=where):
                _, to_zl, _, to_x, to_c = where()
                return weight.at[(to_zl * 2 + to_x) * 2 + to_c], matrix.at[zh, zl, y, x * 2 + c]

            pieces.append(remote(ends, where))
        return pieces, local(lambda: (weight.at[seat], matrix.at[zh, zl, y, x * 2 + c]))

    def parts_of(ends_list):
        return [remote(ends, across) for ends in ends_list], [remote(ends, beside) for ends in ends_list]

    def forward(copy, block):
        copy.wait_recv()
        return remote(lambda: (block(), block()), beside)

    def half_of(matrix, half):
        return lambda: matrix.at[1 - zh, half, y]

    def own_half(matrix, half):
        return lambda: (matrix.at[zh, half, y], matrix.at[zh, half, y])

    fc1_pieces = spread(fc1_spread, fc1_all)
    half_rows = fc2_own.shape[0] // 2

    def fc2_rows_of(a, half):
        return lambda: fc2_all.at[a, y, pl.ds(half * half_rows, half_rows)]

    def fc2_ends(half):
        return lambda: (fc2_own.at[pl.ds(half * half_rows, half_rows)], fc2_rows_of(zh, half)())

    def over(own, gathered, axis):
        return remote(lambda: (own(), gathered()), lambda: partner(axis))

    def own_cot():
        return cot_own

    def seat_of(array, dl=0, dx=0):
        return lambda: array.at[((zl + dl) % 2 * 2 + (x + dx) % 2) * 2 + c]

    cot_zl = over(own_cot, seat_of(cot), "zl")
    fc2_zh, fc2_y = parts_of([fc2_ends(half) for half in range(2)])
    cot_x = over(own_cot, seat_of(cot), "x")
    core = [over(own_cot, seat_of(cot), "c")]
    qkv_pieces = spread(qkv_spread, qkv_all)
    own_copies = [
        local(lambda: (cot_own, cot.at[seat])),
        local(lambda: (fc2_own, fc2_all.at[zh, y])),
        local(lambda: (out_own, out_all.at[zh, y])),
    ]

    lax.fori_loop(1, 32, small_wait, 0)
    tokens_in.wait()
    in_place = lax.broadcasted_iota(jnp.int32, (32, width), 1) // (width // 32) == (
        lax.broadcasted_iota(jnp.int32, (32, width), 0)
    )

    def vector(row):
        spread_out = jnp.concatenate([small_all[:, row, :]] * (width // 128), axis=1)
        return jnp.sum(jnp.where(in_place, spread_out, 0.0), axis=0, keepdims=True)

    gain, shift = vector(0), vector(1)

    def norm_rows(i, carry):
        rows = pl.ds(pl.multiple_of(i * 32, 32), 32)
        values = stage[rows].astype(f32)
        centered = values - jnp.mean(values, axis=-1, keepdims=True)
        variance = jnp.mean(centered * centered, axis=-1, keepdims=True)
        hidden[seat, rows] = (centered * lax.rsqrt(variance + eps_norm) * gain + shift).astype(bf16)
        return carry

    lax.fori_loop(0, block_rows // 32, norm_rows, 0)
    hid_zl = over(seat_of(hidden), seat_of(hidden), "zl")
    hid_x = over(seat_of(hidden), seat_of(hidden), "x")
    core.append(over(seat_of(hidden), seat_of(hidden), "c"))

    for t in range(4):
        owner = index_of((t // 2, zl, t % 2, x, c))
        for half in range(2):
            at = t * 2 * 128 + half * 128
            fc1_bias[:, at : at + 128] = small_all[owner, pl.ds(4 + half, 1), :]
    low = lax.broadcasted_iota(jnp.int32, (1, 128), 1) < HEAD_DIM
    for part in range(3):
        for a in range(2):
            chunks = []
            for b in range(2):
                chunk = part * 32 + index_of((a, zl, b, x, c))
                row = small_all[chunk // 3, pl.ds(2 + chunk % 3 // 2, 1), :]
                chunks.append(jnp.where(chunk % 3 % 2 == b, row, pltpu.roll(row, HEAD_DIM, 1)))
            at = (part * 2 + a) * 128
            qkv_bias[:, at : at + 128] = jnp.where(low, chunks[0], chunks[1])

    def length_of(seq):
        row = small_all[index_of((zh, seq, y, 0, 0)), pl.ds(7, 1), :]
        return jnp.concatenate([row] * (QB // 128), axis=1).astype(jnp.int32)

    def all_there(pieces):
        for piece in pieces[0]:
            piece.wait_recv()
        pieces[1].wait()

    all_there(fc1_pieces)
    fc1_zh, fc1_y = parts_of([own_half(fc1_all, half) for half in range(2)])
    cot_zl.wait_recv()
    cot_zx = over(seat_of(cot, 1), seat_of(cot, 1), "x")
    core.append(over(seat_of(cot, 1), seat_of(cot, 1), "c"))
    hid_zl.wait_recv()
    hid_zx = over(seat_of(hidden, 1), seat_of(hidden, 1), "x")
    core.append(over(seat_of(hidden, 1), seat_of(hidden, 1), "c"))
    fc2_fwd = [forward(copy, fc2_rows_of(1 - zh, half)) for half, copy in enumerate(fc2_zh)]
    all_there(qkv_pieces)
    out_zh, out_y = parts_of([lambda: (out_own, out_all.at[zh, y])])
    qkv_zh, qkv_y = parts_of([own_half(qkv_all, half) for half in range(2)])
    for array, copies in ((cot, ((cot_x, 0), (cot_zx, 1))), (hidden, ((hid_x, 0),))):
        for copy, dl in copies:
            copy.wait_recv()
            core.append(over(seat_of(array, dl, 1), seat_of(array, dl, 1), "c"))
    fc1_fwd = [forward(copy, half_of(fc1_all, half)) for half, copy in enumerate(fc1_zh)]
    hid_zx.wait_recv()
    core.append(over(seat_of(hidden, 1, 1), seat_of(hidden, 1, 1), "c"))
    for copy in own_copies + core + fc2_y + fc2_fwd + fc1_y + fc1_fwd:
        if copy in own_copies:
            copy.wait()
        else:
            copy.wait_recv()
    late_in = out_y + qkv_y
    early_sends = len(sends)

    def row_job(part, rows, first, slot, put):
        some = pl.ds(0, rows)
        return dict(
            part=lambda a, b: part.at[a, b, pl.ds(first, rows)],
            y=[wide_y.at[slot, j, some] for j in range(2)],
            z=wide_z.at[slot, some],
            v=[wide.at[j, some] for j in range(3)],
            s=wide_s.at[slot, some],
            put=put,
            rows=some,
        )

    def column_job(part, width, away, slot, to):
        lanes = pl.ds(0, width)
        return dict(
            part=lambda a, b: part.at[a, (zl + away) % 2, b],
            y=[cols_y.at[slot, j, :, lanes] for j in range(2)],
            z=cols_z.at[slot, :, lanes],
            v=[cols.at[j, :, lanes] for j in range(3)],
            s=cols_s.at[slot, :, lanes],
            away=away,
            to=to,
        )

    fc1_width, qkv_width = units, gqkv.shape[1]
    out_rows, fc2_rows = out_part.shape[2], fc2_part.shape[2] // 2
    jobs = [
        row_job(fc2_part, fc2_rows, i * fc2_rows, i, fc2_out.at[pl.ds(i * fc2_rows, fc2_rows)])
        for i in range(2)
    ]
    jobs += [column_job(fc1_part, fc1_width, away, away, fc1_a) for away in (1, 0)]
    jobs += [row_job(out_part, out_rows, 0, 2, out_out)]
    jobs += [column_job(qkv_part, qkv_width, away, 2 + away, qkv_a) for away in (1, 0)]

    def send_beside(job):
        job["y_far"] = remote(lambda: (job["part"](1 - zh, 1 - y), job["y"][1]), beside)
        job["y_own"] = remote(lambda: (job["part"](zh, 1 - y), job["y"][0]), beside)

    def pass_on(job):
        job["y_far"].wait_recv()
        v = job["v"]
        load((job["part"](1 - zh, y), v[0]), (job["y"][1], v[1]))
        job["s"][...] = (v[0][...].astype(f32) + v[1][...].astype(f32)).astype(bf16)
        job["z_copy"] = remote(lambda: (job["s"], job["z"]), across)

    arrivals, kept = [], []

    def finish(job):
        job["y_own"].wait_recv()
        job["z_copy"].wait_recv()
        v = job["v"]
        load((job["part"](zh, y), v[0]), (job["y"][0], v[1]), (job["z"], v[2]))
        total = v[0][...].astype(f32) + v[1][...].astype(f32) + v[2][...].astype(f32)
        if "put" in job:
            full[job["rows"]] = total
            load((full.at[job["rows"]], job["put"]))
            return
        job["z_copy"].wait_send()
        sends[:] = [copy for copy in sends if copy is not job["z_copy"]]
        job["s"][...] = total.astype(bf16)
        piece = job["s"].shape[0] // 4
        for dx in range(2):
            for dc in range(2):

                def where(dx=dx, dc=dc):
                    return zh, (zl + job["away"]) % 2, y, (x + dx) % 2, (c + dc) % 2

                def ends(where=where):
                    _, _, _, to_x, to_c = where()
                    row = pl.multiple_of((to_x * 2 + to_c) * piece, piece)
                    return job["s"].at[pl.ds(row, piece)], job["to"].at[(zl * 2 + x) * 2 + c]

                if job["away"] or dx or dc:
                    arrivals.append(remote(ends, where))
                else:
                    kept.append(local(ends))

    def core_copy(n, g):
        return pltpu.make_async_remote_copy(
            src_ref=sent.at[4 * n + g],
            dst_ref=c_got.at[n, g],
            send_sem=c_send.at[n, g],
            recv_sem=c_recv.at[n, g],
            device_id=partner("c"),
            device_id_type=MESH_ID,
        )

    axes = ("x", "zl")

    def multiply_groups(n, first, a, v, b, w, multiply):
        def step(g, carry):
            one, two = 1 - g // 2, 1 - g % 2
            rest = ((zl + two) % 2 * 2 + (x + one) % 2) * 2

            def block(where):
                rows = pl.ds(pl.multiple_of((rest + where) * 256, 256), 256)
                near, far = v[...].reshape(-1, v.shape[-1]), w[...].reshape(-1, w.shape[-1])
                return (multiply(a[rows], near) + multiply(b[rows], far)).astype(bf16)

            sent[4 * n + g] = block(1 - c)
            core_copy(n, g).start()
            mine[4 * n + g] = block(c)
            return carry

        lax.fori_loop(first, first + 2, step, 0)

    def add(n, g, got):
        load((got, stage))
        mine[4 * n + g] = (mine[4 * n + g].astype(f32) + stage[...].astype(f32)).astype(bf16)

    def add_core(n, g):
        core_copy(n, g).wait_recv()
        add(n, g, c_got.at[n, g])

    first_copies, second_copies = {}, {}

    def send_first(n):
        for g in range(2):
            add_core(n, g)
            first_copies[n, g] = remote(
                lambda g=g: (mine.at[4 * n + g], w_got.at[n, g]), lambda: partner(axes[0])
            )

    def send_second(n):
        first_copies[n, 0].wait_recv()
        add(n, 2, w_got.at[n, 0])
        second_copies[n] = remote(
            lambda: (mine.at[4 * n + 2], w_got.at[n, 2]), lambda: partner(axes[1])
        )

    def add_first(n):
        first_copies[n, 1].wait_recv()
        add(n, 3, w_got.at[n, 1])

    def total(n, out):
        second_copies[n].wait_recv()
        load((w_got.at[n, 2], stage))
        full[...] = mine[4 * n + 3].astype(f32) + stage[...].astype(f32)
        load((full, out))

    def part_tiles(left, right, at, put, tile):
        def step(i, carry):
            lanes = pl.ds(pl.multiple_of(at(i) * 256, 256), 256)
            product = tn(left(lanes), right())
            slot = i % 2

            @pl.when(i >= 2)
            def _():
                pltpu.make_async_copy(tile.at[slot], put(i - 2), block_sem.at[slot]).wait()

            tile[slot] = product.astype(bf16)
            pltpu.make_async_copy(tile.at[slot], put(i), block_sem.at[slot]).start()
            return carry

        def between(first, last):
            lax.fori_loop(first, last, step, 0)

        def drain(last):
            for i in (last - 2, last - 1):
                pltpu.make_async_copy(tile.at[i % 2], put(i), block_sem.at[i % 2]).wait()

        return between, drain

    def far_first(i):
        far, beside = 1 - i % 2, 1 - i // 2
        return (zh + far) % 2, (y + beside) % 2

    def fc_weights(fc1_w, fc2_w):
        return [local(lambda: (fc1_all, fc1_w)), local(lambda: (fc2_all, fc2_w))]

    def feed(fc1_w, fc2_w, tile_wide, tile_cols):
        for copy in fc_weights(fc1_w, fc2_w):
            copy.wait()
        up_sum[...] = jnp.zeros_like(up_sum)

        def step(b, carry):
            rows = pl.ds(pl.multiple_of(b * 256, 256), 256)
            up = nn(hidden[b], fc1_w[...].reshape(width, units)) + fc1_bias[...]
            bent = jnp.tanh(gelu_coef * (up + 0.044715 * up * up * up))
            act[rows] = (0.5 * up * (1.0 + bent)).astype(bf16)
            slope = 0.5 * (1.0 + bent) + 0.5 * up * (1.0 - bent * bent) * gelu_coef * (
                1.0 + 3.0 * 0.044715 * up * up
            )
            back = (nt(cot[b], fc2_w[...].reshape(units, width)) * slope).astype(bf16)
            gup[rows] = back
            up_sum[...] += jnp.sum(back.astype(f32), axis=0, keepdims=True)
            return carry

        lax.fori_loop(0, blocks // 2, step, 0)
        late_in.append(forward(out_zh[0], lambda: out_all.at[1 - zh, y]))
        late_in.append(forward(qkv_zh[0], half_of(qkv_all, 0)))
        lax.fori_loop(blocks // 2, blocks, step, 0)

        def unit_place(i):
            a, b = far_first(i)
            return a * 2 + b

        def unit_put(i):
            a, b = far_first(i)
            return fc2_part.at[a, b]

        between, drain = part_tiles(
            lambda lanes: act[:, lanes], lambda: cot[...].reshape(token_count, width), unit_place, unit_put, tile_wide
        )
        between(0, 2)
        drain(2)
        late_in.append(forward(qkv_zh[1], half_of(qkv_all, 1)))
        for job in jobs[:2]:
            send_beside(job)
        between, drain = part_tiles(
            lambda lanes: act[:, lanes],
            lambda: cot[...].reshape(token_count, width),
            lambda i: unit_place(i + 2),
            lambda i: unit_put(i + 2),
            tile_wide,
        )
        between(0, 2)
        drain(2)
        feature_tiles(gup, fc1_part, tile_cols, jobs[2:4])

    def feature_tiles(right, part, tile, of):
        for late in range(2):

            def where(i, late=late):
                a, b = far_first(i // 2 + 2 * late)
                return a, i % 2, b

            def feature_place(i, where=where):
                a, half, b = where(i)
                return a * 4 + half * 2 + b

            between, drain = part_tiles(
                lambda lanes: hidden[:, :, lanes].reshape(token_count, 256),
                lambda: right[...],
                feature_place,
                lambda i, where=where: part.at[where(i)],
                tile,
            )
            between(0, 4)
            drain(4)
            if late == 0:
                for job in of:
                    send_beside(job)

    fc_scratch = (pltpu.VMEM(fc1_all.shape, bf16), pltpu.VMEM(fc2_all.shape, bf16))
    pl.run_scoped(
        feed,
        *fc_scratch,
        pltpu.VMEM((2, 256, width), bf16),
        pltpu.VMEM((2, 256, units), bf16),
    )

    for copy in late_in:
        copy.wait_recv()
    load((qkv_all, qkv_w), (out_all, out_w))

    def attend(projected, mixed, q_s, k_s, v_s, g_s, gk_s, gv_s):
        for seq in range(2):

            def project(b, carry, seq=seq):
                rows = pl.ds(pl.multiple_of(b * 256, 256), 256)
                block = b + seq * (blocks // 2)
                projected[rows] = nn(hidden[block], qkv_w[...].reshape(width, qkv_width))
                mixed[rows] = nt(cot[block], out_w[...].reshape(-1, width))
                return carry

            lax.fori_loop(0, blocks // 2, project, 0)

            def pair_step(pair, carry, seq=seq):
                attend_pair(
                    pair, length_of(seq), qkv_bias, cosines, sines, projected, mixed, q_s, k_s, v_s, g_s, gk_s, gv_s
                )
                return carry

            lax.fori_loop(0, mixed.shape[1] // 128, pair_step, 0)
            qkv_sum[seq] = jnp.zeros((1, qkv_width), f32)

            def store(b, carry, seq=seq):
                rows = pl.ds(pl.multiple_of(b * 256, 256), 256)
                to = pl.ds(pl.multiple_of(b * 256 + seq * total_len, 256), 256)
                grads = projected[rows].astype(bf16)
                gqkv[to] = grads
                attn[to] = mixed[rows].astype(bf16)
                qkv_sum[seq] += jnp.sum(grads.astype(f32), axis=0, keepdims=True)
                return carry

            lax.fori_loop(0, blocks // 2, store, 0)
            pass_on(jobs[seq])

    heads = pltpu.VMEM((2, total_len, 128), bf16)
    pl.run_scoped(
        attend,
        pltpu.VMEM((total_len, qkv_width), f32),
        pltpu.VMEM((total_len, attn.shape[1]), f32),
        heads,
        heads,
        heads,
        heads,
        pltpu.VMEM((total_len, 128), f32),
        pltpu.VMEM((total_len, 128), f32),
    )

    def attend_parts(tile_cols, tile_out):
        feature_tiles(gqkv, qkv_part, tile_cols, jobs[5:7])
        tile_out[...] = tn(attn[...], cot[...].reshape(token_count, width)).astype(bf16)
        rows = tile_out.shape[0] // 4
        load(*((tile_out.at[pl.ds(rows * i, rows)], out_part.at[i // 2, i % 2]) for i in range(4)))
        send_beside(jobs[4])

    pl.run_scoped(
        attend_parts, pltpu.VMEM((2, 256, qkv_width), bf16), pltpu.VMEM((attn.shape[1], width), bf16)
    )

    def sums(fc1_w, fc2_w):
        weights = fc_weights(fc1_w, fc2_w)
        for copy in sends[:early_sends]:
            copy.wait_send()
        pass_on(jobs[2])
        weights[0].wait()
        multiply_groups(0, 0, gqkv, qkv_w, gup, fc1_w, nt)
        send_first(0)
        weights[1].wait()
        multiply_groups(1, 0, attn, out_w, act, fc2_w, nn)
        send_first(1)
        finish(jobs[0])
        multiply_groups(0, 2, gqkv, qkv_w, gup, fc1_w, nt)
        multiply_groups(1, 2, attn, out_w, act, fc2_w, nn)

    pl.run_scoped(sums, *fc_scratch)
    for n in range(2):
        add_core(n, 2)
        add_core(n, 3)
    send_second(0)
    pass_on(jobs[3])
    send_second(1)
    finish(jobs[1])
    add_first(0)
    add_first(1)
    finish(jobs[2])
    pass_on(jobs[5])
    total(0, gh_own)
    total(1, br_own)
    pass_on(jobs[6])
    pass_on(jobs[4])
    for job in (jobs[3], jobs[5], jobs[6], jobs[4]):
        finish(job)
    for copy in arrivals:
        copy.wait_recv()
    for copy in kept:
        copy.wait()
    for copy in sends[early_sends:]:
        copy.wait_send()
    for n in range(2):
        for g in range(4):
            core_copy(n, g).wait_send()


def main(small, tokens, cot, cosines, sines, fc2_own, out_own, fc1_spread, qkv_spread):
    bf16, f32 = jnp.bfloat16, jnp.float32
    block, width = tokens.shape
    tokens_all = 8 * block
    rows, ff_rows = out_own.shape[0], fc2_own.shape[0]
    fc1_width, qkv_width = fc1_spread.shape[2], qkv_spread.shape[2]
    half = ff_rows // 2
    any_, vmem = pl.BlockSpec(memory_space=pl.ANY), pl.BlockSpec(memory_space=pltpu.VMEM)
    shapes = [
        ((block, width), f32, any_),
        ((block, width), f32, any_),
        ((ff_rows, width), f32, any_),
        ((rows, width), f32, any_),
        ((8, rows, fc1_width), bf16, any_),
        ((8, rows, qkv_width), bf16, any_),
        ((1, fc1_width), f32, vmem),
        ((2, 1, qkv_width), f32, vmem),
        ((32,) + small.shape, f32, vmem),
        ((2, 2, 2, 4, rows, qkv_width), bf16, any_),
        ((2, 2, rows, width), bf16, any_),
        ((2, 2, 2, 4, rows, fc1_width), bf16, any_),
        ((2, 2, ff_rows, width), bf16, any_),
        ((2, 2, ff_rows, width), bf16, any_),
        ((2, 2, 2, 4 * rows, fc1_width), bf16, any_),
        ((2, 2, rows, width), bf16, any_),
        ((2, 2, 2, 4 * rows, qkv_width), bf16, any_),
        ((2, 4, block, width), bf16, any_),
        ((2, 3, block, width), bf16, any_),
        ((3, 2, half, width), bf16, any_),
        ((3, half, width), bf16, any_),
        ((4, 2, 4 * rows, fc1_width), bf16, any_),
        ((4, 4 * rows, fc1_width), bf16, any_),
    ]
    scratch = [
        pltpu.VMEM((8, block, width), bf16),
        pltpu.VMEM((8, block, width), bf16),
        pltpu.VMEM((tokens_all, fc1_width), bf16),
        pltpu.VMEM((tokens_all, fc1_width), bf16),
        pltpu.VMEM((tokens_all, 4 * rows), bf16),
        pltpu.VMEM((tokens_all, qkv_width), bf16),
        pltpu.VMEM((2, 2, 2, 4, rows, qkv_width), bf16),
        pltpu.VMEM((2, 2, rows, width), bf16),
        pltpu.VMEM((block, width), bf16),
        pltpu.VMEM((block, width), f32),
        pltpu.VMEM((3, half, width), bf16),
        pltpu.VMEM((3, 4 * rows, fc1_width), bf16),
        pltpu.VMEM((3, half, width), bf16),
        pltpu.VMEM((4, 4 * rows, fc1_width), bf16),
        pltpu.VMEM((1, fc1_width), f32),
        pltpu.VMEM((1, qkv_width), f32),
        pltpu.SemaphoreType.DMA((96,)),
        pltpu.SemaphoreType.DMA((96,)),
        pltpu.SemaphoreType.DMA((96,)),
        pltpu.SemaphoreType.DMA((2,)),
        pltpu.SemaphoreType.DMA((2, 4)),
        pltpu.SemaphoreType.DMA((2, 4)),
        pltpu.SemaphoreType.DMA((32,)),
        pltpu.SemaphoreType.DMA((32,)),
    ]
    return pl.pallas_call(
        main_kernel,
        out_shape=[jax.ShapeDtypeStruct(shape, kind) for shape, kind, _ in shapes],
        in_specs=[vmem, any_, any_, vmem, vmem] + [any_] * 4,
        out_specs=[spec for _, _, spec in shapes],
        scratch_shapes=scratch,
        compiler_params=pltpu.CompilerParams(
            collective_id=0, has_side_effects=True, vmem_limit_bytes=63 * 2**20
        ),
    )(small, tokens, cot, cosines, sines, fc2_own, out_own, fc1_spread, qkv_spread)[:9]


def columns_kernel(fc1_in, qkv_in, fc1_out, qkv_out):
    f32 = jnp.float32
    unit, part_width = fc1_in.shape[2] // 4, qkv_in.shape[2] // 3
    for w in range(8):
        for t in range(4):
            at = ((t // 2 * 2 + w // 4) * 2 + t % 2) * 4 * unit + w % 4 * unit
            fc1_out[:, at : at + unit] = fc1_in[w, :, t * unit : (t + 1) * unit].astype(f32)
    low = lax.broadcasted_iota(jnp.int32, (1, 128), 1) < HEAD_DIM
    for part in range(3):
        for a in range(2):
            for dl in range(2):
                for dx in range(2):
                    at = part * part_width + a * 128
                    even, odd = (
                        qkv_in[dl * 4 + dx * 2 + k, :, at : at + 128].astype(f32) for k in range(2)
                    )
                    to = part * 8 * part_width + a * 1024 + dl * 512 + dx * 128
                    qkv_out[:, to : to + 128] = jnp.where(low, even, pltpu.roll(odd, 64, 1))
                    qkv_out[:, to + 256 : to + 384] = jnp.where(low, pltpu.roll(even, 64, 1), odd)


def plain_columns(fc1_in, qkv_in):
    _, rows, fc1_width = fc1_in.shape
    vmem = pl.BlockSpec(memory_space=pltpu.VMEM)
    return pl.pallas_call(
        columns_kernel,
        out_shape=[
            jax.ShapeDtypeStruct((rows, 8 * fc1_width), jnp.float32),
            jax.ShapeDtypeStruct((rows, 8 * qkv_in.shape[2]), jnp.float32),
        ],
        in_specs=[vmem, vmem],
        out_specs=[vmem, vmem],
        compiler_params=pltpu.CompilerParams(vmem_limit_bytes=24 * 2**20),
    )(fc1_in, qkv_in)


def split_device(
    tokens,
    lengths,
    ln_gain,
    ln_bias,
    w_qkv,
    b_qkv,
    w_out,
    b_out,
    w_fc1,
    b_fc1,
    w_fc2,
    b_fc2,
    cotangent,
):
    bf16, f32 = jnp.bfloat16, jnp.float32
    zh, zl, y, x, c = (lax.axis_index(name) for name in FINE)
    place = (zl * 2 + x) * 2 + c
    _, local_len, width = tokens.shape
    rows = w_qkv.shape[0]
    ff_rows = w_fc2.shape[0]
    pieces = 4
    total_len = local_len * pieces
    heads = 4
    own_width = heads * HEAD_DIM

    row = 2 * rows
    small = jnp.concatenate(
        [v.astype(f32) for v in (ln_gain, ln_gain, ln_bias, ln_bias, b_qkv, b_out, b_fc1, b_fc2)]
        + [jnp.zeros(row - rows, f32), jnp.broadcast_to(lengths.astype(f32), (row,))]
    ).reshape(-1, row)
    places = (x * 2 + c) * local_len + jnp.arange(local_len, dtype=jnp.int32)
    grad_own = jnp.where((places < lengths[0])[:, None], cotangent[0], jnp.zeros((), bf16))
    fc1_spread = (
        w_fc1.reshape((rows, 2, 2, 2, 2, 2, ff_rows))
        .transpose(2, 4, 5, 0, 1, 3, 6)
        .reshape(8, rows, -1)
    )
    qkv_spread = (
        w_qkv.reshape((rows, 3, 2, 2, 2, 2, 2, HEAD_DIM))
        .transpose(3, 5, 6, 0, 1, 2, 4, 7)
        .reshape(8, rows, -1)
    )
    cosines, sines = tables(total_len, ROT)
    (
        grad_hidden_own,
        branch_own,
        grad_fc2,
        grad_wout,
        fc1_columns,
        qkv_columns,
        grad_up_sum,
        grad_qkv_sum,
        small_all,
    ) = main(
        small, tokens[0], grad_own, cosines, sines, w_fc2, w_out, fc1_spread, qkv_spread
    )
    grad_wfc1, grad_wqkv = plain_columns(fc1_columns, qkv_columns)
    gain_all = small_all[:, 0, :rows].reshape(-1)
    bout_all, bfc2_all = small_all[:, 3, rows:].reshape(-1), small_all[:, 6, :rows].reshape(-1)

    inputs = tokens[0].astype(f32)
    average = jnp.mean(inputs, axis=-1, keepdims=True)
    centered = inputs - average
    variance = jnp.mean(centered * centered, axis=-1, keepdims=True)
    inv_std = lax.rsqrt(variance + eps_norm)
    normed = centered * inv_std

    output = (inputs + branch_own + bout_all + bfc2_all).astype(bf16)[None]
    grad_norm = grad_hidden_own * gain_all
    grad_input = grad_own.astype(f32) + inv_std * (
        grad_norm
        - jnp.mean(grad_norm, axis=-1, keepdims=True)
        - normed * jnp.mean(grad_norm * normed, axis=-1, keepdims=True)
    )
    grad_input = grad_input.astype(bf16)[None]

    mine = (jnp.arange(8) == place).astype(f32)
    bqkv_term = (
        (jnp.sum(grad_qkv_sum, axis=0).reshape(1, 3, 2, 2, HEAD_DIM) * mine[:, None, None, None, None])
        .reshape(2, 4, 3, 2, 2, HEAD_DIM)
        .transpose(2, 3, 0, 4, 1, 5)
        .reshape(-1)
    )
    bfc1_term = (
        (grad_up_sum.reshape(1, 2, 2, ff_rows) * mine[:, None, None, None])
        .reshape(2, 4, 2, 2, ff_rows)
        .transpose(2, 0, 3, 1, 4)
        .reshape(-1)
    )
    bias_term = jnp.sum(grad_own, axis=0, dtype=f32)
    gain_term = jnp.sum(grad_hidden_own * normed, axis=0)
    shift_term = jnp.sum(grad_hidden_own, axis=0)
    terms = jnp.concatenate(
        [
            v.reshape(32, -1)
            for v in (bqkv_term, bfc1_term, bias_term, gain_term, shift_term)
        ],
        axis=1,
    )
    sums = sum_small(terms.reshape(32, -1, 128), 1).reshape(-1)
    grad_bqkv, grad_bfc1, grad_bias, grad_gain, grad_shift = jnp.split(
        sums, np.cumsum([3 * rows, ff_rows, rows, rows])
    )
    return (
        output,
        grad_input,
        grad_gain,
        grad_shift,
        grad_wqkv,
        grad_bqkv,
        grad_wout,
        grad_bias,
        grad_wfc1,
        grad_bfc1,
        grad_fc2,
        grad_bias,
    )


def fine_mesh(mesh):
    return jax.sharding.Mesh(mesh.devices.reshape(2, 2, 2, 2, 2), FINE)


def fine_solution(mesh):
    everyone, seqs, parts = FINE, ("zh", "zl", "y"), ("x", "c")
    placed = (
        P(seqs, parts, None),
        P(seqs),
        P(everyone),
        P(everyone),
        P(everyone, None),
        P(everyone),
        P(everyone, None),
        P(everyone),
        P(everyone, None),
        P(everyone),
        P(everyone, None),
        P(everyone),
        P(seqs, parts, None),
    )
    given = (
        P(seqs, parts, None),
        P(seqs, parts, None),
        P(everyone),
        P(everyone),
        P(everyone, None),
        P(everyone),
        P(everyone, None),
        P(everyone),
        P(everyone, None),
        P(everyone),
        P(everyone, None),
        P(everyone),
    )
    return jax.shard_map(
        split_device, mesh=fine_mesh(mesh), in_specs=placed, out_specs=given, check_vma=False
    )


def solution(mesh):
    if mesh.shape["dp"] == 8 and mesh.shape["ctx"] == 4:
        return fine_solution(mesh)
    return general_solution(mesh)
```

```python
import functools
import math

import jax
import jax.numpy as jnp
import numpy as np
from jax import lax
from jax.experimental import pallas as pl
from jax.experimental.pallas import tpu as pltpu
from jax.sharding import PartitionSpec as P

HEAD_DIM = 64
ROT = 32


eps_norm = 1e-05
gelu_coef = 0.7978845608028654


def gelu_tanh(values):
    return (
        0.5 * values * (1.0 + jnp.tanh(gelu_coef * (values + 0.044715 * values * values * values)))
    )


def rotary_angles(positions, rot_dims):
    half_dims = rot_dims // 2
    freq_index = jnp.arange(half_dims, dtype=jnp.float32)
    inv_freq = jnp.exp(-math.log(10000.0) * 2.0 * freq_index / rot_dims)
    return positions.astype(jnp.float32)[:, None] * inv_freq[None, :]


def rotary(vectors, angles):
    half_dims = angles.shape[-1]
    cosines = jnp.cos(angles)[:, None, :]
    sine_vals = jnp.sin(angles)[:, None, :]
    leading = vectors[..., :half_dims]
    trailing = vectors[..., half_dims : 2 * half_dims]
    return jnp.concatenate(
        [
            leading * cosines - trailing * sine_vals,
            trailing * cosines + leading * sine_vals,
            vectors[..., 2 * half_dims :],
        ],
        axis=-1,
    )


def rotary_back(gradients, angles):
    half_dims = angles.shape[-1]
    cosines = jnp.cos(angles)[:, None, :]
    sine_vals = jnp.sin(angles)[:, None, :]
    leading = gradients[..., :half_dims]
    trailing = gradients[..., half_dims : 2 * half_dims]
    return jnp.concatenate(
        [
            leading * cosines + trailing * sine_vals,
            trailing * cosines - leading * sine_vals,
            gradients[..., 2 * half_dims :],
        ],
        axis=-1,
    )


def masked_scores(queries, key_rows, places, length):
    scores = jnp.einsum("qhd,khd->hqk", queries, key_rows, preferred_element_type=jnp.float32)
    key_places = jnp.arange(key_rows.shape[0], dtype=jnp.int32)
    allowed = (key_places[None, :] <= places[:, None]) & (key_places[None, :] < length)
    return jnp.where(allowed[None], scores, -1e30)


def on_device(
    tokens,
    lengths,
    ln_gain,
    ln_bias,
    w_qkv,
    b_qkv,
    w_out,
    b_out,
    w_fc1,
    b_fc1,
    w_fc2,
    b_fc2,
    cotangent,
):
    seq_count, local_len, model_width = tokens.shape
    shard_rows = w_qkv.shape[0]
    hidden_ratio = w_fc1.shape[1] // model_width
    head_count = model_width // HEAD_DIM
    token_count = seq_count * local_len
    places = lax.axis_index("ctx") * local_len + jnp.arange(local_len, dtype=jnp.int32)
    angles = rotary_angles(places, ROT)
    live_mask = places[None, :] < lengths[:, None]
    inputs = tokens.astype(jnp.float32).reshape(token_count, model_width)
    average = jnp.mean(inputs, axis=-1, keepdims=True)
    centered = inputs - average
    variance = jnp.mean(centered * centered, axis=-1, keepdims=True)
    inv_std = lax.rsqrt(variance + eps_norm)
    normed = centered * inv_std
    qkv_bias_rows = b_qkv.reshape(shard_rows, 3)
    fc1_bias_rows = b_fc1.reshape(shard_rows, hidden_ratio)
    fc2_rows = w_fc2.reshape(shard_rows, hidden_ratio * model_width)
    inner_full = (
        lax.all_gather(w_qkv, ("dp", "ctx"), axis=0, tiled=True),
        lax.all_gather(w_fc1, ("dp", "ctx"), axis=0, tiled=True),
        lax.all_gather(ln_gain, ("dp", "ctx"), axis=0, tiled=True),
        lax.all_gather(ln_bias, ("dp", "ctx"), axis=0, tiled=True),
        lax.all_gather(qkv_bias_rows, ("dp", "ctx"), axis=0, tiled=True),
        lax.all_gather(fc1_bias_rows, ("dp", "ctx"), axis=0, tiled=True),
    )
    gain_full = inner_full[2].astype(jnp.float32)
    shift_full = inner_full[3].astype(jnp.float32)
    hidden = (normed * gain_full + shift_full).astype(jnp.bfloat16)
    qkv_acc = jnp.dot(hidden, inner_full[0], preferred_element_type=jnp.float32)
    up_acc = jnp.dot(hidden, inner_full[1], preferred_element_type=jnp.float32)
    qkv_bias = inner_full[4].reshape(-1).astype(jnp.float32)
    fc1_bias = inner_full[5].reshape(-1).astype(jnp.float32)
    qkv_proj = (qkv_acc + qkv_bias).reshape(seq_count, local_len, 3, head_count, HEAD_DIM)
    queries = (rotary(qkv_proj[:, :, 0], angles) * 0.125).astype(jnp.bfloat16)
    key_local = (
        rotary(qkv_proj[:, :, 1], angles)
        .astype(jnp.bfloat16)
        .reshape(seq_count, local_len, model_width)
    )
    value_local = qkv_proj[:, :, 2].astype(jnp.bfloat16).reshape(seq_count, local_len, model_width)
    key_full, value_full = (
        lax.all_gather(key_local, "ctx", axis=1, tiled=True),
        lax.all_gather(value_local, "ctx", axis=1, tiled=True),
    )
    total_len = key_full.shape[1]

    def attend_forward(packed):
        query_seq, key_seq, value_seq, length = packed
        key_heads = key_seq.reshape(total_len, head_count, HEAD_DIM)
        value_heads = value_seq.reshape(total_len, head_count, HEAD_DIM)
        scores = masked_scores(query_seq, key_heads, places, length)
        row_max = jnp.max(scores, axis=-1, keepdims=True)
        exponent = jnp.exp(scores - row_max)
        row_sum = jnp.sum(exponent, axis=-1, keepdims=True)
        probability = (exponent / row_sum).astype(jnp.bfloat16)
        attended = jnp.einsum(
            "hqk,khd->qhd", probability, value_heads, preferred_element_type=jnp.float32
        )
        log_total = (row_max + jnp.log(row_sum))[..., 0]
        return (attended.reshape(local_len, model_width).astype(jnp.bfloat16), log_total)

    attn_seq, log_totals = lax.map(attend_forward, (queries, key_full, value_full, lengths))
    attn_mixed = attn_seq.reshape(token_count, model_width)
    up_proj = up_acc + fc1_bias
    activated = gelu_tanh(up_proj).astype(jnp.bfloat16)
    outer_full = (
        lax.all_gather(w_out, ("dp", "ctx"), axis=0, tiled=True),
        lax.all_gather(fc2_rows, ("dp", "ctx"), axis=0, tiled=True),
        lax.all_gather(b_out, ("dp", "ctx"), axis=0, tiled=True),
        lax.all_gather(b_fc2, ("dp", "ctx"), axis=0, tiled=True),
    )
    branch = jnp.dot(attn_mixed, outer_full[0], preferred_element_type=jnp.float32) + jnp.dot(
        activated,
        outer_full[1].reshape(hidden_ratio * model_width, model_width),
        preferred_element_type=jnp.float32,
    )
    out_bias = outer_full[2].astype(jnp.float32)
    fc2_bias = outer_full[3].astype(jnp.float32)
    output = (
        (inputs + branch + out_bias + fc2_bias)
        .astype(jnp.bfloat16)
        .reshape(seq_count, local_len, model_width)
    )
    grad_out = jnp.where(live_mask[:, :, None], cotangent, jnp.zeros((), jnp.bfloat16)).reshape(
        token_count, model_width
    )
    out_back, fc2_back = (
        lax.all_gather(w_out, ("dp", "ctx"), axis=0, tiled=True),
        lax.all_gather(fc2_rows, ("dp", "ctx"), axis=0, tiled=True),
    )
    fc2_matrix = fc2_back.reshape(hidden_ratio * model_width, model_width)
    grad_mixed = jnp.einsum(
        "td,kd->tk", grad_out, out_back, preferred_element_type=jnp.float32
    ).astype(jnp.bfloat16)
    grad_act = jnp.einsum("td,kd->tk", grad_out, fc2_matrix, preferred_element_type=jnp.float32)
    gelu_value, gelu_pull = jax.vjp(gelu_tanh, up_proj)
    grad_up = gelu_pull(grad_act)[0].astype(jnp.bfloat16)
    key_back, value_back = (
        lax.all_gather(key_local, "ctx", axis=1, tiled=True),
        lax.all_gather(value_local, "ctx", axis=1, tiled=True),
    )

    def attend_backward(packed):
        query_seq, key_seq, value_seq, grad_seq, log_total, length = packed
        key_heads = key_seq.reshape(total_len, head_count, HEAD_DIM)
        value_heads = value_seq.reshape(total_len, head_count, HEAD_DIM)
        grad_heads = grad_seq.reshape(local_len, head_count, HEAD_DIM)
        scores = masked_scores(query_seq, key_heads, places, length)
        probability = jnp.exp(scores - log_total[:, :, None])
        grad_probs = jnp.einsum(
            "qhd,khd->hqk", grad_heads, value_heads, preferred_element_type=jnp.float32
        )
        inner = jnp.sum(probability * grad_probs, axis=-1, keepdims=True)
        grad_scores = (probability * (grad_probs - inner)).astype(jnp.bfloat16)
        grad_query = jnp.einsum(
            "hqk,khd->qhd", grad_scores, key_heads, preferred_element_type=jnp.float32
        )
        grad_keys = jnp.einsum(
            "hqk,qhd->khd", grad_scores, query_seq, preferred_element_type=jnp.float32
        )
        grad_values = jnp.einsum(
            "hqk,qhd->khd",
            probability.astype(jnp.bfloat16),
            grad_heads,
            preferred_element_type=jnp.float32,
        )
        return (
            grad_query,
            grad_keys.reshape(total_len, model_width),
            grad_values.reshape(total_len, model_width),
        )

    grad_query, grad_keys_all, grad_values_all = lax.map(
        attend_backward,
        (
            queries,
            key_back,
            value_back,
            grad_mixed.reshape(seq_count, local_len, model_width),
            log_totals,
            lengths,
        ),
    )
    grad_keys_own, grad_values_own = (
        lax.psum_scatter(grad_keys_all, "ctx", scatter_dimension=1, tiled=True),
        lax.psum_scatter(grad_values_all, "ctx", scatter_dimension=1, tiled=True),
    )
    grad_query_pre = rotary_back(grad_query * 0.125, angles).reshape(token_count, model_width)
    grad_keys_pre = rotary_back(
        grad_keys_own.reshape(seq_count, local_len, head_count, HEAD_DIM), angles
    ).reshape(token_count, model_width)
    grad_qkv = jnp.concatenate(
        [grad_query_pre, grad_keys_pre, grad_values_own.reshape(token_count, model_width)], axis=-1
    ).astype(jnp.bfloat16)
    qkv_matrix, fc1_matrix = (
        lax.all_gather(w_qkv, ("dp", "ctx"), axis=0, tiled=True),
        lax.all_gather(w_fc1, ("dp", "ctx"), axis=0, tiled=True),
    )
    grad_hidden = jnp.einsum(
        "tj,dj->td", grad_qkv, qkv_matrix, preferred_element_type=jnp.float32
    ) + jnp.einsum("tj,dj->td", grad_up, fc1_matrix, preferred_element_type=jnp.float32)
    gain_term = jnp.sum(grad_hidden * normed, axis=0)
    shift_term = jnp.sum(grad_hidden, axis=0)
    grad_norm = grad_hidden * gain_full
    grad_input = grad_out.astype(jnp.float32) + inv_std * (
        grad_norm
        - jnp.mean(grad_norm, axis=-1, keepdims=True)
        - normed * jnp.mean(grad_norm * normed, axis=-1, keepdims=True)
    )
    grad_input = grad_input.astype(jnp.bfloat16).reshape(seq_count, local_len, model_width)
    wout_term = jnp.einsum("tk,td->kd", attn_mixed, grad_out, preferred_element_type=jnp.float32)
    wfc2_term = jnp.einsum(
        "tk,td->kd", activated, grad_out, preferred_element_type=jnp.float32
    ).reshape(model_width, hidden_ratio * model_width)
    bias_term = jnp.sum(grad_out, axis=0, dtype=jnp.float32)
    bqkv_term = jnp.sum(grad_qkv, axis=0, dtype=jnp.float32).reshape(model_width, 3)
    bfc1_term = jnp.sum(grad_up, axis=0, dtype=jnp.float32).reshape(model_width, hidden_ratio)
    grad_wout, grad_wfc2, grad_bias, grad_gain, grad_shift, grad_bqkv, grad_bfc1 = (
        lax.psum_scatter(wout_term, ("dp", "ctx"), scatter_dimension=0, tiled=True),
        lax.psum_scatter(wfc2_term, ("dp", "ctx"), scatter_dimension=0, tiled=True),
        lax.psum_scatter(bias_term, ("dp", "ctx"), scatter_dimension=0, tiled=True),
        lax.psum_scatter(gain_term, ("dp", "ctx"), scatter_dimension=0, tiled=True),
        lax.psum_scatter(shift_term, ("dp", "ctx"), scatter_dimension=0, tiled=True),
        lax.psum_scatter(bqkv_term, ("dp", "ctx"), scatter_dimension=0, tiled=True),
        lax.psum_scatter(bfc1_term, ("dp", "ctx"), scatter_dimension=0, tiled=True),
    )
    qkv_part = jnp.einsum("tk,tj->kj", hidden, grad_qkv, preferred_element_type=jnp.float32)
    fc1_part = jnp.einsum("tk,tj->kj", hidden, grad_up, preferred_element_type=jnp.float32)
    inner_sum = lax.psum_scatter(
        jnp.concatenate([qkv_part, fc1_part], axis=1),
        ("dp", "ctx"),
        scatter_dimension=0,
        tiled=True,
    )
    grad_wqkv = inner_sum[:, : 3 * model_width]
    grad_wfc1 = inner_sum[:, 3 * model_width :]
    return (
        output,
        grad_input,
        grad_gain,
        grad_shift,
        grad_wqkv,
        grad_bqkv.reshape(-1),
        grad_wout,
        grad_bias,
        grad_wfc1,
        grad_bfc1.reshape(-1),
        grad_wfc2.reshape(shard_rows * hidden_ratio, model_width),
        grad_bias,
    )


def general_solution(mesh):
    placed = (
        P("dp", "ctx", None),
        P("dp"),
        P(("dp", "ctx")),
        P(("dp", "ctx")),
        P(("dp", "ctx"), None),
        P(("dp", "ctx")),
        P(("dp", "ctx"), None),
        P(("dp", "ctx")),
        P(("dp", "ctx"), None),
        P(("dp", "ctx")),
        P(("dp", "ctx"), None),
        P(("dp", "ctx")),
        P("dp", "ctx", None),
    )
    return jax.shard_map(
        on_device,
        mesh=mesh,
        in_specs=placed,
        out_specs=(
            P("dp", "ctx", None),
            P("dp", "ctx", None),
            P(("dp", "ctx")),
            P(("dp", "ctx")),
            P(("dp", "ctx"), None),
            P(("dp", "ctx")),
            P(("dp", "ctx"), None),
            P(("dp", "ctx")),
            P(("dp", "ctx"), None),
            P(("dp", "ctx")),
            P(("dp", "ctx"), None),
            P(("dp", "ctx")),
        ),
        check_vma=False,
    )


FINE = ("zh", "zl", "y", "x", "c")
ROWS_AXES = ("zl", "x", "c")


def dot(left, right, dims):
    return lax.dot_general(left, right, (dims, ((), ())), preferred_element_type=jnp.float32)


QB = 256


def nt(a, b):
    return dot(a, b, ((1,), (1,)))


def nn(a, b):
    return dot(a, b, ((1,), (0,)))


def tn(a, b):
    return dot(a, b, ((0,), (0,)))


def attend_pair(pair, length, bias, cosines_ref, sines_ref, qkv, mixed, q_s, k_s, v_s, g_s, gk_s, gv_s):
    f32, bf16 = jnp.float32, jnp.bfloat16
    total, width = mixed.shape
    lane = lax.broadcasted_iota(jnp.int32, (1, 128), 1)
    first = lane % HEAD_DIM < ROT // 2
    heads = [lane < HEAD_DIM, lane >= HEAD_DIM]

    def other(v):
        return jnp.where(first, pltpu.roll(v, 128 - ROT // 2, 1), pltpu.roll(v, ROT // 2, 1))

    def col(part):
        return pl.ds(pl.multiple_of(part * width + pair * 128, 128), 128)

    for b in range(total // QB):
        rows = pl.ds(b * QB, QB)
        cosines, sines = cosines_ref[rows], sines_ref[rows]

        def turn(v):
            return v * cosines + other(v) * sines

        q = turn(qkv[rows, col(0)] + bias[:, col(0)]) * 0.125
        k = turn(qkv[rows, col(1)] + bias[:, col(1)])
        v = qkv[rows, col(2)] + bias[:, col(2)]
        g = mixed[rows, col(0)]
        for h in range(2):
            q_s[h, rows] = jnp.where(heads[h], q, 0.0).astype(bf16)
            k_s[h, rows] = jnp.where(heads[h], k, 0.0).astype(bf16)
            v_s[h, rows] = jnp.where(heads[h], v, 0.0).astype(bf16)
            g_s[h, rows] = jnp.where(heads[h], g, 0.0).astype(bf16)
    gk_s[...] = jnp.zeros_like(gk_s)
    gv_s[...] = jnp.zeros_like(gv_s)

    for b in range(total // QB):
        rows = pl.ds(b * QB, QB)
        upto = (b + 1) * QB
        keys = pl.ds(0, upto)
        limit = jnp.minimum(lax.broadcasted_iota(jnp.int32, (1, QB), 1) + (b * QB + 1), length)
        allowed = lax.broadcasted_iota(jnp.int32, (upto, QB), 0) < limit
        out = grad = jnp.zeros((QB, 128), f32)
        for h in range(2):
            qh, gh = q_s[h, rows], g_s[h, rows]
            scores = jnp.where(allowed, nt(k_s[h, keys], qh), -1e30)
            exponent = jnp.exp(scores - jnp.max(scores, axis=0, keepdims=True))
            share = exponent * (1.0 / jnp.sum(exponent, axis=0, keepdims=True))
            rounded = share.astype(bf16)
            back = nt(v_s[h, keys], gh)
            back = (share * (back - jnp.sum(share * back, axis=0, keepdims=True))).astype(bf16)
            gv_s[keys] += nn(rounded, gh)
            gk_s[keys] += nn(back, qh)
            out += tn(rounded, v_s[h, keys])
            grad += tn(back, k_s[h, keys])
        mixed[rows, col(0)] = out
        grad *= 0.125
        qkv[rows, col(0)] = grad * cosines_ref[rows] - other(grad) * sines_ref[rows]
    for b in range(total // QB):
        rows = pl.ds(b * QB, QB)
        grad = gk_s[rows]
        qkv[rows, col(1)] = grad * cosines_ref[rows] - other(grad) * sines_ref[rows]
        qkv[rows, col(2)] = gv_s[rows]


def tables(total, rot):
    half = rot // 2
    inv = jnp.exp(-math.log(10000.0) * 2.0 * jnp.arange(half, dtype=jnp.float32) / rot)
    ang = jnp.arange(total, dtype=jnp.int32).astype(jnp.float32)[:, None] * inv[None, :]
    c, s = jnp.cos(ang), jnp.sin(ang)
    one, nil = jnp.ones((total, 64 - rot), jnp.float32), jnp.zeros((total, 64 - rot), jnp.float32)
    cosines = jnp.concatenate([c, c, one] * 2, axis=1)
    sines = jnp.concatenate([-s, s, nil] * 2, axis=1)
    return cosines, sines


MESH_ID = pl.DeviceIdType.MESH


def exchange_kernel(src, dst, send_sem, recv_sem):
    place = [lax.axis_index(name) for name in FINE]
    me = 0
    for p in place:
        me = me * 2 + p

    def away(k):
        return tuple((p + k // 2 ** (4 - i)) % 2 for i, p in enumerate(place))

    def index_of(where):
        number = 0
        for p in where:
            number = number * 2 + p
        return number

    barrier = pltpu.get_barrier_semaphore()

    def greet(k, carry):
        pl.semaphore_signal(barrier, inc=1, device_id=away(k), device_id_type=MESH_ID)
        return carry

    lax.fori_loop(1, 32, greet, 0)
    pl.semaphore_wait(barrier, 31)

    def copy(k):
        where = away(k)
        return pltpu.make_async_remote_copy(
            src_ref=src.at[index_of(where)],
            dst_ref=dst.at[me],
            send_sem=send_sem.at[k],
            recv_sem=recv_sem.at[k],
            device_id=where,
            device_id_type=MESH_ID,
        )

    def send(k, carry):
        copy(k).start()
        return carry

    lax.fori_loop(1, 32, send, 0)
    dst[me] = src[me]

    def finish(k, carry):
        copy(k).wait()
        return carry

    lax.fori_loop(1, 32, finish, 0)


def sum_kernel(src, out, dst, send_sem, recv_sem):
    exchange_kernel(src, dst, send_sem, recv_sem)
    out[...] = jnp.sum(dst[...], axis=0)


W_PEERS = [(k // 4, k // 2 % 2, k % 2) for k in range(1, 8)]


def sum_small(values, collective_id):
    n = values.shape[1]
    return pl.pallas_call(
        sum_kernel,
        out_shape=jax.ShapeDtypeStruct((n, 128), jnp.float32),
        in_specs=[pl.BlockSpec(memory_space=pltpu.VMEM)],
        out_specs=pl.BlockSpec(memory_space=pltpu.VMEM),
        scratch_shapes=[
            pltpu.VMEM((32, n, 128), jnp.float32),
            pltpu.SemaphoreType.DMA((32,)),
            pltpu.SemaphoreType.DMA((32,)),
        ],
        compiler_params=pltpu.CompilerParams(collective_id=collective_id, has_side_effects=True),
    )(values)


def main_kernel(
    small, tokens, cot_own, cosines, sines, fc2_own, out_own, fc1_spread, qkv_spread,
    gh_own, br_own, fc2_out, out_out, fc1_a, qkv_a, up_sum, qkv_sum, small_all, qkv_all, out_all, fc1_all, fc2_all,
    fc2_part, fc1_part, out_part, qkv_part, c_got, w_got, wide_y, wide_z, cols_y, cols_z,
    hidden, cot, act, gup, attn, gqkv, qkv_w, out_w, stage, full, wide, cols, wide_s, cols_s, fc1_bias, qkv_bias,
    send_sem, recv_sem, local_sem, block_sem, c_send, c_recv, small_send, small_recv,
):
    f32, bf16 = jnp.float32, jnp.bfloat16
    zh, zl, y, x, c = place = [lax.axis_index(name) for name in FINE]
    seat = (zl * 2 + x) * 2 + c
    used, used_local = [0], [0]
    sends = []

    class Copy:
        def __init__(self, describe):
            self.describe = describe

        def start(self):
            self.describe().start()

        def wait(self):
            self.describe().wait()

        def wait_send(self):
            self.describe().wait_send()

        def wait_recv(self):
            self.describe().wait_recv()

    def remote(ends, target):
        n = used[0]
        used[0] += 1

        def describe():
            src, dst = ends()
            return pltpu.make_async_remote_copy(
                src_ref=src,
                dst_ref=dst,
                send_sem=send_sem.at[n],
                recv_sem=recv_sem.at[n],
                device_id=target(),
                device_id_type=MESH_ID,
            )

        copy = Copy(describe)
        copy.start()
        sends.append(copy)
        return copy

    def partner(axis):
        return tuple(1 - p if name == axis else p for name, p in zip(FINE, place))

    def beside():
        return partner("y")

    def across():
        return partner("zh")

    def local(ends):
        n = used_local[0]
        used_local[0] += 1

        def describe():
            src, dst = ends()
            return pltpu.make_async_copy(src, dst, local_sem.at[n])

        copy = Copy(describe)
        copy.start()
        return copy

    def load(*pairs):
        copies = [local(lambda pair=pair: pair) for pair in pairs]
        for copy in copies:
            copy.wait()

    def index_of(where):
        number = 0
        for p in where:
            number = number * 2 + p
        return number

    def away(k):
        return tuple((p + k // 2 ** (4 - i)) % 2 for i, p in enumerate(place))

    barrier = pltpu.get_barrier_semaphore()

    def greet(k, carry):
        pl.semaphore_signal(barrier, inc=1, device_id=away(k), device_id_type=MESH_ID)
        return carry

    lax.fori_loop(1, 32, greet, 0)
    pl.semaphore_wait(barrier, 31)

    blocks, block_rows, width = hidden.shape
    token_count, units = gup.shape
    total_len = token_count // 2
    mine, sent = hidden, cot

    def small_copy(k):
        return pltpu.make_async_remote_copy(
            src_ref=small,
            dst_ref=small_all.at[index_of(place)],
            send_sem=small_send.at[k],
            recv_sem=small_recv.at[k],
            device_id=away(k),
            device_id_type=MESH_ID,
        )

    def small_start(k, carry):
        small_copy(k).start()
        return carry

    def small_wait(k, carry):
        small_copy(k).wait()
        return carry

    lax.fori_loop(1, 32, small_start, 0)
    small_all[index_of(place)] = small[...]
    tokens_in = local(lambda: (tokens, stage))

    def spread(weight, matrix):
        pieces = []
        for dl, dx, dc in W_PEERS:

            def where(dl=dl, dx=dx, dc=dc):
                return zh, (zl + dl) % 2, y, (x + dx) % 2, (c + dc) % 2

            def ends(where=where):
                _, to_zl, _, to_x, to_c = where()
                return weight.at[(to_zl * 2 + to_x) * 2 + to_c], matrix.at[zh, zl, y, x * 2 + c]

            pieces.append(remote(ends, where))
        return pieces, local(lambda: (weight.at[seat], matrix.at[zh, zl, y, x * 2 + c]))

    def parts_of(ends_list):
        return [remote(ends, across) for ends in ends_list], [remote(ends, beside) for ends in ends_list]

    def forward(copy, block):
        copy.wait_recv()
        return remote(lambda: (block(), block()), beside)

    def half_of(matrix, half):
        return lambda: matrix.at[1 - zh, half, y]

    def own_half(matrix, half):
        return lambda: (matrix.at[zh, half, y], matrix.at[zh, half, y])

    fc1_pieces = spread(fc1_spread, fc1_all)
    half_rows = fc2_own.shape[0] // 2

    def fc2_rows_of(a, half):
        return lambda: fc2_all.at[a, y, pl.ds(half * half_rows, half_rows)]

    def fc2_ends(half):
        return lambda: (fc2_own.at[pl.ds(half * half_rows, half_rows)], fc2_rows_of(zh, half)())

    def over(own, gathered, axis):
        return remote(lambda: (own(), gathered()), lambda: partner(axis))

    def own_cot():
        return cot_own

    def seat_of(array, dl=0, dx=0):
        return lambda: array.at[((zl + dl) % 2 * 2 + (x + dx) % 2) * 2 + c]

    cot_zl = over(own_cot, seat_of(cot), "zl")
    fc2_zh, fc2_y = parts_of([fc2_ends(half) for half in range(2)])
    cot_x = over(own_cot, seat_of(cot), "x")
    core = {("cot", 0, 0): over(own_cot, seat_of(cot), "c")}
    own_copies = [
        local(lambda: (cot_own, cot.at[seat])),
        local(lambda: (fc2_own, fc2_all.at[zh, y])),
        local(lambda: (out_own, out_all.at[zh, y])),
    ]

    lax.fori_loop(1, 32, small_wait, 0)
    tokens_in.wait()
    in_place = lax.broadcasted_iota(jnp.int32, (32, width), 1) // (width // 32) == (
        lax.broadcasted_iota(jnp.int32, (32, width), 0)
    )

    def vector(row):
        spread_out = jnp.concatenate([small_all[:, row, :]] * (width // 128), axis=1)
        return jnp.sum(jnp.where(in_place, spread_out, 0.0), axis=0, keepdims=True)

    gain, shift = vector(0), vector(1)

    def norm_rows(i, carry):
        rows = pl.ds(pl.multiple_of(i * 32, 32), 32)
        values = stage[rows].astype(f32)
        centered = values - jnp.mean(values, axis=-1, keepdims=True)
        variance = jnp.mean(centered * centered, axis=-1, keepdims=True)
        hidden[seat, rows] = (centered * lax.rsqrt(variance + eps_norm) * gain + shift).astype(bf16)
        return carry

    lax.fori_loop(0, block_rows // 32, norm_rows, 0)
    hid_zl = over(seat_of(hidden), seat_of(hidden), "zl")
    hid_x = over(seat_of(hidden), seat_of(hidden), "x")
    core["hidden", 0, 0] = over(seat_of(hidden), seat_of(hidden), "c")

    for t in range(4):
        owner = index_of((t // 2, zl, t % 2, x, c))
        for half in range(2):
            at = t * 2 * 128 + half * 128
            fc1_bias[:, at : at + 128] = small_all[owner, pl.ds(4 + half, 1), :]
    low = lax.broadcasted_iota(jnp.int32, (1, 128), 1) < HEAD_DIM
    for part in range(3):
        for a in range(2):
            chunks = []
            for b in range(2):
                chunk = part * 32 + index_of((a, zl, b, x, c))
                row = small_all[chunk // 3, pl.ds(2 + chunk % 3 // 2, 1), :]
                chunks.append(jnp.where(chunk % 3 % 2 == b, row, pltpu.roll(row, HEAD_DIM, 1)))
            at = (part * 2 + a) * 128
            qkv_bias[:, at : at + 128] = jnp.where(low, chunks[0], chunks[1])

    def length_of(seq):
        row = small_all[index_of((zh, seq, y, 0, 0)), pl.ds(7, 1), :]
        return jnp.concatenate([row] * (QB // 128), axis=1).astype(jnp.int32)

    def all_there(pieces):
        for piece in pieces[0]:
            piece.wait_recv()
        pieces[1].wait()

    def to_core(name, copy, dl, dx):
        array = {"cot": cot, "hidden": hidden}[name]
        copy.wait_recv()
        core[name, dl, dx] = over(seat_of(array, dl, dx), seat_of(array, dl, dx), "c")

    all_there(fc1_pieces)
    fc1_zh, fc1_y = parts_of([own_half(fc1_all, half) for half in range(2)])
    to_core("cot", cot_zl, 1, 0)
    cot_zx = over(seat_of(cot, 1), seat_of(cot, 1), "x")
    fc2_fwd = [forward(fc2_zh[0], fc2_rows_of(1 - zh, 0))]
    to_core("cot", cot_x, 0, 1)
    fc2_fwd.append(forward(fc2_zh[1], fc2_rows_of(1 - zh, 1)))
    to_core("hidden", hid_zl, 1, 0)
    hid_zx = over(seat_of(hidden, 1), seat_of(hidden, 1), "x")
    qkv_pieces = spread(qkv_spread, qkv_all)
    to_core("hidden", hid_x, 0, 1)
    fc1_fwd = [forward(fc1_zh[0], half_of(fc1_all, 0))]
    to_core("cot", cot_zx, 1, 1)
    fc1_fwd.append(forward(fc1_zh[1], half_of(fc1_all, 1)))
    all_there(qkv_pieces)
    out_zh, out_y = parts_of([lambda: (out_own, out_all.at[zh, y])])
    qkv_zh, qkv_y = parts_of([own_half(qkv_all, half) for half in range(2)])
    for copy in own_copies:
        copy.wait()
    for copy in fc2_y + fc2_fwd + fc1_y + fc1_fwd:
        copy.wait_recv()

    def tokens_here(dl, dx):
        for name in ("cot", "hidden"):
            core[name, dl, dx].wait_recv()

    late_in = out_y + qkv_y

    def row_job(part, rows, first, slot, put):
        some = pl.ds(0, rows)
        return dict(
            part=lambda a, b: part.at[a, b, pl.ds(first, rows)],
            y=[wide_y.at[slot, j, some] for j in range(2)],
            z=wide_z.at[slot, some],
            v=[wide.at[j, some] for j in range(3)],
            s=wide_s.at[slot, some],
            put=put,
            rows=some,
        )

    def column_job(part, width, away, slot, to):
        lanes = pl.ds(0, width)
        return dict(
            part=lambda a, b: part.at[a, (zl + away) % 2, b],
            y=[cols_y.at[slot, j, :, lanes] for j in range(2)],
            z=cols_z.at[slot, :, lanes],
            v=[cols.at[j, :, lanes] for j in range(3)],
            s=cols_s.at[slot, :, lanes],
            away=away,
            to=to,
        )

    fc1_width, qkv_width = units, gqkv.shape[1]
    out_rows, fc2_rows = out_part.shape[2], fc2_part.shape[2] // 2
    jobs = [
        row_job(fc2_part, fc2_rows, i * fc2_rows, i, fc2_out.at[pl.ds(i * fc2_rows, fc2_rows)])
        for i in range(2)
    ]
    jobs += [column_job(fc1_part, fc1_width, away, away, fc1_a) for away in (1, 0)]
    jobs += [row_job(out_part, out_rows, 0, 2, out_out)]
    jobs += [column_job(qkv_part, qkv_width, away, 2 + away, qkv_a) for away in (1, 0)]

    def send_beside(job):
        job["y_far"] = remote(lambda: (job["part"](1 - zh, 1 - y), job["y"][1]), beside)
        job["y_own"] = remote(lambda: (job["part"](zh, 1 - y), job["y"][0]), beside)

    def pass_on(job):
        job["y_far"].wait_recv()
        v = job["v"]
        load((job["part"](1 - zh, y), v[0]), (job["y"][1], v[1]))
        job["s"][...] = (v[0][...].astype(f32) + v[1][...].astype(f32)).astype(bf16)
        job["z_copy"] = remote(lambda: (job["s"], job["z"]), across)

    arrivals, kept = [], []

    def finish(job):
        job["y_own"].wait_recv()
        job["z_copy"].wait_recv()
        v = job["v"]
        load((job["part"](zh, y), v[0]), (job["y"][0], v[1]), (job["z"], v[2]))
        total = v[0][...].astype(f32) + v[1][...].astype(f32) + v[2][...].astype(f32)
        if "put" in job:
            full[job["rows"]] = total
            load((full.at[job["rows"]], job["put"]))
            return
        job["z_copy"].wait_send()
        sends[:] = [copy for copy in sends if copy is not job["z_copy"]]
        job["s"][...] = total.astype(bf16)
        piece = job["s"].shape[0] // 4
        for dx in range(2):
            for dc in range(2):

                def where(dx=dx, dc=dc):
                    return zh, (zl + job["away"]) % 2, y, (x + dx) % 2, (c + dc) % 2

                def ends(where=where):
                    _, _, _, to_x, to_c = where()
                    row = pl.multiple_of((to_x * 2 + to_c) * piece, piece)
                    return job["s"].at[pl.ds(row, piece)], job["to"].at[(zl * 2 + x) * 2 + c]

                if job["away"] or dx or dc:
                    arrivals.append(remote(ends, where))
                else:
                    kept.append(local(ends))

    def core_copy(n, g):
        return pltpu.make_async_remote_copy(
            src_ref=sent.at[4 * n + g],
            dst_ref=c_got.at[n, g],
            send_sem=c_send.at[n, g],
            recv_sem=c_recv.at[n, g],
            device_id=partner("c"),
            device_id_type=MESH_ID,
        )

    axes = (("x", "zl"), ("x", "zl"))

    def multiply_groups(n, first, a, v, b, w, multiply):
        def step(g, carry):
            one, two = 1 - g // 2, 1 - g % 2
            dl, dx = two, one
            rest = ((zl + dl) % 2 * 2 + (x + dx) % 2) * 2

            def block(where):
                rows = pl.ds(pl.multiple_of((rest + where) * 256, 256), 256)
                near, far = v[...].reshape(-1, v.shape[-1]), w[...].reshape(-1, w.shape[-1])
                return (multiply(a[rows], near) + multiply(b[rows], far)).astype(bf16)

            sent[4 * n + g] = block(1 - c)
            core_copy(n, g).start()
            mine[4 * n + g] = block(c)
            return carry

        lax.fori_loop(first, first + 2, step, 0)

    def add(n, g, got):
        load((got, stage))
        mine[4 * n + g] = (mine[4 * n + g].astype(f32) + stage[...].astype(f32)).astype(bf16)

    def add_core(n, g):
        core_copy(n, g).wait_recv()
        add(n, g, c_got.at[n, g])

    first_copies, second_copies = {}, {}

    def send_first(n):
        for g in range(2):
            add_core(n, g)
            first_copies[n, g] = remote(
                lambda g=g: (mine.at[4 * n + g], w_got.at[n, g]), lambda: partner(axes[n][0])
            )

    def send_second(n):
        first_copies[n, 0].wait_recv()
        add(n, 2, w_got.at[n, 0])
        second_copies[n] = remote(
            lambda: (mine.at[4 * n + 2], w_got.at[n, 2]), lambda: partner(axes[n][1])
        )

    def add_first(n):
        first_copies[n, 1].wait_recv()
        add(n, 3, w_got.at[n, 1])

    def total(n, out):
        second_copies[n].wait_recv()
        load((w_got.at[n, 2], stage))
        full[...] = mine[4 * n + 3].astype(f32) + stage[...].astype(f32)
        load((full, out))

    def part_tiles(left, right, at, put, tile):
        def step(i, carry):
            lanes = pl.ds(pl.multiple_of(at(i) * 256, 256), 256)
            product = tn(left(lanes), right())
            slot = i % 2

            @pl.when(i >= 2)
            def _():
                pltpu.make_async_copy(tile.at[slot], put(i - 2), block_sem.at[slot]).wait()

            tile[slot] = product.astype(bf16)
            pltpu.make_async_copy(tile.at[slot], put(i), block_sem.at[slot]).start()
            return carry

        def between(first, last):
            lax.fori_loop(first, last, step, 0)

        def drain(last):
            for i in (last - 2, last - 1):
                pltpu.make_async_copy(tile.at[i % 2], put(i), block_sem.at[i % 2]).wait()

        return between, drain

    def far_first(i):
        far, beside = 1 - i % 2, 1 - i // 2
        return (zh + far) % 2, (y + beside) % 2

    def fc_weights(fc1_w, fc2_w):
        return [local(lambda: (fc1_all, fc1_w)), local(lambda: (fc2_all, fc2_w))]

    def feed(fc1_w, fc2_w, tile_wide, tile_cols):
        for copy in fc_weights(fc1_w, fc2_w):
            copy.wait()
        up_sum[...] = jnp.zeros_like(up_sum)

        def step(i, carry):
            b = ((zl + i // 2) % 2 * 2 + (x + i // 4) % 2) * 2 + (c + i) % 2
            rows = pl.ds(pl.multiple_of(b * 256, 256), 256)
            up = nn(hidden[b], fc1_w[...].reshape(width, units)) + fc1_bias[...]
            bent = jnp.tanh(gelu_coef * (up + 0.044715 * up * up * up))
            act[rows] = (0.5 * up * (1.0 + bent)).astype(bf16)
            slope = 0.5 * (1.0 + bent) + 0.5 * up * (1.0 - bent * bent) * gelu_coef * (
                1.0 + 3.0 * 0.044715 * up * up
            )
            back = (nt(cot[b], fc2_w[...].reshape(units, width)) * slope).astype(bf16)
            gup[rows] = back
            up_sum[...] += jnp.sum(back.astype(f32), axis=0, keepdims=True)
            return carry

        tokens_here(0, 0)
        tokens_here(1, 0)
        lax.fori_loop(0, 4, step, 0)
        to_core("hidden", hid_zx, 1, 1)
        tokens_here(0, 1)
        lax.fori_loop(4, 6, step, 0)
        late_in.append(forward(out_zh[0], lambda: out_all.at[1 - zh, y]))
        late_in.append(forward(qkv_zh[0], half_of(qkv_all, 0)))
        tokens_here(1, 1)
        lax.fori_loop(6, 8, step, 0)

        def unit_place(i):
            a, b = far_first(i)
            return a * 2 + b

        def unit_put(i):
            a, b = far_first(i)
            return fc2_part.at[a, b]

        between, drain = part_tiles(
            lambda lanes: act[:, lanes], lambda: cot[...].reshape(token_count, width), unit_place, unit_put, tile_wide
        )
        between(0, 2)
        drain(2)
        late_in.append(forward(qkv_zh[1], half_of(qkv_all, 1)))
        for job in jobs[:2]:
            send_beside(job)
        between, drain = part_tiles(
            lambda lanes: act[:, lanes],
            lambda: cot[...].reshape(token_count, width),
            lambda i: unit_place(i + 2),
            lambda i: unit_put(i + 2),
            tile_wide,
        )
        between(0, 2)
        drain(2)
        feature_tiles(gup, fc1_part, tile_cols, jobs[2:4])

    def feature_tiles(right, part, tile, of):
        for late in range(2):

            def where(i, late=late):
                a, b = far_first(i // 2 + 2 * late)
                return a, i % 2, b

            def feature_place(i, where=where):
                a, half, b = where(i)
                return a * 4 + half * 2 + b

            between, drain = part_tiles(
                lambda lanes: hidden[:, :, lanes].reshape(token_count, 256),
                lambda: right[...],
                feature_place,
                lambda i, where=where: part.at[where(i)],
                tile,
            )
            between(0, 4)
            drain(4)
            if late == 0:
                for job in of:
                    send_beside(job)

    fc_scratch = (pltpu.VMEM(fc1_all.shape, bf16), pltpu.VMEM(fc2_all.shape, bf16))
    pl.run_scoped(
        feed,
        *fc_scratch,
        pltpu.VMEM((2, 256, width), bf16),
        pltpu.VMEM((2, 256, units), bf16),
    )

    for copy in late_in:
        copy.wait_recv()
    load((qkv_all, qkv_w), (out_all, out_w))

    def attend(projected, mixed, q_s, k_s, v_s, g_s, gk_s, gv_s):
        for seq in range(2):

            def project(b, carry, seq=seq):
                rows = pl.ds(pl.multiple_of(b * 256, 256), 256)
                block = b + seq * (blocks // 2)
                projected[rows] = nn(hidden[block], qkv_w[...].reshape(width, qkv_width))
                mixed[rows] = nt(cot[block], out_w[...].reshape(-1, width))
                return carry

            lax.fori_loop(0, blocks // 2, project, 0)

            def pair_step(pair, carry, seq=seq):
                attend_pair(
                    pair, length_of(seq), qkv_bias, cosines, sines, projected, mixed, q_s, k_s, v_s, g_s, gk_s, gv_s
                )
                return carry

            lax.fori_loop(0, mixed.shape[1] // 128, pair_step, 0)
            qkv_sum[seq] = jnp.zeros((1, qkv_width), f32)

            def store(b, carry, seq=seq):
                rows = pl.ds(pl.multiple_of(b * 256, 256), 256)
                to = pl.ds(pl.multiple_of(b * 256 + seq * total_len, 256), 256)
                grads = projected[rows].astype(bf16)
                gqkv[to] = grads
                attn[to] = mixed[rows].astype(bf16)
                qkv_sum[seq] += jnp.sum(grads.astype(f32), axis=0, keepdims=True)
                return carry

            lax.fori_loop(0, blocks // 2, store, 0)
            pass_on(jobs[seq])

    heads = pltpu.VMEM((2, total_len, 128), bf16)
    pl.run_scoped(
        attend,
        pltpu.VMEM((total_len, qkv_width), f32),
        pltpu.VMEM((total_len, attn.shape[1]), f32),
        heads,
        heads,
        heads,
        heads,
        pltpu.VMEM((total_len, 128), f32),
        pltpu.VMEM((total_len, 128), f32),
    )

    def attend_parts(tile_cols, tile_out):
        feature_tiles(gqkv, qkv_part, tile_cols, jobs[5:7])
        tile_out[...] = tn(attn[...], cot[...].reshape(token_count, width)).astype(bf16)
        rows = tile_out.shape[0] // 4
        load(*((tile_out.at[pl.ds(rows * i, rows)], out_part.at[i // 2, i % 2]) for i in range(4)))
        send_beside(jobs[4])

    pl.run_scoped(
        attend_parts, pltpu.VMEM((2, 256, qkv_width), bf16), pltpu.VMEM((attn.shape[1], width), bf16)
    )

    early_sends = list(core.values()) + [cot_zl, cot_x, cot_zx, hid_zl, hid_x, hid_zx]

    def sums(fc1_w, fc2_w):
        weights = fc_weights(fc1_w, fc2_w)
        for copy in early_sends:
            copy.wait_send()
        weights[0].wait()
        multiply_groups(0, 0, gqkv, qkv_w, gup, fc1_w, nt)
        send_first(0)
        weights[1].wait()
        multiply_groups(1, 0, attn, out_w, act, fc2_w, nn)
        send_first(1)
        pass_on(jobs[2])
        finish(jobs[0])
        multiply_groups(0, 2, gqkv, qkv_w, gup, fc1_w, nt)
        multiply_groups(1, 2, attn, out_w, act, fc2_w, nn)

    pl.run_scoped(sums, *fc_scratch)
    for n in range(2):
        add_core(n, 2)
        add_core(n, 3)
    pass_on(jobs[3])
    finish(jobs[1])
    send_second(0)
    finish(jobs[2])
    pass_on(jobs[5])
    add_first(0)
    pass_on(jobs[6])
    pass_on(jobs[4])
    finish(jobs[3])
    send_second(1)
    add_first(1)
    total(0, gh_own)
    finish(jobs[5])
    finish(jobs[6])
    finish(jobs[4])
    total(1, br_own)
    for copy in arrivals:
        copy.wait_recv()
    for copy in kept:
        copy.wait()
    for copy in sends:
        if not any(copy is early for early in early_sends):
            copy.wait_send()
    for n in range(2):
        for g in range(4):
            core_copy(n, g).wait_send()


def main(small, tokens, cot, cosines, sines, fc2_own, out_own, fc1_spread, qkv_spread):
    bf16, f32 = jnp.bfloat16, jnp.float32
    block, width = tokens.shape
    tokens_all = 8 * block
    rows, ff_rows = out_own.shape[0], fc2_own.shape[0]
    fc1_width, qkv_width = fc1_spread.shape[2], qkv_spread.shape[2]
    half = ff_rows // 2
    any_, vmem = pl.BlockSpec(memory_space=pl.ANY), pl.BlockSpec(memory_space=pltpu.VMEM)
    shapes = [
        ((block, width), f32, any_),
        ((block, width), f32, any_),
        ((ff_rows, width), f32, any_),
        ((rows, width), f32, any_),
        ((8, rows, fc1_width), bf16, any_),
        ((8, rows, qkv_width), bf16, any_),
        ((1, fc1_width), f32, vmem),
        ((2, 1, qkv_width), f32, vmem),
        ((32,) + small.shape, f32, vmem),
        ((2, 2, 2, 4, rows, qkv_width), bf16, any_),
        ((2, 2, rows, width), bf16, any_),
        ((2, 2, 2, 4, rows, fc1_width), bf16, any_),
        ((2, 2, ff_rows, width), bf16, any_),
        ((2, 2, ff_rows, width), bf16, any_),
        ((2, 2, 2, 4 * rows, fc1_width), bf16, any_),
        ((2, 2, rows, width), bf16, any_),
        ((2, 2, 2, 4 * rows, qkv_width), bf16, any_),
        ((2, 4, block, width), bf16, any_),
        ((2, 3, block, width), bf16, any_),
        ((3, 2, half, width), bf16, any_),
        ((3, half, width), bf16, any_),
        ((4, 2, 4 * rows, fc1_width), bf16, any_),
        ((4, 4 * rows, fc1_width), bf16, any_),
    ]
    scratch = [
        pltpu.VMEM((8, block, width), bf16),
        pltpu.VMEM((8, block, width), bf16),
        pltpu.VMEM((tokens_all, fc1_width), bf16),
        pltpu.VMEM((tokens_all, fc1_width), bf16),
        pltpu.VMEM((tokens_all, 4 * rows), bf16),
        pltpu.VMEM((tokens_all, qkv_width), bf16),
        pltpu.VMEM((2, 2, 2, 4, rows, qkv_width), bf16),
        pltpu.VMEM((2, 2, rows, width), bf16),
        pltpu.VMEM((block, width), bf16),
        pltpu.VMEM((block, width), f32),
        pltpu.VMEM((3, half, width), bf16),
        pltpu.VMEM((3, 4 * rows, fc1_width), bf16),
        pltpu.VMEM((3, half, width), bf16),
        pltpu.VMEM((4, 4 * rows, fc1_width), bf16),
        pltpu.VMEM((1, fc1_width), f32),
        pltpu.VMEM((1, qkv_width), f32),
        pltpu.SemaphoreType.DMA((96,)),
        pltpu.SemaphoreType.DMA((96,)),
        pltpu.SemaphoreType.DMA((96,)),
        pltpu.SemaphoreType.DMA((2,)),
        pltpu.SemaphoreType.DMA((2, 4)),
        pltpu.SemaphoreType.DMA((2, 4)),
        pltpu.SemaphoreType.DMA((32,)),
        pltpu.SemaphoreType.DMA((32,)),
    ]
    return pl.pallas_call(
        main_kernel,
        out_shape=[jax.ShapeDtypeStruct(shape, kind) for shape, kind, _ in shapes],
        in_specs=[vmem, any_, any_, vmem, vmem] + [any_] * 4,
        out_specs=[spec for _, _, spec in shapes],
        scratch_shapes=scratch,
        compiler_params=pltpu.CompilerParams(
            collective_id=0, has_side_effects=True, vmem_limit_bytes=63 * 2**20
        ),
    )(small, tokens, cot, cosines, sines, fc2_own, out_own, fc1_spread, qkv_spread)[:9]


def columns_kernel(fc1_in, qkv_in, fc1_out, qkv_out):
    f32 = jnp.float32
    unit, part_width = fc1_in.shape[2] // 4, qkv_in.shape[2] // 3
    for w in range(8):
        for t in range(4):
            at = ((t // 2 * 2 + w // 4) * 2 + t % 2) * 4 * unit + w % 4 * unit
            fc1_out[:, at : at + unit] = fc1_in[w, :, t * unit : (t + 1) * unit].astype(f32)
    low = lax.broadcasted_iota(jnp.int32, (1, 128), 1) < HEAD_DIM
    for part in range(3):
        for a in range(2):
            for dl in range(2):
                for dx in range(2):
                    at = part * part_width + a * 128
                    even, odd = (
                        qkv_in[dl * 4 + dx * 2 + k, :, at : at + 128].astype(f32) for k in range(2)
                    )
                    to = part * 8 * part_width + a * 1024 + dl * 512 + dx * 128
                    qkv_out[:, to : to + 128] = jnp.where(low, even, pltpu.roll(odd, 64, 1))
                    qkv_out[:, to + 256 : to + 384] = jnp.where(low, pltpu.roll(even, 64, 1), odd)


def plain_columns(fc1_in, qkv_in):
    _, rows, fc1_width = fc1_in.shape
    vmem = pl.BlockSpec(memory_space=pltpu.VMEM)
    return pl.pallas_call(
        columns_kernel,
        out_shape=[
            jax.ShapeDtypeStruct((rows, 8 * fc1_width), jnp.float32),
            jax.ShapeDtypeStruct((rows, 8 * qkv_in.shape[2]), jnp.float32),
        ],
        in_specs=[vmem, vmem],
        out_specs=[vmem, vmem],
        compiler_params=pltpu.CompilerParams(vmem_limit_bytes=24 * 2**20),
    )(fc1_in, qkv_in)


def split_device(
    tokens,
    lengths,
    ln_gain,
    ln_bias,
    w_qkv,
    b_qkv,
    w_out,
    b_out,
    w_fc1,
    b_fc1,
    w_fc2,
    b_fc2,
    cotangent,
):
    bf16, f32 = jnp.bfloat16, jnp.float32
    zh, zl, y, x, c = (lax.axis_index(name) for name in FINE)
    place = (zl * 2 + x) * 2 + c
    _, local_len, width = tokens.shape
    rows = w_qkv.shape[0]
    ff_rows = w_fc2.shape[0]
    pieces = 4
    total_len = local_len * pieces
    heads = 4
    own_width = heads * HEAD_DIM

    row = 2 * rows
    small = jnp.concatenate(
        [v.astype(f32) for v in (ln_gain, ln_gain, ln_bias, ln_bias, b_qkv, b_out, b_fc1, b_fc2)]
        + [jnp.zeros(row - rows, f32), jnp.broadcast_to(lengths.astype(f32), (row,))]
    ).reshape(-1, row)
    places = (x * 2 + c) * local_len + jnp.arange(local_len, dtype=jnp.int32)
    grad_own = jnp.where((places < lengths[0])[:, None], cotangent[0], jnp.zeros((), bf16))
    fc1_spread = (
        w_fc1.reshape((rows, 2, 2, 2, 2, 2, ff_rows))
        .transpose(2, 4, 5, 0, 1, 3, 6)
        .reshape(8, rows, -1)
    )
    qkv_spread = (
        w_qkv.reshape((rows, 3, 2, 2, 2, 2, 2, HEAD_DIM))
        .transpose(3, 5, 6, 0, 1, 2, 4, 7)
        .reshape(8, rows, -1)
    )
    cosines, sines = tables(total_len, ROT)
    (
        grad_hidden_own,
        branch_own,
        grad_fc2,
        grad_wout,
        fc1_columns,
        qkv_columns,
        grad_up_sum,
        grad_qkv_sum,
        small_all,
    ) = main(
        small, tokens[0], grad_own, cosines, sines, w_fc2, w_out, fc1_spread, qkv_spread
    )
    grad_wfc1, grad_wqkv = plain_columns(fc1_columns, qkv_columns)
    gain_all = small_all[:, 0, :rows].reshape(-1)
    bout_all, bfc2_all = small_all[:, 3, rows:].reshape(-1), small_all[:, 6, :rows].reshape(-1)

    inputs = tokens[0].astype(f32)
    average = jnp.mean(inputs, axis=-1, keepdims=True)
    centered = inputs - average
    variance = jnp.mean(centered * centered, axis=-1, keepdims=True)
    inv_std = lax.rsqrt(variance + eps_norm)
    normed = centered * inv_std

    output = (inputs + branch_own + bout_all + bfc2_all).astype(bf16)[None]
    grad_norm = grad_hidden_own * gain_all
    grad_input = grad_own.astype(f32) + inv_std * (
        grad_norm
        - jnp.mean(grad_norm, axis=-1, keepdims=True)
        - normed * jnp.mean(grad_norm * normed, axis=-1, keepdims=True)
    )
    grad_input = grad_input.astype(bf16)[None]

    mine = (jnp.arange(8) == place).astype(f32)
    bqkv_term = (
        (jnp.sum(grad_qkv_sum, axis=0).reshape(1, 3, 2, 2, HEAD_DIM) * mine[:, None, None, None, None])
        .reshape(2, 4, 3, 2, 2, HEAD_DIM)
        .transpose(2, 3, 0, 4, 1, 5)
        .reshape(-1)
    )
    bfc1_term = (
        (grad_up_sum.reshape(1, 2, 2, ff_rows) * mine[:, None, None, None])
        .reshape(2, 4, 2, 2, ff_rows)
        .transpose(2, 0, 3, 1, 4)
        .reshape(-1)
    )
    bias_term = jnp.sum(grad_own, axis=0, dtype=f32)
    gain_term = jnp.sum(grad_hidden_own * normed, axis=0)
    shift_term = jnp.sum(grad_hidden_own, axis=0)
    terms = jnp.concatenate(
        [
            v.reshape(32, -1)
            for v in (bqkv_term, bfc1_term, bias_term, gain_term, shift_term)
        ],
        axis=1,
    )
    sums = sum_small(terms.reshape(32, -1, 128), 1).reshape(-1)
    grad_bqkv, grad_bfc1, grad_bias, grad_gain, grad_shift = jnp.split(
        sums, np.cumsum([3 * rows, ff_rows, rows, rows])
    )
    return (
        output,
        grad_input,
        grad_gain,
        grad_shift,
        grad_wqkv,
        grad_bqkv,
        grad_wout,
        grad_bias,
        grad_wfc1,
        grad_bfc1,
        grad_fc2,
        grad_bias,
    )


def fine_mesh(mesh):
    return jax.sharding.Mesh(mesh.devices.reshape(2, 2, 2, 2, 2), FINE)


def fine_solution(mesh):
    everyone, seqs, parts = FINE, ("zh", "zl", "y"), ("x", "c")
    placed = (
        P(seqs, parts, None),
        P(seqs),
        P(everyone),
        P(everyone),
        P(everyone, None),
        P(everyone),
        P(everyone, None),
        P(everyone),
        P(everyone, None),
        P(everyone),
        P(everyone, None),
        P(everyone),
        P(seqs, parts, None),
    )
    given = (
        P(seqs, parts, None),
        P(seqs, parts, None),
        P(everyone),
        P(everyone),
        P(everyone, None),
        P(everyone),
        P(everyone, None),
        P(everyone),
        P(everyone, None),
        P(everyone),
        P(everyone, None),
        P(everyone),
    )
    return jax.shard_map(
        split_device, mesh=fine_mesh(mesh), in_specs=placed, out_specs=given, check_vma=False
    )


def solution(mesh):
    if mesh.shape["dp"] == 8 and mesh.shape["ctx"] == 4:
        return fine_solution(mesh)
    return general_solution(mesh)
```

```python
import functools
import math

import jax
import jax.numpy as jnp
import numpy as np
from jax import lax
from jax.experimental import pallas as pl
from jax.experimental.pallas import tpu as pltpu
from jax.sharding import PartitionSpec as P

HEAD_DIM = 64
ROT = 32


eps_norm = 1e-05
gelu_coef = 0.7978845608028654


def gelu_tanh(values):
    return (
        0.5 * values * (1.0 + jnp.tanh(gelu_coef * (values + 0.044715 * values * values * values)))
    )


def rotary_angles(positions, rot_dims):
    half_dims = rot_dims // 2
    freq_index = jnp.arange(half_dims, dtype=jnp.float32)
    inv_freq = jnp.exp(-math.log(10000.0) * 2.0 * freq_index / rot_dims)
    return positions.astype(jnp.float32)[:, None] * inv_freq[None, :]


def rotary(vectors, angles):
    half_dims = angles.shape[-1]
    cosines = jnp.cos(angles)[:, None, :]
    sine_vals = jnp.sin(angles)[:, None, :]
    leading = vectors[..., :half_dims]
    trailing = vectors[..., half_dims : 2 * half_dims]
    return jnp.concatenate(
        [
            leading * cosines - trailing * sine_vals,
            trailing * cosines + leading * sine_vals,
            vectors[..., 2 * half_dims :],
        ],
        axis=-1,
    )


def rotary_back(gradients, angles):
    half_dims = angles.shape[-1]
    cosines = jnp.cos(angles)[:, None, :]
    sine_vals = jnp.sin(angles)[:, None, :]
    leading = gradients[..., :half_dims]
    trailing = gradients[..., half_dims : 2 * half_dims]
    return jnp.concatenate(
        [
            leading * cosines + trailing * sine_vals,
            trailing * cosines - leading * sine_vals,
            gradients[..., 2 * half_dims :],
        ],
        axis=-1,
    )


def masked_scores(queries, key_rows, places, length):
    scores = jnp.einsum("qhd,khd->hqk", queries, key_rows, preferred_element_type=jnp.float32)
    key_places = jnp.arange(key_rows.shape[0], dtype=jnp.int32)
    allowed = (key_places[None, :] <= places[:, None]) & (key_places[None, :] < length)
    return jnp.where(allowed[None], scores, -1e30)


def on_device(
    tokens,
    lengths,
    ln_gain,
    ln_bias,
    w_qkv,
    b_qkv,
    w_out,
    b_out,
    w_fc1,
    b_fc1,
    w_fc2,
    b_fc2,
    cotangent,
):
    seq_count, local_len, model_width = tokens.shape
    shard_rows = w_qkv.shape[0]
    hidden_ratio = w_fc1.shape[1] // model_width
    head_count = model_width // HEAD_DIM
    token_count = seq_count * local_len
    places = lax.axis_index("ctx") * local_len + jnp.arange(local_len, dtype=jnp.int32)
    angles = rotary_angles(places, ROT)
    live_mask = places[None, :] < lengths[:, None]
    inputs = tokens.astype(jnp.float32).reshape(token_count, model_width)
    average = jnp.mean(inputs, axis=-1, keepdims=True)
    centered = inputs - average
    variance = jnp.mean(centered * centered, axis=-1, keepdims=True)
    inv_std = lax.rsqrt(variance + eps_norm)
    normed = centered * inv_std
    qkv_bias_rows = b_qkv.reshape(shard_rows, 3)
    fc1_bias_rows = b_fc1.reshape(shard_rows, hidden_ratio)
    fc2_rows = w_fc2.reshape(shard_rows, hidden_ratio * model_width)
    inner_full = (
        lax.all_gather(w_qkv, ("dp", "ctx"), axis=0, tiled=True),
        lax.all_gather(w_fc1, ("dp", "ctx"), axis=0, tiled=True),
        lax.all_gather(ln_gain, ("dp", "ctx"), axis=0, tiled=True),
        lax.all_gather(ln_bias, ("dp", "ctx"), axis=0, tiled=True),
        lax.all_gather(qkv_bias_rows, ("dp", "ctx"), axis=0, tiled=True),
        lax.all_gather(fc1_bias_rows, ("dp", "ctx"), axis=0, tiled=True),
    )
    gain_full = inner_full[2].astype(jnp.float32)
    shift_full = inner_full[3].astype(jnp.float32)
    hidden = (normed * gain_full + shift_full).astype(jnp.bfloat16)
    qkv_acc = jnp.dot(hidden, inner_full[0], preferred_element_type=jnp.float32)
    up_acc = jnp.dot(hidden, inner_full[1], preferred_element_type=jnp.float32)
    qkv_bias = inner_full[4].reshape(-1).astype(jnp.float32)
    fc1_bias = inner_full[5].reshape(-1).astype(jnp.float32)
    qkv_proj = (qkv_acc + qkv_bias).reshape(seq_count, local_len, 3, head_count, HEAD_DIM)
    queries = (rotary(qkv_proj[:, :, 0], angles) * 0.125).astype(jnp.bfloat16)
    key_local = (
        rotary(qkv_proj[:, :, 1], angles)
        .astype(jnp.bfloat16)
        .reshape(seq_count, local_len, model_width)
    )
    value_local = qkv_proj[:, :, 2].astype(jnp.bfloat16).reshape(seq_count, local_len, model_width)
    key_full, value_full = (
        lax.all_gather(key_local, "ctx", axis=1, tiled=True),
        lax.all_gather(value_local, "ctx", axis=1, tiled=True),
    )
    total_len = key_full.shape[1]

    def attend_forward(packed):
        query_seq, key_seq, value_seq, length = packed
        key_heads = key_seq.reshape(total_len, head_count, HEAD_DIM)
        value_heads = value_seq.reshape(total_len, head_count, HEAD_DIM)
        scores = masked_scores(query_seq, key_heads, places, length)
        row_max = jnp.max(scores, axis=-1, keepdims=True)
        exponent = jnp.exp(scores - row_max)
        row_sum = jnp.sum(exponent, axis=-1, keepdims=True)
        probability = (exponent / row_sum).astype(jnp.bfloat16)
        attended = jnp.einsum(
            "hqk,khd->qhd", probability, value_heads, preferred_element_type=jnp.float32
        )
        log_total = (row_max + jnp.log(row_sum))[..., 0]
        return (attended.reshape(local_len, model_width).astype(jnp.bfloat16), log_total)

    attn_seq, log_totals = lax.map(attend_forward, (queries, key_full, value_full, lengths))
    attn_mixed = attn_seq.reshape(token_count, model_width)
    up_proj = up_acc + fc1_bias
    activated = gelu_tanh(up_proj).astype(jnp.bfloat16)
    outer_full = (
        lax.all_gather(w_out, ("dp", "ctx"), axis=0, tiled=True),
        lax.all_gather(fc2_rows, ("dp", "ctx"), axis=0, tiled=True),
        lax.all_gather(b_out, ("dp", "ctx"), axis=0, tiled=True),
        lax.all_gather(b_fc2, ("dp", "ctx"), axis=0, tiled=True),
    )
    branch = jnp.dot(attn_mixed, outer_full[0], preferred_element_type=jnp.float32) + jnp.dot(
        activated,
        outer_full[1].reshape(hidden_ratio * model_width, model_width),
        preferred_element_type=jnp.float32,
    )
    out_bias = outer_full[2].astype(jnp.float32)
    fc2_bias = outer_full[3].astype(jnp.float32)
    output = (
        (inputs + branch + out_bias + fc2_bias)
        .astype(jnp.bfloat16)
        .reshape(seq_count, local_len, model_width)
    )
    grad_out = jnp.where(live_mask[:, :, None], cotangent, jnp.zeros((), jnp.bfloat16)).reshape(
        token_count, model_width
    )
    out_back, fc2_back = (
        lax.all_gather(w_out, ("dp", "ctx"), axis=0, tiled=True),
        lax.all_gather(fc2_rows, ("dp", "ctx"), axis=0, tiled=True),
    )
    fc2_matrix = fc2_back.reshape(hidden_ratio * model_width, model_width)
    grad_mixed = jnp.einsum(
        "td,kd->tk", grad_out, out_back, preferred_element_type=jnp.float32
    ).astype(jnp.bfloat16)
    grad_act = jnp.einsum("td,kd->tk", grad_out, fc2_matrix, preferred_element_type=jnp.float32)
    gelu_value, gelu_pull = jax.vjp(gelu_tanh, up_proj)
    grad_up = gelu_pull(grad_act)[0].astype(jnp.bfloat16)
    key_back, value_back = (
        lax.all_gather(key_local, "ctx", axis=1, tiled=True),
        lax.all_gather(value_local, "ctx", axis=1, tiled=True),
    )

    def attend_backward(packed):
        query_seq, key_seq, value_seq, grad_seq, log_total, length = packed
        key_heads = key_seq.reshape(total_len, head_count, HEAD_DIM)
        value_heads = value_seq.reshape(total_len, head_count, HEAD_DIM)
        grad_heads = grad_seq.reshape(local_len, head_count, HEAD_DIM)
        scores = masked_scores(query_seq, key_heads, places, length)
        probability = jnp.exp(scores - log_total[:, :, None])
        grad_probs = jnp.einsum(
            "qhd,khd->hqk", grad_heads, value_heads, preferred_element_type=jnp.float32
        )
        inner = jnp.sum(probability * grad_probs, axis=-1, keepdims=True)
        grad_scores = (probability * (grad_probs - inner)).astype(jnp.bfloat16)
        grad_query = jnp.einsum(
            "hqk,khd->qhd", grad_scores, key_heads, preferred_element_type=jnp.float32
        )
        grad_keys = jnp.einsum(
            "hqk,qhd->khd", grad_scores, query_seq, preferred_element_type=jnp.float32
        )
        grad_values = jnp.einsum(
            "hqk,qhd->khd",
            probability.astype(jnp.bfloat16),
            grad_heads,
            preferred_element_type=jnp.float32,
        )
        return (
            grad_query,
            grad_keys.reshape(total_len, model_width),
            grad_values.reshape(total_len, model_width),
        )

    grad_query, grad_keys_all, grad_values_all = lax.map(
        attend_backward,
        (
            queries,
            key_back,
            value_back,
            grad_mixed.reshape(seq_count, local_len, model_width),
            log_totals,
            lengths,
        ),
    )
    grad_keys_own, grad_values_own = (
        lax.psum_scatter(grad_keys_all, "ctx", scatter_dimension=1, tiled=True),
        lax.psum_scatter(grad_values_all, "ctx", scatter_dimension=1, tiled=True),
    )
    grad_query_pre = rotary_back(grad_query * 0.125, angles).reshape(token_count, model_width)
    grad_keys_pre = rotary_back(
        grad_keys_own.reshape(seq_count, local_len, head_count, HEAD_DIM), angles
    ).reshape(token_count, model_width)
    grad_qkv = jnp.concatenate(
        [grad_query_pre, grad_keys_pre, grad_values_own.reshape(token_count, model_width)], axis=-1
    ).astype(jnp.bfloat16)
    qkv_matrix, fc1_matrix = (
        lax.all_gather(w_qkv, ("dp", "ctx"), axis=0, tiled=True),
        lax.all_gather(w_fc1, ("dp", "ctx"), axis=0, tiled=True),
    )
    grad_hidden = jnp.einsum(
        "tj,dj->td", grad_qkv, qkv_matrix, preferred_element_type=jnp.float32
    ) + jnp.einsum("tj,dj->td", grad_up, fc1_matrix, preferred_element_type=jnp.float32)
    gain_term = jnp.sum(grad_hidden * normed, axis=0)
    shift_term = jnp.sum(grad_hidden, axis=0)
    grad_norm = grad_hidden * gain_full
    grad_input = grad_out.astype(jnp.float32) + inv_std * (
        grad_norm
        - jnp.mean(grad_norm, axis=-1, keepdims=True)
        - normed * jnp.mean(grad_norm * normed, axis=-1, keepdims=True)
    )
    grad_input = grad_input.astype(jnp.bfloat16).reshape(seq_count, local_len, model_width)
    wout_term = jnp.einsum("tk,td->kd", attn_mixed, grad_out, preferred_element_type=jnp.float32)
    wfc2_term = jnp.einsum(
        "tk,td->kd", activated, grad_out, preferred_element_type=jnp.float32
    ).reshape(model_width, hidden_ratio * model_width)
    bias_term = jnp.sum(grad_out, axis=0, dtype=jnp.float32)
    bqkv_term = jnp.sum(grad_qkv, axis=0, dtype=jnp.float32).reshape(model_width, 3)
    bfc1_term = jnp.sum(grad_up, axis=0, dtype=jnp.float32).reshape(model_width, hidden_ratio)
    grad_wout, grad_wfc2, grad_bias, grad_gain, grad_shift, grad_bqkv, grad_bfc1 = (
        lax.psum_scatter(wout_term, ("dp", "ctx"), scatter_dimension=0, tiled=True),
        lax.psum_scatter(wfc2_term, ("dp", "ctx"), scatter_dimension=0, tiled=True),
        lax.psum_scatter(bias_term, ("dp", "ctx"), scatter_dimension=0, tiled=True),
        lax.psum_scatter(gain_term, ("dp", "ctx"), scatter_dimension=0, tiled=True),
        lax.psum_scatter(shift_term, ("dp", "ctx"), scatter_dimension=0, tiled=True),
        lax.psum_scatter(bqkv_term, ("dp", "ctx"), scatter_dimension=0, tiled=True),
        lax.psum_scatter(bfc1_term, ("dp", "ctx"), scatter_dimension=0, tiled=True),
    )
    qkv_part = jnp.einsum("tk,tj->kj", hidden, grad_qkv, preferred_element_type=jnp.float32)
    fc1_part = jnp.einsum("tk,tj->kj", hidden, grad_up, preferred_element_type=jnp.float32)
    inner_sum = lax.psum_scatter(
        jnp.concatenate([qkv_part, fc1_part], axis=1),
        ("dp", "ctx"),
        scatter_dimension=0,
        tiled=True,
    )
    grad_wqkv = inner_sum[:, : 3 * model_width]
    grad_wfc1 = inner_sum[:, 3 * model_width :]
    return (
        output,
        grad_input,
        grad_gain,
        grad_shift,
        grad_wqkv,
        grad_bqkv.reshape(-1),
        grad_wout,
        grad_bias,
        grad_wfc1,
        grad_bfc1.reshape(-1),
        grad_wfc2.reshape(shard_rows * hidden_ratio, model_width),
        grad_bias,
    )


def general_solution(mesh):
    placed = (
        P("dp", "ctx", None),
        P("dp"),
        P(("dp", "ctx")),
        P(("dp", "ctx")),
        P(("dp", "ctx"), None),
        P(("dp", "ctx")),
        P(("dp", "ctx"), None),
        P(("dp", "ctx")),
        P(("dp", "ctx"), None),
        P(("dp", "ctx")),
        P(("dp", "ctx"), None),
        P(("dp", "ctx")),
        P("dp", "ctx", None),
    )
    return jax.shard_map(
        on_device,
        mesh=mesh,
        in_specs=placed,
        out_specs=(
            P("dp", "ctx", None),
            P("dp", "ctx", None),
            P(("dp", "ctx")),
            P(("dp", "ctx")),
            P(("dp", "ctx"), None),
            P(("dp", "ctx")),
            P(("dp", "ctx"), None),
            P(("dp", "ctx")),
            P(("dp", "ctx"), None),
            P(("dp", "ctx")),
            P(("dp", "ctx"), None),
            P(("dp", "ctx")),
        ),
        check_vma=False,
    )


FINE = ("zh", "zl", "y", "x", "c")
ROWS_AXES = ("zl", "x", "c")


def dot(left, right, dims):
    return lax.dot_general(left, right, (dims, ((), ())), preferred_element_type=jnp.float32)


QB = 256


def nt(a, b):
    return dot(a, b, ((1,), (1,)))


def nn(a, b):
    return dot(a, b, ((1,), (0,)))


def tn(a, b):
    return dot(a, b, ((0,), (0,)))


def attend_pair(pair, length, bias, cosines_ref, sines_ref, qkv, mixed, q_s, k_s, v_s, g_s, gk_s, gv_s):
    f32, bf16 = jnp.float32, jnp.bfloat16
    total, width = mixed.shape
    lane = lax.broadcasted_iota(jnp.int32, (1, 128), 1)
    first = lane % HEAD_DIM < ROT // 2
    heads = [lane < HEAD_DIM, lane >= HEAD_DIM]

    def other(v):
        return jnp.where(first, pltpu.roll(v, 128 - ROT // 2, 1), pltpu.roll(v, ROT // 2, 1))

    def col(part):
        return pl.ds(pl.multiple_of(part * width + pair * 128, 128), 128)

    for b in range(total // QB):
        rows = pl.ds(b * QB, QB)
        cosines, sines = cosines_ref[rows], sines_ref[rows]

        def turn(v):
            return v * cosines + other(v) * sines

        q = turn(qkv[rows, col(0)] + bias[:, col(0)]) * 0.125
        k = turn(qkv[rows, col(1)] + bias[:, col(1)])
        v = qkv[rows, col(2)] + bias[:, col(2)]
        g = mixed[rows, col(0)]
        for h in range(2):
            q_s[h, rows] = jnp.where(heads[h], q, 0.0).astype(bf16)
            k_s[h, rows] = jnp.where(heads[h], k, 0.0).astype(bf16)
            v_s[h, rows] = jnp.where(heads[h], v, 0.0).astype(bf16)
            g_s[h, rows] = jnp.where(heads[h], g, 0.0).astype(bf16)
    gk_s[...] = jnp.zeros_like(gk_s)
    gv_s[...] = jnp.zeros_like(gv_s)

    for b in range(total // QB):
        rows = pl.ds(b * QB, QB)
        upto = (b + 1) * QB
        keys = pl.ds(0, upto)
        limit = jnp.minimum(lax.broadcasted_iota(jnp.int32, (1, QB), 1) + (b * QB + 1), length)
        allowed = lax.broadcasted_iota(jnp.int32, (upto, QB), 0) < limit
        out = grad = jnp.zeros((QB, 128), f32)
        for h in range(2):
            qh, gh = q_s[h, rows], g_s[h, rows]
            scores = jnp.where(allowed, nt(k_s[h, keys], qh), -1e30)
            exponent = jnp.exp(scores - jnp.max(scores, axis=0, keepdims=True))
            share = exponent * (1.0 / jnp.sum(exponent, axis=0, keepdims=True))
            rounded = share.astype(bf16)
            back = nt(v_s[h, keys], gh)
            back = (share * (back - jnp.sum(share * back, axis=0, keepdims=True))).astype(bf16)
            gv_s[keys] += nn(rounded, gh)
            gk_s[keys] += nn(back, qh)
            out += tn(rounded, v_s[h, keys])
            grad += tn(back, k_s[h, keys])
        mixed[rows, col(0)] = out
        grad *= 0.125
        qkv[rows, col(0)] = grad * cosines_ref[rows] - other(grad) * sines_ref[rows]
    for b in range(total // QB):
        rows = pl.ds(b * QB, QB)
        grad = gk_s[rows]
        qkv[rows, col(1)] = grad * cosines_ref[rows] - other(grad) * sines_ref[rows]
        qkv[rows, col(2)] = gv_s[rows]


def tables(total, rot):
    half = rot // 2
    inv = jnp.exp(-math.log(10000.0) * 2.0 * jnp.arange(half, dtype=jnp.float32) / rot)
    ang = jnp.arange(total, dtype=jnp.int32).astype(jnp.float32)[:, None] * inv[None, :]
    c, s = jnp.cos(ang), jnp.sin(ang)
    one, nil = jnp.ones((total, 64 - rot), jnp.float32), jnp.zeros((total, 64 - rot), jnp.float32)
    cosines = jnp.concatenate([c, c, one] * 2, axis=1)
    sines = jnp.concatenate([-s, s, nil] * 2, axis=1)
    return cosines, sines


MESH_ID = pl.DeviceIdType.MESH


W_PEERS = [(k // 4, k // 2 % 2, k % 2) for k in range(1, 8)]


def sum_small(values, collective_id):
    n = values.shape[1]
    return pl.pallas_call(
        sum_kernel,
        out_shape=jax.ShapeDtypeStruct((n, 128), jnp.float32),
        in_specs=[pl.BlockSpec(memory_space=pltpu.VMEM)],
        out_specs=pl.BlockSpec(memory_space=pltpu.VMEM),
        scratch_shapes=[
            pltpu.VMEM((32, n, 128), jnp.float32),
            pltpu.SemaphoreType.DMA((32,)),
            pltpu.SemaphoreType.DMA((32,)),
        ],
        compiler_params=pltpu.CompilerParams(collective_id=collective_id, has_side_effects=True),
    )(values)


def main_kernel(
    small, tokens, cot_own, cosines, sines, fc2_own, out_own, fc1_spread, qkv_spread,
    grad_in, output, sums_out, fc2_out, out_out, fc1_a, qkv_a, up_sum, qkv_sum, small_all, qkv_all, out_all, fc1_all, fc2_all,
    fc2_part, fc1_part, out_part, qkv_part, c_got, w_got, wide_y, wide_z, cols_y, cols_z,
    hidden, cot, act, gup, attn, gqkv, qkv_w, out_w, stage, full, wide, cols, wide_s, cols_s, fc1_bias, qkv_bias, terms, terms_got,
    send_sem, recv_sem, local_sem, block_sem, c_send, c_recv, small_send, small_recv, terms_send, terms_recv,
):
    f32, bf16 = jnp.float32, jnp.bfloat16
    zh, zl, y, x, c = place = [lax.axis_index(name) for name in FINE]
    seat = (zl * 2 + x) * 2 + c
    used, used_local = [0], [0]
    sends = []

    class Copy:
        def __init__(self, describe):
            self.describe = describe

        def start(self):
            self.describe().start()

        def wait(self):
            self.describe().wait()

        def wait_send(self):
            self.describe().wait_send()

        def wait_recv(self):
            self.describe().wait_recv()

    def remote(ends, target):
        n = used[0]
        used[0] += 1

        def describe():
            src, dst = ends()
            return pltpu.make_async_remote_copy(
                src_ref=src,
                dst_ref=dst,
                send_sem=send_sem.at[n],
                recv_sem=recv_sem.at[n],
                device_id=target(),
                device_id_type=MESH_ID,
            )

        copy = Copy(describe)
        copy.start()
        sends.append(copy)
        return copy

    def partner(axis):
        return tuple(1 - p if name == axis else p for name, p in zip(FINE, place))

    def beside():
        return partner("y")

    def across():
        return partner("zh")

    def local(ends):
        n = used_local[0]
        used_local[0] += 1

        def describe():
            src, dst = ends()
            return pltpu.make_async_copy(src, dst, local_sem.at[n])

        copy = Copy(describe)
        copy.start()
        return copy

    def load(*pairs):
        copies = [local(lambda pair=pair: pair) for pair in pairs]
        for copy in copies:
            copy.wait()

    def index_of(where):
        number = 0
        for p in where:
            number = number * 2 + p
        return number

    def away(k):
        return tuple((p + k // 2 ** (4 - i)) % 2 for i, p in enumerate(place))

    barrier = pltpu.get_barrier_semaphore()

    def greet(k, carry):
        pl.semaphore_signal(barrier, inc=1, device_id=away(k), device_id_type=MESH_ID)
        return carry

    lax.fori_loop(1, 32, greet, 0)
    pl.semaphore_wait(barrier, 31)

    blocks, block_rows, width = hidden.shape
    token_count, units = gup.shape
    total_len = token_count // 2
    mine, sent = hidden, cot

    def small_copy(k):
        return pltpu.make_async_remote_copy(
            src_ref=small,
            dst_ref=small_all.at[index_of(place)],
            send_sem=small_send.at[k],
            recv_sem=small_recv.at[k],
            device_id=away(k),
            device_id_type=MESH_ID,
        )

    def small_start(k, carry):
        small_copy(k).start()
        return carry

    def small_wait(k, carry):
        small_copy(k).wait()
        return carry

    lax.fori_loop(1, 32, small_start, 0)
    small_all[index_of(place)] = small[...]
    tokens_in = local(lambda: (tokens, stage))

    def spread(weight, matrix):
        pieces = []
        for dl, dx, dc in W_PEERS:

            def where(dl=dl, dx=dx, dc=dc):
                return zh, (zl + dl) % 2, y, (x + dx) % 2, (c + dc) % 2

            def ends(where=where):
                _, to_zl, _, to_x, to_c = where()
                return weight.at[(to_zl * 2 + to_x) * 2 + to_c], matrix.at[zh, zl, y, x * 2 + c]

            pieces.append(remote(ends, where))
        return pieces, local(lambda: (weight.at[seat], matrix.at[zh, zl, y, x * 2 + c]))

    def parts_of(ends_list):
        return [remote(ends, across) for ends in ends_list], [remote(ends, beside) for ends in ends_list]

    def forward(copy, block):
        copy.wait_recv()
        return remote(lambda: (block(), block()), beside)

    def half_of(matrix, half):
        return lambda: matrix.at[1 - zh, half, y]

    def own_half(matrix, half):
        return lambda: (matrix.at[zh, half, y], matrix.at[zh, half, y])

    fc1_pieces = spread(fc1_spread, fc1_all)
    half_rows = fc2_own.shape[0] // 2

    def fc2_rows_of(a, half):
        return lambda: fc2_all.at[a, y, pl.ds(half * half_rows, half_rows)]

    def fc2_ends(half):
        return lambda: (fc2_own.at[pl.ds(half * half_rows, half_rows)], fc2_rows_of(zh, half)())

    def over(own, gathered, axis):
        return remote(lambda: (own(), gathered()), lambda: partner(axis))

    def own_cot():
        return cot_own

    def seat_of(array, dl=0, dx=0):
        return lambda: array.at[((zl + dl) % 2 * 2 + (x + dx) % 2) * 2 + c]

    cot_zl = over(own_cot, seat_of(cot), "zl")
    fc2_zh, fc2_y = parts_of([fc2_ends(half) for half in range(2)])
    cot_x = over(own_cot, seat_of(cot), "x")
    core = {("cot", 0, 0): over(own_cot, seat_of(cot), "c")}
    own_copies = [
        local(lambda: (cot_own, cot.at[seat])),
        local(lambda: (fc2_own, fc2_all.at[zh, y])),
        local(lambda: (out_own, out_all.at[zh, y])),
    ]

    lax.fori_loop(1, 32, small_wait, 0)
    tokens_in.wait()
    in_place = lax.broadcasted_iota(jnp.int32, (32, width), 1) // (width // 32) == (
        lax.broadcasted_iota(jnp.int32, (32, width), 0)
    )

    def vector(row):
        spread_out = jnp.concatenate([small_all[:, row, :]] * (width // 128), axis=1)
        return jnp.sum(jnp.where(in_place, spread_out, 0.0), axis=0, keepdims=True)

    gain, shift = vector(0), vector(1)

    def norm_rows(i, carry):
        rows = pl.ds(pl.multiple_of(i * 32, 32), 32)
        values = stage[rows].astype(f32)
        centered = values - jnp.mean(values, axis=-1, keepdims=True)
        variance = jnp.mean(centered * centered, axis=-1, keepdims=True)
        hidden[seat, rows] = (centered * lax.rsqrt(variance + eps_norm) * gain + shift).astype(bf16)
        return carry

    lax.fori_loop(0, block_rows // 32, norm_rows, 0)
    hid_zl = over(seat_of(hidden), seat_of(hidden), "zl")
    hid_x = over(seat_of(hidden), seat_of(hidden), "x")
    core["hidden", 0, 0] = over(seat_of(hidden), seat_of(hidden), "c")

    for t in range(4):
        owner = index_of((t // 2, zl, t % 2, x, c))
        for half in range(2):
            at = t * 2 * 128 + half * 128
            fc1_bias[:, at : at + 128] = small_all[owner, pl.ds(4 + half, 1), :]
    low = lax.broadcasted_iota(jnp.int32, (1, 128), 1) < HEAD_DIM
    for part in range(3):
        for a in range(2):
            chunks = []
            for b in range(2):
                chunk = part * 32 + index_of((a, zl, b, x, c))
                row = small_all[chunk // 3, pl.ds(2 + chunk % 3 // 2, 1), :]
                chunks.append(jnp.where(chunk % 3 % 2 == b, row, pltpu.roll(row, HEAD_DIM, 1)))
            at = (part * 2 + a) * 128
            qkv_bias[:, at : at + 128] = jnp.where(low, chunks[0], chunks[1])

    def length_of(seq):
        row = small_all[index_of((zh, seq, y, 0, 0)), pl.ds(7, 1), :]
        return jnp.concatenate([row] * (QB // 128), axis=1).astype(jnp.int32)

    def all_there(pieces):
        for piece in pieces[0]:
            piece.wait_recv()
        pieces[1].wait()

    def to_core(name, copy, dl, dx):
        array = {"cot": cot, "hidden": hidden}[name]
        copy.wait_recv()
        core[name, dl, dx] = over(seat_of(array, dl, dx), seat_of(array, dl, dx), "c")

    all_there(fc1_pieces)
    fc1_zh, fc1_y = parts_of([own_half(fc1_all, half) for half in range(2)])
    to_core("cot", cot_zl, 1, 0)
    cot_zx = over(seat_of(cot, 1), seat_of(cot, 1), "x")
    fc2_fwd = [forward(fc2_zh[0], fc2_rows_of(1 - zh, 0))]
    to_core("cot", cot_x, 0, 1)
    fc2_fwd.append(forward(fc2_zh[1], fc2_rows_of(1 - zh, 1)))
    to_core("hidden", hid_zl, 1, 0)
    hid_zx = over(seat_of(hidden, 1), seat_of(hidden, 1), "x")
    qkv_pieces = spread(qkv_spread, qkv_all)
    to_core("hidden", hid_x, 0, 1)
    fc1_fwd = [forward(fc1_zh[0], half_of(fc1_all, 0))]
    to_core("cot", cot_zx, 1, 1)
    fc1_fwd.append(forward(fc1_zh[1], half_of(fc1_all, 1)))
    all_there(qkv_pieces)
    out_zh, out_y = parts_of([lambda: (out_own, out_all.at[zh, y])])
    qkv_zh, qkv_y = parts_of([own_half(qkv_all, half) for half in range(2)])
    for copy in own_copies:
        copy.wait()
    for copy in fc2_y + fc2_fwd + fc1_y + fc1_fwd:
        copy.wait_recv()

    def tokens_here(dl, dx):
        for name in ("cot", "hidden"):
            core[name, dl, dx].wait_recv()

    late_in = out_y + qkv_y

    def row_job(part, rows, first, slot, put):
        some = pl.ds(0, rows)
        return dict(
            part=lambda a, b: part.at[a, b, pl.ds(first, rows)],
            y=[wide_y.at[slot, j, some] for j in range(2)],
            z=wide_z.at[slot, some],
            v=[wide.at[j, some] for j in range(3)],
            s=wide_s.at[slot, some],
            put=put,
            rows=some,
        )

    def column_job(part, width, away, slot, to):
        lanes = pl.ds(0, width)
        return dict(
            part=lambda a, b: part.at[a, (zl + away) % 2, b],
            y=[cols_y.at[slot, j, :, lanes] for j in range(2)],
            z=cols_z.at[slot, :, lanes],
            v=[cols.at[j, :, lanes] for j in range(3)],
            s=cols_s.at[slot, :, lanes],
            away=away,
            to=to,
        )

    fc1_width, qkv_width = units, gqkv.shape[1]
    out_rows, fc2_rows = out_part.shape[2], fc2_part.shape[2] // 2
    jobs = [
        row_job(fc2_part, fc2_rows, i * fc2_rows, i, fc2_out.at[pl.ds(i * fc2_rows, fc2_rows)])
        for i in range(2)
    ]
    jobs += [column_job(fc1_part, fc1_width, away, away, fc1_a) for away in (1, 0)]
    jobs += [row_job(out_part, out_rows, 0, 2, out_out)]
    jobs += [column_job(qkv_part, qkv_width, away, 2 + away, qkv_a) for away in (1, 0)]

    def send_beside(job):
        job["y_far"] = remote(lambda: (job["part"](1 - zh, 1 - y), job["y"][1]), beside)
        job["y_own"] = remote(lambda: (job["part"](zh, 1 - y), job["y"][0]), beside)

    def pass_on(job):
        job["y_far"].wait_recv()
        v = job["v"]
        load((job["part"](1 - zh, y), v[0]), (job["y"][1], v[1]))
        job["s"][...] = (v[0][...].astype(f32) + v[1][...].astype(f32)).astype(bf16)
        job["z_copy"] = remote(lambda: (job["s"], job["z"]), across)

    arrivals, kept = [], []

    def finish(job):
        job["y_own"].wait_recv()
        job["z_copy"].wait_recv()
        v = job["v"]
        load((job["part"](zh, y), v[0]), (job["y"][0], v[1]), (job["z"], v[2]))
        total = v[0][...].astype(f32) + v[1][...].astype(f32) + v[2][...].astype(f32)
        if "put" in job:
            full[job["rows"]] = total
            load((full.at[job["rows"]], job["put"]))
            return
        job["z_copy"].wait_send()
        sends[:] = [copy for copy in sends if copy is not job["z_copy"]]
        job["s"][...] = total.astype(bf16)
        piece = job["s"].shape[0] // 4
        for dx in range(2):
            for dc in range(2):

                def where(dx=dx, dc=dc):
                    return zh, (zl + job["away"]) % 2, y, (x + dx) % 2, (c + dc) % 2

                def ends(where=where):
                    _, _, _, to_x, to_c = where()
                    row = pl.multiple_of((to_x * 2 + to_c) * piece, piece)
                    return job["s"].at[pl.ds(row, piece)], job["to"].at[(zl * 2 + x) * 2 + c]

                if job["away"] or dx or dc:
                    arrivals.append(remote(ends, where))
                else:
                    kept.append(local(ends))

    def core_copy(n, g):
        return pltpu.make_async_remote_copy(
            src_ref=sent.at[4 * n + g],
            dst_ref=c_got.at[n, g],
            send_sem=c_send.at[n, g],
            recv_sem=c_recv.at[n, g],
            device_id=partner("c"),
            device_id_type=MESH_ID,
        )

    axes = (("x", "zl"), ("x", "zl"))

    def multiply_groups(n, first, a, v, b, w, multiply):
        def step(g, carry):
            one, two = 1 - g // 2, 1 - g % 2
            dl, dx = two, one
            rest = ((zl + dl) % 2 * 2 + (x + dx) % 2) * 2

            def block(where):
                rows = pl.ds(pl.multiple_of((rest + where) * 256, 256), 256)
                near, far = v[...].reshape(-1, v.shape[-1]), w[...].reshape(-1, w.shape[-1])
                return (multiply(a[rows], near) + multiply(b[rows], far)).astype(bf16)

            sent[4 * n + g] = block(1 - c)
            core_copy(n, g).start()
            mine[4 * n + g] = block(c)
            return carry

        lax.fori_loop(first, first + 2, step, 0)

    def add(n, g, got):
        load((got, stage))
        mine[4 * n + g] = (mine[4 * n + g].astype(f32) + stage[...].astype(f32)).astype(bf16)

    def add_core(n, g):
        core_copy(n, g).wait_recv()
        add(n, g, c_got.at[n, g])

    first_copies, second_copies = {}, {}

    def send_first(n):
        for g in range(2):
            add_core(n, g)
            first_copies[n, g] = remote(
                lambda g=g: (mine.at[4 * n + g], w_got.at[n, g]), lambda: partner(axes[n][0])
            )

    def send_second(n):
        first_copies[n, 0].wait_recv()
        add(n, 2, w_got.at[n, 0])
        second_copies[n] = remote(
            lambda: (mine.at[4 * n + 2], w_got.at[n, 2]), lambda: partner(axes[n][1])
        )

    def add_first(n):
        first_copies[n, 1].wait_recv()
        add(n, 3, w_got.at[n, 1])

    def total(n):
        second_copies[n].wait_recv()
        load((w_got.at[n, 2], stage))
        full[...] = mine[4 * n + 3].astype(f32) + stage[...].astype(f32)

    def chunk(i):
        return pl.ds(pl.multiple_of(i * 32, 32), 32)

    def normalized(values):
        centered = values - jnp.mean(values, axis=-1, keepdims=True)
        inv_std = lax.rsqrt(jnp.mean(centered * centered, axis=-1, keepdims=True) + eps_norm)
        return centered * inv_std, inv_std

    def terms_copy(k):
        return pltpu.make_async_remote_copy(
            src_ref=terms.at[index_of(away(k))],
            dst_ref=terms_got.at[index_of(place)],
            send_sem=terms_send.at[k],
            recv_sem=terms_recv.at[k],
            device_id=away(k),
            device_id_type=MESH_ID,
        )

    def finish_input():
        total(0)
        for g in range(4):
            core_copy(0, g).wait_send()
        load((tokens, sent.at[0]), (cot_own, sent.at[1]))
        gain_row = vector(0)

        def back_rows(i, carry):
            gain_sum, shift_sum, bias_sum = carry
            rows = chunk(i)
            normed, inv_std = normalized(sent[0, rows].astype(f32))
            cotangent = sent[1, rows].astype(f32)
            grads = full[rows]
            scaled = grads * gain_row
            sent[2, rows] = (
                cotangent
                + inv_std
                * (
                    scaled
                    - jnp.mean(scaled, axis=-1, keepdims=True)
                    - normed * jnp.mean(scaled * normed, axis=-1, keepdims=True)
                )
            ).astype(bf16)
            return (
                gain_sum + jnp.sum(grads * normed, axis=0, keepdims=True),
                shift_sum + jnp.sum(grads, axis=0, keepdims=True),
                bias_sum + jnp.sum(cotangent, axis=0, keepdims=True),
            )

        nothing = jnp.zeros((1, width), f32)
        gain_sum, shift_sum, bias_sum = lax.fori_loop(
            0, block_rows // 32, back_rows, (nothing, nothing, nothing)
        )
        load((sent.at[2], grad_in))
        terms[...] = jnp.zeros_like(terms)
        for t in range(4):
            owner = index_of((t // 2, zl, t % 2, x, c))
            for half in range(2):
                at = t * 2 * 128 + half * 128
                terms[owner, pl.ds(2 + half, 1), :] = up_sum[:, at : at + 128]
        side = lax.broadcasted_iota(jnp.int32, (1, 128), 1) // HEAD_DIM
        for part in range(3):
            for a in range(2):
                at = (part * 2 + a) * 128
                both = qkv_sum[0, :, at : at + 128] + qkv_sum[1, :, at : at + 128]
                turned = pltpu.roll(both, HEAD_DIM, 1)
                for b in range(2):
                    piece = part * 32 + index_of((a, zl, b, x, c))
                    owner, row, half = piece // 3, pl.ds(piece % 3 // 2, 1), piece % 3 % 2
                    value = jnp.where(half == b, both, turned)
                    terms[owner, row, :] = jnp.where(side == half, value, terms[owner, row, :])
        for i in range(width // 128):
            for row, vector_sum in ((4, bias_sum), (5, gain_sum), (6, shift_sum)):
                for b in range(2):
                    terms[2 * i + b, row : row + 1, :] = vector_sum[:, i * 128 : (i + 1) * 128]
        terms_got[index_of(place)] = terms[index_of(place)]

        def start(k, carry):
            terms_copy(k).start()
            return carry

        lax.fori_loop(1, 32, start, 0)

    def finish_output():
        total(1)
        bias_row = vector(6)

        def out_rows_of(i, carry):
            rows = chunk(i)
            sent[3, rows] = (sent[0, rows].astype(f32) + full[rows] + bias_row).astype(bf16)
            return carry

        lax.fori_loop(0, block_rows // 32, out_rows_of, 0)
        load((sent.at[3], output))

    def part_tiles(left, right, at, put, tile):
        def step(i, carry):
            lanes = pl.ds(pl.multiple_of(at(i) * 256, 256), 256)
            product = tn(left(lanes), right())
            slot = i % 2

            @pl.when(i >= 2)
            def _():
                pltpu.make_async_copy(tile.at[slot], put(i - 2), block_sem.at[slot]).wait()

            tile[slot] = product.astype(bf16)
            pltpu.make_async_copy(tile.at[slot], put(i), block_sem.at[slot]).start()
            return carry

        def between(first, last):
            lax.fori_loop(first, last, step, 0)

        def drain(last):
            for i in (last - 2, last - 1):
                pltpu.make_async_copy(tile.at[i % 2], put(i), block_sem.at[i % 2]).wait()

        return between, drain

    def far_first(i):
        far, beside = 1 - i % 2, 1 - i // 2
        return (zh + far) % 2, (y + beside) % 2

    def fc_weights(fc1_w, fc2_w):
        return [local(lambda: (fc1_all, fc1_w)), local(lambda: (fc2_all, fc2_w))]

    def feed(fc1_w, fc2_w, tile_wide, tile_cols):
        for copy in fc_weights(fc1_w, fc2_w):
            copy.wait()
        up_sum[...] = jnp.zeros_like(up_sum)

        def step(i, carry):
            b = ((zl + i // 2) % 2 * 2 + (x + i // 4) % 2) * 2 + (c + i) % 2
            rows = pl.ds(pl.multiple_of(b * 256, 256), 256)
            up = nn(hidden[b], fc1_w[...].reshape(width, units)) + fc1_bias[...]
            bent = jnp.tanh(gelu_coef * (up + 0.044715 * up * up * up))
            act[rows] = (0.5 * up * (1.0 + bent)).astype(bf16)
            slope = 0.5 * (1.0 + bent) + 0.5 * up * (1.0 - bent * bent) * gelu_coef * (
                1.0 + 3.0 * 0.044715 * up * up
            )
            back = (nt(cot[b], fc2_w[...].reshape(units, width)) * slope).astype(bf16)
            gup[rows] = back
            up_sum[...] += jnp.sum(back.astype(f32), axis=0, keepdims=True)
            return carry

        tokens_here(0, 0)
        tokens_here(1, 0)
        lax.fori_loop(0, 4, step, 0)
        to_core("hidden", hid_zx, 1, 1)
        tokens_here(0, 1)
        lax.fori_loop(4, 6, step, 0)
        late_in.append(forward(out_zh[0], lambda: out_all.at[1 - zh, y]))
        late_in.append(forward(qkv_zh[0], half_of(qkv_all, 0)))
        tokens_here(1, 1)
        lax.fori_loop(6, 8, step, 0)

        def unit_place(i):
            a, b = far_first(i)
            return a * 2 + b

        def unit_put(i):
            a, b = far_first(i)
            return fc2_part.at[a, b]

        between, drain = part_tiles(
            lambda lanes: act[:, lanes], lambda: cot[...].reshape(token_count, width), unit_place, unit_put, tile_wide
        )
        between(0, 2)
        drain(2)
        late_in.append(forward(qkv_zh[1], half_of(qkv_all, 1)))
        for job in jobs[:2]:
            send_beside(job)
        between, drain = part_tiles(
            lambda lanes: act[:, lanes],
            lambda: cot[...].reshape(token_count, width),
            lambda i: unit_place(i + 2),
            lambda i: unit_put(i + 2),
            tile_wide,
        )
        between(0, 2)
        drain(2)
        feature_tiles(gup, fc1_part, tile_cols, jobs[2:4])

    def feature_tiles(right, part, tile, of):
        for late in range(2):

            def where(i, late=late):
                a, b = far_first(i // 2 + 2 * late)
                return a, i % 2, b

            def feature_place(i, where=where):
                a, half, b = where(i)
                return a * 4 + half * 2 + b

            between, drain = part_tiles(
                lambda lanes: hidden[:, :, lanes].reshape(token_count, 256),
                lambda: right[...],
                feature_place,
                lambda i, where=where: part.at[where(i)],
                tile,
            )
            between(0, 4)
            drain(4)
            if late == 0:
                for job in of:
                    send_beside(job)

    fc_scratch = (pltpu.VMEM(fc1_all.shape, bf16), pltpu.VMEM(fc2_all.shape, bf16))
    pl.run_scoped(
        feed,
        *fc_scratch,
        pltpu.VMEM((2, 256, width), bf16),
        pltpu.VMEM((2, 256, units), bf16),
    )

    for copy in late_in:
        copy.wait_recv()
    load((qkv_all, qkv_w), (out_all, out_w))

    def attend(projected, mixed, q_s, k_s, v_s, g_s, gk_s, gv_s):
        for seq in range(2):

            def project(b, carry, seq=seq):
                rows = pl.ds(pl.multiple_of(b * 256, 256), 256)
                block = b + seq * (blocks // 2)
                projected[rows] = nn(hidden[block], qkv_w[...].reshape(width, qkv_width))
                mixed[rows] = nt(cot[block], out_w[...].reshape(-1, width))
                return carry

            lax.fori_loop(0, blocks // 2, project, 0)

            def pair_step(pair, carry, seq=seq):
                attend_pair(
                    pair, length_of(seq), qkv_bias, cosines, sines, projected, mixed, q_s, k_s, v_s, g_s, gk_s, gv_s
                )
                return carry

            lax.fori_loop(0, mixed.shape[1] // 128, pair_step, 0)
            qkv_sum[seq] = jnp.zeros((1, qkv_width), f32)

            def store(b, carry, seq=seq):
                rows = pl.ds(pl.multiple_of(b * 256, 256), 256)
                to = pl.ds(pl.multiple_of(b * 256 + seq * total_len, 256), 256)
                grads = projected[rows].astype(bf16)
                gqkv[to] = grads
                attn[to] = mixed[rows].astype(bf16)
                qkv_sum[seq] += jnp.sum(grads.astype(f32), axis=0, keepdims=True)
                return carry

            lax.fori_loop(0, blocks // 2, store, 0)
            pass_on(jobs[seq])

    heads = pltpu.VMEM((2, total_len, 128), bf16)
    pl.run_scoped(
        attend,
        pltpu.VMEM((total_len, qkv_width), f32),
        pltpu.VMEM((total_len, attn.shape[1]), f32),
        heads,
        heads,
        heads,
        heads,
        pltpu.VMEM((total_len, 128), f32),
        pltpu.VMEM((total_len, 128), f32),
    )

    def attend_parts(tile_cols, tile_out):
        feature_tiles(gqkv, qkv_part, tile_cols, jobs[5:7])
        tile_out[...] = tn(attn[...], cot[...].reshape(token_count, width)).astype(bf16)
        rows = tile_out.shape[0] // 4
        load(*((tile_out.at[pl.ds(rows * i, rows)], out_part.at[i // 2, i % 2]) for i in range(4)))
        send_beside(jobs[4])

    pl.run_scoped(
        attend_parts, pltpu.VMEM((2, 256, qkv_width), bf16), pltpu.VMEM((attn.shape[1], width), bf16)
    )

    early_sends = list(core.values()) + [cot_zl, cot_x, cot_zx, hid_zl, hid_x, hid_zx]

    def sums(fc1_w, fc2_w):
        weights = fc_weights(fc1_w, fc2_w)
        for copy in early_sends:
            copy.wait_send()
        weights[0].wait()
        multiply_groups(0, 0, gqkv, qkv_w, gup, fc1_w, nt)
        send_first(0)
        weights[1].wait()
        multiply_groups(1, 0, attn, out_w, act, fc2_w, nn)
        send_first(1)
        pass_on(jobs[2])
        finish(jobs[0])
        multiply_groups(0, 2, gqkv, qkv_w, gup, fc1_w, nt)
        multiply_groups(1, 2, attn, out_w, act, fc2_w, nn)

    pl.run_scoped(sums, *fc_scratch)
    for n in range(2):
        add_core(n, 2)
        add_core(n, 3)
    pass_on(jobs[3])
    finish(jobs[1])
    send_second(0)
    finish(jobs[2])
    pass_on(jobs[5])
    add_first(0)
    pass_on(jobs[6])
    pass_on(jobs[4])
    finish(jobs[3])
    send_second(1)
    add_first(1)
    finish_input()
    finish(jobs[5])
    finish(jobs[6])
    finish(jobs[4])
    finish_output()

    def terms_wait(k, carry):
        terms_copy(k).wait()
        return carry

    lax.fori_loop(1, 32, terms_wait, 0)
    sums_out[...] = jnp.sum(terms_got[...], axis=0)
    for copy in arrivals:
        copy.wait_recv()
    for copy in kept:
        copy.wait()
    for copy in sends:
        if not any(copy is early for early in early_sends):
            copy.wait_send()
    for g in range(4):
        core_copy(1, g).wait_send()


def main(small, tokens, cot, cosines, sines, fc2_own, out_own, fc1_spread, qkv_spread):
    bf16, f32 = jnp.bfloat16, jnp.float32
    block, width = tokens.shape
    tokens_all = 8 * block
    rows, ff_rows = out_own.shape[0], fc2_own.shape[0]
    fc1_width, qkv_width = fc1_spread.shape[2], qkv_spread.shape[2]
    half = ff_rows // 2
    any_, vmem = pl.BlockSpec(memory_space=pl.ANY), pl.BlockSpec(memory_space=pltpu.VMEM)
    shapes = [
        ((block, width), bf16, any_),
        ((block, width), bf16, any_),
        (small.shape, f32, vmem),
        ((ff_rows, width), f32, any_),
        ((rows, width), f32, any_),
        ((8, rows, fc1_width), bf16, any_),
        ((8, rows, qkv_width), bf16, any_),
        ((1, fc1_width), f32, vmem),
        ((2, 1, qkv_width), f32, vmem),
        ((32,) + small.shape, f32, vmem),
        ((2, 2, 2, 4, rows, qkv_width), bf16, any_),
        ((2, 2, rows, width), bf16, any_),
        ((2, 2, 2, 4, rows, fc1_width), bf16, any_),
        ((2, 2, ff_rows, width), bf16, any_),
        ((2, 2, ff_rows, width), bf16, any_),
        ((2, 2, 2, 4 * rows, fc1_width), bf16, any_),
        ((2, 2, rows, width), bf16, any_),
        ((2, 2, 2, 4 * rows, qkv_width), bf16, any_),
        ((2, 4, block, width), bf16, any_),
        ((2, 3, block, width), bf16, any_),
        ((3, 2, half, width), bf16, any_),
        ((3, half, width), bf16, any_),
        ((4, 2, 4 * rows, fc1_width), bf16, any_),
        ((4, 4 * rows, fc1_width), bf16, any_),
    ]
    scratch = [
        pltpu.VMEM((8, block, width), bf16),
        pltpu.VMEM((8, block, width), bf16),
        pltpu.VMEM((tokens_all, fc1_width), bf16),
        pltpu.VMEM((tokens_all, fc1_width), bf16),
        pltpu.VMEM((tokens_all, 4 * rows), bf16),
        pltpu.VMEM((tokens_all, qkv_width), bf16),
        pltpu.VMEM((2, 2, 2, 4, rows, qkv_width), bf16),
        pltpu.VMEM((2, 2, rows, width), bf16),
        pltpu.VMEM((block, width), bf16),
        pltpu.VMEM((block, width), f32),
        pltpu.VMEM((3, half, width), bf16),
        pltpu.VMEM((3, 4 * rows, fc1_width), bf16),
        pltpu.VMEM((3, half, width), bf16),
        pltpu.VMEM((4, 4 * rows, fc1_width), bf16),
        pltpu.VMEM((1, fc1_width), f32),
        pltpu.VMEM((1, qkv_width), f32),
        pltpu.VMEM((32,) + small.shape, f32),
        pltpu.VMEM((32,) + small.shape, f32),
        pltpu.SemaphoreType.DMA((96,)),
        pltpu.SemaphoreType.DMA((96,)),
        pltpu.SemaphoreType.DMA((96,)),
        pltpu.SemaphoreType.DMA((2,)),
        pltpu.SemaphoreType.DMA((2, 4)),
        pltpu.SemaphoreType.DMA((2, 4)),
        pltpu.SemaphoreType.DMA((32,)),
        pltpu.SemaphoreType.DMA((32,)),
        pltpu.SemaphoreType.DMA((32,)),
        pltpu.SemaphoreType.DMA((32,)),
    ]
    return pl.pallas_call(
        main_kernel,
        out_shape=[jax.ShapeDtypeStruct(shape, kind) for shape, kind, _ in shapes],
        in_specs=[vmem, any_, any_, vmem, vmem] + [any_] * 4,
        out_specs=[spec for _, _, spec in shapes],
        scratch_shapes=scratch,
        compiler_params=pltpu.CompilerParams(
            collective_id=0, has_side_effects=True, vmem_limit_bytes=63 * 2**20
        ),
    )(small, tokens, cot, cosines, sines, fc2_own, out_own, fc1_spread, qkv_spread)[:7]


def columns_kernel(fc1_in, qkv_in, fc1_out, qkv_out):
    f32 = jnp.float32
    unit, part_width = fc1_in.shape[2] // 4, qkv_in.shape[2] // 3
    for w in range(8):
        for t in range(4):
            at = ((t // 2 * 2 + w // 4) * 2 + t % 2) * 4 * unit + w % 4 * unit
            fc1_out[:, at : at + unit] = fc1_in[w, :, t * unit : (t + 1) * unit].astype(f32)
    low = lax.broadcasted_iota(jnp.int32, (1, 128), 1) < HEAD_DIM
    for part in range(3):
        for a in range(2):
            for dl in range(2):
                for dx in range(2):
                    at = part * part_width + a * 128
                    even, odd = (
                        qkv_in[dl * 4 + dx * 2 + k, :, at : at + 128].astype(f32) for k in range(2)
                    )
                    to = part * 8 * part_width + a * 1024 + dl * 512 + dx * 128
                    qkv_out[:, to : to + 128] = jnp.where(low, even, pltpu.roll(odd, 64, 1))
                    qkv_out[:, to + 256 : to + 384] = jnp.where(low, pltpu.roll(even, 64, 1), odd)


def plain_columns(fc1_in, qkv_in):
    _, rows, fc1_width = fc1_in.shape
    vmem = pl.BlockSpec(memory_space=pltpu.VMEM)
    return pl.pallas_call(
        columns_kernel,
        out_shape=[
            jax.ShapeDtypeStruct((rows, 8 * fc1_width), jnp.float32),
            jax.ShapeDtypeStruct((rows, 8 * qkv_in.shape[2]), jnp.float32),
        ],
        in_specs=[vmem, vmem],
        out_specs=[vmem, vmem],
        compiler_params=pltpu.CompilerParams(vmem_limit_bytes=24 * 2**20),
    )(fc1_in, qkv_in)


def split_device(
    tokens,
    lengths,
    ln_gain,
    ln_bias,
    w_qkv,
    b_qkv,
    w_out,
    b_out,
    w_fc1,
    b_fc1,
    w_fc2,
    b_fc2,
    cotangent,
):
    bf16, f32 = jnp.bfloat16, jnp.float32
    zh, zl, y, x, c = (lax.axis_index(name) for name in FINE)
    place = (zl * 2 + x) * 2 + c
    _, local_len, width = tokens.shape
    rows = w_qkv.shape[0]
    ff_rows = w_fc2.shape[0]
    pieces = 4
    total_len = local_len * pieces
    heads = 4
    own_width = heads * HEAD_DIM

    row = 2 * rows
    out_bias = b_out.astype(f32) + b_fc2.astype(f32)
    small = jnp.concatenate(
        [v.astype(f32) for v in (ln_gain, ln_gain, ln_bias, ln_bias, b_qkv, b_out, b_fc1)]
        + [out_bias, out_bias, jnp.broadcast_to(lengths.astype(f32), (row,))]
    ).reshape(-1, row)
    places = (x * 2 + c) * local_len + jnp.arange(local_len, dtype=jnp.int32)
    grad_own = jnp.where((places < lengths[0])[:, None], cotangent[0], jnp.zeros((), bf16))
    fc1_spread = (
        w_fc1.reshape((rows, 2, 2, 2, 2, 2, ff_rows))
        .transpose(2, 4, 5, 0, 1, 3, 6)
        .reshape(8, rows, -1)
    )
    qkv_spread = (
        w_qkv.reshape((rows, 3, 2, 2, 2, 2, 2, HEAD_DIM))
        .transpose(3, 5, 6, 0, 1, 2, 4, 7)
        .reshape(8, rows, -1)
    )
    cosines, sines = tables(total_len, ROT)
    grad_input, output, sums, grad_fc2, grad_wout, fc1_columns, qkv_columns = main(
        small, tokens[0], grad_own, cosines, sines, w_fc2, w_out, fc1_spread, qkv_spread
    )
    output, grad_input = output[None], grad_input[None]
    grad_wfc1, grad_wqkv = plain_columns(fc1_columns, qkv_columns)
    grad_bqkv, grad_bfc1 = sums[0:2].reshape(-1)[: 3 * rows], sums[2:4].reshape(-1)
    grad_bias, grad_gain, grad_shift = lax.dynamic_slice(sums, (4, c * rows), (3, rows))
    return (
        output,
        grad_input,
        grad_gain,
        grad_shift,
        grad_wqkv,
        grad_bqkv,
        grad_wout,
        grad_bias,
        grad_wfc1,
        grad_bfc1,
        grad_fc2,
        grad_bias,
    )


def fine_mesh(mesh):
    return jax.sharding.Mesh(mesh.devices.reshape(2, 2, 2, 2, 2), FINE)


def fine_solution(mesh):
    everyone, seqs, parts = FINE, ("zh", "zl", "y"), ("x", "c")
    placed = (
        P(seqs, parts, None),
        P(seqs),
        P(everyone),
        P(everyone),
        P(everyone, None),
        P(everyone),
        P(everyone, None),
        P(everyone),
        P(everyone, None),
        P(everyone),
        P(everyone, None),
        P(everyone),
        P(seqs, parts, None),
    )
    given = (
        P(seqs, parts, None),
        P(seqs, parts, None),
        P(everyone),
        P(everyone),
        P(everyone, None),
        P(everyone),
        P(everyone, None),
        P(everyone),
        P(everyone, None),
        P(everyone),
        P(everyone, None),
        P(everyone),
    )
    return jax.shard_map(
        split_device, mesh=fine_mesh(mesh), in_specs=placed, out_specs=given, check_vma=False
    )


def solution(mesh):
    if mesh.shape["dp"] == 8 and mesh.shape["ctx"] == 4:
        return fine_solution(mesh)
    return general_solution(mesh)
```

```python
import functools
import math

import jax
import jax.numpy as jnp
import numpy as np
from jax import lax
from jax.experimental import pallas as pl
from jax.experimental.pallas import tpu as pltpu
from jax.sharding import PartitionSpec as P

HEAD_DIM = 64
ROT = 32


eps_norm = 1e-05
gelu_coef = 0.7978845608028654


def gelu_tanh(values):
    return (
        0.5 * values * (1.0 + jnp.tanh(gelu_coef * (values + 0.044715 * values * values * values)))
    )


def rotary_angles(positions, rot_dims):
    half_dims = rot_dims // 2
    freq_index = jnp.arange(half_dims, dtype=jnp.float32)
    inv_freq = jnp.exp(-math.log(10000.0) * 2.0 * freq_index / rot_dims)
    return positions.astype(jnp.float32)[:, None] * inv_freq[None, :]


def rotary(vectors, angles):
    half_dims = angles.shape[-1]
    cosines = jnp.cos(angles)[:, None, :]
    sine_vals = jnp.sin(angles)[:, None, :]
    leading = vectors[..., :half_dims]
    trailing = vectors[..., half_dims : 2 * half_dims]
    return jnp.concatenate(
        [
            leading * cosines - trailing * sine_vals,
            trailing * cosines + leading * sine_vals,
            vectors[..., 2 * half_dims :],
        ],
        axis=-1,
    )


def rotary_back(gradients, angles):
    half_dims = angles.shape[-1]
    cosines = jnp.cos(angles)[:, None, :]
    sine_vals = jnp.sin(angles)[:, None, :]
    leading = gradients[..., :half_dims]
    trailing = gradients[..., half_dims : 2 * half_dims]
    return jnp.concatenate(
        [
            leading * cosines + trailing * sine_vals,
            trailing * cosines - leading * sine_vals,
            gradients[..., 2 * half_dims :],
        ],
        axis=-1,
    )


def masked_scores(queries, key_rows, places, length):
    scores = jnp.einsum("qhd,khd->hqk", queries, key_rows, preferred_element_type=jnp.float32)
    key_places = jnp.arange(key_rows.shape[0], dtype=jnp.int32)
    allowed = (key_places[None, :] <= places[:, None]) & (key_places[None, :] < length)
    return jnp.where(allowed[None], scores, -1e30)


def on_device(
    tokens,
    lengths,
    ln_gain,
    ln_bias,
    w_qkv,
    b_qkv,
    w_out,
    b_out,
    w_fc1,
    b_fc1,
    w_fc2,
    b_fc2,
    cotangent,
):
    seq_count, local_len, model_width = tokens.shape
    shard_rows = w_qkv.shape[0]
    hidden_ratio = w_fc1.shape[1] // model_width
    head_count = model_width // HEAD_DIM
    token_count = seq_count * local_len
    places = lax.axis_index("ctx") * local_len + jnp.arange(local_len, dtype=jnp.int32)
    angles = rotary_angles(places, ROT)
    live_mask = places[None, :] < lengths[:, None]
    inputs = tokens.astype(jnp.float32).reshape(token_count, model_width)
    average = jnp.mean(inputs, axis=-1, keepdims=True)
    centered = inputs - average
    variance = jnp.mean(centered * centered, axis=-1, keepdims=True)
    inv_std = lax.rsqrt(variance + eps_norm)
    normed = centered * inv_std
    qkv_bias_rows = b_qkv.reshape(shard_rows, 3)
    fc1_bias_rows = b_fc1.reshape(shard_rows, hidden_ratio)
    fc2_rows = w_fc2.reshape(shard_rows, hidden_ratio * model_width)
    inner_full = (
        lax.all_gather(w_qkv, ("dp", "ctx"), axis=0, tiled=True),
        lax.all_gather(w_fc1, ("dp", "ctx"), axis=0, tiled=True),
        lax.all_gather(ln_gain, ("dp", "ctx"), axis=0, tiled=True),
        lax.all_gather(ln_bias, ("dp", "ctx"), axis=0, tiled=True),
        lax.all_gather(qkv_bias_rows, ("dp", "ctx"), axis=0, tiled=True),
        lax.all_gather(fc1_bias_rows, ("dp", "ctx"), axis=0, tiled=True),
    )
    gain_full = inner_full[2].astype(jnp.float32)
    shift_full = inner_full[3].astype(jnp.float32)
    hidden = (normed * gain_full + shift_full).astype(jnp.bfloat16)
    qkv_acc = jnp.dot(hidden, inner_full[0], preferred_element_type=jnp.float32)
    up_acc = jnp.dot(hidden, inner_full[1], preferred_element_type=jnp.float32)
    qkv_bias = inner_full[4].reshape(-1).astype(jnp.float32)
    fc1_bias = inner_full[5].reshape(-1).astype(jnp.float32)
    qkv_proj = (qkv_acc + qkv_bias).reshape(seq_count, local_len, 3, head_count, HEAD_DIM)
    queries = (rotary(qkv_proj[:, :, 0], angles) * 0.125).astype(jnp.bfloat16)
    key_local = (
        rotary(qkv_proj[:, :, 1], angles)
        .astype(jnp.bfloat16)
        .reshape(seq_count, local_len, model_width)
    )
    value_local = qkv_proj[:, :, 2].astype(jnp.bfloat16).reshape(seq_count, local_len, model_width)
    key_full, value_full = (
        lax.all_gather(key_local, "ctx", axis=1, tiled=True),
        lax.all_gather(value_local, "ctx", axis=1, tiled=True),
    )
    total_len = key_full.shape[1]

    def attend_forward(packed):
        query_seq, key_seq, value_seq, length = packed
        key_heads = key_seq.reshape(total_len, head_count, HEAD_DIM)
        value_heads = value_seq.reshape(total_len, head_count, HEAD_DIM)
        scores = masked_scores(query_seq, key_heads, places, length)
        row_max = jnp.max(scores, axis=-1, keepdims=True)
        exponent = jnp.exp(scores - row_max)
        row_sum = jnp.sum(exponent, axis=-1, keepdims=True)
        probability = (exponent / row_sum).astype(jnp.bfloat16)
        attended = jnp.einsum(
            "hqk,khd->qhd", probability, value_heads, preferred_element_type=jnp.float32
        )
        log_total = (row_max + jnp.log(row_sum))[..., 0]
        return (attended.reshape(local_len, model_width).astype(jnp.bfloat16), log_total)

    attn_seq, log_totals = lax.map(attend_forward, (queries, key_full, value_full, lengths))
    attn_mixed = attn_seq.reshape(token_count, model_width)
    up_proj = up_acc + fc1_bias
    activated = gelu_tanh(up_proj).astype(jnp.bfloat16)
    outer_full = (
        lax.all_gather(w_out, ("dp", "ctx"), axis=0, tiled=True),
        lax.all_gather(fc2_rows, ("dp", "ctx"), axis=0, tiled=True),
        lax.all_gather(b_out, ("dp", "ctx"), axis=0, tiled=True),
        lax.all_gather(b_fc2, ("dp", "ctx"), axis=0, tiled=True),
    )
    branch = jnp.dot(attn_mixed, outer_full[0], preferred_element_type=jnp.float32) + jnp.dot(
        activated,
        outer_full[1].reshape(hidden_ratio * model_width, model_width),
        preferred_element_type=jnp.float32,
    )
    out_bias = outer_full[2].astype(jnp.float32)
    fc2_bias = outer_full[3].astype(jnp.float32)
    output = (
        (inputs + branch + out_bias + fc2_bias)
        .astype(jnp.bfloat16)
        .reshape(seq_count, local_len, model_width)
    )
    grad_out = jnp.where(live_mask[:, :, None], cotangent, jnp.zeros((), jnp.bfloat16)).reshape(
        token_count, model_width
    )
    out_back, fc2_back = (
        lax.all_gather(w_out, ("dp", "ctx"), axis=0, tiled=True),
        lax.all_gather(fc2_rows, ("dp", "ctx"), axis=0, tiled=True),
    )
    fc2_matrix = fc2_back.reshape(hidden_ratio * model_width, model_width)
    grad_mixed = jnp.einsum(
        "td,kd->tk", grad_out, out_back, preferred_element_type=jnp.float32
    ).astype(jnp.bfloat16)
    grad_act = jnp.einsum("td,kd->tk", grad_out, fc2_matrix, preferred_element_type=jnp.float32)
    gelu_value, gelu_pull = jax.vjp(gelu_tanh, up_proj)
    grad_up = gelu_pull(grad_act)[0].astype(jnp.bfloat16)
    key_back, value_back = (
        lax.all_gather(key_local, "ctx", axis=1, tiled=True),
        lax.all_gather(value_local, "ctx", axis=1, tiled=True),
    )

    def attend_backward(packed):
        query_seq, key_seq, value_seq, grad_seq, log_total, length = packed
        key_heads = key_seq.reshape(total_len, head_count, HEAD_DIM)
        value_heads = value_seq.reshape(total_len, head_count, HEAD_DIM)
        grad_heads = grad_seq.reshape(local_len, head_count, HEAD_DIM)
        scores = masked_scores(query_seq, key_heads, places, length)
        probability = jnp.exp(scores - log_total[:, :, None])
        grad_probs = jnp.einsum(
            "qhd,khd->hqk", grad_heads, value_heads, preferred_element_type=jnp.float32
        )
        inner = jnp.sum(probability * grad_probs, axis=-1, keepdims=True)
        grad_scores = (probability * (grad_probs - inner)).astype(jnp.bfloat16)
        grad_query = jnp.einsum(
            "hqk,khd->qhd", grad_scores, key_heads, preferred_element_type=jnp.float32
        )
        grad_keys = jnp.einsum(
            "hqk,qhd->khd", grad_scores, query_seq, preferred_element_type=jnp.float32
        )
        grad_values = jnp.einsum(
            "hqk,qhd->khd",
            probability.astype(jnp.bfloat16),
            grad_heads,
            preferred_element_type=jnp.float32,
        )
        return (
            grad_query,
            grad_keys.reshape(total_len, model_width),
            grad_values.reshape(total_len, model_width),
        )

    grad_query, grad_keys_all, grad_values_all = lax.map(
        attend_backward,
        (
            queries,
            key_back,
            value_back,
            grad_mixed.reshape(seq_count, local_len, model_width),
            log_totals,
            lengths,
        ),
    )
    grad_keys_own, grad_values_own = (
        lax.psum_scatter(grad_keys_all, "ctx", scatter_dimension=1, tiled=True),
        lax.psum_scatter(grad_values_all, "ctx", scatter_dimension=1, tiled=True),
    )
    grad_query_pre = rotary_back(grad_query * 0.125, angles).reshape(token_count, model_width)
    grad_keys_pre = rotary_back(
        grad_keys_own.reshape(seq_count, local_len, head_count, HEAD_DIM), angles
    ).reshape(token_count, model_width)
    grad_qkv = jnp.concatenate(
        [grad_query_pre, grad_keys_pre, grad_values_own.reshape(token_count, model_width)], axis=-1
    ).astype(jnp.bfloat16)
    qkv_matrix, fc1_matrix = (
        lax.all_gather(w_qkv, ("dp", "ctx"), axis=0, tiled=True),
        lax.all_gather(w_fc1, ("dp", "ctx"), axis=0, tiled=True),
    )
    grad_hidden = jnp.einsum(
        "tj,dj->td", grad_qkv, qkv_matrix, preferred_element_type=jnp.float32
    ) + jnp.einsum("tj,dj->td", grad_up, fc1_matrix, preferred_element_type=jnp.float32)
    gain_term = jnp.sum(grad_hidden * normed, axis=0)
    shift_term = jnp.sum(grad_hidden, axis=0)
    grad_norm = grad_hidden * gain_full
    grad_input = grad_out.astype(jnp.float32) + inv_std * (
        grad_norm
        - jnp.mean(grad_norm, axis=-1, keepdims=True)
        - normed * jnp.mean(grad_norm * normed, axis=-1, keepdims=True)
    )
    grad_input = grad_input.astype(jnp.bfloat16).reshape(seq_count, local_len, model_width)
    wout_term = jnp.einsum("tk,td->kd", attn_mixed, grad_out, preferred_element_type=jnp.float32)
    wfc2_term = jnp.einsum(
        "tk,td->kd", activated, grad_out, preferred_element_type=jnp.float32
    ).reshape(model_width, hidden_ratio * model_width)
    bias_term = jnp.sum(grad_out, axis=0, dtype=jnp.float32)
    bqkv_term = jnp.sum(grad_qkv, axis=0, dtype=jnp.float32).reshape(model_width, 3)
    bfc1_term = jnp.sum(grad_up, axis=0, dtype=jnp.float32).reshape(model_width, hidden_ratio)
    grad_wout, grad_wfc2, grad_bias, grad_gain, grad_shift, grad_bqkv, grad_bfc1 = (
        lax.psum_scatter(wout_term, ("dp", "ctx"), scatter_dimension=0, tiled=True),
        lax.psum_scatter(wfc2_term, ("dp", "ctx"), scatter_dimension=0, tiled=True),
        lax.psum_scatter(bias_term, ("dp", "ctx"), scatter_dimension=0, tiled=True),
        lax.psum_scatter(gain_term, ("dp", "ctx"), scatter_dimension=0, tiled=True),
        lax.psum_scatter(shift_term, ("dp", "ctx"), scatter_dimension=0, tiled=True),
        lax.psum_scatter(bqkv_term, ("dp", "ctx"), scatter_dimension=0, tiled=True),
        lax.psum_scatter(bfc1_term, ("dp", "ctx"), scatter_dimension=0, tiled=True),
    )
    qkv_part = jnp.einsum("tk,tj->kj", hidden, grad_qkv, preferred_element_type=jnp.float32)
    fc1_part = jnp.einsum("tk,tj->kj", hidden, grad_up, preferred_element_type=jnp.float32)
    inner_sum = lax.psum_scatter(
        jnp.concatenate([qkv_part, fc1_part], axis=1),
        ("dp", "ctx"),
        scatter_dimension=0,
        tiled=True,
    )
    grad_wqkv = inner_sum[:, : 3 * model_width]
    grad_wfc1 = inner_sum[:, 3 * model_width :]
    return (
        output,
        grad_input,
        grad_gain,
        grad_shift,
        grad_wqkv,
        grad_bqkv.reshape(-1),
        grad_wout,
        grad_bias,
        grad_wfc1,
        grad_bfc1.reshape(-1),
        grad_wfc2.reshape(shard_rows * hidden_ratio, model_width),
        grad_bias,
    )


def general_solution(mesh):
    placed = (
        P("dp", "ctx", None),
        P("dp"),
        P(("dp", "ctx")),
        P(("dp", "ctx")),
        P(("dp", "ctx"), None),
        P(("dp", "ctx")),
        P(("dp", "ctx"), None),
        P(("dp", "ctx")),
        P(("dp", "ctx"), None),
        P(("dp", "ctx")),
        P(("dp", "ctx"), None),
        P(("dp", "ctx")),
        P("dp", "ctx", None),
    )
    return jax.shard_map(
        on_device,
        mesh=mesh,
        in_specs=placed,
        out_specs=(
            P("dp", "ctx", None),
            P("dp", "ctx", None),
            P(("dp", "ctx")),
            P(("dp", "ctx")),
            P(("dp", "ctx"), None),
            P(("dp", "ctx")),
            P(("dp", "ctx"), None),
            P(("dp", "ctx")),
            P(("dp", "ctx"), None),
            P(("dp", "ctx")),
            P(("dp", "ctx"), None),
            P(("dp", "ctx")),
        ),
        check_vma=False,
    )


FINE = ("zh", "zl", "y", "x", "c")
ROWS_AXES = ("zl", "x", "c")


def dot(left, right, dims):
    return lax.dot_general(left, right, (dims, ((), ())), preferred_element_type=jnp.float32)


QB = 256


def nt(a, b):
    return dot(a, b, ((1,), (1,)))


def nn(a, b):
    return dot(a, b, ((1,), (0,)))


def tn(a, b):
    return dot(a, b, ((0,), (0,)))


def attend_pair(pair, length, bias, cosines_ref, sines_ref, qkv, mixed, q_s, k_s, v_s, g_s, gk_s, gv_s):
    f32, bf16 = jnp.float32, jnp.bfloat16
    total, width = mixed.shape
    lane = lax.broadcasted_iota(jnp.int32, (1, 128), 1)
    first = lane % HEAD_DIM < ROT // 2
    heads = [lane < HEAD_DIM, lane >= HEAD_DIM]

    def other(v):
        return jnp.where(first, pltpu.roll(v, 128 - ROT // 2, 1), pltpu.roll(v, ROT // 2, 1))

    def col(part):
        return pl.ds(pl.multiple_of(part * width + pair * 128, 128), 128)

    for b in range(total // QB):
        rows = pl.ds(b * QB, QB)
        cosines, sines = cosines_ref[rows], sines_ref[rows]

        def turn(v):
            return v * cosines + other(v) * sines

        q = turn(qkv[rows, col(0)] + bias[:, col(0)]) * 0.125
        k = turn(qkv[rows, col(1)] + bias[:, col(1)])
        v = qkv[rows, col(2)] + bias[:, col(2)]
        g = mixed[rows, col(0)]
        for h in range(2):
            q_s[h, rows] = jnp.where(heads[h], q, 0.0).astype(bf16)
            k_s[h, rows] = jnp.where(heads[h], k, 0.0).astype(bf16)
            v_s[h, rows] = jnp.where(heads[h], v, 0.0).astype(bf16)
            g_s[h, rows] = jnp.where(heads[h], g, 0.0).astype(bf16)
    gk_s[...] = jnp.zeros_like(gk_s)
    gv_s[...] = jnp.zeros_like(gv_s)

    for b in range(total // QB):
        rows = pl.ds(b * QB, QB)
        upto = (b + 1) * QB
        keys = pl.ds(0, upto)
        limit = jnp.minimum(lax.broadcasted_iota(jnp.int32, (1, QB), 1) + (b * QB + 1), length)
        allowed = lax.broadcasted_iota(jnp.int32, (upto, QB), 0) < limit
        out = grad = jnp.zeros((QB, 128), f32)
        for h in range(2):
            qh, gh = q_s[h, rows], g_s[h, rows]
            scores = jnp.where(allowed, nt(k_s[h, keys], qh), -1e30)
            exponent = jnp.exp(scores - jnp.max(scores, axis=0, keepdims=True))
            share = exponent * (1.0 / jnp.sum(exponent, axis=0, keepdims=True))
            rounded = share.astype(bf16)
            back = nt(v_s[h, keys], gh)
            back = (share * (back - jnp.sum(share * back, axis=0, keepdims=True))).astype(bf16)
            gv_s[keys] += nn(rounded, gh)
            gk_s[keys] += nn(back, qh)
            out += tn(rounded, v_s[h, keys])
            grad += tn(back, k_s[h, keys])
        mixed[rows, col(0)] = out
        grad *= 0.125
        qkv[rows, col(0)] = grad * cosines_ref[rows] - other(grad) * sines_ref[rows]
    for b in range(total // QB):
        rows = pl.ds(b * QB, QB)
        grad = gk_s[rows]
        qkv[rows, col(1)] = grad * cosines_ref[rows] - other(grad) * sines_ref[rows]
        qkv[rows, col(2)] = gv_s[rows]


def tables(total, rot):
    half = rot // 2
    steps = np.arange(half, dtype=np.float32)
    inv_freq = np.exp(np.float32(-math.log(10000.0) * 2.0) * steps / np.float32(rot))
    angles = np.arange(total, dtype=np.float32)[:, None] * inv_freq[None, :].astype(np.float32)
    cosines, sines = np.cos(angles), np.sin(angles)
    rest = (total, HEAD_DIM - rot)
    cosines = np.concatenate([cosines, cosines, np.ones(rest, np.float32)] * 2, axis=1)
    sines = np.concatenate([-sines, sines, np.zeros(rest, np.float32)] * 2, axis=1)
    return jnp.asarray(cosines, jnp.float32), jnp.asarray(sines, jnp.float32)


MESH_ID = pl.DeviceIdType.MESH


W_PEERS = [(k // 4, k // 2 % 2, k % 2) for k in range(1, 8)]


def sum_small(values, collective_id):
    n = values.shape[1]
    return pl.pallas_call(
        sum_kernel,
        out_shape=jax.ShapeDtypeStruct((n, 128), jnp.float32),
        in_specs=[pl.BlockSpec(memory_space=pltpu.VMEM)],
        out_specs=pl.BlockSpec(memory_space=pltpu.VMEM),
        scratch_shapes=[
            pltpu.VMEM((32, n, 128), jnp.float32),
            pltpu.SemaphoreType.DMA((32,)),
            pltpu.SemaphoreType.DMA((32,)),
        ],
        compiler_params=pltpu.CompilerParams(collective_id=collective_id, has_side_effects=True),
    )(values)


def main_kernel(
    small, tokens, cot_own, cosines, sines, fc2_own, out_own, fc1_spread, qkv_spread,
    grad_in, output, sums_out, fc2_out, out_out, fc1_a, qkv_a, up_sum, qkv_sum, small_all, qkv_all, out_all, fc1_all, fc2_all,
    fc2_part, fc1_part, out_part, qkv_part, c_got, w_got, wide_y, wide_z, cols_y, cols_z,
    hidden, cot, act, gup, attn, gqkv, qkv_w, out_w, stage, full, wide, cols, wide_s, cols_s, fc1_bias, qkv_bias, terms, terms_got,
    send_sem, recv_sem, local_sem, block_sem, c_send, c_recv, small_send, small_recv, terms_send, terms_recv,
):
    f32, bf16 = jnp.float32, jnp.bfloat16
    zh, zl, y, x, c = place = [lax.axis_index(name) for name in FINE]
    seat = (zl * 2 + x) * 2 + c
    used, used_local = [0], [0]
    sends = []

    class Copy:
        def __init__(self, describe):
            self.describe = describe

        def start(self):
            self.describe().start()

        def wait(self):
            self.describe().wait()

        def wait_send(self):
            self.describe().wait_send()

        def wait_recv(self):
            self.describe().wait_recv()

    def remote(ends, target):
        n = used[0]
        used[0] += 1

        def describe():
            src, dst = ends()
            return pltpu.make_async_remote_copy(
                src_ref=src,
                dst_ref=dst,
                send_sem=send_sem.at[n],
                recv_sem=recv_sem.at[n],
                device_id=target(),
                device_id_type=MESH_ID,
            )

        copy = Copy(describe)
        copy.start()
        sends.append(copy)
        return copy

    def partner(axis):
        return tuple(1 - p if name == axis else p for name, p in zip(FINE, place))

    def beside():
        return partner("y")

    def across():
        return partner("zh")

    def local(ends):
        n = used_local[0]
        used_local[0] += 1

        def describe():
            src, dst = ends()
            return pltpu.make_async_copy(src, dst, local_sem.at[n])

        copy = Copy(describe)
        copy.start()
        return copy

    def load(*pairs):
        copies = [local(lambda pair=pair: pair) for pair in pairs]
        for copy in copies:
            copy.wait()

    def index_of(where):
        number = 0
        for p in where:
            number = number * 2 + p
        return number

    def away(k):
        return tuple((p + k // 2 ** (4 - i)) % 2 for i, p in enumerate(place))

    barrier = pltpu.get_barrier_semaphore()

    def greet(k, carry):
        pl.semaphore_signal(barrier, inc=1, device_id=away(k), device_id_type=MESH_ID)
        return carry

    lax.fori_loop(1, 32, greet, 0)
    pl.semaphore_wait(barrier, 31)

    blocks, block_rows, width = hidden.shape
    token_count, units = gup.shape
    total_len = token_count // 2
    mine, sent = hidden, cot

    def small_copy(k):
        return pltpu.make_async_remote_copy(
            src_ref=small,
            dst_ref=small_all.at[index_of(place)],
            send_sem=small_send.at[k],
            recv_sem=small_recv.at[k],
            device_id=away(k),
            device_id_type=MESH_ID,
        )

    def small_start(k, carry):
        small_copy(k).start()
        return carry

    def small_wait(k, carry):
        small_copy(k).wait()
        return carry

    lax.fori_loop(1, 32, small_start, 0)
    small_all[index_of(place)] = small[...]
    tokens_in = local(lambda: (tokens, stage))

    def spread(weight, matrix):
        pieces = []
        for dl, dx, dc in W_PEERS:

            def where(dl=dl, dx=dx, dc=dc):
                return zh, (zl + dl) % 2, y, (x + dx) % 2, (c + dc) % 2

            def ends(where=where):
                _, to_zl, _, to_x, to_c = where()
                return weight.at[(to_zl * 2 + to_x) * 2 + to_c], matrix.at[zh, zl, y, x * 2 + c]

            pieces.append(remote(ends, where))
        return pieces, local(lambda: (weight.at[seat], matrix.at[zh, zl, y, x * 2 + c]))

    def parts_of(ends_list):
        return [remote(ends, across) for ends in ends_list], [remote(ends, beside) for ends in ends_list]

    def forward(copy, block):
        copy.wait_recv()
        return remote(lambda: (block(), block()), beside)

    def half_of(matrix, half):
        return lambda: matrix.at[1 - zh, half, y]

    def own_half(matrix, half):
        return lambda: (matrix.at[zh, half, y], matrix.at[zh, half, y])

    fc1_pieces = spread(fc1_spread, fc1_all)
    half_rows = fc2_own.shape[0] // 2

    def fc2_rows_of(a, half):
        return lambda: fc2_all.at[a, y, pl.ds(half * half_rows, half_rows)]

    def fc2_ends(half):
        return lambda: (fc2_own.at[pl.ds(half * half_rows, half_rows)], fc2_rows_of(zh, half)())

    def over(own, gathered, axis):
        return remote(lambda: (own(), gathered()), lambda: partner(axis))

    def own_cot():
        return cot_own

    def seat_of(array, dl=0, dx=0):
        return lambda: array.at[((zl + dl) % 2 * 2 + (x + dx) % 2) * 2 + c]

    cot_zl = over(own_cot, seat_of(cot), "zl")
    fc2_zh, fc2_y = parts_of([fc2_ends(half) for half in range(2)])
    cot_x = over(own_cot, seat_of(cot), "x")
    core = {("cot", 0, 0): over(own_cot, seat_of(cot), "c")}
    own_copies = [
        local(lambda: (cot_own, cot.at[seat])),
        local(lambda: (fc2_own, fc2_all.at[zh, y])),
        local(lambda: (out_own, out_all.at[zh, y])),
    ]

    lax.fori_loop(1, 32, small_wait, 0)
    tokens_in.wait()
    in_place = lax.broadcasted_iota(jnp.int32, (32, width), 1) // (width // 32) == (
        lax.broadcasted_iota(jnp.int32, (32, width), 0)
    )

    def vector(row):
        spread_out = jnp.concatenate([small_all[:, row, :]] * (width // 128), axis=1)
        return jnp.sum(jnp.where(in_place, spread_out, 0.0), axis=0, keepdims=True)

    gain, shift = vector(0), vector(1)

    def norm_rows(i, carry):
        rows = pl.ds(pl.multiple_of(i * 32, 32), 32)
        values = stage[rows].astype(f32)
        centered = values - jnp.mean(values, axis=-1, keepdims=True)
        variance = jnp.mean(centered * centered, axis=-1, keepdims=True)
        hidden[seat, rows] = (centered * lax.rsqrt(variance + eps_norm) * gain + shift).astype(bf16)
        return carry

    lax.fori_loop(0, block_rows // 32, norm_rows, 0)
    hid_zl = over(seat_of(hidden), seat_of(hidden), "zl")
    hid_x = over(seat_of(hidden), seat_of(hidden), "x")
    core["hidden", 0, 0] = over(seat_of(hidden), seat_of(hidden), "c")

    for t in range(4):
        owner = index_of((t // 2, zl, t % 2, x, c))
        for half in range(2):
            at = t * 2 * 128 + half * 128
            fc1_bias[:, at : at + 128] = small_all[owner, pl.ds(4 + half, 1), :]
    low = lax.broadcasted_iota(jnp.int32, (1, 128), 1) < HEAD_DIM
    for part in range(3):
        for a in range(2):
            chunks = []
            for b in range(2):
                chunk = part * 32 + index_of((a, zl, b, x, c))
                row = small_all[chunk // 3, pl.ds(2 + chunk % 3 // 2, 1), :]
                chunks.append(jnp.where(chunk % 3 % 2 == b, row, pltpu.roll(row, HEAD_DIM, 1)))
            at = (part * 2 + a) * 128
            qkv_bias[:, at : at + 128] = jnp.where(low, chunks[0], chunks[1])

    def length_of(seq):
        row = small_all[index_of((zh, seq, y, 0, 0)), pl.ds(7, 1), :]
        return jnp.concatenate([row] * (QB // 128), axis=1).astype(jnp.int32)

    def all_there(pieces):
        for piece in pieces[0]:
            piece.wait_recv()
        pieces[1].wait()

    def to_core(name, copy, dl, dx):
        array = {"cot": cot, "hidden": hidden}[name]
        copy.wait_recv()
        core[name, dl, dx] = over(seat_of(array, dl, dx), seat_of(array, dl, dx), "c")

    all_there(fc1_pieces)
    fc1_zh, fc1_y = parts_of([own_half(fc1_all, half) for half in range(2)])
    to_core("cot", cot_zl, 1, 0)
    cot_zx = over(seat_of(cot, 1), seat_of(cot, 1), "x")
    fc2_fwd = [forward(fc2_zh[0], fc2_rows_of(1 - zh, 0))]
    to_core("cot", cot_x, 0, 1)
    fc2_fwd.append(forward(fc2_zh[1], fc2_rows_of(1 - zh, 1)))
    qkv_pieces = spread(qkv_spread, qkv_all)
    to_core("hidden", hid_zl, 1, 0)
    hid_zx = over(seat_of(hidden, 1), seat_of(hidden, 1), "x")
    to_core("hidden", hid_x, 0, 1)
    fc1_fwd = [forward(fc1_zh[0], half_of(fc1_all, 0))]
    to_core("cot", cot_zx, 1, 1)
    fc1_fwd.append(forward(fc1_zh[1], half_of(fc1_all, 1)))
    all_there(qkv_pieces)
    out_zh, out_y = parts_of([lambda: (out_own, out_all.at[zh, y])])
    qkv_zh, qkv_y = parts_of([own_half(qkv_all, half) for half in range(2)])
    for copy in own_copies:
        copy.wait()
    for copy in fc2_y + fc2_fwd + fc1_y + fc1_fwd:
        copy.wait_recv()

    def tokens_here(dl, dx):
        for name in ("cot", "hidden"):
            core[name, dl, dx].wait_recv()

    late_in = out_y + qkv_y

    def row_job(part, rows, first, slot, put):
        some = pl.ds(0, rows)
        return dict(
            part=lambda a, b: part.at[a, b, pl.ds(first, rows)],
            y=[wide_y.at[slot, j, some] for j in range(2)],
            z=wide_z.at[slot, some],
            v=[wide.at[j, some] for j in range(3)],
            s=wide_s.at[slot, some],
            put=put,
            rows=some,
        )

    def column_job(part, width, away, slot, to):
        lanes = pl.ds(0, width)
        return dict(
            part=lambda a, b: part.at[a, (zl + away) % 2, b],
            y=[cols_y.at[slot, j, :, lanes] for j in range(2)],
            z=cols_z.at[slot, :, lanes],
            v=[cols.at[j, :, lanes] for j in range(3)],
            s=cols_s.at[slot, :, lanes],
            away=away,
            to=to,
        )

    fc1_width, qkv_width = units, gqkv.shape[1]
    out_rows, fc2_rows = out_part.shape[2], fc2_part.shape[2] // 2
    jobs = [
        row_job(fc2_part, fc2_rows, i * fc2_rows, i, fc2_out.at[pl.ds(i * fc2_rows, fc2_rows)])
        for i in range(2)
    ]
    jobs += [column_job(fc1_part, fc1_width, away, away, fc1_a) for away in (1, 0)]
    jobs += [row_job(out_part, out_rows, 0, 2, out_out)]
    jobs += [column_job(qkv_part, qkv_width, away, 2 + away, qkv_a) for away in (1, 0)]

    def send_beside(job):
        job["y_far"] = remote(lambda: (job["part"](1 - zh, 1 - y), job["y"][1]), beside)
        job["y_own"] = remote(lambda: (job["part"](zh, 1 - y), job["y"][0]), beside)

    def pass_on(job):
        job["y_far"].wait_recv()
        v = job["v"]
        load((job["part"](1 - zh, y), v[0]), (job["y"][1], v[1]))
        job["s"][...] = (v[0][...].astype(f32) + v[1][...].astype(f32)).astype(bf16)
        job["z_copy"] = remote(lambda: (job["s"], job["z"]), across)

    arrivals, kept = [], []

    def finish(job):
        job["y_own"].wait_recv()
        job["z_copy"].wait_recv()
        v = job["v"]
        load((job["part"](zh, y), v[0]), (job["y"][0], v[1]), (job["z"], v[2]))
        total = v[0][...].astype(f32) + v[1][...].astype(f32) + v[2][...].astype(f32)
        if "put" in job:
            full[job["rows"]] = total
            load((full.at[job["rows"]], job["put"]))
            return
        job["z_copy"].wait_send()
        sends[:] = [copy for copy in sends if copy is not job["z_copy"]]
        job["s"][...] = total.astype(bf16)
        piece = job["s"].shape[0] // 4
        for dx in range(2):
            for dc in range(2):

                def where(dx=dx, dc=dc):
                    return zh, (zl + job["away"]) % 2, y, (x + dx) % 2, (c + dc) % 2

                def ends(where=where):
                    _, _, _, to_x, to_c = where()
                    row = pl.multiple_of((to_x * 2 + to_c) * piece, piece)
                    return job["s"].at[pl.ds(row, piece)], job["to"].at[(zl * 2 + x) * 2 + c]

                if job["away"] or dx or dc:
                    arrivals.append(remote(ends, where))
                else:
                    kept.append(local(ends))

    def core_copy(n, g):
        return pltpu.make_async_remote_copy(
            src_ref=sent.at[4 * n + g],
            dst_ref=c_got.at[n, g],
            send_sem=c_send.at[n, g],
            recv_sem=c_recv.at[n, g],
            device_id=partner("c"),
            device_id_type=MESH_ID,
        )

    axes = (("x", "zl"), ("x", "zl"))

    def multiply_groups(n, first, a, v, b, w, multiply):
        def step(g, carry):
            one, two = 1 - g // 2, 1 - g % 2
            dl, dx = two, one
            rest = ((zl + dl) % 2 * 2 + (x + dx) % 2) * 2

            def block(where):
                rows = pl.ds(pl.multiple_of((rest + where) * 256, 256), 256)
                near, far = v[...].reshape(-1, v.shape[-1]), w[...].reshape(-1, w.shape[-1])
                return (multiply(a[rows], near) + multiply(b[rows], far)).astype(bf16)

            sent[4 * n + g] = block(1 - c)
            core_copy(n, g).start()
            mine[4 * n + g] = block(c)
            return carry

        lax.fori_loop(first, first + 2, step, 0)

    def add(n, g, got):
        load((got, stage))
        mine[4 * n + g] = (mine[4 * n + g].astype(f32) + stage[...].astype(f32)).astype(bf16)

    def add_core(n, g):
        core_copy(n, g).wait_recv()
        add(n, g, c_got.at[n, g])

    first_copies, second_copies = {}, {}

    def send_first(n):
        for g in range(2):
            add_core(n, g)
            first_copies[n, g] = remote(
                lambda g=g: (mine.at[4 * n + g], w_got.at[n, g]), lambda: partner(axes[n][0])
            )

    def send_second(n):
        first_copies[n, 0].wait_recv()
        add(n, 2, w_got.at[n, 0])
        second_copies[n] = remote(
            lambda: (mine.at[4 * n + 2], w_got.at[n, 2]), lambda: partner(axes[n][1])
        )

    def add_first(n):
        first_copies[n, 1].wait_recv()
        add(n, 3, w_got.at[n, 1])

    def total(n):
        second_copies[n].wait_recv()
        load((w_got.at[n, 2], stage))
        full[...] = mine[4 * n + 3].astype(f32) + stage[...].astype(f32)

    def chunk(i):
        return pl.ds(pl.multiple_of(i * 32, 32), 32)

    def normalized(values):
        centered = values - jnp.mean(values, axis=-1, keepdims=True)
        inv_std = lax.rsqrt(jnp.mean(centered * centered, axis=-1, keepdims=True) + eps_norm)
        return centered * inv_std, inv_std

    def terms_copy(k):
        return pltpu.make_async_remote_copy(
            src_ref=terms.at[index_of(away(k))],
            dst_ref=terms_got.at[index_of(place)],
            send_sem=terms_send.at[k],
            recv_sem=terms_recv.at[k],
            device_id=away(k),
            device_id_type=MESH_ID,
        )

    def finish_input():
        total(0)
        for g in range(4):
            core_copy(0, g).wait_send()
        load((tokens, sent.at[0]), (cot_own, sent.at[1]))
        gain_row = vector(0)

        def back_rows(i, carry):
            gain_sum, shift_sum, bias_sum = carry
            rows = chunk(i)
            normed, inv_std = normalized(sent[0, rows].astype(f32))
            cotangent = sent[1, rows].astype(f32)
            grads = full[rows]
            scaled = grads * gain_row
            sent[2, rows] = (
                cotangent
                + inv_std
                * (
                    scaled
                    - jnp.mean(scaled, axis=-1, keepdims=True)
                    - normed * jnp.mean(scaled * normed, axis=-1, keepdims=True)
                )
            ).astype(bf16)
            return (
                gain_sum + jnp.sum(grads * normed, axis=0, keepdims=True),
                shift_sum + jnp.sum(grads, axis=0, keepdims=True),
                bias_sum + jnp.sum(cotangent, axis=0, keepdims=True),
            )

        nothing = jnp.zeros((1, width), f32)
        gain_sum, shift_sum, bias_sum = lax.fori_loop(
            0, block_rows // 32, back_rows, (nothing, nothing, nothing)
        )
        load((sent.at[2], grad_in))
        terms[...] = jnp.zeros_like(terms)
        for t in range(4):
            owner = index_of((t // 2, zl, t % 2, x, c))
            for half in range(2):
                at = t * 2 * 128 + half * 128
                terms[owner, pl.ds(2 + half, 1), :] = up_sum[:, at : at + 128]
        side = lax.broadcasted_iota(jnp.int32, (1, 128), 1) // HEAD_DIM
        for part in range(3):
            for a in range(2):
                at = (part * 2 + a) * 128
                both = qkv_sum[0, :, at : at + 128] + qkv_sum[1, :, at : at + 128]
                turned = pltpu.roll(both, HEAD_DIM, 1)
                for b in range(2):
                    piece = part * 32 + index_of((a, zl, b, x, c))
                    owner, row, half = piece // 3, pl.ds(piece % 3 // 2, 1), piece % 3 % 2
                    value = jnp.where(half == b, both, turned)
                    terms[owner, row, :] = jnp.where(side == half, value, terms[owner, row, :])
        for i in range(width // 128):
            for row, vector_sum in ((4, bias_sum), (5, gain_sum), (6, shift_sum)):
                for b in range(2):
                    terms[2 * i + b, row : row + 1, :] = vector_sum[:, i * 128 : (i + 1) * 128]
        terms_got[index_of(place)] = terms[index_of(place)]

        def start(k, carry):
            terms_copy(k).start()
            return carry

        lax.fori_loop(1, 32, start, 0)

    def finish_output():
        total(1)
        bias_row = vector(6)

        def out_rows_of(i, carry):
            rows = chunk(i)
            sent[3, rows] = (sent[0, rows].astype(f32) + full[rows] + bias_row).astype(bf16)
            return carry

        lax.fori_loop(0, block_rows // 32, out_rows_of, 0)
        load((sent.at[3], output))

    def part_tiles(left, right, at, put, tile):
        def step(i, carry):
            lanes = pl.ds(pl.multiple_of(at(i) * 256, 256), 256)
            product = tn(left(lanes), right())
            slot = i % 2

            @pl.when(i >= 2)
            def _():
                pltpu.make_async_copy(tile.at[slot], put(i - 2), block_sem.at[slot]).wait()

            tile[slot] = product.astype(bf16)
            pltpu.make_async_copy(tile.at[slot], put(i), block_sem.at[slot]).start()
            return carry

        def between(first, last):
            lax.fori_loop(first, last, step, 0)

        def drain(last):
            for i in (last - 2, last - 1):
                pltpu.make_async_copy(tile.at[i % 2], put(i), block_sem.at[i % 2]).wait()

        return between, drain

    def far_first(i):
        far, beside = 1 - i % 2, 1 - i // 2
        return (zh + far) % 2, (y + beside) % 2

    def fc_weights(fc1_w, fc2_w):
        return [local(lambda: (fc1_all, fc1_w)), local(lambda: (fc2_all, fc2_w))]

    def feed(fc1_w, fc2_w, tile_wide, tile_cols):
        for copy in fc_weights(fc1_w, fc2_w):
            copy.wait()
        up_sum[...] = jnp.zeros_like(up_sum)

        def step(i, carry):
            b = ((zl + i // 2) % 2 * 2 + (x + i // 4) % 2) * 2 + (c + i) % 2
            rows = pl.ds(pl.multiple_of(b * 256, 256), 256)
            up = nn(hidden[b], fc1_w[...].reshape(width, units)) + fc1_bias[...]
            bent = jnp.tanh(gelu_coef * (up + 0.044715 * up * up * up))
            act[rows] = (0.5 * up * (1.0 + bent)).astype(bf16)
            slope = 0.5 * (1.0 + bent) + 0.5 * up * (1.0 - bent * bent) * gelu_coef * (
                1.0 + 3.0 * 0.044715 * up * up
            )
            back = (nt(cot[b], fc2_w[...].reshape(units, width)) * slope).astype(bf16)
            gup[rows] = back
            up_sum[...] += jnp.sum(back.astype(f32), axis=0, keepdims=True)
            return carry

        tokens_here(0, 0)
        tokens_here(1, 0)
        lax.fori_loop(0, 4, step, 0)
        to_core("hidden", hid_zx, 1, 1)
        tokens_here(0, 1)
        lax.fori_loop(4, 6, step, 0)
        late_in.append(forward(out_zh[0], lambda: out_all.at[1 - zh, y]))
        late_in.append(forward(qkv_zh[0], half_of(qkv_all, 0)))
        tokens_here(1, 1)
        lax.fori_loop(6, 8, step, 0)

        def unit_place(i):
            a, b = far_first(i)
            return a * 2 + b

        def unit_put(i):
            a, b = far_first(i)
            return fc2_part.at[a, b]

        between, drain = part_tiles(
            lambda lanes: act[:, lanes], lambda: cot[...].reshape(token_count, width), unit_place, unit_put, tile_wide
        )
        between(0, 2)
        drain(2)
        late_in.append(forward(qkv_zh[1], half_of(qkv_all, 1)))
        for job in jobs[:2]:
            send_beside(job)
        between, drain = part_tiles(
            lambda lanes: act[:, lanes],
            lambda: cot[...].reshape(token_count, width),
            lambda i: unit_place(i + 2),
            lambda i: unit_put(i + 2),
            tile_wide,
        )
        between(0, 2)
        drain(2)
        feature_tiles(gup, fc1_part, tile_cols, jobs[2:4])

    def feature_tiles(right, part, tile, of):
        for late in range(2):

            def where(i, late=late):
                a, b = far_first(i // 2 + 2 * late)
                return a, i % 2, b

            def feature_place(i, where=where):
                a, half, b = where(i)
                return a * 4 + half * 2 + b

            between, drain = part_tiles(
                lambda lanes: hidden[:, :, lanes].reshape(token_count, 256),
                lambda: right[...],
                feature_place,
                lambda i, where=where: part.at[where(i)],
                tile,
            )
            between(0, 4)
            drain(4)
            if late == 0:
                for job in of:
                    send_beside(job)

    fc_scratch = (pltpu.VMEM(fc1_all.shape, bf16), pltpu.VMEM(fc2_all.shape, bf16))
    pl.run_scoped(
        feed,
        *fc_scratch,
        pltpu.VMEM((2, 256, width), bf16),
        pltpu.VMEM((2, 256, units), bf16),
    )

    for copy in late_in:
        copy.wait_recv()
    load((qkv_all, qkv_w), (out_all, out_w))

    def attend(projected, mixed, q_s, k_s, v_s, g_s, gk_s, gv_s):
        for seq in range(2):

            def project(b, carry, seq=seq):
                rows = pl.ds(pl.multiple_of(b * 256, 256), 256)
                block = b + seq * (blocks // 2)
                projected[rows] = nn(hidden[block], qkv_w[...].reshape(width, qkv_width))
                mixed[rows] = nt(cot[block], out_w[...].reshape(-1, width))
                return carry

            lax.fori_loop(0, blocks // 2, project, 0)

            def pair_step(pair, carry, seq=seq):
                attend_pair(
                    pair, length_of(seq), qkv_bias, cosines, sines, projected, mixed, q_s, k_s, v_s, g_s, gk_s, gv_s
                )
                return carry

            lax.fori_loop(0, mixed.shape[1] // 128, pair_step, 0)
            qkv_sum[seq] = jnp.zeros((1, qkv_width), f32)

            def store(b, carry, seq=seq):
                rows = pl.ds(pl.multiple_of(b * 256, 256), 256)
                to = pl.ds(pl.multiple_of(b * 256 + seq * total_len, 256), 256)
                grads = projected[rows].astype(bf16)
                gqkv[to] = grads
                attn[to] = mixed[rows].astype(bf16)
                qkv_sum[seq] += jnp.sum(grads.astype(f32), axis=0, keepdims=True)
                return carry

            lax.fori_loop(0, blocks // 2, store, 0)
            pass_on(jobs[seq])

    heads = pltpu.VMEM((2, total_len, 128), bf16)
    pl.run_scoped(
        attend,
        pltpu.VMEM((total_len, qkv_width), f32),
        pltpu.VMEM((total_len, attn.shape[1]), f32),
        heads,
        heads,
        heads,
        heads,
        pltpu.VMEM((total_len, 128), f32),
        pltpu.VMEM((total_len, 128), f32),
    )

    def attend_parts(tile_cols, tile_out):
        feature_tiles(gqkv, qkv_part, tile_cols, jobs[5:7])
        tile_out[...] = tn(attn[...], cot[...].reshape(token_count, width)).astype(bf16)
        rows = tile_out.shape[0] // 4
        load(*((tile_out.at[pl.ds(rows * i, rows)], out_part.at[i // 2, i % 2]) for i in range(4)))
        send_beside(jobs[4])

    pl.run_scoped(
        attend_parts, pltpu.VMEM((2, 256, qkv_width), bf16), pltpu.VMEM((attn.shape[1], width), bf16)
    )

    early_sends = list(core.values()) + [cot_zl, cot_x, cot_zx, hid_zl, hid_x, hid_zx]

    def sums(fc1_w, fc2_w):
        weights = fc_weights(fc1_w, fc2_w)
        for copy in early_sends:
            copy.wait_send()
        weights[0].wait()
        multiply_groups(0, 0, gqkv, qkv_w, gup, fc1_w, nt)
        send_first(0)
        weights[1].wait()
        multiply_groups(1, 0, attn, out_w, act, fc2_w, nn)
        send_first(1)
        pass_on(jobs[2])
        finish(jobs[0])
        multiply_groups(0, 2, gqkv, qkv_w, gup, fc1_w, nt)
        multiply_groups(1, 2, attn, out_w, act, fc2_w, nn)

    pl.run_scoped(sums, *fc_scratch)
    for n in range(2):
        add_core(n, 2)
        add_core(n, 3)
    send_second(0)
    pass_on(jobs[3])
    finish(jobs[1])
    add_first(0)
    send_second(1)
    finish(jobs[2])
    pass_on(jobs[5])
    pass_on(jobs[6])
    pass_on(jobs[4])
    finish(jobs[3])
    finish_input()
    add_first(1)
    finish(jobs[5])
    finish(jobs[6])
    finish(jobs[4])
    finish_output()

    def terms_wait(k, carry):
        terms_copy(k).wait()
        return carry

    lax.fori_loop(1, 32, terms_wait, 0)
    sums_out[...] = jnp.sum(terms_got[...], axis=0)
    for copy in arrivals:
        copy.wait_recv()
    for copy in kept:
        copy.wait()
    for copy in sends:
        if not any(copy is early for early in early_sends):
            copy.wait_send()
    for g in range(4):
        core_copy(1, g).wait_send()


def main(small, tokens, cot, cosines, sines, fc2_own, out_own, fc1_spread, qkv_spread):
    bf16, f32 = jnp.bfloat16, jnp.float32
    block, width = tokens.shape
    tokens_all = 8 * block
    rows, ff_rows = out_own.shape[0], fc2_own.shape[0]
    fc1_width, qkv_width = fc1_spread.shape[2], qkv_spread.shape[2]
    half = ff_rows // 2
    any_, vmem = pl.BlockSpec(memory_space=pl.ANY), pl.BlockSpec(memory_space=pltpu.VMEM)
    shapes = [
        ((block, width), bf16, any_),
        ((block, width), bf16, any_),
        (small.shape, f32, vmem),
        ((ff_rows, width), f32, any_),
        ((rows, width), f32, any_),
        ((8, rows, fc1_width), bf16, any_),
        ((8, rows, qkv_width), bf16, any_),
        ((1, fc1_width), f32, vmem),
        ((2, 1, qkv_width), f32, vmem),
        ((32,) + small.shape, f32, vmem),
        ((2, 2, 2, 4, rows, qkv_width), bf16, any_),
        ((2, 2, rows, width), bf16, any_),
        ((2, 2, 2, 4, rows, fc1_width), bf16, any_),
        ((2, 2, ff_rows, width), bf16, any_),
        ((2, 2, ff_rows, width), bf16, any_),
        ((2, 2, 2, 4 * rows, fc1_width), bf16, any_),
        ((2, 2, rows, width), bf16, any_),
        ((2, 2, 2, 4 * rows, qkv_width), bf16, any_),
        ((2, 4, block, width), bf16, any_),
        ((2, 3, block, width), bf16, any_),
        ((3, 2, half, width), bf16, any_),
        ((3, half, width), bf16, any_),
        ((4, 2, 4 * rows, fc1_width), bf16, any_),
        ((4, 4 * rows, fc1_width), bf16, any_),
    ]
    scratch = [
        pltpu.VMEM((8, block, width), bf16),
        pltpu.VMEM((8, block, width), bf16),
        pltpu.VMEM((tokens_all, fc1_width), bf16),
        pltpu.VMEM((tokens_all, fc1_width), bf16),
        pltpu.VMEM((tokens_all, 4 * rows), bf16),
        pltpu.VMEM((tokens_all, qkv_width), bf16),
        pltpu.VMEM((2, 2, 2, 4, rows, qkv_width), bf16),
        pltpu.VMEM((2, 2, rows, width), bf16),
        pltpu.VMEM((block, width), bf16),
        pltpu.VMEM((block, width), f32),
        pltpu.VMEM((3, half, width), bf16),
        pltpu.VMEM((3, 4 * rows, fc1_width), bf16),
        pltpu.VMEM((3, half, width), bf16),
        pltpu.VMEM((4, 4 * rows, fc1_width), bf16),
        pltpu.VMEM((1, fc1_width), f32),
        pltpu.VMEM((1, qkv_width), f32),
        pltpu.VMEM((32,) + small.shape, f32),
        pltpu.VMEM((32,) + small.shape, f32),
        pltpu.SemaphoreType.DMA((96,)),
        pltpu.SemaphoreType.DMA((96,)),
        pltpu.SemaphoreType.DMA((96,)),
        pltpu.SemaphoreType.DMA((2,)),
        pltpu.SemaphoreType.DMA((2, 4)),
        pltpu.SemaphoreType.DMA((2, 4)),
        pltpu.SemaphoreType.DMA((32,)),
        pltpu.SemaphoreType.DMA((32,)),
        pltpu.SemaphoreType.DMA((32,)),
        pltpu.SemaphoreType.DMA((32,)),
    ]
    return pl.pallas_call(
        main_kernel,
        out_shape=[jax.ShapeDtypeStruct(shape, kind) for shape, kind, _ in shapes],
        in_specs=[vmem, any_, any_, vmem, vmem] + [any_] * 4,
        out_specs=[spec for _, _, spec in shapes],
        scratch_shapes=scratch,
        compiler_params=pltpu.CompilerParams(
            collective_id=0, has_side_effects=True, vmem_limit_bytes=63 * 2**20
        ),
    )(small, tokens, cot, cosines, sines, fc2_own, out_own, fc1_spread, qkv_spread)[:7]


def columns_kernel(fc1_in, qkv_in, fc1_out, qkv_out):
    f32 = jnp.float32
    unit, part_width = fc1_in.shape[2] // 4, qkv_in.shape[2] // 3
    for w in range(8):
        for t in range(4):
            at = ((t // 2 * 2 + w // 4) * 2 + t % 2) * 4 * unit + w % 4 * unit
            fc1_out[:, at : at + unit] = fc1_in[w, :, t * unit : (t + 1) * unit].astype(f32)
    low = lax.broadcasted_iota(jnp.int32, (1, 128), 1) < HEAD_DIM
    for part in range(3):
        for a in range(2):
            for dl in range(2):
                for dx in range(2):
                    at = part * part_width + a * 128
                    even, odd = (
                        qkv_in[dl * 4 + dx * 2 + k, :, at : at + 128].astype(f32) for k in range(2)
                    )
                    to = part * 8 * part_width + a * 1024 + dl * 512 + dx * 128
                    qkv_out[:, to : to + 128] = jnp.where(low, even, pltpu.roll(odd, 64, 1))
                    qkv_out[:, to + 256 : to + 384] = jnp.where(low, pltpu.roll(even, 64, 1), odd)


def plain_columns(fc1_in, qkv_in):
    _, rows, fc1_width = fc1_in.shape
    vmem = pl.BlockSpec(memory_space=pltpu.VMEM)
    return pl.pallas_call(
        columns_kernel,
        out_shape=[
            jax.ShapeDtypeStruct((rows, 8 * fc1_width), jnp.float32),
            jax.ShapeDtypeStruct((rows, 8 * qkv_in.shape[2]), jnp.float32),
        ],
        in_specs=[vmem, vmem],
        out_specs=[vmem, vmem],
        compiler_params=pltpu.CompilerParams(vmem_limit_bytes=24 * 2**20),
    )(fc1_in, qkv_in)


def split_device(
    tokens,
    lengths,
    ln_gain,
    ln_bias,
    w_qkv,
    b_qkv,
    w_out,
    b_out,
    w_fc1,
    b_fc1,
    w_fc2,
    b_fc2,
    cotangent,
):
    bf16, f32 = jnp.bfloat16, jnp.float32
    zh, zl, y, x, c = (lax.axis_index(name) for name in FINE)
    place = (zl * 2 + x) * 2 + c
    _, local_len, width = tokens.shape
    rows = w_qkv.shape[0]
    ff_rows = w_fc2.shape[0]
    pieces = 4
    total_len = local_len * pieces
    heads = 4
    own_width = heads * HEAD_DIM

    row = 2 * rows
    out_bias = b_out.astype(f32) + b_fc2.astype(f32)
    small = jnp.concatenate(
        [v.astype(f32) for v in (ln_gain, ln_gain, ln_bias, ln_bias, b_qkv, b_out, b_fc1)]
        + [out_bias, out_bias, jnp.broadcast_to(lengths.astype(f32), (row,))]
    ).reshape(-1, row)
    places = (x * 2 + c) * local_len + jnp.arange(local_len, dtype=jnp.int32)
    grad_own = jnp.where((places < lengths[0])[:, None], cotangent[0], jnp.zeros((), bf16))
    fc1_spread = (
        w_fc1.reshape((rows, 2, 2, 2, 2, 2, ff_rows))
        .transpose(2, 4, 5, 0, 1, 3, 6)
        .reshape(8, rows, -1)
    )
    qkv_spread = (
        w_qkv.reshape((rows, 3, 2, 2, 2, 2, 2, HEAD_DIM))
        .transpose(3, 5, 6, 0, 1, 2, 4, 7)
        .reshape(8, rows, -1)
    )
    cosines, sines = tables(total_len, ROT)
    grad_input, output, sums, grad_fc2, grad_wout, fc1_columns, qkv_columns = main(
        small, tokens[0], grad_own, cosines, sines, w_fc2, w_out, fc1_spread, qkv_spread
    )
    output, grad_input = output[None], grad_input[None]
    grad_wfc1, grad_wqkv = plain_columns(fc1_columns, qkv_columns)
    grad_bqkv, grad_bfc1 = sums[0:2].reshape(-1)[: 3 * rows], sums[2:4].reshape(-1)
    grad_bias, grad_gain, grad_shift = lax.dynamic_slice(sums, (4, c * rows), (3, rows))
    return (
        output,
        grad_input,
        grad_gain,
        grad_shift,
        grad_wqkv,
        grad_bqkv,
        grad_wout,
        grad_bias,
        grad_wfc1,
        grad_bfc1,
        grad_fc2,
        grad_bias,
    )


def fine_mesh(mesh):
    return jax.sharding.Mesh(mesh.devices.reshape(2, 2, 2, 2, 2), FINE)


def fine_solution(mesh):
    everyone, seqs, parts = FINE, ("zh", "zl", "y"), ("x", "c")
    placed = (
        P(seqs, parts, None),
        P(seqs),
        P(everyone),
        P(everyone),
        P(everyone, None),
        P(everyone),
        P(everyone, None),
        P(everyone),
        P(everyone, None),
        P(everyone),
        P(everyone, None),
        P(everyone),
        P(seqs, parts, None),
    )
    given = (
        P(seqs, parts, None),
        P(seqs, parts, None),
        P(everyone),
        P(everyone),
        P(everyone, None),
        P(everyone),
        P(everyone, None),
        P(everyone),
        P(everyone, None),
        P(everyone),
        P(everyone, None),
        P(everyone),
    )
    return jax.shard_map(
        split_device, mesh=fine_mesh(mesh), in_specs=placed, out_specs=given, check_vma=False
    )


def solution(mesh):
    if mesh.shape["dp"] == 8 and mesh.shape["ctx"] == 4:
        return fine_solution(mesh)
    return general_solution(mesh)
```

```python
import functools
import math

import jax
import jax.numpy as jnp
import numpy as np
from jax import lax
from jax.experimental import pallas as pl
from jax.experimental.pallas import tpu as pltpu
from jax.sharding import PartitionSpec as P

HEAD_DIM = 64
ROT = 32


eps_norm = 1e-05
gelu_coef = 0.7978845608028654


def gelu_tanh(values):
    return (
        0.5 * values * (1.0 + jnp.tanh(gelu_coef * (values + 0.044715 * values * values * values)))
    )


def rotary_angles(positions, rot_dims):
    half_dims = rot_dims // 2
    freq_index = jnp.arange(half_dims, dtype=jnp.float32)
    inv_freq = jnp.exp(-math.log(10000.0) * 2.0 * freq_index / rot_dims)
    return positions.astype(jnp.float32)[:, None] * inv_freq[None, :]


def rotary(vectors, angles):
    half_dims = angles.shape[-1]
    cosines = jnp.cos(angles)[:, None, :]
    sine_vals = jnp.sin(angles)[:, None, :]
    leading = vectors[..., :half_dims]
    trailing = vectors[..., half_dims : 2 * half_dims]
    return jnp.concatenate(
        [
            leading * cosines - trailing * sine_vals,
            trailing * cosines + leading * sine_vals,
            vectors[..., 2 * half_dims :],
        ],
        axis=-1,
    )


def rotary_back(gradients, angles):
    half_dims = angles.shape[-1]
    cosines = jnp.cos(angles)[:, None, :]
    sine_vals = jnp.sin(angles)[:, None, :]
    leading = gradients[..., :half_dims]
    trailing = gradients[..., half_dims : 2 * half_dims]
    return jnp.concatenate(
        [
            leading * cosines + trailing * sine_vals,
            trailing * cosines - leading * sine_vals,
            gradients[..., 2 * half_dims :],
        ],
        axis=-1,
    )


def masked_scores(queries, key_rows, places, length):
    scores = jnp.einsum("qhd,khd->hqk", queries, key_rows, preferred_element_type=jnp.float32)
    key_places = jnp.arange(key_rows.shape[0], dtype=jnp.int32)
    allowed = (key_places[None, :] <= places[:, None]) & (key_places[None, :] < length)
    return jnp.where(allowed[None], scores, -1e30)


def on_device(
    tokens,
    lengths,
    ln_gain,
    ln_bias,
    w_qkv,
    b_qkv,
    w_out,
    b_out,
    w_fc1,
    b_fc1,
    w_fc2,
    b_fc2,
    cotangent,
):
    seq_count, local_len, model_width = tokens.shape
    shard_rows = w_qkv.shape[0]
    hidden_ratio = w_fc1.shape[1] // model_width
    head_count = model_width // HEAD_DIM
    token_count = seq_count * local_len
    places = lax.axis_index("ctx") * local_len + jnp.arange(local_len, dtype=jnp.int32)
    angles = rotary_angles(places, ROT)
    live_mask = places[None, :] < lengths[:, None]
    inputs = tokens.astype(jnp.float32).reshape(token_count, model_width)
    average = jnp.mean(inputs, axis=-1, keepdims=True)
    centered = inputs - average
    variance = jnp.mean(centered * centered, axis=-1, keepdims=True)
    inv_std = lax.rsqrt(variance + eps_norm)
    normed = centered * inv_std
    qkv_bias_rows = b_qkv.reshape(shard_rows, 3)
    fc1_bias_rows = b_fc1.reshape(shard_rows, hidden_ratio)
    fc2_rows = w_fc2.reshape(shard_rows, hidden_ratio * model_width)
    inner_full = (
        lax.all_gather(w_qkv, ("dp", "ctx"), axis=0, tiled=True),
        lax.all_gather(w_fc1, ("dp", "ctx"), axis=0, tiled=True),
        lax.all_gather(ln_gain, ("dp", "ctx"), axis=0, tiled=True),
        lax.all_gather(ln_bias, ("dp", "ctx"), axis=0, tiled=True),
        lax.all_gather(qkv_bias_rows, ("dp", "ctx"), axis=0, tiled=True),
        lax.all_gather(fc1_bias_rows, ("dp", "ctx"), axis=0, tiled=True),
    )
    gain_full = inner_full[2].astype(jnp.float32)
    shift_full = inner_full[3].astype(jnp.float32)
    hidden = (normed * gain_full + shift_full).astype(jnp.bfloat16)
    qkv_acc = jnp.dot(hidden, inner_full[0], preferred_element_type=jnp.float32)
    up_acc = jnp.dot(hidden, inner_full[1], preferred_element_type=jnp.float32)
    qkv_bias = inner_full[4].reshape(-1).astype(jnp.float32)
    fc1_bias = inner_full[5].reshape(-1).astype(jnp.float32)
    qkv_proj = (qkv_acc + qkv_bias).reshape(seq_count, local_len, 3, head_count, HEAD_DIM)
    queries = (rotary(qkv_proj[:, :, 0], angles) * 0.125).astype(jnp.bfloat16)
    key_local = (
        rotary(qkv_proj[:, :, 1], angles)
        .astype(jnp.bfloat16)
        .reshape(seq_count, local_len, model_width)
    )
    value_local = qkv_proj[:, :, 2].astype(jnp.bfloat16).reshape(seq_count, local_len, model_width)
    key_full, value_full = (
        lax.all_gather(key_local, "ctx", axis=1, tiled=True),
        lax.all_gather(value_local, "ctx", axis=1, tiled=True),
    )
    total_len = key_full.shape[1]

    def attend_forward(packed):
        query_seq, key_seq, value_seq, length = packed
        key_heads = key_seq.reshape(total_len, head_count, HEAD_DIM)
        value_heads = value_seq.reshape(total_len, head_count, HEAD_DIM)
        scores = masked_scores(query_seq, key_heads, places, length)
        row_max = jnp.max(scores, axis=-1, keepdims=True)
        exponent = jnp.exp(scores - row_max)
        row_sum = jnp.sum(exponent, axis=-1, keepdims=True)
        probability = (exponent / row_sum).astype(jnp.bfloat16)
        attended = jnp.einsum(
            "hqk,khd->qhd", probability, value_heads, preferred_element_type=jnp.float32
        )
        log_total = (row_max + jnp.log(row_sum))[..., 0]
        return (attended.reshape(local_len, model_width).astype(jnp.bfloat16), log_total)

    attn_seq, log_totals = lax.map(attend_forward, (queries, key_full, value_full, lengths))
    attn_mixed = attn_seq.reshape(token_count, model_width)
    up_proj = up_acc + fc1_bias
    activated = gelu_tanh(up_proj).astype(jnp.bfloat16)
    outer_full = (
        lax.all_gather(w_out, ("dp", "ctx"), axis=0, tiled=True),
        lax.all_gather(fc2_rows, ("dp", "ctx"), axis=0, tiled=True),
        lax.all_gather(b_out, ("dp", "ctx"), axis=0, tiled=True),
        lax.all_gather(b_fc2, ("dp", "ctx"), axis=0, tiled=True),
    )
    branch = jnp.dot(attn_mixed, outer_full[0], preferred_element_type=jnp.float32) + jnp.dot(
        activated,
        outer_full[1].reshape(hidden_ratio * model_width, model_width),
        preferred_element_type=jnp.float32,
    )
    out_bias = outer_full[2].astype(jnp.float32)
    fc2_bias = outer_full[3].astype(jnp.float32)
    output = (
        (inputs + branch + out_bias + fc2_bias)
        .astype(jnp.bfloat16)
        .reshape(seq_count, local_len, model_width)
    )
    grad_out = jnp.where(live_mask[:, :, None], cotangent, jnp.zeros((), jnp.bfloat16)).reshape(
        token_count, model_width
    )
    out_back, fc2_back = (
        lax.all_gather(w_out, ("dp", "ctx"), axis=0, tiled=True),
        lax.all_gather(fc2_rows, ("dp", "ctx"), axis=0, tiled=True),
    )
    fc2_matrix = fc2_back.reshape(hidden_ratio * model_width, model_width)
    grad_mixed = jnp.einsum(
        "td,kd->tk", grad_out, out_back, preferred_element_type=jnp.float32
    ).astype(jnp.bfloat16)
    grad_act = jnp.einsum("td,kd->tk", grad_out, fc2_matrix, preferred_element_type=jnp.float32)
    gelu_value, gelu_pull = jax.vjp(gelu_tanh, up_proj)
    grad_up = gelu_pull(grad_act)[0].astype(jnp.bfloat16)
    key_back, value_back = (
        lax.all_gather(key_local, "ctx", axis=1, tiled=True),
        lax.all_gather(value_local, "ctx", axis=1, tiled=True),
    )

    def attend_backward(packed):
        query_seq, key_seq, value_seq, grad_seq, log_total, length = packed
        key_heads = key_seq.reshape(total_len, head_count, HEAD_DIM)
        value_heads = value_seq.reshape(total_len, head_count, HEAD_DIM)
        grad_heads = grad_seq.reshape(local_len, head_count, HEAD_DIM)
        scores = masked_scores(query_seq, key_heads, places, length)
        probability = jnp.exp(scores - log_total[:, :, None])
        grad_probs = jnp.einsum(
            "qhd,khd->hqk", grad_heads, value_heads, preferred_element_type=jnp.float32
        )
        inner = jnp.sum(probability * grad_probs, axis=-1, keepdims=True)
        grad_scores = (probability * (grad_probs - inner)).astype(jnp.bfloat16)
        grad_query = jnp.einsum(
            "hqk,khd->qhd", grad_scores, key_heads, preferred_element_type=jnp.float32
        )
        grad_keys = jnp.einsum(
            "hqk,qhd->khd", grad_scores, query_seq, preferred_element_type=jnp.float32
        )
        grad_values = jnp.einsum(
            "hqk,qhd->khd",
            probability.astype(jnp.bfloat16),
            grad_heads,
            preferred_element_type=jnp.float32,
        )
        return (
            grad_query,
            grad_keys.reshape(total_len, model_width),
            grad_values.reshape(total_len, model_width),
        )

    grad_query, grad_keys_all, grad_values_all = lax.map(
        attend_backward,
        (
            queries,
            key_back,
            value_back,
            grad_mixed.reshape(seq_count, local_len, model_width),
            log_totals,
            lengths,
        ),
    )
    grad_keys_own, grad_values_own = (
        lax.psum_scatter(grad_keys_all, "ctx", scatter_dimension=1, tiled=True),
        lax.psum_scatter(grad_values_all, "ctx", scatter_dimension=1, tiled=True),
    )
    grad_query_pre = rotary_back(grad_query * 0.125, angles).reshape(token_count, model_width)
    grad_keys_pre = rotary_back(
        grad_keys_own.reshape(seq_count, local_len, head_count, HEAD_DIM), angles
    ).reshape(token_count, model_width)
    grad_qkv = jnp.concatenate(
        [grad_query_pre, grad_keys_pre, grad_values_own.reshape(token_count, model_width)], axis=-1
    ).astype(jnp.bfloat16)
    qkv_matrix, fc1_matrix = (
        lax.all_gather(w_qkv, ("dp", "ctx"), axis=0, tiled=True),
        lax.all_gather(w_fc1, ("dp", "ctx"), axis=0, tiled=True),
    )
    grad_hidden = jnp.einsum(
        "tj,dj->td", grad_qkv, qkv_matrix, preferred_element_type=jnp.float32
    ) + jnp.einsum("tj,dj->td", grad_up, fc1_matrix, preferred_element_type=jnp.float32)
    gain_term = jnp.sum(grad_hidden * normed, axis=0)
    shift_term = jnp.sum(grad_hidden, axis=0)
    grad_norm = grad_hidden * gain_full
    grad_input = grad_out.astype(jnp.float32) + inv_std * (
        grad_norm
        - jnp.mean(grad_norm, axis=-1, keepdims=True)
        - normed * jnp.mean(grad_norm * normed, axis=-1, keepdims=True)
    )
    grad_input = grad_input.astype(jnp.bfloat16).reshape(seq_count, local_len, model_width)
    wout_term = jnp.einsum("tk,td->kd", attn_mixed, grad_out, preferred_element_type=jnp.float32)
    wfc2_term = jnp.einsum(
        "tk,td->kd", activated, grad_out, preferred_element_type=jnp.float32
    ).reshape(model_width, hidden_ratio * model_width)
    bias_term = jnp.sum(grad_out, axis=0, dtype=jnp.float32)
    bqkv_term = jnp.sum(grad_qkv, axis=0, dtype=jnp.float32).reshape(model_width, 3)
    bfc1_term = jnp.sum(grad_up, axis=0, dtype=jnp.float32).reshape(model_width, hidden_ratio)
    grad_wout, grad_wfc2, grad_bias, grad_gain, grad_shift, grad_bqkv, grad_bfc1 = (
        lax.psum_scatter(wout_term, ("dp", "ctx"), scatter_dimension=0, tiled=True),
        lax.psum_scatter(wfc2_term, ("dp", "ctx"), scatter_dimension=0, tiled=True),
        lax.psum_scatter(bias_term, ("dp", "ctx"), scatter_dimension=0, tiled=True),
        lax.psum_scatter(gain_term, ("dp", "ctx"), scatter_dimension=0, tiled=True),
        lax.psum_scatter(shift_term, ("dp", "ctx"), scatter_dimension=0, tiled=True),
        lax.psum_scatter(bqkv_term, ("dp", "ctx"), scatter_dimension=0, tiled=True),
        lax.psum_scatter(bfc1_term, ("dp", "ctx"), scatter_dimension=0, tiled=True),
    )
    qkv_part = jnp.einsum("tk,tj->kj", hidden, grad_qkv, preferred_element_type=jnp.float32)
    fc1_part = jnp.einsum("tk,tj->kj", hidden, grad_up, preferred_element_type=jnp.float32)
    inner_sum = lax.psum_scatter(
        jnp.concatenate([qkv_part, fc1_part], axis=1),
        ("dp", "ctx"),
        scatter_dimension=0,
        tiled=True,
    )
    grad_wqkv = inner_sum[:, : 3 * model_width]
    grad_wfc1 = inner_sum[:, 3 * model_width :]
    return (
        output,
        grad_input,
        grad_gain,
        grad_shift,
        grad_wqkv,
        grad_bqkv.reshape(-1),
        grad_wout,
        grad_bias,
        grad_wfc1,
        grad_bfc1.reshape(-1),
        grad_wfc2.reshape(shard_rows * hidden_ratio, model_width),
        grad_bias,
    )


def general_solution(mesh):
    placed = (
        P("dp", "ctx", None),
        P("dp"),
        P(("dp", "ctx")),
        P(("dp", "ctx")),
        P(("dp", "ctx"), None),
        P(("dp", "ctx")),
        P(("dp", "ctx"), None),
        P(("dp", "ctx")),
        P(("dp", "ctx"), None),
        P(("dp", "ctx")),
        P(("dp", "ctx"), None),
        P(("dp", "ctx")),
        P("dp", "ctx", None),
    )
    return jax.shard_map(
        on_device,
        mesh=mesh,
        in_specs=placed,
        out_specs=(
            P("dp", "ctx", None),
            P("dp", "ctx", None),
            P(("dp", "ctx")),
            P(("dp", "ctx")),
            P(("dp", "ctx"), None),
            P(("dp", "ctx")),
            P(("dp", "ctx"), None),
            P(("dp", "ctx")),
            P(("dp", "ctx"), None),
            P(("dp", "ctx")),
            P(("dp", "ctx"), None),
            P(("dp", "ctx")),
        ),
        check_vma=False,
    )


FINE = ("zh", "zl", "y", "x", "c")
ROWS_AXES = ("zl", "x", "c")


def dot(left, right, dims):
    return lax.dot_general(left, right, (dims, ((), ())), preferred_element_type=jnp.float32)


QB = 256


def nt(a, b):
    return dot(a, b, ((1,), (1,)))


def nn(a, b):
    return dot(a, b, ((1,), (0,)))


def tn(a, b):
    return dot(a, b, ((0,), (0,)))


def attend_pair(pair, length, bias, cosines_ref, sines_ref, qkv, mixed, q_s, k_s, v_s, g_s, gk_s, gv_s):
    f32, bf16 = jnp.float32, jnp.bfloat16
    total, width = mixed.shape
    lane = lax.broadcasted_iota(jnp.int32, (1, 128), 1)
    first = lane % HEAD_DIM < ROT // 2
    heads = [lane < HEAD_DIM, lane >= HEAD_DIM]

    def other(v):
        return jnp.where(first, pltpu.roll(v, 128 - ROT // 2, 1), pltpu.roll(v, ROT // 2, 1))

    def col(part):
        return pl.ds(pl.multiple_of(part * width + pair * 128, 128), 128)

    for b in range(total // QB):
        rows = pl.ds(b * QB, QB)
        cosines, sines = cosines_ref[rows], sines_ref[rows]

        def turn(v):
            return v * cosines + other(v) * sines

        q = turn(qkv[rows, col(0)] + bias[:, col(0)]) * 0.125
        k = turn(qkv[rows, col(1)] + bias[:, col(1)])
        v = qkv[rows, col(2)] + bias[:, col(2)]
        g = mixed[rows, col(0)]
        for h in range(2):
            q_s[h, rows] = jnp.where(heads[h], q, 0.0).astype(bf16)
            k_s[h, rows] = jnp.where(heads[h], k, 0.0).astype(bf16)
            v_s[h, rows] = jnp.where(heads[h], v, 0.0).astype(bf16)
            g_s[h, rows] = jnp.where(heads[h], g, 0.0).astype(bf16)
    gk_s[...] = jnp.zeros_like(gk_s)
    gv_s[...] = jnp.zeros_like(gv_s)

    for b in range(total // QB):
        rows = pl.ds(b * QB, QB)
        upto = (b + 1) * QB
        keys = pl.ds(0, upto)
        limit = jnp.minimum(lax.broadcasted_iota(jnp.int32, (1, QB), 1) + (b * QB + 1), length)
        allowed = lax.broadcasted_iota(jnp.int32, (upto, QB), 0) < limit
        out = grad = jnp.zeros((QB, 128), f32)
        for h in range(2):
            qh, gh = q_s[h, rows], g_s[h, rows]
            scores = jnp.where(allowed, nt(k_s[h, keys], qh), -1e30)
            exponent = jnp.exp(scores - jnp.max(scores, axis=0, keepdims=True))
            share = exponent * (1.0 / jnp.sum(exponent, axis=0, keepdims=True))
            rounded = share.astype(bf16)
            back = nt(v_s[h, keys], gh)
            back = (share * (back - jnp.sum(share * back, axis=0, keepdims=True))).astype(bf16)
            gv_s[keys] += nn(rounded, gh)
            gk_s[keys] += nn(back, qh)
            out += tn(rounded, v_s[h, keys])
            grad += tn(back, k_s[h, keys])
        mixed[rows, col(0)] = out
        grad *= 0.125
        qkv[rows, col(0)] = grad * cosines_ref[rows] - other(grad) * sines_ref[rows]
    for b in range(total // QB):
        rows = pl.ds(b * QB, QB)
        grad = gk_s[rows]
        qkv[rows, col(1)] = grad * cosines_ref[rows] - other(grad) * sines_ref[rows]
        qkv[rows, col(2)] = gv_s[rows]


def tables(total, rot):
    half = rot // 2
    steps = np.arange(half, dtype=np.float32)
    inv_freq = np.exp(np.float32(-math.log(10000.0) * 2.0) * steps / np.float32(rot))
    angles = np.arange(total, dtype=np.float32)[:, None] * inv_freq[None, :].astype(np.float32)
    cosines, sines = np.cos(angles), np.sin(angles)
    rest = (total, HEAD_DIM - rot)
    cosines = np.concatenate([cosines, cosines, np.ones(rest, np.float32)] * 2, axis=1)
    sines = np.concatenate([-sines, sines, np.zeros(rest, np.float32)] * 2, axis=1)
    return jnp.asarray(cosines, jnp.float32), jnp.asarray(sines, jnp.float32)


MESH_ID = pl.DeviceIdType.MESH


W_PEERS = [(k // 4, k // 2 % 2, k % 2) for k in range(1, 8)]


def sum_small(values, collective_id):
    n = values.shape[1]
    return pl.pallas_call(
        sum_kernel,
        out_shape=jax.ShapeDtypeStruct((n, 128), jnp.float32),
        in_specs=[pl.BlockSpec(memory_space=pltpu.VMEM)],
        out_specs=pl.BlockSpec(memory_space=pltpu.VMEM),
        scratch_shapes=[
            pltpu.VMEM((32, n, 128), jnp.float32),
            pltpu.SemaphoreType.DMA((32,)),
            pltpu.SemaphoreType.DMA((32,)),
        ],
        compiler_params=pltpu.CompilerParams(collective_id=collective_id, has_side_effects=True),
    )(values)


def main_kernel(
    small, tokens, cot_own, cosines, sines, fc2_own, out_own, fc1_spread, qkv_spread,
    grad_in, output, sums_out, fc2_out, out_out, fc1_a, qkv_a, up_sum, qkv_sum, small_all, qkv_all, out_all, fc1_all, fc2_all,
    fc2_part, fc1_part, out_part, qkv_part, c_got, w_got, wide_y, wide_z, cols_y, cols_z,
    hidden, cot, act, gup, attn, gqkv, qkv_w, out_w, stage, full, wide, cols, wide_s, cols_s, fc1_bias, qkv_bias, terms, terms_got,
    send_sem, recv_sem, local_sem, block_sem, c_send, c_recv, small_send, small_recv, terms_send, terms_recv,
):
    f32, bf16 = jnp.float32, jnp.bfloat16
    zh, zl, y, x, c = place = [lax.axis_index(name) for name in FINE]
    seat = (zl * 2 + x) * 2 + c
    used, used_local = [0], [0]
    sends = []

    class Copy:
        def __init__(self, describe):
            self.describe = describe

        def start(self):
            self.describe().start()

        def wait(self):
            self.describe().wait()

        def wait_send(self):
            self.describe().wait_send()

        def wait_recv(self):
            self.describe().wait_recv()

    def remote(ends, target):
        n = used[0]
        used[0] += 1

        def describe():
            src, dst = ends()
            return pltpu.make_async_remote_copy(
                src_ref=src,
                dst_ref=dst,
                send_sem=send_sem.at[n],
                recv_sem=recv_sem.at[n],
                device_id=target(),
                device_id_type=MESH_ID,
            )

        copy = Copy(describe)
        copy.start()
        sends.append(copy)
        return copy

    def partner(axis):
        return tuple(1 - p if name == axis else p for name, p in zip(FINE, place))

    def beside():
        return partner("y")

    def across():
        return partner("zh")

    def local(ends):
        n = used_local[0]
        used_local[0] += 1

        def describe():
            src, dst = ends()
            return pltpu.make_async_copy(src, dst, local_sem.at[n])

        copy = Copy(describe)
        copy.start()
        return copy

    def load(*pairs):
        copies = [local(lambda pair=pair: pair) for pair in pairs]
        for copy in copies:
            copy.wait()

    def index_of(where):
        number = 0
        for p in where:
            number = number * 2 + p
        return number

    def away(k):
        return tuple((p + k // 2 ** (4 - i)) % 2 for i, p in enumerate(place))

    barrier = pltpu.get_barrier_semaphore()

    def greet(k, carry):
        pl.semaphore_signal(barrier, inc=1, device_id=away(k), device_id_type=MESH_ID)
        return carry

    lax.fori_loop(1, 32, greet, 0)
    pl.semaphore_wait(barrier, 31)

    blocks, block_rows, width = hidden.shape
    token_count, units = gup.shape
    total_len = token_count // 2
    mine, sent = hidden, cot

    def small_copy(k):
        return pltpu.make_async_remote_copy(
            src_ref=small,
            dst_ref=small_all.at[index_of(place)],
            send_sem=small_send.at[k],
            recv_sem=small_recv.at[k],
            device_id=away(k),
            device_id_type=MESH_ID,
        )

    def small_start(k, carry):
        small_copy(k).start()
        return carry

    def small_wait(k, carry):
        small_copy(k).wait()
        return carry

    lax.fori_loop(1, 32, small_start, 0)
    small_all[index_of(place)] = small[...]
    tokens_in = local(lambda: (tokens, stage))

    def spread(weight, matrix):
        pieces = []
        for dl, dx, dc in W_PEERS:

            def where(dl=dl, dx=dx, dc=dc):
                return zh, (zl + dl) % 2, y, (x + dx) % 2, (c + dc) % 2

            def ends(where=where):
                _, to_zl, _, to_x, to_c = where()
                return weight.at[(to_zl * 2 + to_x) * 2 + to_c], matrix.at[zh, zl, y, x * 2 + c]

            pieces.append(remote(ends, where))
        return pieces, local(lambda: (weight.at[seat], matrix.at[zh, zl, y, x * 2 + c]))

    def parts_of(ends_list):
        return [remote(ends, across) for ends in ends_list], [remote(ends, beside) for ends in ends_list]

    def forward(copy, block):
        copy.wait_recv()
        return remote(lambda: (block(), block()), beside)

    def half_of(matrix, half):
        return lambda: matrix.at[1 - zh, half, y]

    def own_half(matrix, half):
        return lambda: (matrix.at[zh, half, y], matrix.at[zh, half, y])

    fc1_pieces = spread(fc1_spread, fc1_all)
    half_rows = fc2_own.shape[0] // 2

    def fc2_rows_of(a, half):
        return lambda: fc2_all.at[a, y, pl.ds(half * half_rows, half_rows)]

    def fc2_ends(half):
        return lambda: (fc2_own.at[pl.ds(half * half_rows, half_rows)], fc2_rows_of(zh, half)())

    def over(own, gathered, axis):
        return remote(lambda: (own(), gathered()), lambda: partner(axis))

    def own_cot():
        return cot_own

    def seat_of(array, dl=0, dx=0):
        return lambda: array.at[((zl + dl) % 2 * 2 + (x + dx) % 2) * 2 + c]

    cot_zl = over(own_cot, seat_of(cot), "zl")
    fc2_zh, fc2_y = parts_of([fc2_ends(half) for half in range(2)])
    cot_x = over(own_cot, seat_of(cot), "x")
    core = {("cot", 0, 0): over(own_cot, seat_of(cot), "c")}
    own_copies = [
        local(lambda: (cot_own, cot.at[seat])),
        local(lambda: (fc2_own, fc2_all.at[zh, y])),
        local(lambda: (out_own, out_all.at[zh, y])),
    ]

    lax.fori_loop(1, 32, small_wait, 0)
    tokens_in.wait()
    in_place = lax.broadcasted_iota(jnp.int32, (32, width), 1) // (width // 32) == (
        lax.broadcasted_iota(jnp.int32, (32, width), 0)
    )

    def vector(row):
        spread_out = jnp.concatenate([small_all[:, row, :]] * (width // 128), axis=1)
        return jnp.sum(jnp.where(in_place, spread_out, 0.0), axis=0, keepdims=True)

    gain, shift = vector(0), vector(1)

    def norm_rows(i, carry):
        rows = pl.ds(pl.multiple_of(i * 32, 32), 32)
        values = stage[rows].astype(f32)
        centered = values - jnp.mean(values, axis=-1, keepdims=True)
        variance = jnp.mean(centered * centered, axis=-1, keepdims=True)
        hidden[seat, rows] = (centered * lax.rsqrt(variance + eps_norm) * gain + shift).astype(bf16)
        return carry

    lax.fori_loop(0, block_rows // 32, norm_rows, 0)
    hid_zl = over(seat_of(hidden), seat_of(hidden), "zl")
    hid_x = over(seat_of(hidden), seat_of(hidden), "x")
    core["hidden", 0, 0] = over(seat_of(hidden), seat_of(hidden), "c")

    for t in range(4):
        owner = index_of((t // 2, zl, t % 2, x, c))
        for half in range(2):
            at = t * 2 * 128 + half * 128
            fc1_bias[:, at : at + 128] = small_all[owner, pl.ds(4 + half, 1), :]
    low = lax.broadcasted_iota(jnp.int32, (1, 128), 1) < HEAD_DIM
    for part in range(3):
        for a in range(2):
            chunks = []
            for b in range(2):
                chunk = part * 32 + index_of((a, zl, b, x, c))
                row = small_all[chunk // 3, pl.ds(2 + chunk % 3 // 2, 1), :]
                chunks.append(jnp.where(chunk % 3 % 2 == b, row, pltpu.roll(row, HEAD_DIM, 1)))
            at = (part * 2 + a) * 128
            qkv_bias[:, at : at + 128] = jnp.where(low, chunks[0], chunks[1])

    def length_of(seq):
        row = small_all[index_of((zh, seq, y, 0, 0)), pl.ds(7, 1), :]
        return jnp.concatenate([row] * (QB // 128), axis=1).astype(jnp.int32)

    def all_there(pieces):
        for piece in pieces[0]:
            piece.wait_recv()
        pieces[1].wait()

    def to_core(name, copy, dl, dx):
        array = {"cot": cot, "hidden": hidden}[name]
        copy.wait_recv()
        core[name, dl, dx] = over(seat_of(array, dl, dx), seat_of(array, dl, dx), "c")

    all_there(fc1_pieces)
    fc1_zh, fc1_y = parts_of([own_half(fc1_all, half) for half in range(2)])
    to_core("cot", cot_zl, 1, 0)
    cot_zx = over(seat_of(cot, 1), seat_of(cot, 1), "x")
    fc2_fwd = [forward(fc2_zh[0], fc2_rows_of(1 - zh, 0))]
    to_core("cot", cot_x, 0, 1)
    fc2_fwd.append(forward(fc2_zh[1], fc2_rows_of(1 - zh, 1)))
    qkv_pieces = spread(qkv_spread, qkv_all)
    to_core("hidden", hid_zl, 1, 0)
    hid_zx = over(seat_of(hidden, 1), seat_of(hidden, 1), "x")
    to_core("hidden", hid_x, 0, 1)
    fc1_fwd = [forward(fc1_zh[0], half_of(fc1_all, 0))]
    to_core("cot", cot_zx, 1, 1)
    fc1_fwd.append(forward(fc1_zh[1], half_of(fc1_all, 1)))
    all_there(qkv_pieces)
    out_zh, out_y = parts_of([lambda: (out_own, out_all.at[zh, y])])
    qkv_zh, qkv_y = parts_of([own_half(qkv_all, half) for half in range(2)])
    for copy in own_copies:
        copy.wait()
    for copy in fc2_y + fc2_fwd + fc1_y + fc1_fwd:
        copy.wait_recv()

    def tokens_here(dl, dx):
        for name in ("cot", "hidden"):
            core[name, dl, dx].wait_recv()

    late_in = out_y + qkv_y

    def row_job(part, rows, first, slot, put):
        some = pl.ds(0, rows)
        return dict(
            part=lambda a, b: part.at[a, b, pl.ds(first, rows)],
            y=[wide_y.at[slot, j, some] for j in range(2)],
            z=wide_z.at[slot, some],
            v=[wide.at[j, some] for j in range(3)],
            s=wide_s.at[slot, some],
            put=put,
            rows=some,
        )

    def column_job(part, width, away, slot, to):
        lanes = pl.ds(0, width)
        return dict(
            part=lambda a, b: part.at[a, (zl + away) % 2, b],
            y=[cols_y.at[slot, j, :, lanes] for j in range(2)],
            z=cols_z.at[slot, :, lanes],
            v=[cols.at[j, :, lanes] for j in range(3)],
            s=cols_s.at[slot, :, lanes],
            away=away,
            to=to,
        )

    fc1_width, qkv_width = units, gqkv.shape[1]
    out_rows, fc2_rows = out_part.shape[2], fc2_part.shape[2] // 2
    jobs = [
        row_job(fc2_part, fc2_rows, i * fc2_rows, i, fc2_out.at[pl.ds(i * fc2_rows, fc2_rows)])
        for i in range(2)
    ]
    jobs += [column_job(fc1_part, fc1_width, away, away, fc1_a) for away in (1, 0)]
    jobs += [row_job(out_part, out_rows, 0, 2, out_out)]
    jobs += [column_job(qkv_part, qkv_width, away, 2 + away, qkv_a) for away in (1, 0)]

    def send_beside(job):
        job["y_far"] = remote(lambda: (job["part"](1 - zh, 1 - y), job["y"][1]), beside)
        job["y_own"] = remote(lambda: (job["part"](zh, 1 - y), job["y"][0]), beside)

    def pass_on(job):
        job["y_far"].wait_recv()
        v = job["v"]
        load((job["part"](1 - zh, y), v[0]), (job["y"][1], v[1]))
        job["s"][...] = (v[0][...].astype(f32) + v[1][...].astype(f32)).astype(bf16)
        job["z_copy"] = remote(lambda: (job["s"], job["z"]), across)

    arrivals, kept = [], []

    def finish(job):
        job["y_own"].wait_recv()
        job["z_copy"].wait_recv()
        v = job["v"]
        load((job["part"](zh, y), v[0]), (job["y"][0], v[1]), (job["z"], v[2]))
        total = v[0][...].astype(f32) + v[1][...].astype(f32) + v[2][...].astype(f32)
        if "put" in job:
            full[job["rows"]] = total
            load((full.at[job["rows"]], job["put"]))
            return
        job["z_copy"].wait_send()
        sends[:] = [copy for copy in sends if copy is not job["z_copy"]]
        job["s"][...] = total.astype(bf16)
        piece = job["s"].shape[0] // 4
        for dx in range(2):
            for dc in range(2):

                def where(dx=dx, dc=dc):
                    return zh, (zl + job["away"]) % 2, y, (x + dx) % 2, (c + dc) % 2

                def ends(where=where):
                    _, _, _, to_x, to_c = where()
                    row = pl.multiple_of((to_x * 2 + to_c) * piece, piece)
                    return job["s"].at[pl.ds(row, piece)], job["to"].at[(zl * 2 + x) * 2 + c]

                if job["away"] or dx or dc:
                    arrivals.append(remote(ends, where))
                else:
                    kept.append(local(ends))

    def core_copy(n, g):
        return pltpu.make_async_remote_copy(
            src_ref=sent.at[4 * n + g],
            dst_ref=c_got.at[n, g],
            send_sem=c_send.at[n, g],
            recv_sem=c_recv.at[n, g],
            device_id=partner("c"),
            device_id_type=MESH_ID,
        )

    axes = (("x", "zl"), ("x", "zl"))

    def multiply_groups(n, first, a, v, b, w, multiply):
        def step(g, carry):
            one, two = 1 - g // 2, 1 - g % 2
            dl, dx = two, one
            rest = ((zl + dl) % 2 * 2 + (x + dx) % 2) * 2

            def block(where):
                rows = pl.ds(pl.multiple_of((rest + where) * 256, 256), 256)
                near, far = v[...].reshape(-1, v.shape[-1]), w[...].reshape(-1, w.shape[-1])
                return (multiply(a[rows], near) + multiply(b[rows], far)).astype(bf16)

            sent[4 * n + g] = block(1 - c)
            core_copy(n, g).start()
            mine[4 * n + g] = block(c)
            return carry

        lax.fori_loop(first, first + 2, step, 0)

    def add(n, g, got):
        load((got, stage))
        mine[4 * n + g] = (mine[4 * n + g].astype(f32) + stage[...].astype(f32)).astype(bf16)

    def add_core(n, g):
        core_copy(n, g).wait_recv()
        add(n, g, c_got.at[n, g])

    first_copies, second_copies = {}, {}

    def send_first(n):
        for g in range(2):
            add_core(n, g)
            first_copies[n, g] = remote(
                lambda g=g: (mine.at[4 * n + g], w_got.at[n, g]), lambda: partner(axes[n][0])
            )

    def send_second(n):
        first_copies[n, 0].wait_recv()
        add(n, 2, w_got.at[n, 0])
        second_copies[n] = remote(
            lambda: (mine.at[4 * n + 2], w_got.at[n, 2]), lambda: partner(axes[n][1])
        )

    def add_first(n):
        first_copies[n, 1].wait_recv()
        add(n, 3, w_got.at[n, 1])

    def total(n):
        second_copies[n].wait_recv()
        load((w_got.at[n, 2], stage))
        full[...] = mine[4 * n + 3].astype(f32) + stage[...].astype(f32)

    def chunk(i):
        return pl.ds(pl.multiple_of(i * 32, 32), 32)

    def normalized(values):
        centered = values - jnp.mean(values, axis=-1, keepdims=True)
        inv_std = lax.rsqrt(jnp.mean(centered * centered, axis=-1, keepdims=True) + eps_norm)
        return centered * inv_std, inv_std

    def terms_copy(k):
        return pltpu.make_async_remote_copy(
            src_ref=terms.at[index_of(away(k))],
            dst_ref=terms_got.at[index_of(place)],
            send_sem=terms_send.at[k],
            recv_sem=terms_recv.at[k],
            device_id=away(k),
            device_id_type=MESH_ID,
        )

    def finish_input():
        total(0)
        for g in range(4):
            core_copy(0, g).wait_send()
        load((tokens, sent.at[0]), (cot_own, sent.at[1]))
        gain_row = vector(0)

        def back_rows(i, carry):
            gain_sum, shift_sum, bias_sum = carry
            rows = chunk(i)
            normed, inv_std = normalized(sent[0, rows].astype(f32))
            cotangent = sent[1, rows].astype(f32)
            grads = full[rows]
            scaled = grads * gain_row
            sent[2, rows] = (
                cotangent
                + inv_std
                * (
                    scaled
                    - jnp.mean(scaled, axis=-1, keepdims=True)
                    - normed * jnp.mean(scaled * normed, axis=-1, keepdims=True)
                )
            ).astype(bf16)
            return (
                gain_sum + jnp.sum(grads * normed, axis=0, keepdims=True),
                shift_sum + jnp.sum(grads, axis=0, keepdims=True),
                bias_sum + jnp.sum(cotangent, axis=0, keepdims=True),
            )

        nothing = jnp.zeros((1, width), f32)
        gain_sum, shift_sum, bias_sum = lax.fori_loop(
            0, block_rows // 32, back_rows, (nothing, nothing, nothing)
        )
        load((sent.at[2], grad_in))
        terms[...] = jnp.zeros_like(terms)
        for t in range(4):
            owner = index_of((t // 2, zl, t % 2, x, c))
            for half in range(2):
                at = t * 2 * 128 + half * 128
                terms[owner, pl.ds(2 + half, 1), :] = up_sum[:, at : at + 128]
        side = lax.broadcasted_iota(jnp.int32, (1, 128), 1) // HEAD_DIM
        for part in range(3):
            for a in range(2):
                at = (part * 2 + a) * 128
                both = qkv_sum[0, :, at : at + 128] + qkv_sum[1, :, at : at + 128]
                turned = pltpu.roll(both, HEAD_DIM, 1)
                for b in range(2):
                    piece = part * 32 + index_of((a, zl, b, x, c))
                    owner, row, half = piece // 3, pl.ds(piece % 3 // 2, 1), piece % 3 % 2
                    value = jnp.where(half == b, both, turned)
                    terms[owner, row, :] = jnp.where(side == half, value, terms[owner, row, :])
        for i in range(width // 128):
            for row, vector_sum in ((4, bias_sum), (5, gain_sum), (6, shift_sum)):
                for b in range(2):
                    terms[2 * i + b, row : row + 1, :] = vector_sum[:, i * 128 : (i + 1) * 128]
        terms_got[index_of(place)] = terms[index_of(place)]

        def start(k, carry):
            terms_copy(k).start()
            return carry

        lax.fori_loop(1, 32, start, 0)

    def finish_output():
        total(1)
        bias_row = vector(6)

        def out_rows_of(i, carry):
            rows = chunk(i)
            sent[3, rows] = (sent[0, rows].astype(f32) + full[rows] + bias_row).astype(bf16)
            return carry

        lax.fori_loop(0, block_rows // 32, out_rows_of, 0)
        load((sent.at[3], output))

    def part_tiles(left, right, at, put, tile):
        def step(i, carry):
            lanes = pl.ds(pl.multiple_of(at(i) * 256, 256), 256)
            product = tn(left(lanes), right())
            slot = i % 2

            @pl.when(i >= 2)
            def _():
                pltpu.make_async_copy(tile.at[slot], put(i - 2), block_sem.at[slot]).wait()

            tile[slot] = product.astype(bf16)
            pltpu.make_async_copy(tile.at[slot], put(i), block_sem.at[slot]).start()
            return carry

        def between(first, last):
            lax.fori_loop(first, last, step, 0)

        def drain(last):
            for i in (last - 2, last - 1):
                pltpu.make_async_copy(tile.at[i % 2], put(i), block_sem.at[i % 2]).wait()

        return between, drain

    def far_first(i):
        far, beside = 1 - i % 2, 1 - i // 2
        return (zh + far) % 2, (y + beside) % 2

    def fc_weights(fc1_w, fc2_w):
        return [local(lambda: (fc1_all, fc1_w)), local(lambda: (fc2_all, fc2_w))]

    def feed(fc1_w, fc2_w, tile_wide, tile_cols):
        for copy in fc_weights(fc1_w, fc2_w):
            copy.wait()
        up_sum[...] = jnp.zeros_like(up_sum)

        def step(i, carry):
            b = ((zl + i // 2) % 2 * 2 + (x + i // 4) % 2) * 2 + (c + i) % 2
            rows = pl.ds(pl.multiple_of(b * 256, 256), 256)
            up = nn(hidden[b], fc1_w[...].reshape(width, units)) + fc1_bias[...]
            bent = jnp.tanh(gelu_coef * (up + 0.044715 * up * up * up))
            act[rows] = (0.5 * up * (1.0 + bent)).astype(bf16)
            slope = 0.5 * (1.0 + bent) + 0.5 * up * (1.0 - bent * bent) * gelu_coef * (
                1.0 + 3.0 * 0.044715 * up * up
            )
            back = (nt(cot[b], fc2_w[...].reshape(units, width)) * slope).astype(bf16)
            gup[rows] = back
            up_sum[...] += jnp.sum(back.astype(f32), axis=0, keepdims=True)
            return carry

        tokens_here(0, 0)
        tokens_here(1, 0)
        lax.fori_loop(0, 4, step, 0)
        to_core("hidden", hid_zx, 1, 1)
        tokens_here(0, 1)
        lax.fori_loop(4, 6, step, 0)
        late_in.append(forward(out_zh[0], lambda: out_all.at[1 - zh, y]))
        late_in.append(forward(qkv_zh[0], half_of(qkv_all, 0)))
        tokens_here(1, 1)
        lax.fori_loop(6, 8, step, 0)

        def unit_place(i):
            a, b = far_first(i)
            return a * 2 + b

        def unit_put(i):
            a, b = far_first(i)
            return fc2_part.at[a, b]

        between, drain = part_tiles(
            lambda lanes: act[:, lanes], lambda: cot[...].reshape(token_count, width), unit_place, unit_put, tile_wide
        )
        between(0, 2)
        drain(2)
        late_in.append(forward(qkv_zh[1], half_of(qkv_all, 1)))
        for job in jobs[:2]:
            send_beside(job)
        between, drain = part_tiles(
            lambda lanes: act[:, lanes],
            lambda: cot[...].reshape(token_count, width),
            lambda i: unit_place(i + 2),
            lambda i: unit_put(i + 2),
            tile_wide,
        )
        between(0, 2)
        drain(2)
        feature_tiles(gup, fc1_part, tile_cols, jobs[2:4])

    def feature_tiles(right, part, tile, of):
        for late in range(2):

            def where(i, late=late):
                a, b = far_first(i // 2 + 2 * late)
                return a, i % 2, b

            def feature_place(i, where=where):
                a, half, b = where(i)
                return a * 4 + half * 2 + b

            between, drain = part_tiles(
                lambda lanes: hidden[:, :, lanes].reshape(token_count, 256),
                lambda: right[...],
                feature_place,
                lambda i, where=where: part.at[where(i)],
                tile,
            )
            between(0, 4)
            drain(4)
            if late == 0:
                for job in of:
                    send_beside(job)

    fc_scratch = (pltpu.VMEM(fc1_all.shape, bf16), pltpu.VMEM(fc2_all.shape, bf16))
    pl.run_scoped(
        feed,
        *fc_scratch,
        pltpu.VMEM((2, 256, width), bf16),
        pltpu.VMEM((2, 256, units), bf16),
    )

    for copy in late_in:
        copy.wait_recv()
    load((qkv_all, qkv_w), (out_all, out_w))

    def attend(projected, mixed, q_s, k_s, v_s, g_s, gk_s, gv_s):
        for seq in range(2):

            def project(b, carry, seq=seq):
                rows = pl.ds(pl.multiple_of(b * 256, 256), 256)
                block = b + seq * (blocks // 2)
                projected[rows] = nn(hidden[block], qkv_w[...].reshape(width, qkv_width))
                mixed[rows] = nt(cot[block], out_w[...].reshape(-1, width))
                return carry

            lax.fori_loop(0, blocks // 2, project, 0)

            def pair_step(pair, carry, seq=seq):
                attend_pair(
                    pair, length_of(seq), qkv_bias, cosines, sines, projected, mixed, q_s, k_s, v_s, g_s, gk_s, gv_s
                )
                return carry

            lax.fori_loop(0, mixed.shape[1] // 128, pair_step, 0)
            qkv_sum[seq] = jnp.zeros((1, qkv_width), f32)

            def store(b, carry, seq=seq):
                rows = pl.ds(pl.multiple_of(b * 256, 256), 256)
                to = pl.ds(pl.multiple_of(b * 256 + seq * total_len, 256), 256)
                grads = projected[rows].astype(bf16)
                gqkv[to] = grads
                attn[to] = mixed[rows].astype(bf16)
                qkv_sum[seq] += jnp.sum(grads.astype(f32), axis=0, keepdims=True)
                return carry

            lax.fori_loop(0, blocks // 2, store, 0)
            pass_on(jobs[seq])

    heads = pltpu.VMEM((2, total_len, 128), bf16)
    pl.run_scoped(
        attend,
        pltpu.VMEM((total_len, qkv_width), f32),
        pltpu.VMEM((total_len, attn.shape[1]), f32),
        heads,
        heads,
        heads,
        heads,
        pltpu.VMEM((total_len, 128), f32),
        pltpu.VMEM((total_len, 128), f32),
    )

    def attend_parts(tile_cols, tile_out):
        feature_tiles(gqkv, qkv_part, tile_cols, jobs[5:7])
        tile_out[...] = tn(attn[...], cot[...].reshape(token_count, width)).astype(bf16)
        rows = tile_out.shape[0] // 4
        load(*((tile_out.at[pl.ds(rows * i, rows)], out_part.at[i // 2, i % 2]) for i in range(4)))
        send_beside(jobs[4])

    pl.run_scoped(
        attend_parts, pltpu.VMEM((2, 256, qkv_width), bf16), pltpu.VMEM((attn.shape[1], width), bf16)
    )

    early_sends = list(core.values()) + [cot_zl, cot_x, cot_zx, hid_zl, hid_x, hid_zx]

    def sums(fc1_w, fc2_w):
        weights = fc_weights(fc1_w, fc2_w)
        for copy in early_sends:
            copy.wait_send()
        weights[0].wait()
        multiply_groups(0, 0, gqkv, qkv_w, gup, fc1_w, nt)
        send_first(0)
        weights[1].wait()
        multiply_groups(1, 0, attn, out_w, act, fc2_w, nn)
        send_first(1)
        pass_on(jobs[2])
        finish(jobs[0])
        multiply_groups(0, 2, gqkv, qkv_w, gup, fc1_w, nt)
        multiply_groups(1, 2, attn, out_w, act, fc2_w, nn)

    pl.run_scoped(sums, *fc_scratch)
    for n in range(2):
        add_core(n, 2)
        add_core(n, 3)
    send_second(0)
    pass_on(jobs[3])
    finish(jobs[1])
    add_first(0)
    send_second(1)
    finish(jobs[2])
    pass_on(jobs[5])
    pass_on(jobs[6])
    pass_on(jobs[4])
    finish(jobs[3])
    finish_input()
    add_first(1)
    finish(jobs[5])
    finish(jobs[6])
    finish(jobs[4])
    finish_output()

    def terms_wait(k, carry):
        terms_copy(k).wait()
        return carry

    lax.fori_loop(1, 32, terms_wait, 0)
    sums_out[...] = jnp.sum(terms_got[...], axis=0)
    for copy in arrivals:
        copy.wait_recv()
    for copy in kept:
        copy.wait()
    for copy in sends:
        if not any(copy is early for early in early_sends):
            copy.wait_send()
    for g in range(4):
        core_copy(1, g).wait_send()


def main(small, tokens, cot, cosines, sines, fc2_own, out_own, fc1_spread, qkv_spread):
    bf16, f32 = jnp.bfloat16, jnp.float32
    block, width = tokens.shape
    tokens_all = 8 * block
    rows, ff_rows = out_own.shape[0], fc2_own.shape[0]
    fc1_width, qkv_width = fc1_spread.shape[2], qkv_spread.shape[2]
    half = ff_rows // 2
    any_, vmem = pl.BlockSpec(memory_space=pl.ANY), pl.BlockSpec(memory_space=pltpu.VMEM)
    shapes = [
        ((block, width), bf16, any_),
        ((block, width), bf16, any_),
        (small.shape, f32, vmem),
        ((ff_rows, width), f32, any_),
        ((rows, width), f32, any_),
        ((8, rows, fc1_width), bf16, any_),
        ((8, rows, qkv_width), bf16, any_),
        ((1, fc1_width), f32, vmem),
        ((2, 1, qkv_width), f32, vmem),
        ((32,) + small.shape, f32, vmem),
        ((2, 2, 2, 4, rows, qkv_width), bf16, any_),
        ((2, 2, rows, width), bf16, any_),
        ((2, 2, 2, 4, rows, fc1_width), bf16, any_),
        ((2, 2, ff_rows, width), bf16, any_),
        ((2, 2, ff_rows, width), bf16, any_),
        ((2, 2, 2, 4 * rows, fc1_width), bf16, any_),
        ((2, 2, rows, width), bf16, any_),
        ((2, 2, 2, 4 * rows, qkv_width), bf16, any_),
        ((2, 4, block, width), bf16, any_),
        ((2, 3, block, width), bf16, any_),
        ((3, 2, half, width), bf16, any_),
        ((3, half, width), bf16, any_),
        ((4, 2, 4 * rows, fc1_width), bf16, any_),
        ((4, 4 * rows, fc1_width), bf16, any_),
    ]
    scratch = [
        pltpu.VMEM((8, block, width), bf16),
        pltpu.VMEM((8, block, width), bf16),
        pltpu.VMEM((tokens_all, fc1_width), bf16),
        pltpu.VMEM((tokens_all, fc1_width), bf16),
        pltpu.VMEM((tokens_all, 4 * rows), bf16),
        pltpu.VMEM((tokens_all, qkv_width), bf16),
        pltpu.VMEM((2, 2, 2, 4, rows, qkv_width), bf16),
        pltpu.VMEM((2, 2, rows, width), bf16),
        pltpu.VMEM((block, width), bf16),
        pltpu.VMEM((block, width), f32),
        pltpu.VMEM((3, half, width), bf16),
        pltpu.VMEM((3, 4 * rows, fc1_width), bf16),
        pltpu.VMEM((3, half, width), bf16),
        pltpu.VMEM((4, 4 * rows, fc1_width), bf16),
        pltpu.VMEM((1, fc1_width), f32),
        pltpu.VMEM((1, qkv_width), f32),
        pltpu.VMEM((32,) + small.shape, f32),
        pltpu.VMEM((32,) + small.shape, f32),
        pltpu.SemaphoreType.DMA((96,)),
        pltpu.SemaphoreType.DMA((96,)),
        pltpu.SemaphoreType.DMA((96,)),
        pltpu.SemaphoreType.DMA((2,)),
        pltpu.SemaphoreType.DMA((2, 4)),
        pltpu.SemaphoreType.DMA((2, 4)),
        pltpu.SemaphoreType.DMA((32,)),
        pltpu.SemaphoreType.DMA((32,)),
        pltpu.SemaphoreType.DMA((32,)),
        pltpu.SemaphoreType.DMA((32,)),
    ]
    return pl.pallas_call(
        main_kernel,
        out_shape=[jax.ShapeDtypeStruct(shape, kind) for shape, kind, _ in shapes],
        in_specs=[vmem, any_, any_, vmem, vmem] + [any_] * 4,
        out_specs=[spec for _, _, spec in shapes],
        scratch_shapes=scratch,
        compiler_params=pltpu.CompilerParams(
            collective_id=0, has_side_effects=True, vmem_limit_bytes=63 * 2**20
        ),
    )(small, tokens, cot, cosines, sines, fc2_own, out_own, fc1_spread, qkv_spread)[:7]


def columns_kernel(fc1_in, qkv_in, fc1_out, qkv_out):
    f32 = jnp.float32
    unit, part_width = fc1_in.shape[2] // 4, qkv_in.shape[2] // 3
    for w in range(8):
        for t in range(4):
            at = ((t // 2 * 2 + w // 4) * 2 + t % 2) * 4 * unit + w % 4 * unit
            fc1_out[:, at : at + unit] = fc1_in[w, :, t * unit : (t + 1) * unit].astype(f32)
    low = lax.broadcasted_iota(jnp.int32, (1, 128), 1) < HEAD_DIM
    for part in range(3):
        for a in range(2):
            for dl in range(2):
                for dx in range(2):
                    at = part * part_width + a * 128
                    even, odd = (
                        qkv_in[dl * 4 + dx * 2 + k, :, at : at + 128].astype(f32) for k in range(2)
                    )
                    to = part * 8 * part_width + a * 1024 + dl * 512 + dx * 128
                    qkv_out[:, to : to + 128] = jnp.where(low, even, pltpu.roll(odd, 64, 1))
                    qkv_out[:, to + 256 : to + 384] = jnp.where(low, pltpu.roll(even, 64, 1), odd)


def plain_columns(fc1_in, qkv_in):
    _, rows, fc1_width = fc1_in.shape
    vmem = pl.BlockSpec(memory_space=pltpu.VMEM)
    return pl.pallas_call(
        columns_kernel,
        out_shape=[
            jax.ShapeDtypeStruct((rows, 8 * fc1_width), jnp.float32),
            jax.ShapeDtypeStruct((rows, 8 * qkv_in.shape[2]), jnp.float32),
        ],
        in_specs=[vmem, vmem],
        out_specs=[vmem, vmem],
        compiler_params=pltpu.CompilerParams(vmem_limit_bytes=24 * 2**20),
    )(fc1_in, qkv_in)


def split_device(
    tokens,
    lengths,
    ln_gain,
    ln_bias,
    w_qkv,
    b_qkv,
    w_out,
    b_out,
    w_fc1,
    b_fc1,
    w_fc2,
    b_fc2,
    cotangent,
):
    bf16, f32 = jnp.bfloat16, jnp.float32
    zh, zl, y, x, c = (lax.axis_index(name) for name in FINE)
    place = (zl * 2 + x) * 2 + c
    _, local_len, width = tokens.shape
    rows = w_qkv.shape[0]
    ff_rows = w_fc2.shape[0]
    pieces = 4
    total_len = local_len * pieces
    heads = 4
    own_width = heads * HEAD_DIM

    row = 2 * rows
    out_bias = b_out.astype(f32) + b_fc2.astype(f32)
    small = jnp.concatenate(
        [jnp.concatenate([ln_gain, ln_gain, ln_bias, ln_bias, b_qkv, b_out, b_fc1]).astype(f32)]
        + [out_bias, out_bias, jnp.broadcast_to(lengths.astype(f32), (row,))]
    ).reshape(-1, row)
    places = (x * 2 + c) * local_len + jnp.arange(local_len, dtype=jnp.int32)
    grad_own = jnp.where((places < lengths[0])[:, None], cotangent[0], jnp.zeros((), bf16))
    fc1_spread = (
        w_fc1.reshape((rows, 2, 2, 2, 2, 2, ff_rows))
        .transpose(2, 4, 5, 0, 1, 3, 6)
        .reshape(8, rows, -1)
    )
    qkv_spread = (
        w_qkv.reshape((rows, 3, 2, 2, 2, 2, 2, HEAD_DIM))
        .transpose(3, 5, 6, 0, 1, 2, 4, 7)
        .reshape(8, rows, -1)
    )
    cosines, sines = tables(total_len, ROT)
    grad_input, output, sums, grad_fc2, grad_wout, fc1_columns, qkv_columns = main(
        small, tokens[0], grad_own, cosines, sines, w_fc2, w_out, fc1_spread, qkv_spread
    )
    output, grad_input = output[None], grad_input[None]
    grad_wfc1, grad_wqkv = plain_columns(fc1_columns, qkv_columns)
    grad_bqkv, grad_bfc1 = sums[0:2].reshape(-1)[: 3 * rows], sums[2:4].reshape(-1)
    grad_bias, grad_gain, grad_shift = lax.dynamic_slice(sums, (4, c * rows), (3, rows))
    return (
        output,
        grad_input,
        grad_gain,
        grad_shift,
        grad_wqkv,
        grad_bqkv,
        grad_wout,
        grad_bias,
        grad_wfc1,
        grad_bfc1,
        grad_fc2,
        grad_bias,
    )


def fine_mesh(mesh):
    return jax.sharding.Mesh(mesh.devices.reshape(2, 2, 2, 2, 2), FINE)


def fine_solution(mesh):
    everyone, seqs, parts = FINE, ("zh", "zl", "y"), ("x", "c")
    placed = (
        P(seqs, parts, None),
        P(seqs),
        P(everyone),
        P(everyone),
        P(everyone, None),
        P(everyone),
        P(everyone, None),
        P(everyone),
        P(everyone, None),
        P(everyone),
        P(everyone, None),
        P(everyone),
        P(seqs, parts, None),
    )
    given = (
        P(seqs, parts, None),
        P(seqs, parts, None),
        P(everyone),
        P(everyone),
        P(everyone, None),
        P(everyone),
        P(everyone, None),
        P(everyone),
        P(everyone, None),
        P(everyone),
        P(everyone, None),
        P(everyone),
    )
    return jax.shard_map(
        split_device, mesh=fine_mesh(mesh), in_specs=placed, out_specs=given, check_vma=False
    )


def solution(mesh):
    if mesh.shape["dp"] == 8 and mesh.shape["ctx"] == 4:
        return fine_solution(mesh)
    return general_solution(mesh)
```
